32 devices in a mesh: groups: 2 (over x), patch: 16 (over z, y, core).
Axes of the slice: x: 2, y: 2, z: 4, core: 2. Of those that a mesh axis runs over, the one named last changes fastest.
Arguments:
- node_features: bfloat16 [4, 2048, 512], P('groups', 'patch'), parts along dimension 0, may hold values from -6 to 6
- out_grad: bfloat16 [4, 2048, 512], P('groups', 'patch'), parts along dimension 0, may hold values from -6 to 6
- w_query: bfloat16 [512, 512], replicated, may hold values from -0.25 to 0.25
- w_key: bfloat16 [512, 512], replicated, may hold values from -0.25 to 0.25
- w_value: bfloat16 [512, 512], replicated, may hold values from -0.25 to 0.25
- w_out: bfloat16 [512, 512], replicated, may hold values from -0.25 to 0.25
- neighbours: int32 [2048, 256], P('patch'), may hold values from 0 to 255, as said below
- neighbour_count: int32 [2048], P('patch'), may hold values from 128 to 256
- send_rows: int32 [16, 8, 16], P('patch'), may hold values from 0 to 127, as said below
Outputs:
- node_grad: bfloat16 [4, 2048, 512], P('groups', 'patch'), parts along dimension 0
- weight_grad: float32 [1024, 2048], P(('groups', 'patch')), parts along dimension 0
The draws below stay inside these ranges and needn't reach their ends.
There are 2 independent parts, one for each index of `groups`. The reference program is written for one: setup_inputs(seed, part) draws one part's arguments, and reference() takes and returns one part's arrays. A program takes and returns all parts, laid end to end along the dimension named above; an argument that names none is the same for every part. Nothing has to cross between parts.
Inputs may be any that keep to these rules, and one draw needn't show every extreme that they name: Each row holds 256 distinct columns of its patch's extended table; only the first neighbour_count entries are neighbours. `send_rows`: entry [q, k, s] is a row of patch q's block of nodes; the 16 rows for one pair (q, k) are distinct.
All inputs are finite; a program needn't handle non-finite values.
Results may differ from the reference program's by a relative error of at most 0.0086.
Values may be sent and summed in bfloat16 or wider, within the bound.
No kernel may reach another device: no remote copies, remote signals or barrier semaphores. Data moves between devices by JAX's collectives and lax.ppermute only.
A program may use at most 64 MiB of HBM per device.

```python
import math
import jax
import jax.numpy as jnp
from jax import lax

D = 512
HEADS = 16
NEIGH = 256
ADJ = 8
MEMBERS = 2
NODE_DEV = 128
HALO_CAP = 16
PCOLS = 4
NODES = 2048
EXT = 256
N_PATCH = 16


cell_span = 256


def node_positions(key):
    return jax.random.randint(jax.random.fold_in(key, 101), (NODES, 2), 0, cell_span, dtype=jnp.int32)


def direction_steps():
    steps_x = jnp.array([1, -1, 0, 0, -1, 1, 1, -1], dtype=jnp.int32)
    steps_y = jnp.array([0, 0, 1, -1, 1, -1, 1, -1], dtype=jnp.int32)
    return (steps_x, steps_y)


def halo_lists(positions):
    steps_x, steps_y = direction_steps()
    coords = positions.reshape(N_PATCH, 1, NODE_DEV, 2)
    coord_x = coords[..., 0]
    coord_y = coords[..., 1]
    step_x = steps_x[None, :, None]
    step_y = steps_y[None, :, None]
    gap_x = jnp.where(step_x == 1, cell_span - coord_x, jnp.where(step_x == -1, coord_x + 1, 0))
    gap_y = jnp.where(step_y == 1, cell_span - coord_y, jnp.where(step_y == -1, coord_y + 1, 0))
    row_ids = jnp.arange(NODE_DEV, dtype=jnp.int32)[None, None, :]
    scores = (gap_x * gap_x + gap_y * gap_y) * NODE_DEV + row_ids
    first = (jnp.arange(N_PATCH, dtype=jnp.int32)[:, None, None] == 0) & (jnp.arange(ADJ, dtype=jnp.int32)[None, :, None] == 0)
    scores = jnp.where(first & (row_ids == NODE_DEV - 1), -2, jnp.where(first & (row_ids == 0), -1, scores))
    return jnp.argsort(scores, axis=2, stable=True)[:, :, :HALO_CAP].astype(jnp.int32)


def draw_send_rows(key, part):
    positions = node_positions(key)
    return halo_lists(positions)


def draw_neighbours(key, part):
    positions = node_positions(key)
    sent = halo_lists(positions)
    steps_x, steps_y = direction_steps()
    offsets = steps_x + PCOLS * steps_y
    patch_ids = jnp.arange(N_PATCH, dtype=jnp.int32)
    senders = jnp.mod(patch_ids[:, None] - offsets[None, :], N_PATCH).astype(jnp.int32)
    chosen = sent[senders, jnp.arange(ADJ, dtype=jnp.int32)[None, :]]
    halo_pos = positions[senders[:, :, None] * NODE_DEV + chosen]
    moved = jnp.stack([steps_x, steps_y], axis=-1) * cell_span
    halo_pos = halo_pos - moved[None, :, None, :]
    table = jnp.concatenate([positions.reshape(N_PATCH, NODE_DEV, 2), halo_pos.reshape(N_PATCH, ADJ * HALO_CAP, 2)], axis=1)
    delta = positions.reshape(N_PATCH, NODE_DEV, 1, 2) - table[:, None, :, :]
    dist = jnp.sum(delta * delta, axis=-1)
    column_ids = jnp.arange(EXT, dtype=jnp.int32)[None, None, :]
    scores = dist * EXT + column_ids
    leading = (jnp.arange(NODE_DEV, dtype=jnp.int32) == 0)[None, :, None]
    scores = jnp.where(leading & (column_ids == EXT - 1), -2, jnp.where(leading & (column_ids == 0), -1, scores))
    ordered = jnp.argsort(scores, axis=2, stable=True)[:, :, :NEIGH]
    return ordered.reshape(NODES, NEIGH).astype(jnp.int32)


def draw_neighbour_count(key, part):
    key = jax.random.fold_in(key, 12)
    counts = jax.random.randint(key, (NODES,), NEIGH // 2, NEIGH + 1, dtype=jnp.int32)
    leading = jnp.arange(NODES, dtype=jnp.int32) % NODE_DEV == 0
    return jnp.where(leading, NEIGH, counts).astype(jnp.int32)


def with_spikes(entries, key, source, target, blocks, factor):
    def block_of(dim):
        return (jnp.arange(entries.shape[dim]) // (entries.shape[dim] // blocks)).reshape((-1,) + (1,) * (entries.ndim - 1 - dim))

    first = jax.random.permutation(key, blocks)[block_of(target)]
    second = (block_of(target) + blocks // 2) % blocks
    return jnp.where((block_of(source) == first) | (block_of(source) == second), factor * entries, entries)


def block_scale(stream_key, extent, split, low, high):
    def one(position, shards_of):
        steps = jax.random.uniform(jax.random.fold_in(jax.random.fold_in(stream_key, 6), position), (shards_of,), jnp.float32, low / len(split), high / len(split))
        return jnp.repeat(jnp.exp(steps), extent[position] // shards_of).reshape((-1,) + (1,) * (len(extent) - position - 1))

    loudness = one(*split[0])
    for cut in split[1:]:
        loudness = loudness * one(*cut)
    return loudness


def centred(own_key, shape, width, limit, shards=(), kind=jnp.bfloat16):
    drawn = width * jax.random.normal(own_key, shape, jnp.float32)
    if shards:
        drawn = drawn * block_scale(own_key, shape, shards, -0.22, 0.18)
    return jnp.clip(drawn, -limit, limit).astype(kind)


def noise_with(rng, extent, deviation, limit, pieces, heavy, kind=jnp.bfloat16):
    entries = deviation * jax.random.normal(rng, extent, jnp.float32)
    if pieces:
        entries = entries * block_scale(rng, extent, pieces, -0.22, 0.18)
    return jnp.clip(with_spikes(entries, jax.random.fold_in(rng, 3), *heavy), -limit, limit).astype(kind)


def setup_inputs(seed: int = 0, part: int = 0) -> dict:
    keys = jax.random.split(jax.random.key(seed), 10)
    part_keys = jax.random.split(jax.random.fold_in(keys[9], part), 10)
    node_features = noise_with(part_keys[0], (MEMBERS, NODES, D), 1.0, 6.0, ((1, 16),), (1, 2, 16, 2.0))
    out_grad = centred(part_keys[1], (MEMBERS, NODES, D), 1.0, 6.0, ((1, 16),))
    w_query = centred(keys[2], (D, D), D ** -0.5, 0.25)
    w_key = centred(keys[3], (D, D), D ** -0.5, 0.25)
    w_value = centred(keys[4], (D, D), D ** -0.5, 0.25)
    w_out = centred(keys[5], (D, D), D ** -0.5, 0.25)
    neighbours = draw_neighbours(jax.random.fold_in(keys[9], 71), part)
    neighbour_count = draw_neighbour_count(jax.random.fold_in(keys[9], 71), part)
    send_rows = draw_send_rows(jax.random.fold_in(keys[9], 71), part)
    return {"node_features": node_features, "out_grad": out_grad, "w_query": w_query, "w_key": w_key, "w_value": w_value, "w_out": w_out, "neighbours": neighbours, "neighbour_count": neighbour_count, "send_rows": send_rows}


score_cap = 5.0

def times_transpose(left_rows, weight):
    return jnp.dot(left_rows, weight.T, preferred_element_type=jnp.float32)

def column_nodes(send_rows, patch_index):
    local_part = patch_index * NODE_DEV + jnp.arange(NODE_DEV, dtype=jnp.int32)
    offsets = jnp.array([1, -1, PCOLS, -PCOLS, PCOLS - 1, 1 - PCOLS, PCOLS + 1, -PCOLS - 1], dtype=jnp.int32)
    senders = jnp.mod(patch_index - offsets, N_PATCH).astype(jnp.int32)
    chosen = send_rows[senders, jnp.arange(ADJ, dtype=jnp.int32)]
    halo_part = (senders[:, None] * NODE_DEV + chosen).reshape(-1)
    return jnp.concatenate([local_part, halo_part.astype(jnp.int32)]).astype(jnp.int32)

def build_mask(neighbours, neighbour_count, table_size):
    node_rows = neighbours.shape[0]
    is_valid = jnp.arange(neighbours.shape[1], dtype=jnp.int32)[None, :] < neighbour_count[:, None]
    target = jnp.where(is_valid, neighbours, table_size)
    row_index = jnp.broadcast_to(jnp.arange(node_rows, dtype=jnp.int32)[:, None], neighbours.shape)
    return jnp.zeros((node_rows, table_size), jnp.float32).at[row_index, target].set(1.0, mode='drop')

def widen(values):
    return lax.optimization_barrier(values).astype(jnp.float32)

def member_backward(query_rows, key_table, value_table, grad_rows, neighbour_mask):
    node_rows = query_rows.shape[0]
    table_size = key_table.shape[0]
    head_size = D // HEADS
    query_heads = widen(query_rows).reshape(node_rows, HEADS, head_size)
    key_heads = widen(key_table).reshape(table_size, HEADS, head_size)
    value_heads = widen(value_table).reshape(table_size, HEADS, head_size)
    grad_heads = widen(grad_rows).reshape(node_rows, HEADS, head_size)
    raw_scores = jnp.einsum('rhd,chd->hrc', query_heads, key_heads) / math.sqrt(head_size)
    capped = score_cap * jnp.tanh(raw_scores / score_cap)
    score_exp = jnp.exp(capped) * neighbour_mask[None]
    attn_prob = score_exp / lax.optimization_barrier(jnp.sum(score_exp, axis=-1, keepdims=True))
    attn_prob_b = attn_prob.astype(jnp.bfloat16)
    prob_wide = widen(attn_prob_b)
    attended = jnp.einsum('hrc,chd->rhd', prob_wide, value_heads).reshape(node_rows, D).astype(jnp.bfloat16)
    prob_grad = jnp.einsum('rhd,chd->hrc', grad_heads, value_heads)
    row_inner = lax.optimization_barrier(jnp.sum(attn_prob * prob_grad, axis=-1, keepdims=True))
    slope = 1.0 - capped / score_cap * (capped / score_cap)
    score_grad = (attn_prob * (prob_grad - row_inner) * slope / math.sqrt(head_size)).astype(jnp.bfloat16)
    grad_wide = widen(score_grad)
    d_query = jnp.einsum('hrc,chd->rhd', grad_wide, key_heads).reshape(node_rows, D).astype(jnp.bfloat16)
    d_key = jnp.einsum('hrc,rhd->chd', grad_wide, query_heads).reshape(table_size, D).astype(jnp.bfloat16)
    d_value = jnp.einsum('hrc,rhd->chd', prob_wide, grad_heads).reshape(table_size, D).astype(jnp.bfloat16)
    return (attended, d_query, d_key, d_value)

def reference(node_features, out_grad, w_query, w_key, w_value, w_out, neighbours, neighbour_count, send_rows):
    flat_nodes = node_features.reshape(MEMBERS * NODES, D)

    def project(weight):
        return jnp.dot(flat_nodes, weight, preferred_element_type=jnp.float32).astype(jnp.bfloat16).reshape(MEMBERS, NODES, D)
    query_all = project(w_query)
    key_all = project(w_key)
    value_all = project(w_value)
    grad_all = times_transpose(out_grad.reshape(MEMBERS * NODES, D), w_out).astype(jnp.bfloat16).reshape(MEMBERS, NODES, D)
    table_size = NODE_DEV + ADJ * HALO_CAP

    def one_patch(carried, patch_index):
        node_acc, weight_acc = carried
        table_nodes = column_nodes(send_rows, patch_index)
        first_node = patch_index * NODE_DEV
        neighbour_mask = build_mask(lax.dynamic_slice_in_dim(neighbours, first_node, NODE_DEV, 0), lax.dynamic_slice_in_dim(neighbour_count, first_node, NODE_DEV, 0), table_size)
        local_query = lax.dynamic_slice_in_dim(query_all, first_node, NODE_DEV, 1)
        local_grad = lax.dynamic_slice_in_dim(grad_all, first_node, NODE_DEV, 1)
        results = [member_backward(local_query[member], key_all[member][table_nodes], value_all[member][table_nodes], local_grad[member], neighbour_mask) for member in range(MEMBERS)]
        attended = jnp.concatenate([result[0] for result in results], axis=0)
        query_grad = jnp.concatenate([result[1] for result in results], axis=0)
        key_grad = jnp.concatenate([result[2] for result in results], axis=0)
        value_grad = jnp.concatenate([result[3] for result in results], axis=0)
        local_x = lax.dynamic_slice_in_dim(node_features, first_node, NODE_DEV, 1).reshape(MEMBERS * NODE_DEV, D)
        local_out = lax.dynamic_slice_in_dim(out_grad, first_node, NODE_DEV, 1).reshape(MEMBERS * NODE_DEV, D)
        table_x = node_features[:, table_nodes].reshape(MEMBERS * table_size, D)
        node_acc = node_acc.at[:, table_nodes[:NODE_DEV]].add(times_transpose(query_grad, w_query).reshape(MEMBERS, NODE_DEV, D))
        spread = times_transpose(key_grad, w_key) + times_transpose(value_grad, w_value)
        node_acc = node_acc.at[:, table_nodes].add(spread.reshape(MEMBERS, table_size, D))
        weight_terms = jnp.concatenate([jnp.dot(local_x.T, query_grad, preferred_element_type=jnp.float32), jnp.dot(table_x.T, key_grad, preferred_element_type=jnp.float32), jnp.dot(table_x.T, value_grad, preferred_element_type=jnp.float32), jnp.dot(attended.T, local_out, preferred_element_type=jnp.float32)], axis=1)
        return ((node_acc, weight_acc + weight_terms), None)
    initial = (jnp.zeros((MEMBERS, NODES, D), jnp.float32), jnp.zeros((D, 4 * D), jnp.float32))
    finals = lax.scan(one_patch, initial, jnp.arange(N_PATCH, dtype=jnp.int32))[0]
    return (finals[0].astype(jnp.bfloat16), finals[1])
```

```python
import functools
import math

import jax
import jax.numpy as jnp
from jax import lax
from jax.experimental import pallas as pl
from jax.experimental.pallas import tpu as pltpu
from jax.sharding import PartitionSpec as P

HEADS = 16
score_cap = 5.0
VMEM = pltpu.CompilerParams(vmem_limit_bytes=56 * 1024 * 1024)
f32 = jnp.float32
bf16 = jnp.bfloat16


def nn(a, b):
    return lax.dot_general(a, b, (((1,), (0,)), ((), ())), preferred_element_type=f32)


def nt(a, b):
    return lax.dot_general(a, b, (((1,), (1,)), ((), ())), preferred_element_type=f32)


def shifted(shard, by):
    count = lax.axis_size("patch")
    return lax.ppermute(shard, "patch", [(i, (i + by) % count) for i in range(count)])


def sent_selector(send_rows, node_rows):
    adjacent, slots = send_rows.shape
    halo = adjacent * slots
    wide = jnp.concatenate([send_rows] * adjacent, axis=1)
    own = lax.broadcasted_iota(jnp.int32, (adjacent, halo), 1) // slots == lax.broadcasted_iota(
        jnp.int32, (adjacent, halo), 0
    )
    ids = jnp.sum(jnp.where(own, wide, 0), axis=0, keepdims=True)
    nodes = lax.broadcasted_iota(jnp.int32, (node_rows, halo), 0)
    return jnp.where(nodes == ids, 1.0, 0.0).astype(f32)


def gather_kernel(slots, send_ref, x_ref, plus_ref, minus_ref, right_ref, left_ref):
    members, node_rows, _ = x_ref.shape
    pick = sent_selector(send_ref[0], node_rows).T.astype(bf16)
    for m in range(members):
        rows = nn(pick, x_ref[m]).astype(bf16)

        def part(k):
            return rows[k * slots : (k + 1) * slots]

        for i, k in enumerate((2, 6, 4)):
            plus_ref[m, i] = part(k)
        for i, k in enumerate((3, 5, 7)):
            minus_ref[m, i] = part(k)
        right_ref[m, 0] = part(0)
        left_ref[m, 0] = part(1)


def local_kernel(
    x_ref, og_ref, wq_ref, wk_ref, wv_ref, wo_ref, neigh_ref, count_ref,
    q_ref, qt_ref, k_ref, kt_ref, v_ref, vt_ref, g_ref, gt_ref, xt_ref, mask_ref,
):
    members, node_rows, width = x_ref.shape
    groups = width // 128
    x = x_ref[...].reshape(members * node_rows, width)
    og = og_ref[...].reshape(members * node_rows, width)

    def put(rows, nat_ref, t_ref):
        for m in range(members):
            for g in range(groups):
                block = rows[m * node_rows : (m + 1) * node_rows, g * 128 : (g + 1) * 128]
                nat_ref[m, g] = block
                t_ref[m, g] = block.T

    put(nn(x, wq_ref[...]).astype(bf16), q_ref, qt_ref)
    put(nn(x, wk_ref[...]).astype(bf16), k_ref, kt_ref)
    put(nn(x, wv_ref[...]).astype(bf16), v_ref, vt_ref)
    put(nt(og, wo_ref[...]).astype(bf16), g_ref, gt_ref)
    for m in range(members):
        xt_ref[m] = x_ref[m].T

    neigh = neigh_ref[...].T
    slots = neigh.shape[0]
    table = mask_ref.shape[0]
    order = lax.broadcasted_iota(jnp.int32, neigh.shape, 0)
    tail = jnp.where(order >= count_ref[...], neigh, -1)[slots // 2 :]
    half = table // 2
    for part in range(2):
        columns = lax.broadcasted_iota(jnp.int32, (half, node_rows), 0) + part * half
        kept = jnp.ones((half, node_rows), f32)
        for j in range(slots // 2):
            kept = jnp.where(tail[j : j + 1] == columns, 0.0, kept)
        mask_ref[part * half : (part + 1) * half] = kept


def attention_kernel(
    me_ref, x_ref, og_ref, xt_ref, q_ref, qt_ref, k_ref, kt_ref, v_ref, vt_ref, g_ref, gt_ref, mask_ref,
    plus_ref, minus_ref, right_ref, left_ref, wq_ref, wk_ref, wv_ref,
    keep_ref, send_ref, node_ref, back_left_ref, back_right_ref, back_minus_ref, back_plus_ref,
    kf, ktf, vf, vtf, xtf, att, dq, dk, dv, score, grad, dw,
):
    members, node_rows, width = x_ref.shape
    groups = width // 128
    slots = plus_ref.shape[2]
    table = mask_ref.shape[0]
    head = width // HEADS
    per = 128 // head
    scale = 1.0 / math.sqrt(head)

    for m in range(members):
        pieces = [None] * 8
        for ref, order in (
            (right_ref, (0, 6, 5)),
            (left_ref, (1, 4, 7)),
            (plus_ref, (2,)),
            (minus_ref, (3,)),
        ):
            for i, k in enumerate(order):
                pieces[k] = ref[m, i]
        halo = jnp.concatenate(pieces, axis=0)
        xtf[m, :, :node_rows] = xt_ref[m]
        xtf[m, :, node_rows:] = halo.T
        for w_ref, nat, trans, lnat, ltrans in (
            (wk_ref, kf, ktf, k_ref, kt_ref),
            (wv_ref, vf, vtf, v_ref, vt_ref),
        ):
            rows = nn(halo, w_ref[...]).astype(bf16)
            for g in range(groups):
                block = rows[:, g * 128 : (g + 1) * 128]
                nat[m, g, :node_rows] = lnat[m, g]
                nat[m, g, node_rows:] = block
                trans[m, g, :, :node_rows] = ltrans[m, g]
                trans[m, g, :, node_rows:] = block.T

    row_head = lax.broadcasted_iota(jnp.int32, (128, node_rows), 0) // head
    lane_head = lax.broadcasted_iota(jnp.int32, (node_rows, 128), 1) // head

    def spread_t(block):
        zero = jnp.zeros_like(block)
        return jnp.concatenate([jnp.where(row_head == h, block, zero) for h in range(per)], axis=1)

    def spread_n(block):
        zero = jnp.zeros_like(block)
        return jnp.concatenate([jnp.where(lane_head == h, block, zero) for h in range(per)], axis=0)

    strip = 64

    def step(i, _):
        m = i // groups
        g = i % groups
        kg, vg = kf[m, g], vf[m, g]
        score[...] = nn(kg, spread_t(qt_ref[m, g]))
        grad[...] = nn(vg, spread_t(gt_ref[m, g]))
        probs = []
        slopes = []
        for h in range(per):
            lanes = slice(h * node_rows, (h + 1) * node_rows)
            den = jnp.zeros((8, node_rows), f32)
            inner = jnp.zeros((8, node_rows), f32)
            for c in range(0, table, strip):
                t = jnp.tanh(score[c : c + strip, lanes] * (scale / score_cap))
                e = jnp.exp(t * score_cap) * mask_ref[c : c + strip]
                den = den + jnp.sum(e.reshape(strip // 8, 8, node_rows), axis=0)
                inner = inner + jnp.sum(
                    (e * grad[c : c + strip, lanes]).reshape(strip // 8, 8, node_rows), axis=0
                )
                score[c : c + strip, lanes] = e
                slopes.append(e * (scale - scale * (t * t)))
            r = 1.0 / jnp.sum(den, axis=0, keepdims=True)
            inner = jnp.sum(inner, axis=0, keepdims=True) * r
            column = []
            scores = []
            for j, c in enumerate(range(0, table, strip)):
                column.append((score[c : c + strip, lanes] * r).astype(bf16))
                w = slopes[h * (table // strip) + j]
                scores.append(((w * r) * (grad[c : c + strip, lanes] - inner)).astype(bf16))
            probs.append((jnp.concatenate(column, axis=0), jnp.concatenate(scores, axis=0)))
        pb = jnp.concatenate([p for p, _ in probs], axis=1)
        ds = jnp.concatenate([s for _, s in probs], axis=1)
        ktg, vtg = ktf[m, g], vtf[m, g]
        for h in range(0, per, 2):
            lanes = slice(h * node_rows, (h + 2) * node_rows)
            rows = slice(h * head, (h + 2) * head)
            a = nn(vtg[rows], pb[:, lanes])
            b = nn(ktg[rows], ds[:, lanes])
            for j in range(2):
                inside = (slice(j * head, (j + 1) * head), slice(j * node_rows, (j + 1) * node_rows))
                att[m, g, (h + j) * head : (h + j + 1) * head, :] = a[inside].astype(bf16)
                dq[m, g, (h + j) * head : (h + j + 1) * head, :] = b[inside].astype(bf16)
        dk[m, g] = nn(ds, spread_n(q_ref[m, g])).astype(bf16)
        dv[m, g] = nn(pb, spread_n(g_ref[m, g])).astype(bf16)
        return 0

    lax.fori_loop(0, members * groups, step, 0)

    def whole(ref, m):
        return jnp.concatenate([ref[m, g] for g in range(groups)], axis=1)

    blocks, rows = dw.shape[0] * 2, dw.shape[2]
    c = me_ref[0] % 2
    dqs = [jnp.concatenate([dq[m, g].T for g in range(groups)], axis=1) for m in range(members)]
    dks = [whole(dk, m) for m in range(members)]
    dvs = [whole(dv, m) for m in range(members)]
    atts = [att[m].reshape(width, node_rows) for m in range(members)]

    def emit(n, pairs):
        total = None
        for a, b in pairs:
            term = nn(a, b)
            total = term if total is None else total + term
        dw[...] = total.reshape(blocks // 2, 2, rows, width)
        lanes = slice(n * width, (n + 1) * width)
        keep_ref[:, :, lanes] = dw[:, pl.ds(c, 1)][:, 0]
        send_ref[:, :, lanes] = dw[:, pl.ds(1 - c, 1)][:, 0].astype(bf16)

    emit(0, [(xt_ref[m], dqs[m]) for m in range(members)])
    emit(1, [(xtf[m], dks[m]) for m in range(members)])
    emit(2, [(xtf[m], dvs[m]) for m in range(members)])
    emit(3, [(atts[m], og_ref[m]) for m in range(members)])
    for m in range(members):
        spread = nt(dks[m], wk_ref[...]) + nt(dvs[m], wv_ref[...])
        node_ref[m] = spread[:node_rows] + nt(dqs[m], wq_ref[...])
        halo = spread[node_rows:].astype(bf16)
        for ref, order in (
            (back_left_ref, (0, 6, 5)),
            (back_right_ref, (1, 4, 7)),
            (back_minus_ref, (2,)),
            (back_plus_ref, (3,)),
        ):
            for i, k in enumerate(order):
                ref[m, i] = halo[k * slots : (k + 1) * slots]


def finish_kernel(send_ref, node_ref, left_ref, right_ref, minus_ref, plus_ref, out_ref):
    members, node_rows, _ = node_ref.shape
    pick = sent_selector(send_ref[0], node_rows).astype(bf16)
    for m in range(members):
        pieces = [None] * 8
        for ref, order in (
            (left_ref, (0,)),
            (right_ref, (1,)),
            (minus_ref, (2, 6, 4)),
            (plus_ref, (3, 5, 7)),
        ):
            for i, k in enumerate(order):
                pieces[k] = ref[m, i]
        arriving = jnp.concatenate(pieces, axis=0)
        out_ref[m] = (node_ref[m] + nn(pick, arriving)).astype(bf16)


def call(kernel, outs, scratch=(), smem=0, cost=None):
    return pl.pallas_call(
        kernel,
        out_shape=[jax.ShapeDtypeStruct(*o) for o in outs],
        scratch_shapes=list(scratch),
        compiler_params=VMEM,
        cost_estimate=cost,
        **smem_specs(smem),
    )


def smem_specs(count):
    if not count:
        return {}
    return {
        "in_specs": [pl.BlockSpec(memory_space=pltpu.SMEM)]
        + [pl.BlockSpec(memory_space=pltpu.VMEM)] * count
    }


def scatter_sum(keep, received, me, count):
    stride, left = 2, count // 2
    while left > 1:
        radix = 2 if stride == 2 or left % 4 else 4
        total = (keep + received.astype(f32)) if received is not None else keep
        view = total.reshape(left // radix, radix, *total.shape[1:])
        digit = (me // stride) % radix
        own = lax.dynamic_index_in_dim(view, digit, 1, keepdims=False)
        arrived = []
        for k in range(1, radix):
            outgoing = lax.dynamic_index_in_dim(
                view, (digit + k) % radix, 1, keepdims=False
            ).astype(bf16)
            pairs = []
            for i in range(count):
                d = (i // stride) % radix
                pairs.append((i, i + ((d + k) % radix - d) * stride))
            arrived.append(lax.ppermute(outgoing, "patch", pairs))
        keep = own
        for a in arrived:
            keep = keep + a.astype(f32)
        received = None
        stride, left = stride * radix, left // radix
    return keep


def body(
    node_features, out_grad, w_query, w_key, w_value, w_out, neighbours, neighbour_count, send_rows
):
    members, node_rows, width = node_features.shape
    count = lax.axis_size("patch")
    row_width = min(8, count // 4)
    _, adjacent, slots = send_rows.shape
    table = node_rows + adjacent * slots
    groups = width // 128
    me = lax.axis_index("patch")
    three = ((members, 3, slots, width), bf16)
    one = ((members, 1, slots, width), bf16)

    to_plus, to_minus, own_right, own_left = call(
        functools.partial(gather_kernel, slots), [three, three, one, one]
    )(send_rows, node_features)
    plus = shifted(to_plus, row_width)
    minus = shifted(to_minus, -row_width)
    right = shifted(jnp.concatenate([own_right, plus[:, 1:2], minus[:, 1:2]], axis=1), 1)
    left = shifted(jnp.concatenate([own_left, plus[:, 2:3], minus[:, 2:3]], axis=1), -1)

    nat = ((members, groups, node_rows, 128), bf16)
    trans = ((members, groups, 128, node_rows), bf16)
    q, qt, k, kt, v, vt, g, gt, xt, mask = call(
        local_kernel,
        [nat, trans] * 4 + [((members, width, node_rows), bf16), ((table, node_rows), f32)],
        cost=pl.CostEstimate(flops=10**9, bytes_accessed=6 * 10**6, transcendentals=0),
    )(
        node_features, out_grad, w_query, w_key, w_value, w_out, neighbours,
        neighbour_count.reshape(1, node_rows),
    )

    blocks, rows = count // 2, width // count
    keep, send, node, back_left, back_right, back_minus, back_plus = call(
        attention_kernel,
        [
            ((blocks, rows, 4 * width), f32),
            ((blocks, rows, 4 * width), bf16),
            ((members, node_rows, width), f32),
            three, three, one, one,
        ],
        scratch=[
            pltpu.VMEM((members, groups, table, 128), bf16),
            pltpu.VMEM((members, groups, 128, table), bf16),
            pltpu.VMEM((members, groups, table, 128), bf16),
            pltpu.VMEM((members, groups, 128, table), bf16),
            pltpu.VMEM((members, width, table), bf16),
            pltpu.VMEM((members, groups, 128, node_rows), bf16),
            pltpu.VMEM((members, groups, 128, node_rows), bf16),
            pltpu.VMEM((members, groups, table, 128), bf16),
            pltpu.VMEM((members, groups, table, 128), bf16),
            pltpu.VMEM((table, 512), f32),
            pltpu.VMEM((table, 512), f32),
            pltpu.VMEM((blocks, 2, rows, width), f32),
        ],
        smem=19,
        cost=pl.CostEstimate(flops=3 * 10**9, bytes_accessed=10**7, transcendentals=2 * 10**6),
    )(
        me.reshape(1), node_features, out_grad, xt, q, qt, k, kt, v, vt, g, gt, mask,
        plus, minus, right, left, w_query, w_key, w_value,
    )

    received = lax.ppermute(send, "patch", [(i, i ^ 1) for i in range(count)])
    from_right = shifted(back_left, -1)
    from_left = shifted(back_right, 1)
    weight_grad = scatter_sum(keep, received, me, count)
    from_plus = shifted(
        jnp.concatenate([back_minus, from_right[:, 1:2], from_left[:, 1:2]], axis=1), -row_width
    )
    from_minus = shifted(
        jnp.concatenate([back_plus, from_right[:, 2:3], from_left[:, 2:3]], axis=1), row_width
    )
    (node_grad,) = call(finish_kernel, [((members, node_rows, width), bf16)])(
        send_rows, node, from_right[:, :1], from_left[:, :1], from_plus, from_minus
    )
    return (node_grad, weight_grad.reshape(rows, 4 * width))


def solution(mesh):
    in_specs = (
        P("groups", "patch", None),
        P("groups", "patch", None),
        P(),
        P(),
        P(),
        P(),
        P("patch", None),
        P("patch"),
        P("patch", None, None),
    )
    out_specs = (P("groups", "patch", None), P(("groups", "patch"), None))
    return jax.shard_map(body, mesh=mesh, in_specs=in_specs, out_specs=out_specs, check_vma=False)
```

```python
import functools
import math

import jax
import jax.numpy as jnp
from jax import lax
from jax.experimental import pallas as pl
from jax.experimental.pallas import tpu as pltpu
from jax.sharding import PartitionSpec as P

HEADS = 16
score_cap = 5.0
MIB = 1024 * 1024
f32 = jnp.float32
bf16 = jnp.bfloat16


def nn(a, b):
    return lax.dot_general(a, b, (((1,), (0,)), ((), ())), preferred_element_type=f32)


def nt(a, b):
    return lax.dot_general(a, b, (((1,), (1,)), ((), ())), preferred_element_type=f32)


def shifted(shard, by):
    count = lax.axis_size("patch")
    return lax.ppermute(shard, "patch", [(i, (i + by) % count) for i in range(count)])


def sent_selector(send_rows, node_rows):
    adjacent, slots = send_rows.shape
    halo = adjacent * slots
    wide = jnp.concatenate([send_rows] * adjacent, axis=1)
    own = lax.broadcasted_iota(jnp.int32, (adjacent, halo), 1) // slots == lax.broadcasted_iota(
        jnp.int32, (adjacent, halo), 0
    )
    ids = jnp.sum(jnp.where(own, wide, 0), axis=0, keepdims=True)
    nodes = lax.broadcasted_iota(jnp.int32, (node_rows, halo), 0)
    return jnp.where(nodes == ids, 1.0, 0.0).astype(f32)


def gather_kernel(slots, send_ref, x_ref, plus_ref, minus_ref, right_ref, left_ref):
    members, node_rows, _ = x_ref.shape
    pick = sent_selector(send_ref[0], node_rows).T.astype(bf16)
    for m in range(members):
        rows = nn(pick, x_ref[m]).astype(bf16)

        def part(k):
            return rows[k * slots : (k + 1) * slots]

        for i, k in enumerate((2, 6, 4)):
            plus_ref[m, i] = part(k)
        for i, k in enumerate((3, 5, 7)):
            minus_ref[m, i] = part(k)
        right_ref[m, 0] = part(0)
        left_ref[m, 0] = part(1)


def relay_kernel(after_ref, own_a, own_b, plus_ref, minus_ref, a_ref, b_ref):
    a_ref[:, 0:1] = own_a[...]
    a_ref[:, 1:2] = plus_ref[:, 1:2]
    a_ref[:, 2:3] = minus_ref[:, 1:2]
    b_ref[:, 0:1] = own_b[...]
    b_ref[:, 1:2] = plus_ref[:, 2:3]
    b_ref[:, 2:3] = minus_ref[:, 2:3]


def back_relay_kernel(after_ref, own_minus, own_plus, right_ref, left_ref, minus_ref, plus_ref):
    minus_ref[:, 0:1] = own_minus[...]
    minus_ref[:, 1:2] = right_ref[:, 1:2]
    minus_ref[:, 2:3] = left_ref[:, 1:2]
    plus_ref[:, 0:1] = own_plus[...]
    plus_ref[:, 1:2] = right_ref[:, 2:3]
    plus_ref[:, 2:3] = left_ref[:, 2:3]


Q, K, V, G, QT, KT, VT, GT = range(8)


def local_kernel(after_ref, x_ref, og_ref, wq_ref, wk_ref, wv_ref, wo_ref, *out_refs):
    loc_refs, xt_ref = out_refs[:-1], out_refs[-1]
    members, node_rows, width = x_ref.shape
    x = x_ref[...].reshape(members * node_rows, width)
    og = og_ref[...].reshape(members * node_rows, width)

    def put(rows, kind):
        for m in range(members):
            for g, ref in enumerate(loc_refs):
                block = rows[m * node_rows : (m + 1) * node_rows, g * 128 : (g + 1) * 128]
                ref[kind, m] = block
                ref[kind + 4, m] = block.T

    put(nn(x, wq_ref[...]).astype(bf16), Q)
    put(nn(x, wk_ref[...]).astype(bf16), K)
    put(nn(x, wv_ref[...]).astype(bf16), V)
    put(nt(og, wo_ref[...]).astype(bf16), G)
    for m in range(members):
        xt_ref[m] = x_ref[m].T


def mask_kernel(after_ref, neigh_ref, count_ref, mask_ref):
    neigh = neigh_ref[...].T
    slots, node_rows = neigh.shape
    table = mask_ref.shape[0]
    order = lax.broadcasted_iota(jnp.int32, neigh.shape, 0)
    tail = jnp.where(order >= count_ref[...], neigh, -1)[slots // 2 :]
    half = table // 2
    for part in range(2):
        columns = lax.broadcasted_iota(jnp.int32, (half, node_rows), 0) + part * half
        kept = jnp.ones((half, node_rows), f32)
        for j in range(slots // 2):
            kept = jnp.where(tail[j : j + 1] == columns, 0.0, kept)
        mask_ref[part * half : (part + 1) * half] = kept


def halo_kernel(plus_ref, minus_ref, right_ref, left_ref, xt_ref, wk_ref, wv_ref, *out_refs):
    halo_refs, xtf_ref = out_refs[:-1], out_refs[-1]
    members, _, node_rows = xt_ref.shape
    for m in range(members):
        pieces = [None] * 8
        for ref, order in (
            (right_ref, (0, 6, 5)),
            (left_ref, (1, 4, 7)),
            (plus_ref, (2,)),
            (minus_ref, (3,)),
        ):
            for i, k in enumerate(order):
                pieces[k] = ref[m, i]
        halo = jnp.concatenate(pieces, axis=0)
        xtf_ref[m, :, :node_rows] = xt_ref[m]
        xtf_ref[m, :, node_rows:] = halo.T
        for kind, w_ref in enumerate((wk_ref, wv_ref)):
            rows = nn(halo, w_ref[...]).astype(bf16)
            for g, ref in enumerate(halo_refs):
                block = rows[:, g * 128 : (g + 1) * 128]
                ref[kind, m] = block
                ref[kind + 2, m] = block.T


def attention_kernel(
    extra, me_ref, *refs,
):
    refs = refs[extra:]
    loc, halo, mask_ref, xtf, og_ref = refs[:5]
    own_ref, other_ref, send_ref, dq_ref, dk_ref, dv_ref = refs[5:11]
    score, grad, slope, dw, wos = refs[11:]
    _, members, node_rows, _ = loc.shape
    table = mask_ref.shape[0]
    width = og_ref.shape[2]
    head = width // HEADS
    per = 128 // head
    scale = 1.0 / math.sqrt(head)

    row_head = lax.broadcasted_iota(jnp.int32, (128, node_rows), 0) // head
    lane_head = lax.broadcasted_iota(jnp.int32, (node_rows, 128), 1) // head

    def spread_t(block):
        zero = jnp.zeros_like(block)
        return jnp.concatenate([jnp.where(row_head == h, block, zero) for h in range(per)], axis=1)

    def spread_n(block):
        zero = jnp.zeros_like(block)
        return jnp.concatenate([jnp.where(lane_head == h, block, zero) for h in range(per)], axis=0)

    strip = 64
    for m in range(members):
        kg = jnp.concatenate([loc[K, m], halo[0, m]], axis=0)
        vg = jnp.concatenate([loc[V, m], halo[1, m]], axis=0)
        score[m] = nn(kg, spread_t(loc[QT, m]))
        grad[m] = nn(vg, spread_t(loc[GT, m]))

    wo_total = None
    kv_total = None
    q_total = None
    for m in range(members):
        probs = []
        for h in range(per):
            lanes = slice(h * node_rows, (h + 1) * node_rows)
            den = jnp.zeros((8, node_rows), f32)
            inner = jnp.zeros((8, node_rows), f32)
            for c in range(0, table, strip):
                at = (m, slice(c, c + strip), lanes)
                t = jnp.tanh(score[at] * (scale / score_cap))
                e = jnp.exp2(t * (score_cap / math.log(2.0))) * mask_ref[c : c + strip]
                den = den + jnp.sum(e.reshape(strip // 8, 8, node_rows), axis=0)
                inner = inner + jnp.sum((e * grad[at]).reshape(strip // 8, 8, node_rows), axis=0)
                score[at] = e
                slope[at] = e * (scale - scale * (t * t))
            r = 1.0 / jnp.sum(den, axis=0, keepdims=True)
            inner = jnp.sum(inner, axis=0, keepdims=True) * r
            column = []
            scores = []
            for c in range(0, table, strip):
                at = (m, slice(c, c + strip), lanes)
                column.append((score[at] * r).astype(bf16))
                scores.append(((slope[at] * r) * (grad[at] - inner)).astype(bf16))
            probs.append((jnp.concatenate(column, axis=0), jnp.concatenate(scores, axis=0)))
        pb = jnp.concatenate([p for p, _ in probs], axis=1)
        ds = jnp.concatenate([s for _, s in probs], axis=1)
        ktg = jnp.concatenate([loc[KT, m], halo[2, m]], axis=1)
        vtg = jnp.concatenate([loc[VT, m], halo[3, m]], axis=1)
        att, dqt = [], []
        for h in range(0, per, 2):
            lanes = slice(h * node_rows, (h + 2) * node_rows)
            rows = slice(h * head, (h + 2) * head)
            a = nn(vtg[rows], pb[:, lanes])
            b = nn(ktg[rows], ds[:, lanes])
            for j in range(2):
                inside = (slice(j * head, (j + 1) * head), slice(j * node_rows, (j + 1) * node_rows))
                att.append(a[inside].astype(bf16))
                dqt.append(b[inside].astype(bf16))
        att = jnp.concatenate(att, axis=0)
        dq = jnp.concatenate(dqt, axis=0).T
        dk = nn(ds, spread_n(loc[Q, m])).astype(bf16)
        dv = nn(pb, spread_n(loc[G, m])).astype(bf16)
        dq_ref[m], dk_ref[m], dv_ref[m] = dq, dk, dv
        wo_term = nn(att, og_ref[m])
        kv_term = nn(xtf[m], jnp.concatenate([dk, dv], axis=1))
        q_term = nn(xtf[m, :, :node_rows], dq)
        wo_total = wo_term if m == 0 else wo_total + wo_term
        kv_total = kv_term if m == 0 else kv_total + kv_term
        q_total = q_term if m == 0 else q_total + q_term

    planes, _, _, rows, _ = dw.shape
    inner_planes = wos.shape[0]
    dw[:, :, :, :, :128] = q_total.reshape(planes, 2, 2, rows, 128)
    dw[:, :, :, :, 128:] = kv_total.reshape(planes, 2, 2, rows, 256)
    wos[...] = wo_total.reshape(inner_planes, 2, 2, rows, width)
    me = me_ref[0]
    c, y, z = me % 2, (me // 2) % 2, me // 4
    for k in range(planes):
        zk = (z + k) % planes
        own_ref[k, :, :384] = dw[zk, y, c]
        other_ref[k, :, :384] = dw[zk, 1 - y, c]
        send_ref[0, k, :, :384] = dw[zk, 1 - y, 1 - c].astype(bf16)
        send_ref[1, k, :, :384] = dw[zk, y, 1 - c].astype(bf16)
    for i in range(inner_planes):
        for n in range(width // 128):
            k = n * inner_planes + i
            lanes = slice(n * 128, (n + 1) * 128)
            own_ref[k, :, 384:] = wos[i, y, c, :, lanes]
            other_ref[k, :, 384:] = wos[i, 1 - y, c, :, lanes]
            send_ref[0, k, :, 384:] = wos[i, 1 - y, 1 - c, :, lanes].astype(bf16)
            send_ref[1, k, :, 384:] = wos[i, y, 1 - c, :, lanes].astype(bf16)


def node_kernel(groups, skip, *refs):
    refs = refs[skip:]
    dqs, dks, dvs = refs[:groups], refs[groups : 2 * groups], refs[2 * groups : 3 * groups]
    wq_ref, wk_ref, wv_ref, node_ref, left_ref, right_ref, minus_ref, plus_ref = refs[3 * groups :]
    members, node_rows, _ = dqs[0].shape
    slots = left_ref.shape[2]

    def whole(parts, m):
        return jnp.concatenate([part[m] for part in parts], axis=1)

    for m in range(members):
        spread = nt(whole(dks, m), wk_ref[...]) + nt(whole(dvs, m), wv_ref[...])
        node_ref[m] = spread[:node_rows] + nt(whole(dqs, m), wq_ref[...])
        halo = spread[node_rows:].astype(bf16)
        for ref, order in (
            (left_ref, (0, 6, 5)),
            (right_ref, (1, 4, 7)),
            (minus_ref, (2,)),
            (plus_ref, (3,)),
        ):
            for i, k in enumerate(order):
                ref[m, i] = halo[k * slots : (k + 1) * slots]


def sums(half, refs, k):
    owns, core_in, y_in = refs[:half], refs[half : 2 * half], refs[2 * half : 3 * half]
    return [
        own[k] + core[1, k].astype(f32) + y[k].astype(f32)
        for own, core, y in zip(owns, core_in, y_in)
    ]


def first_kernel(half, skip, *refs):
    ins, outs = refs[skip : skip + 3 * half], refs[skip + 3 * half :]
    own_ref, projection_ref, *sent = outs
    planes = len(sent) + 1
    for k in range(planes):
        parts = sums(half, ins, k)
        gather_projection(parts, k, planes, projection_ref, 0)
        row = jnp.concatenate([part[:, :384] for part in parts], axis=1)
        if k:
            sent[k - 1][...] = row.astype(bf16)
        else:
            own_ref[...] = row


def gather_projection(parts, k, planes, projection_ref, start):
    inner_planes = planes * 128 // projection_ref.shape[2]
    quarter, inner = divmod(k, inner_planes)
    for i, part in enumerate(parts):
        plane = start + i * inner_planes + inner
        projection_ref[plane, :, quarter * 128 : (quarter + 1) * 128] = part[:, 384:]


def second_kernel(half, planes, me_ref, *refs):
    refs = refs[planes:]
    first_ref, ins = refs[0], refs[1 : 1 + 3 * half]
    own_ref, *sent = refs[1 + 3 * half : -1]
    projection_ref = refs[-1]
    done = first_ref.shape[0]
    projection_ref[:done] = first_ref[...]
    rows = []
    for k in range(planes):
        parts = sums(half, ins, k)
        gather_projection(parts, k, planes, projection_ref, done)
        rows.append(jnp.concatenate([part[:, :384] for part in parts], axis=1))
    wide = 384 * half
    z = me_ref[0] // 4
    for k in range(planes):
        projection = projection_ref[(z + k) % planes]
        if k:
            sent[k - 1][:, :wide] = rows[k].astype(bf16)
            sent[k - 1][:, wide:] = projection.astype(bf16)
        else:
            own_ref[:, :wide] = rows[k]
            own_ref[:, wide:] = projection


def weight_kernel(half, planes, after_ref, own_a, own_b, *refs):
    z_a, z_b, out_ref = refs[: planes - 1], refs[planes - 1 : -1], refs[-1]
    a, b = own_a[...], own_b[...]
    for ref in z_a:
        a = a + ref[...].astype(f32)
    for ref in z_b:
        b = b + ref[...].astype(f32)
    width = 256 * half
    for i, part in enumerate((a, b)):
        for j in range(half):
            for n in range(3):
                at = n * width + (i * half + j) * 128
                out_ref[:, at : at + 128] = part[:, j * 384 + n * 128 : j * 384 + (n + 1) * 128]
    out_ref[:, 3 * width :] = b[:, 384 * half :]


def finish_kernel(send_ref, node_ref, left_ref, right_ref, minus_ref, plus_ref, out_ref):
    members, node_rows, _ = node_ref.shape
    pick = sent_selector(send_ref[0], node_rows).astype(bf16)
    for m in range(members):
        pieces = [None] * 8
        for ref, order in (
            (left_ref, (0,)),
            (right_ref, (1,)),
            (minus_ref, (2, 6, 4)),
            (plus_ref, (3, 5, 7)),
        ):
            for i, k in enumerate(order):
                pieces[k] = ref[m, i]
        arriving = jnp.concatenate(pieces, axis=0)
        out_ref[m] = (node_ref[m] + nn(pick, arriving)).astype(bf16)


def call(kernel, outs, operands, specs=None, scratch=(), flops=10**8, limit=12):
    specs = list(specs or ())
    specs += [pltpu.VMEM] * (len(operands) - len(specs))
    return pl.pallas_call(
        kernel,
        out_shape=[jax.ShapeDtypeStruct(*o) for o in outs],
        in_specs=[pl.BlockSpec(memory_space=s) for s in specs],
        scratch_shapes=list(scratch),
        compiler_params=pltpu.CompilerParams(vmem_limit_bytes=limit * MIB),
        cost_estimate=pl.CostEstimate(flops=flops, bytes_accessed=10**6, transcendentals=0),
    )(*operands)


def body(
    node_features, out_grad, w_query, w_key, w_value, w_out, neighbours, neighbour_count, send_rows
):
    members, node_rows, width = node_features.shape
    count = lax.axis_size("patch")
    row_width = min(8, count // 4)
    _, adjacent, slots = send_rows.shape
    table = node_rows + adjacent * slots
    groups = width // 128
    me = lax.axis_index("patch")
    three = ((members, 3, slots, width), bf16)
    one = ((members, 1, slots, width), bf16)

    to_plus, to_minus, own_right, own_left = call(
        functools.partial(gather_kernel, slots), [three, three, one, one],
        (send_rows, node_features),
    )
    plus = shifted(to_plus, row_width)
    minus = shifted(to_minus, -row_width)
    *loc, xt = call(
        local_kernel,
        [((8, members, node_rows, 128), bf16)] * groups + [((members, width, node_rows), bf16)],
        (own_right, node_features, out_grad, w_query, w_key, w_value, w_out),
        specs=[pl.ANY], flops=3 * 10**9, limit=16,
    )
    to_right, to_left = call(
        relay_kernel, [three, three], (loc[0], own_right, own_left, plus, minus), specs=[pl.ANY]
    )
    right = shifted(to_right, 1)
    left = shifted(to_left, -1)
    (mask,) = call(
        mask_kernel, [((table, node_rows), f32)],
        (to_right, neighbours, neighbour_count.reshape(1, node_rows)),
        specs=[pl.ANY], flops=2 * 10**9,
    )
    *halo, xtf = call(
        halo_kernel,
        [((4, members, node_rows, 128), bf16)] * groups + [((members, width, table), bf16)],
        (plus, minus, right, left, xt, w_key, w_value), flops=10**9,
    )

    planes, rows = count // 4, width // count
    inner_planes = planes * 128 // width
    keep = ((planes, rows, 512), f32)
    flip = [(i, i ^ 1) for i in range(count)]
    flop = [(i, i ^ 2) for i in range(count)]
    place = me.reshape(1)
    dqs, dks, dvs, owns, others, core_in, y_out, y_in = [], [], [], [], [], [], [], []

    def pass_y():
        i = len(y_out)
        y_out.append((others[i] + core_in[i][0].astype(f32)).astype(bf16))
        y_in.append(lax.ppermute(y_out[i], "patch", flop))

    for g in range(groups):
        extra = ()
        if g >= 2:
            pass_y()
            extra = tuple(y_out[-1:] + y_in[:-1][-1:])
        own, other, send, dq, dk, dv = call(
            functools.partial(attention_kernel, len(extra)),
            [
                keep, keep, ((2, planes, rows, 512), bf16),
                ((members, node_rows, 128), bf16),
                ((members, table, 128), bf16),
                ((members, table, 128), bf16),
            ],
            (place, *extra, loc[g], halo[g], mask, xtf, out_grad),
            specs=[pltpu.SMEM] + [pl.ANY] * len(extra),
            scratch=[pltpu.VMEM((members, table, 512), f32)] * 3
            + [
                pltpu.VMEM((planes, 2, 2, rows, 384), f32),
                pltpu.VMEM((inner_planes, 2, 2, rows, width), f32),
            ],
            flops=35 * 10**8, limit=20,
        )
        dqs.append(dq)
        dks.append(dk)
        dvs.append(dv)
        owns.append(own)
        others.append(other)
        core_in.append(lax.ppermute(send, "patch", flip))

    def along_z(sent):
        return [
            lax.ppermute(s, "patch", [(i, (i + 4 * k) % count) for i in range(count)])
            for k, s in enumerate(sent, 1)
        ]

    half = groups // 2
    wide = 384 * half
    projection = ((half * inner_planes, rows, width), f32)
    own_a, out_a, *sent = call(
        functools.partial(first_kernel, half, 1),
        [((rows, wide), f32), projection] + [((rows, wide), bf16)] * (planes - 1),
        (owns[-1], *owns[:half], *core_in[:half], *y_in[:half]),
        specs=[pl.ANY],
    )
    z_a = along_z(sent)
    while len(y_out) < groups:
        pass_y()
    node, back_left, back_right, back_minus, back_plus = call(
        functools.partial(node_kernel, groups, planes + 1),
        [((members, node_rows, width), f32), three, three, one, one],
        (*sent, *y_out[half:], *dqs, *dks, *dvs, w_query, w_key, w_value),
        specs=[pl.ANY] * (planes + 1), flops=2 * 10**9,
    )
    from_right = shifted(back_left, -1)
    from_left = shifted(back_right, 1)
    own_b, *sent = call(
        functools.partial(second_kernel, half, planes),
        [((rows, wide + width), f32)] + [((rows, wide + width), bf16)] * (planes - 1),
        (place, node, *z_a, out_a, *owns[half:], *core_in[half:], *y_in[half:]),
        specs=[pltpu.SMEM] + [pl.ANY] * planes,
        scratch=[pltpu.VMEM((planes, rows, width), f32)],
    )
    z_b = along_z(sent)
    to_minus, to_plus = call(
        back_relay_kernel, [three, three],
        (own_b, back_minus, back_plus, from_right, from_left), specs=[pl.ANY],
    )
    from_plus = shifted(to_minus, -row_width)
    from_minus = shifted(to_plus, row_width)
    (node_grad,) = call(
        finish_kernel, [((members, node_rows, width), bf16)],
        (send_rows, node, from_right, from_left, from_plus, from_minus), flops=10**9,
    )
    (weight_grad,) = call(
        functools.partial(weight_kernel, half, planes), [((rows, 4 * width), f32)],
        (node_grad, own_a, own_b, *z_a, *z_b), specs=[pl.ANY],
    )
    return (node_grad, weight_grad)


def solution(mesh):
    in_specs = (
        P("groups", "patch", None),
        P("groups", "patch", None),
        P(),
        P(),
        P(),
        P(),
        P("patch", None),
        P("patch"),
        P("patch", None, None),
    )
    out_specs = (P("groups", "patch", None), P(("groups", "patch"), None))
    return jax.shard_map(body, mesh=mesh, in_specs=in_specs, out_specs=out_specs, check_vma=False)
```

```python
import functools
import math

import jax
import jax.numpy as jnp
from jax import lax
from jax.experimental import pallas as pl
from jax.experimental.pallas import tpu as pltpu
from jax.sharding import PartitionSpec as P

HEADS = 16
score_cap = 5.0
MIB = 1024 * 1024
f32 = jnp.float32
bf16 = jnp.bfloat16


def nn(a, b):
    return lax.dot_general(a, b, (((1,), (0,)), ((), ())), preferred_element_type=f32)


def nt(a, b):
    return lax.dot_general(a, b, (((1,), (1,)), ((), ())), preferred_element_type=f32)


def shifted(shard, by):
    count = lax.axis_size("patch")
    return lax.ppermute(shard, "patch", [(i, (i + by) % count) for i in range(count)])


def sent_selector(send_rows, node_rows):
    adjacent, slots = send_rows.shape
    halo = adjacent * slots
    wide = jnp.concatenate([send_rows] * adjacent, axis=1)
    own = lax.broadcasted_iota(jnp.int32, (adjacent, halo), 1) // slots == lax.broadcasted_iota(
        jnp.int32, (adjacent, halo), 0
    )
    ids = jnp.sum(jnp.where(own, wide, 0), axis=0, keepdims=True)
    nodes = lax.broadcasted_iota(jnp.int32, (node_rows, halo), 0)
    return jnp.where(nodes == ids, 1.0, 0.0).astype(f32)


def gather_kernel(slots, send_hbm, x_hbm, plus_ref, minus_ref, right_ref, left_ref, x_ref, send_ref, sem):
    copies = [
        pltpu.make_async_copy(send_hbm, send_ref, sem.at[0]),
        pltpu.make_async_copy(x_hbm, x_ref, sem.at[1]),
    ]
    for copy in copies:
        copy.start()
    copies[0].wait()
    members, node_rows, _ = x_ref.shape
    pick = sent_selector(send_ref[0], node_rows).T.astype(bf16)
    copies[1].wait()
    for m in range(members):
        rows = nn(pick, x_ref[m]).astype(bf16)

        def part(k):
            return rows[k * slots : (k + 1) * slots]

        for i, k in enumerate((2, 6, 4)):
            plus_ref[m, i] = part(k)
        for i, k in enumerate((3, 5, 7)):
            minus_ref[m, i] = part(k)
        right_ref[m, 0] = part(0)
        left_ref[m, 0] = part(1)


def relay_kernel(after_ref, own_a, own_b, plus_ref, minus_ref, a_ref, b_ref):
    a_ref[:, 0:1] = own_a[...]
    a_ref[:, 1:2] = plus_ref[:, 1:2]
    a_ref[:, 2:3] = minus_ref[:, 1:2]
    b_ref[:, 0:1] = own_b[...]
    b_ref[:, 1:2] = plus_ref[:, 2:3]
    b_ref[:, 2:3] = minus_ref[:, 2:3]


Q, K, V, G, QT, KT, VT, GT = range(8)


def local_kernel(groups, after_ref, x_ref, *refs):
    sources, loc_refs, xt_ref = refs[:5], refs[5 : 5 + groups], refs[5 + groups]
    copied, sem = refs[6 + groups : 11 + groups], refs[-1]
    copies = [
        pltpu.make_async_copy(source, target, sem.at[i])
        for i, (source, target) in enumerate(zip(sources, copied))
    ]
    for copy in copies:
        copy.start()
    members, node_rows, width = x_ref.shape
    x = x_ref[...].reshape(members * node_rows, width)
    for m in range(members):
        xt_ref[m] = x_ref[m].T

    def put(rows, kind):
        for m in range(members):
            for g, ref in enumerate(loc_refs):
                block = rows[m * node_rows : (m + 1) * node_rows, g * 128 : (g + 1) * 128]
                ref[kind, m] = block
                ref[kind + 4, m] = block.T

    wq_ref, wk_ref, wv_ref, og_ref, wo_ref = copied
    for kind, ref in enumerate((wq_ref, wk_ref, wv_ref)):
        copies[kind].wait()
        put(nn(x, ref[...]).astype(bf16), kind)
    copies[3].wait()
    copies[4].wait()
    og = og_ref[...].reshape(members * node_rows, width)
    put(nt(og, wo_ref[...]).astype(bf16), G)


def mask_kernel(after_ref, neigh_ref, count_ref, mask_ref):
    neigh = neigh_ref[...].T
    slots, node_rows = neigh.shape
    table = mask_ref.shape[0]
    order = lax.broadcasted_iota(jnp.int32, neigh.shape, 0)
    tail = jnp.where(order >= count_ref[...], neigh, -1)[slots // 2 :]
    half = table // 2
    for part in range(2):
        columns = lax.broadcasted_iota(jnp.int32, (half, node_rows), 0) + part * half
        kept = jnp.ones((half, node_rows), f32)
        for j in range(slots // 2):
            kept = jnp.where(tail[j : j + 1] == columns, 0.0, kept)
        mask_ref[part * half : (part + 1) * half] = kept


def halo_kernel(plus_ref, minus_ref, right_ref, left_ref, xt_ref, wk_ref, wv_ref, *out_refs):
    halo_refs, xtf_ref = out_refs[:-1], out_refs[-1]
    members, _, node_rows = xt_ref.shape
    for m in range(members):
        pieces = [None] * 8
        for ref, order in (
            (right_ref, (0, 6, 5)),
            (left_ref, (1, 4, 7)),
            (plus_ref, (2,)),
            (minus_ref, (3,)),
        ):
            for i, k in enumerate(order):
                pieces[k] = ref[m, i]
        halo = jnp.concatenate(pieces, axis=0)
        xtf_ref[m, :, :node_rows] = xt_ref[m]
        xtf_ref[m, :, node_rows:] = halo.T
        for kind, w_ref in enumerate((wk_ref, wv_ref)):
            rows = nn(halo, w_ref[...]).astype(bf16)
            for g, ref in enumerate(halo_refs):
                block = rows[:, g * 128 : (g + 1) * 128]
                ref[kind, m] = block
                ref[kind + 2, m] = block.T


def attention_kernel(extra, here, me_ref, *refs):
    refs = refs[extra:]
    locs, halos, refs = refs[:here], refs[here : 2 * here], refs[2 * here :]
    mask_ref, xtf, og_ref = refs[:3]
    outs, grads, scratch = refs[3:7], refs[7 : 7 + 3 * here], refs[7 + 3 * here :]
    for i in range(here):
        attend(
            me_ref, locs[i], halos[i], mask_ref, xtf, og_ref, outs, 512 * i,
            grads[3 * i : 3 * i + 3], scratch,
        )


def attend(me_ref, loc, halo, mask_ref, xtf, og_ref, out_refs, at, grad_refs, scratch):
    own_ref, other_ref, send_other, send_own = out_refs
    dq_ref, dk_ref, dv_ref = grad_refs
    score, grad, slope, dw, wos = scratch
    _, members, node_rows, _ = loc.shape
    table = mask_ref.shape[0]
    width = og_ref.shape[2]
    head = width // HEADS
    per = 128 // head
    scale = 1.0 / math.sqrt(head)

    row_head = lax.broadcasted_iota(jnp.int32, (128, node_rows), 0) // head
    lane_head = lax.broadcasted_iota(jnp.int32, (node_rows, 128), 1) // head

    def spread_t(block):
        zero = jnp.zeros_like(block)
        return jnp.concatenate([jnp.where(row_head == h, block, zero) for h in range(per)], axis=1)

    def spread_n(block):
        zero = jnp.zeros_like(block)
        return jnp.concatenate([jnp.where(lane_head == h, block, zero) for h in range(per)], axis=0)

    strip = 64
    for m in range(members):
        kg = jnp.concatenate([loc[K, m], halo[0, m]], axis=0)
        vg = jnp.concatenate([loc[V, m], halo[1, m]], axis=0)
        score[m] = nn(kg, spread_t(loc[QT, m]))
        grad[m] = nn(vg, spread_t(loc[GT, m]))

    wo_total = None
    kv_total = None
    q_total = None
    for m in range(members):
        probs = []
        for h in range(per):
            lanes = slice(h * node_rows, (h + 1) * node_rows)
            den = jnp.zeros((8, node_rows), f32)
            inner = jnp.zeros((8, node_rows), f32)
            for c in range(0, table, strip):
                box = (m, slice(c, c + strip), lanes)
                t = jnp.tanh(score[box] * (scale / score_cap))
                e = jnp.exp2(t * (score_cap / math.log(2.0))) * mask_ref[c : c + strip]
                den = den + jnp.sum(e.reshape(strip // 8, 8, node_rows), axis=0)
                inner = inner + jnp.sum((e * grad[box]).reshape(strip // 8, 8, node_rows), axis=0)
                score[box] = e
                slope[box] = e * (scale - scale * (t * t))
            r = 1.0 / jnp.sum(den, axis=0, keepdims=True)
            inner = jnp.sum(inner, axis=0, keepdims=True) * r
            column = []
            scores = []
            for c in range(0, table, strip):
                box = (m, slice(c, c + strip), lanes)
                column.append((score[box] * r).astype(bf16))
                scores.append(((slope[box] * r) * (grad[box] - inner)).astype(bf16))
            probs.append((jnp.concatenate(column, axis=0), jnp.concatenate(scores, axis=0)))
        pb = jnp.concatenate([p for p, _ in probs], axis=1)
        ds = jnp.concatenate([s for _, s in probs], axis=1)
        ktg = jnp.concatenate([loc[KT, m], halo[2, m]], axis=1)
        vtg = jnp.concatenate([loc[VT, m], halo[3, m]], axis=1)
        att, dqt = [], []
        for h in range(0, per, 2):
            lanes = slice(h * node_rows, (h + 2) * node_rows)
            rows = slice(h * head, (h + 2) * head)
            a = nn(vtg[rows], pb[:, lanes])
            b = nn(ktg[rows], ds[:, lanes])
            for j in range(2):
                inside = (slice(j * head, (j + 1) * head), slice(j * node_rows, (j + 1) * node_rows))
                att.append(a[inside].astype(bf16))
                dqt.append(b[inside].astype(bf16))
        att = jnp.concatenate(att, axis=0)
        dq = jnp.concatenate(dqt, axis=0).T
        dk = nn(ds, spread_n(loc[Q, m])).astype(bf16)
        dv = nn(pb, spread_n(loc[G, m])).astype(bf16)
        dq_ref[m], dk_ref[m], dv_ref[m] = dq, dk, dv
        wo_term = nn(att, og_ref[m])
        kv_term = nn(xtf[m], jnp.concatenate([dk, dv], axis=1))
        q_term = nn(xtf[m, :, :node_rows], dq)
        wo_total = wo_term if m == 0 else wo_total + wo_term
        kv_total = kv_term if m == 0 else kv_total + kv_term
        q_total = q_term if m == 0 else q_total + q_term

    planes, _, _, rows, _ = dw.shape
    inner_planes = wos.shape[0]
    dw[:, :, :, :, :128] = q_total.reshape(planes, 2, 2, rows, 128)
    dw[:, :, :, :, 128:] = kv_total.reshape(planes, 2, 2, rows, 256)
    wos[...] = wo_total.reshape(inner_planes, 2, 2, rows, width)
    me = me_ref[0]
    c, y, z = me % 2, (me // 2) % 2, me // 4
    qkv = slice(at, at + 384)
    for k in range(planes):
        zk = (z + k) % planes
        own_ref[k, :, qkv] = dw[zk, y, c]
        other_ref[k, :, qkv] = dw[zk, 1 - y, c]
        send_other[k, :, qkv] = dw[zk, 1 - y, 1 - c].astype(bf16)
        send_own[k, :, qkv] = dw[zk, y, 1 - c].astype(bf16)
    last = slice(at + 384, at + 512)
    for i in range(inner_planes):
        for n in range(width // 128):
            k = n * inner_planes + i
            lanes = slice(n * 128, (n + 1) * 128)
            own_ref[k, :, last] = wos[i, y, c, :, lanes]
            other_ref[k, :, last] = wos[i, 1 - y, c, :, lanes]
            send_other[k, :, last] = wos[i, 1 - y, 1 - c, :, lanes].astype(bf16)
            send_own[k, :, last] = wos[i, y, 1 - c, :, lanes].astype(bf16)


def node_kernel(groups, skip, *refs):
    refs = refs[skip:]
    dqs, dks, dvs = refs[:groups], refs[groups : 2 * groups], refs[2 * groups : 3 * groups]
    wq_ref, wk_ref, wv_ref, node_ref, left_ref, right_ref, minus_ref, plus_ref = refs[3 * groups :]
    members, node_rows, _ = dqs[0].shape
    slots = left_ref.shape[2]

    def whole(parts, m):
        return jnp.concatenate([part[m] for part in parts], axis=1)

    for m in range(members):
        spread = nt(whole(dks, m), wk_ref[...]) + nt(whole(dvs, m), wv_ref[...])
        node_ref[m] = spread[:node_rows] + nt(whole(dqs, m), wq_ref[...])
        halo = spread[node_rows:].astype(bf16)
        for ref, order in (
            (left_ref, (0, 6, 5)),
            (right_ref, (1, 4, 7)),
            (minus_ref, (2,)),
            (plus_ref, (3,)),
        ):
            for i, k in enumerate(order):
                ref[m, i] = halo[k * slots : (k + 1) * slots]


def sums(owns, core_in, y_in, k):
    total = jnp.concatenate(
        [own[k] + core[k].astype(f32) for own, core in zip(owns, core_in)], axis=1
    ) + y_in[k].astype(f32)
    return [total[:, at : at + 512] for at in range(0, total.shape[1], 512)]


def gather_projection(parts, k, planes, projection_ref, start):
    inner_planes = planes * 128 // projection_ref.shape[2]
    quarter, inner = divmod(k, inner_planes)
    for i, part in enumerate(parts):
        plane = start + i * inner_planes + inner
        projection_ref[plane, :, quarter * 128 : (quarter + 1) * 128] = part[:, 384:]


def first_kernel(pieces, *refs):
    later, later_core, refs = refs[:pieces], refs[pieces : 2 * pieces], refs[2 * pieces :]
    own, core_in, y_in, next_ref, own_ref, projection_ref, *sent = refs
    for i, (ref, core) in enumerate(zip(later, later_core)):
        next_ref[:, :, i * 512 : (i + 1) * 512] = (ref[...] + core[...].astype(f32)).astype(bf16)
    planes = len(sent) + 1
    for k in range(planes):
        parts = sums([own], [core_in], y_in, k)
        gather_projection(parts, k, planes, projection_ref, 0)
        row = jnp.concatenate([part[:, :384] for part in parts], axis=1)
        if k:
            sent[k - 1][...] = row.astype(bf16)
        else:
            own_ref[...] = row


def second_kernel(planes, pieces, near, me_ref, *refs):
    refs = refs[planes:]
    first_ref, back_plus, back_minus, from_right, from_left, y_in = refs[:6]
    owns, core_in = refs[6 : 6 + pieces], refs[6 + pieces : 6 + 2 * pieces]
    own_ref, *sent = refs[6 + 2 * pieces : -1]
    projection_ref = refs[-1]
    done, rows, width = first_ref.shape
    members = back_plus.shape[0]
    projection_ref[:done] = first_ref[...]
    held = []
    for k in range(planes):
        parts = sums(owns, core_in, y_in, k)
        gather_projection(parts, k, planes, projection_ref, done)
        held.append(jnp.concatenate([part[:, :384] for part in parts], axis=1))
    z = me_ref[0] // 4
    for k in range(planes):
        row = jnp.concatenate([held[k], projection_ref[(z + k) % planes]], axis=1)
        if not k:
            own_ref[...] = row
            continue
        row = row.astype(bf16)
        blocks = row.shape[1] // 256
        for n in range(blocks):
            sent[k - 1][n] = row[:, n * 256 : (n + 1) * 256]
        if k not in near:
            continue
        side = near.index(k)
        relayed = 2 - side
        for m in range(members):
            trio = ((back_plus, back_minus)[side][m, 0], from_right[m, relayed], from_left[m, relayed])
            for i, part in enumerate(trio):
                flat = jnp.concatenate([part[:, :256], part[:, 256:]], axis=0)
                pieces = flat.shape[0] // rows
                at = blocks + (m * 3 + i) * pieces
                sent[k - 1][at : at + pieces] = flat.reshape(pieces, rows, 256)


def finish_kernel(blocks, send_ref, node_ref, left_ref, right_ref, plus_ref, minus_ref, out_ref):
    members, node_rows, _ = node_ref.shape
    slots = left_ref.shape[2]
    pick = sent_selector(send_ref[0], node_rows).astype(bf16)
    rows = plus_ref.shape[1]
    each = 2 * slots // rows

    def arrived(ref, m, i):
        at = blocks + (m * 3 + i) * each
        flat = ref[at : at + each].reshape(2 * slots, 256)
        return jnp.concatenate([flat[:slots], flat[slots:]], axis=1)

    for m in range(members):
        pieces = [None] * 8
        pieces[0] = left_ref[m, 0]
        pieces[1] = right_ref[m, 0]
        for i, k in enumerate((2, 6, 4)):
            pieces[k] = arrived(minus_ref, m, i)
        for i, k in enumerate((3, 5, 7)):
            pieces[k] = arrived(plus_ref, m, i)
        arriving = jnp.concatenate(pieces, axis=0)
        out_ref[m] = (node_ref[m] + nn(pick, arriving)).astype(bf16)


def weight_kernel(planes, after_ref, own_a, own_b, *refs):
    z_a, z_b, out_ref = refs[: planes - 1], refs[planes - 1 : -1], refs[-1]
    a, b = own_a[...], own_b[...]
    blocks = b.shape[1] // 256
    for ref in z_a:
        a = a + ref[...].astype(f32)
    for ref in z_b:
        b = b + jnp.concatenate([ref[n].astype(f32) for n in range(blocks)], axis=1)
    half = a.shape[1] // 384
    width = 256 * half
    for i, part in enumerate((a, b)):
        for j in range(half):
            for n in range(3):
                at = n * width + (i * half + j) * 128
                out_ref[:, at : at + 128] = part[:, j * 384 + n * 128 : j * 384 + (n + 1) * 128]
    out_ref[:, 3 * width :] = b[:, 384 * half :]


def call(kernel, outs, operands, specs=None, scratch=(), flops=10**6, limit=12):
    specs = list(specs or ())
    specs += [pltpu.VMEM] * (len(operands) - len(specs))
    operands = [
        pltpu.with_memory_space_constraint(o, s) if s is pltpu.HBM else o
        for o, s in zip(operands, specs)
    ]
    return pl.pallas_call(
        kernel,
        out_shape=[jax.ShapeDtypeStruct(*o) for o in outs],
        in_specs=[pl.BlockSpec(memory_space=s) for s in specs],
        scratch_shapes=list(scratch),
        compiler_params=pltpu.CompilerParams(vmem_limit_bytes=limit * MIB),
        cost_estimate=pl.CostEstimate(flops=flops, bytes_accessed=10**4, transcendentals=0),
    )(*operands)


def body(
    node_features, out_grad, w_query, w_key, w_value, w_out, neighbours, neighbour_count, send_rows
):
    members, node_rows, width = node_features.shape
    count = lax.axis_size("patch")
    row_width = min(8, count // 4)
    _, adjacent, slots = send_rows.shape
    table = node_rows + adjacent * slots
    groups = width // 128
    me = lax.axis_index("patch")
    three = ((members, 3, slots, width), bf16)
    one = ((members, 1, slots, width), bf16)

    to_plus, to_minus, own_right, own_left, x = call(
        functools.partial(gather_kernel, slots),
        [three, three, one, one, (node_features.shape, bf16)],
        (send_rows, node_features),
        specs=[pltpu.HBM] * 2,
        scratch=[pltpu.VMEM(send_rows.shape, jnp.int32), pltpu.SemaphoreType.DMA((2,))],
    )
    plus = shifted(to_plus, row_width)
    minus = shifted(to_minus, -row_width)
    square = ((width, width), bf16)
    *loc, xt, wq, wk, wv, og = call(
        functools.partial(local_kernel, groups),
        [((8, members, node_rows, 128), bf16)] * groups
        + [((members, width, node_rows), bf16), square, square, square, (out_grad.shape, bf16)],
        (own_right, x, w_query, w_key, w_value, out_grad, w_out),
        specs=[pl.ANY, pltpu.VMEM] + [pltpu.HBM] * 5,
        scratch=[pltpu.VMEM((width, width), bf16), pltpu.SemaphoreType.DMA((5,))],
        limit=16,
    )
    to_right, to_left = call(
        relay_kernel, [three, three], (loc[0], own_right, own_left, plus, minus), specs=[pl.ANY]
    )
    right = shifted(to_right, 1)
    left = shifted(to_left, -1)
    (mask,) = call(
        mask_kernel, [((table, node_rows), f32)],
        (to_right, neighbours, neighbour_count.reshape(1, node_rows)),
        specs=[pl.ANY],
    )
    *halo, xtf = call(
        halo_kernel,
        [((4, members, node_rows, 128), bf16)] * groups + [((members, width, table), bf16)],
        (plus, minus, right, left, xt, wk, wv),
    )

    planes, rows = count // 4, width // count
    inner_planes = planes * 128 // width
    flip = [(i, i ^ 1) for i in range(count)]
    flop = [(i, i ^ 2) for i in range(count)]
    place = me.reshape(1)
    grads = []

    def attention(extra, which):
        wide = 512 * len(which)
        outs = call(
            functools.partial(attention_kernel, len(extra), len(which)),
            [((planes, rows, wide), kind) for kind in (f32, f32, bf16, bf16)]
            + [
                ((members, node_rows, 128), bf16),
                ((members, table, 128), bf16),
                ((members, table, 128), bf16),
            ]
            * len(which),
            (
                place, *extra, *[loc[g] for g in which], *[halo[g] for g in which], mask, xtf, og,
            ),
            specs=[pltpu.SMEM] + [pl.ANY] * len(extra),
            scratch=[pltpu.VMEM((members, table, 512), f32)] * 3
            + [
                pltpu.VMEM((planes, 2, 2, rows, 384), f32),
                pltpu.VMEM((inner_planes, 2, 2, rows, width), f32),
            ],
            limit=24,
        )
        grads.extend(outs[4:])
        own, other, send_other, send_own = outs[:4]
        return own, other, lax.ppermute(send_other, "patch", flip), lax.ppermute(send_own, "patch", flip)

    def along_z(sent):
        return [
            lax.ppermute(s, "patch", [(i, (i + 4 * k) % count) for i in range(count)])
            for k, s in enumerate(sent, 1)
        ]

    half = groups // 2
    wide = 384 * half
    own_a, other, core_other, core_own = attention((), range(half))
    y_sent = (other + core_other.astype(f32)).astype(bf16)
    y_a = lax.ppermute(y_sent, "patch", flop)
    later = []
    for g in range(half, groups):
        later.append(attention((y_sent,) if g == groups - 1 else (), range(g, g + 1)))
    own_b, other_b, core_other_b, core_own_b = zip(*later)
    y_sent, own_a, out_a, *sent = call(
        functools.partial(first_kernel, len(later)),
        [(y_sent.shape, bf16), ((rows, wide), f32), ((half * inner_planes, rows, width), f32)]
        + [((rows, wide), bf16)] * (planes - 1),
        (*other_b, *core_other_b, own_a, core_own, y_a),
    )
    y_b = lax.ppermute(y_sent, "patch", flop)
    node, back_left, back_right, back_minus, back_plus = call(
        functools.partial(node_kernel, groups, planes),
        [((members, node_rows, width), f32), three, three, one, one],
        (y_sent, *sent, *grads[0::3], *grads[1::3], *grads[2::3], wq, wk, wv),
        specs=[pl.ANY] * planes,
    )
    from_right = shifted(back_left, -1)
    from_left = shifted(back_right, 1)
    z_a = along_z(sent)
    near = (row_width // 4, planes - row_width // 4)
    blocks = (wide + width) // 256
    more = members * 6 * slots // rows
    own_b, *sent = call(
        functools.partial(second_kernel, planes, len(later), near),
        [((rows, wide + width), f32)]
        + [((blocks + (more if k in near else 0), rows, 256), bf16) for k in range(1, planes)],
        (
            place, node, *z_a, out_a, back_plus, back_minus, from_right, from_left, y_b,
            *own_b, *core_own_b,
        ),
        specs=[pltpu.SMEM] + [pl.ANY] * planes,
        scratch=[pltpu.VMEM((planes, rows, width), f32)],
    )
    z_b = along_z(sent)
    (node_grad,) = call(
        functools.partial(finish_kernel, blocks), [((members, node_rows, width), bf16)],
        (send_rows, node, from_right, from_left, z_b[near[0] - 1], z_b[near[1] - 1]),
    )
    (weight_grad,) = call(
        functools.partial(weight_kernel, planes), [((rows, 4 * width), f32)],
        (node_grad, own_a, own_b, *z_a, *z_b), specs=[pl.ANY],
    )
    return (node_grad, weight_grad)


def solution(mesh):
    in_specs = (
        P("groups", "patch", None),
        P("groups", "patch", None),
        P(),
        P(),
        P(),
        P(),
        P("patch", None),
        P("patch"),
        P("patch", None, None),
    )
    out_specs = (P("groups", "patch", None), P(("groups", "patch"), None))
    return jax.shard_map(body, mesh=mesh, in_specs=in_specs, out_specs=out_specs, check_vma=False)
```

```python
import functools
import math

import jax
import jax.numpy as jnp
from jax import lax
from jax.experimental import pallas as pl
from jax.experimental.pallas import tpu as pltpu
from jax.sharding import PartitionSpec as P

HEADS = 16
score_cap = 5.0
MIB = 1024 * 1024
f32 = jnp.float32
bf16 = jnp.bfloat16


def nn(a, b):
    return lax.dot_general(a, b, (((1,), (0,)), ((), ())), preferred_element_type=f32)


def nt(a, b):
    return lax.dot_general(a, b, (((1,), (1,)), ((), ())), preferred_element_type=f32)


def neighbours_apart(count, stride):
    first, second = [], []
    for i in range(count):
        up, down = (i + stride) % count, (i - stride) % count
        even = i // stride % 2 == 0
        first.append((i, up if even else down))
        second.append((i, down if even else up))
    return first, second


def swap(pair, stride):
    return [
        lax.ppermute(shard, "patch", perm)
        for shard, perm in zip(pair, neighbours_apart(lax.axis_size("patch"), stride))
    ]


def to_swaps(both, odd, first_ref, second_ref):
    first_ref[...] = both[odd]
    second_ref[...] = both[1 - odd]


def from_swaps(both, odd, first_ref, second_ref):
    both[1 - odd] = first_ref[...]
    both[odd] = second_ref[...]


def sent_selector(send_rows, node_rows):
    adjacent, slots = send_rows.shape
    halo = adjacent * slots
    wide = jnp.concatenate([send_rows] * adjacent, axis=1)
    own = lax.broadcasted_iota(jnp.int32, (adjacent, halo), 1) // slots == lax.broadcasted_iota(
        jnp.int32, (adjacent, halo), 0
    )
    ids = jnp.sum(jnp.where(own, wide, 0), axis=0, keepdims=True)
    nodes = lax.broadcasted_iota(jnp.int32, (node_rows, halo), 0)
    return jnp.where(nodes == ids, 1.0, 0.0).astype(f32)


def gather_kernel(
    slots, stride, me_ref, send_hbm, x_hbm, first_ref, second_ref, right_ref, left_ref, x_ref,
    send_ref, both, sem,
):
    copies = [
        pltpu.make_async_copy(send_hbm, send_ref, sem.at[0]),
        pltpu.make_async_copy(x_hbm, x_ref, sem.at[1]),
    ]
    for copy in copies:
        copy.start()
    copies[0].wait()
    members, node_rows, _ = x_ref.shape
    pick = sent_selector(send_ref[0], node_rows).T.astype(bf16)
    copies[1].wait()
    for m in range(members):
        rows = nn(pick, x_ref[m]).astype(bf16)

        def part(k):
            return rows[k * slots : (k + 1) * slots]

        for side, order in enumerate(((2, 6, 4), (3, 5, 7))):
            for i, k in enumerate(order):
                both[side, m, i] = part(k)
        right_ref[m, 0] = part(0)
        left_ref[m, 0] = part(1)
    to_swaps(both, me_ref[0] // stride % 2, first_ref, second_ref)


def relay_kernel(
    stride, me_ref, after_ref, own_right, own_left, first_in, second_in, first_ref, second_ref,
    plus_ref, minus_ref, came, both,
):
    from_swaps(came, me_ref[0] // stride % 2, first_in, second_in)
    for side, own in enumerate((own_right, own_left)):
        both[side, :, 0:1] = own[...]
        both[side, :, 1:2] = came[0, :, 1 + side : 2 + side]
        both[side, :, 2:3] = came[1, :, 1 + side : 2 + side]
    to_swaps(both, me_ref[0] % 2, first_ref, second_ref)
    plus_ref[...] = came[0, :, 0:1]
    minus_ref[...] = came[1, :, 0:1]


Q, K, V, G, QT, KT, VT, GT = range(8)


def local_kernel(groups, after_ref, x_ref, *refs):
    sources, loc_refs, xt_ref = refs[:7], refs[7 : 7 + groups], refs[7 + groups]
    copied, sem = refs[8 + groups : 15 + groups], refs[-1]
    copies = [
        pltpu.make_async_copy(source, target, sem.at[i])
        for i, (source, target) in enumerate(zip(sources, copied))
    ]
    for copy in copies:
        copy.start()
    members, node_rows, width = x_ref.shape
    x = x_ref[...].reshape(members * node_rows, width)
    for m in range(members):
        xt_ref[m] = x_ref[m].T

    def put(rows, kind):
        for m in range(members):
            for g, ref in enumerate(loc_refs):
                block = rows[m * node_rows : (m + 1) * node_rows, g * 128 : (g + 1) * 128]
                ref[kind, m] = block
                ref[kind + 4, m] = block.T

    wq_ref, wk_ref, wv_ref, og_ref, _, _, wo_ref = copied
    for kind, ref in enumerate((wq_ref, wk_ref, wv_ref)):
        copies[kind].wait()
        put(nn(x, ref[...]).astype(bf16), kind)
    for copy in copies[3:]:
        copy.wait()
    og = og_ref[...].reshape(members * node_rows, width)
    put(nt(og, wo_ref[...]).astype(bf16), G)


def mask_kernel(after_ref, neigh_ref, count_ref, mask_ref):
    neigh = neigh_ref[...].T
    slots, node_rows = neigh.shape
    table = mask_ref.shape[0]
    order = lax.broadcasted_iota(jnp.int32, neigh.shape, 0)
    tail = jnp.where(order >= count_ref[...], neigh, -1)[slots // 2 :]
    half = table // 2
    for part in range(2):
        columns = lax.broadcasted_iota(jnp.int32, (half, node_rows), 0) + part * half
        kept = jnp.ones((half, node_rows), f32)
        for j in range(slots // 2):
            kept = jnp.where(tail[j : j + 1] == columns, 0.0, kept)
        mask_ref[part * half : (part + 1) * half] = kept


def halo_kernel(
    me_ref, plus_ref, minus_ref, first_in, second_in, xt_ref, wk_ref, wv_ref, *refs
):
    halo_refs, xtf_ref, both = refs[:-2], refs[-2], refs[-1]
    members, _, node_rows = xt_ref.shape
    from_swaps(both, me_ref[0] % 2, first_in, second_in)
    for m in range(members):
        pieces = [None] * 8
        for side, order in enumerate(((0, 6, 5), (1, 4, 7))):
            for i, k in enumerate(order):
                pieces[k] = both[side, m, i]
        pieces[2] = plus_ref[m, 0]
        pieces[3] = minus_ref[m, 0]
        halo = jnp.concatenate(pieces, axis=0)
        xtf_ref[m, :, :node_rows] = xt_ref[m]
        xtf_ref[m, :, node_rows:] = halo.T
        for kind, w_ref in enumerate((wk_ref, wv_ref)):
            rows = nn(halo, w_ref[...]).astype(bf16)
            for g, ref in enumerate(halo_refs):
                block = rows[:, g * 128 : (g + 1) * 128]
                ref[kind, m] = block
                ref[kind + 2, m] = block.T


def attention_kernel(extra, here, me_ref, *refs):
    refs = refs[extra:]
    locs, halos, refs = refs[:here], refs[here : 2 * here], refs[2 * here :]
    mask_ref, xtf, og_ref = refs[:3]
    outs, grads, scratch = refs[3:7], refs[7 : 7 + 3 * here], refs[7 + 3 * here :]
    for i in range(here):
        attend(
            me_ref, locs[i], halos[i], mask_ref, xtf, og_ref, outs, 512 * i,
            grads[3 * i : 3 * i + 3], scratch,
        )


def attend(me_ref, loc, halo, mask_ref, xtf, og_ref, out_refs, at, grad_refs, scratch):
    own_ref, other_ref, send_other, send_own = out_refs
    dq_ref, dk_ref, dv_ref = grad_refs
    score, grad, slope, dw, wos = scratch
    _, members, node_rows, _ = loc.shape
    table = mask_ref.shape[0]
    width = og_ref.shape[2]
    head = width // HEADS
    per = 128 // head
    scale = 1.0 / math.sqrt(head)

    row_head = lax.broadcasted_iota(jnp.int32, (128, node_rows), 0) // head
    lane_head = lax.broadcasted_iota(jnp.int32, (node_rows, 128), 1) // head

    def spread_t(block):
        zero = jnp.zeros_like(block)
        return jnp.concatenate([jnp.where(row_head == h, block, zero) for h in range(per)], axis=1)

    def spread_n(block):
        zero = jnp.zeros_like(block)
        return jnp.concatenate([jnp.where(lane_head == h, block, zero) for h in range(per)], axis=0)

    strip = 64
    for m in range(members):
        kg = jnp.concatenate([loc[K, m], halo[0, m]], axis=0)
        vg = jnp.concatenate([loc[V, m], halo[1, m]], axis=0)
        score[m] = nn(kg, spread_t(loc[QT, m]))
        grad[m] = nn(vg, spread_t(loc[GT, m]))

    wo_total = None
    kv_total = None
    q_total = None
    for m in range(members):
        probs = []
        for h in range(per):
            lanes = slice(h * node_rows, (h + 1) * node_rows)
            den = jnp.zeros((8, node_rows), f32)
            inner = jnp.zeros((8, node_rows), f32)
            for c in range(0, table, strip):
                box = (m, slice(c, c + strip), lanes)
                t = jnp.tanh(score[box] * (scale / score_cap))
                e = jnp.exp2(t * (score_cap / math.log(2.0))) * mask_ref[c : c + strip]
                den = den + jnp.sum(e.reshape(strip // 8, 8, node_rows), axis=0)
                inner = inner + jnp.sum((e * grad[box]).reshape(strip // 8, 8, node_rows), axis=0)
                score[box] = e
                slope[box] = e * (scale - scale * (t * t))
            r = 1.0 / jnp.sum(den, axis=0, keepdims=True)
            inner = jnp.sum(inner, axis=0, keepdims=True) * r
            column = []
            scores = []
            for c in range(0, table, strip):
                box = (m, slice(c, c + strip), lanes)
                column.append((score[box] * r).astype(bf16))
                scores.append(((slope[box] * r) * (grad[box] - inner)).astype(bf16))
            probs.append((jnp.concatenate(column, axis=0), jnp.concatenate(scores, axis=0)))
        pb = jnp.concatenate([p for p, _ in probs], axis=1)
        ds = jnp.concatenate([s for _, s in probs], axis=1)
        ktg = jnp.concatenate([loc[KT, m], halo[2, m]], axis=1)
        vtg = jnp.concatenate([loc[VT, m], halo[3, m]], axis=1)
        att, dqt = [], []
        for h in range(0, per, 2):
            lanes = slice(h * node_rows, (h + 2) * node_rows)
            rows = slice(h * head, (h + 2) * head)
            a = nn(vtg[rows], pb[:, lanes])
            b = nn(ktg[rows], ds[:, lanes])
            for j in range(2):
                inside = (slice(j * head, (j + 1) * head), slice(j * node_rows, (j + 1) * node_rows))
                att.append(a[inside].astype(bf16))
                dqt.append(b[inside].astype(bf16))
        att = jnp.concatenate(att, axis=0)
        dq = jnp.concatenate(dqt, axis=0).T
        dk = nn(ds, spread_n(loc[Q, m])).astype(bf16)
        dv = nn(pb, spread_n(loc[G, m])).astype(bf16)
        dq_ref[m], dk_ref[m], dv_ref[m] = dq, dk, dv
        wo_term = nn(att, og_ref[m])
        kv_term = nn(xtf[m], jnp.concatenate([dk, dv], axis=1))
        q_term = nn(xtf[m, :, :node_rows], dq)
        wo_total = wo_term if m == 0 else wo_total + wo_term
        kv_total = kv_term if m == 0 else kv_total + kv_term
        q_total = q_term if m == 0 else q_total + q_term

    planes, _, _, rows, _ = dw.shape
    inner_planes = wos.shape[0]
    dw[:, :, :, :, :128] = q_total.reshape(planes, 2, 2, rows, 128)
    dw[:, :, :, :, 128:] = kv_total.reshape(planes, 2, 2, rows, 256)
    wos[...] = wo_total.reshape(inner_planes, 2, 2, rows, width)
    me = me_ref[0]
    c, y, z = me % 2, (me // 2) % 2, me // 4
    qkv = slice(at, at + 384)
    for k in range(planes):
        zk = (z + k) % planes
        own_ref[k, :, qkv] = dw[zk, y, c]
        other_ref[k, :, qkv] = dw[zk, 1 - y, c]
        send_other[k, :, qkv] = dw[zk, 1 - y, 1 - c].astype(bf16)
        send_own[k, :, qkv] = dw[zk, y, 1 - c].astype(bf16)
    last = slice(at + 384, at + 512)
    for i in range(inner_planes):
        for n in range(width // 128):
            k = n * inner_planes + i
            lanes = slice(n * 128, (n + 1) * 128)
            own_ref[k, :, last] = wos[i, y, c, :, lanes]
            other_ref[k, :, last] = wos[i, 1 - y, c, :, lanes]
            send_other[k, :, last] = wos[i, 1 - y, 1 - c, :, lanes].astype(bf16)
            send_own[k, :, last] = wos[i, y, 1 - c, :, lanes].astype(bf16)


def node_kernel(groups, skip, me_ref, *refs):
    refs = refs[skip:]
    dqs, dks, dvs = refs[:groups], refs[groups : 2 * groups], refs[2 * groups : 3 * groups]
    wq_ref, wk_ref, wv_ref, node_ref, first_ref, second_ref, plus_ref, minus_ref, both = refs[3 * groups :]
    members, node_rows, _ = dqs[0].shape
    slots = plus_ref.shape[2]

    def whole(parts, m):
        return jnp.concatenate([part[m] for part in parts], axis=1)

    for m in range(members):
        spread = nt(whole(dks, m), wk_ref[...]) + nt(whole(dvs, m), wv_ref[...])
        node_ref[m] = spread[:node_rows] + nt(whole(dqs, m), wq_ref[...])
        halo = spread[node_rows:].astype(bf16)
        for ref, order in (
            (both.at[0], (1, 4, 7)),
            (both.at[1], (0, 6, 5)),
            (plus_ref, (3,)),
            (minus_ref, (2,)),
        ):
            for i, k in enumerate(order):
                ref[m, i] = halo[k * slots : (k + 1) * slots]
    to_swaps(both, me_ref[0] % 2, first_ref, second_ref)


def sums(owns, core_in, y_in, k):
    total = jnp.concatenate(
        [own[k] + core[k].astype(f32) for own, core in zip(owns, core_in)], axis=1
    ) + y_in[k].astype(f32)
    return [total[:, at : at + 512] for at in range(0, total.shape[1], 512)]


def gather_projection(parts, k, planes, projection_ref, start):
    inner_planes = planes * 128 // projection_ref.shape[2]
    quarter, inner = divmod(k, inner_planes)
    for i, part in enumerate(parts):
        plane = start + i * inner_planes + inner
        projection_ref[plane, :, quarter * 128 : (quarter + 1) * 128] = part[:, 384:]


def first_kernel(pieces, me_ref, *refs):
    later, later_core, refs = refs[:pieces], refs[pieces : 2 * pieces], refs[2 * pieces :]
    own, core_in, y_in, next_ref, own_ref, projection_ref, sent = refs
    for i, (ref, core) in enumerate(zip(later, later_core)):
        next_ref[:, :, i * 512 : (i + 1) * 512] = (ref[...] + core[...].astype(f32)).astype(bf16)
    planes = sent.shape[0]
    z = me_ref[0] // 4
    for k in range(planes):
        parts = sums([own], [core_in], y_in, k)
        gather_projection(parts, k, planes, projection_ref, 0)
        row = jnp.concatenate([part[:, :384] for part in parts], axis=1)
        sent[(z + k) % planes] = row.astype(bf16)
        if k == 0:
            own_ref[...] = row


def second_kernel(skip, pieces, stride, me_ref, *refs):
    refs = refs[skip:]
    first_ref, back_plus, back_minus, first_in, second_in, y_in = refs[:6]
    owns, core_in = refs[6 : 6 + pieces], refs[6 + pieces : 6 + 2 * pieces]
    own_ref, sent, home_first, home_second = refs[6 + 2 * pieces : -3]
    projection_ref, came, both = refs[-3:]
    done = first_ref.shape[0]
    planes = sent.shape[0]
    projection_ref[:done] = first_ref[...]
    held = []
    for k in range(planes):
        parts = sums(owns, core_in, y_in, k)
        gather_projection(parts, k, planes, projection_ref, done)
        held.append(jnp.concatenate([part[:, :384] for part in parts], axis=1))
    z = me_ref[0] // 4
    for k in range(planes):
        zk = (z + k) % planes
        row = jnp.concatenate([held[k], projection_ref[zk]], axis=1)
        sent[zk] = row.astype(bf16)
        if k == 0:
            own_ref[...] = row
    from_swaps(came, me_ref[0] % 2, first_in, second_in)
    for side, own in enumerate((back_plus, back_minus)):
        both[side, :, 0:1] = own[...]
        both[side, :, 1:2] = came[1, :, 2 - side : 3 - side]
        both[side, :, 2:3] = came[0, :, 2 - side : 3 - side]
    to_swaps(both, me_ref[0] // stride % 2, home_first, home_second)


def finish_kernel(
    stride, me_ref, send_ref, node_ref, first_in, second_in, home_first, home_second, out_ref,
    came, home,
):
    members, node_rows, _ = node_ref.shape
    pick = sent_selector(send_ref[0], node_rows).astype(bf16)
    from_swaps(came, me_ref[0] % 2, first_in, second_in)
    from_swaps(home, me_ref[0] // stride % 2, home_first, home_second)
    for m in range(members):
        pieces = [None] * 8
        pieces[0], pieces[1] = came[1, m, 0], came[0, m, 0]
        for side, order in enumerate(((3, 5, 7), (2, 6, 4))):
            for i, k in enumerate(order):
                pieces[k] = home[side, m, i]
        arriving = jnp.concatenate(pieces, axis=0)
        out_ref[m] = (node_ref[m] + nn(pick, arriving)).astype(bf16)


def weight_kernel(me_ref, after_ref, own_a, own_b, z_a, z_b, out_ref):
    planes = z_a.shape[0]
    z = me_ref[0] // 4
    a, b = own_a[...], own_b[...]
    for k in range(1, planes):
        a = a + z_a[(z + k) % planes].astype(f32)
        b = b + z_b[(z + k) % planes].astype(f32)
    half = a.shape[1] // 384
    width = 256 * half
    for i, part in enumerate((a, b)):
        for j in range(half):
            for n in range(3):
                at = n * width + (i * half + j) * 128
                out_ref[:, at : at + 128] = part[:, j * 384 + n * 128 : j * 384 + (n + 1) * 128]
    out_ref[:, 3 * width :] = b[:, 384 * half :]


def call(kernel, outs, operands, specs=None, scratch=(), limit=12, final=False):
    specs = list(specs or ())
    specs += [pltpu.VMEM] * (len(operands) - len(specs))
    operands = [
        pltpu.with_memory_space_constraint(o, s) if s in (pltpu.HBM, pltpu.VMEM) else o
        for o, s in zip(operands, specs)
    ]
    return pl.pallas_call(
        kernel,
        out_shape=[jax.ShapeDtypeStruct(*o) if final else pltpu.VMEM(*o) for o in outs],
        in_specs=[pl.BlockSpec(memory_space=s) for s in specs],
        scratch_shapes=list(scratch),
        compiler_params=pltpu.CompilerParams(vmem_limit_bytes=limit * MIB),
        cost_estimate=pl.CostEstimate(flops=10**6, bytes_accessed=10**4, transcendentals=0),
    )(*operands)


def body(
    node_features, out_grad, w_query, w_key, w_value, w_out, neighbours, neighbour_count, send_rows
):
    members, node_rows, width = node_features.shape
    count = lax.axis_size("patch")
    row_width = min(8, count // 4)
    _, adjacent, slots = send_rows.shape
    table = node_rows + adjacent * slots
    groups = width // 128
    me = lax.axis_index("patch")
    three = ((members, 3, slots, width), bf16)
    one = ((members, 1, slots, width), bf16)

    place = me.reshape(1)
    trio = pltpu.VMEM((2, *three[0]), bf16)
    *outgoing, own_right, own_left, x = call(
        functools.partial(gather_kernel, slots, row_width),
        [three, three, one, one, (node_features.shape, bf16)],
        (place, send_rows, node_features),
        specs=[pltpu.SMEM] + [pltpu.HBM] * 2,
        scratch=[pltpu.VMEM(send_rows.shape, jnp.int32), trio, pltpu.SemaphoreType.DMA((2,))],
    )
    arrived = swap(outgoing, row_width)
    square = ((width, width), bf16)
    counts = neighbour_count.reshape(1, node_rows)
    *loc, xt, wq, wk, wv, og, neigh, counts = call(
        functools.partial(local_kernel, groups),
        [((8, members, node_rows, 128), bf16)] * groups
        + [((members, width, node_rows), bf16), square, square, square, (out_grad.shape, bf16)]
        + [(neighbours.shape, jnp.int32), (counts.shape, jnp.int32)],
        (own_right, x, w_query, w_key, w_value, out_grad, neighbours, counts, w_out),
        specs=[pl.ANY, pltpu.VMEM] + [pltpu.HBM] * 7,
        scratch=[pltpu.VMEM((width, width), bf16), pltpu.SemaphoreType.DMA((7,))],
        limit=16,
    )
    *outgoing, plus, minus = call(
        functools.partial(relay_kernel, row_width), [three, three, one, one],
        (place, loc[0], own_right, own_left, *arrived), specs=[pltpu.SMEM, pl.ANY],
        scratch=[trio, trio],
    )
    arrived = swap(outgoing, 1)
    (mask,) = call(
        mask_kernel, [((table, node_rows), f32)], (outgoing[0], neigh, counts), specs=[pl.ANY]
    )
    *halo, xtf = call(
        halo_kernel,
        [((4, members, node_rows, 128), bf16)] * groups + [((members, width, table), bf16)],
        (place, plus, minus, *arrived, xt, wk, wv), specs=[pltpu.SMEM], scratch=[trio],
    )

    planes, rows = count // 4, width // count
    inner_planes = planes * 128 // width
    flip = [(i, i ^ 1) for i in range(count)]
    flop = [(i, i ^ 2) for i in range(count)]
    grads = []

    def attention(extra, which):
        wide = 512 * len(which)
        outs = call(
            functools.partial(attention_kernel, len(extra), len(which)),
            [((planes, rows, wide), kind) for kind in (f32, f32, bf16, bf16)]
            + [
                ((members, node_rows, 128), bf16),
                ((members, table, 128), bf16),
                ((members, table, 128), bf16),
            ]
            * len(which),
            (
                place, *extra, *[loc[g] for g in which], *[halo[g] for g in which], mask, xtf, og,
            ),
            specs=[pltpu.SMEM] + [pl.ANY] * len(extra),
            scratch=[pltpu.VMEM((members, table, 512), f32)] * 3
            + [
                pltpu.VMEM((planes, 2, 2, rows, 384), f32),
                pltpu.VMEM((inner_planes, 2, 2, rows, width), f32),
            ],
            limit=24,
        )
        grads.extend(outs[4:])
        own, other, send_other, send_own = outs[:4]
        return own, other, lax.ppermute(send_other, "patch", flip), lax.ppermute(send_own, "patch", flip)

    def along_z(sent):
        lines = [[w + 4 * z for z in range(planes)] for w in range(4)]
        return lax.all_to_all(sent, "patch", 0, 0, axis_index_groups=lines, tiled=True)

    half = groups // 2
    wide = 384 * half
    own_a, other, core_other, core_own = attention((), range(half))
    y_sent = (other + core_other.astype(f32)).astype(bf16)
    y_a = lax.ppermute(y_sent, "patch", flop)
    later = []
    for g in range(half, groups):
        later.append(attention((y_sent,) if g == groups - 1 else (), range(g, g + 1)))
    own_b, other_b, core_other_b, core_own_b = zip(*later)
    y_sent, own_a, out_a, sent = call(
        functools.partial(first_kernel, len(later)),
        [(y_sent.shape, bf16), ((rows, wide), f32), ((half * inner_planes, rows, width), f32)]
        + [((planes, rows, wide), bf16)],
        (place, *other_b, *core_other_b, own_a, core_own, y_a), specs=[pltpu.SMEM],
    )
    y_b = lax.ppermute(y_sent, "patch", flop)
    z_a = along_z(sent)
    node, *outgoing, back_plus, back_minus = call(
        functools.partial(node_kernel, groups, 2),
        [((members, node_rows, width), f32), three, three, one, one],
        (place, y_sent, sent, *grads[0::3], *grads[1::3], *grads[2::3], wq, wk, wv),
        specs=[pltpu.SMEM] + [pl.ANY] * 2, scratch=[trio],
    )
    back = swap(outgoing, 1)
    own_b, sent, *outgoing = call(
        functools.partial(second_kernel, 2, len(later), row_width),
        [((rows, wide + width), f32), ((planes, rows, wide + width), bf16), three, three],
        (
            place, node, z_a, out_a, back_plus, back_minus, *back, y_b, *own_b, *core_own_b,
        ),
        specs=[pltpu.SMEM] + [pl.ANY] * 2,
        scratch=[pltpu.VMEM((planes, rows, width), f32), trio, trio],
    )
    z_b = along_z(sent)
    home = swap(outgoing, row_width)
    (node_grad,) = call(
        functools.partial(finish_kernel, row_width), [((members, node_rows, width), bf16)],
        (place, send_rows, node, *back, *home), specs=[pltpu.SMEM], scratch=[trio, trio],
        final=True,
    )
    (weight_grad,) = call(
        weight_kernel, [((rows, 4 * width), f32)],
        (place, node_grad, own_a, own_b, z_a, z_b), specs=[pltpu.SMEM, pl.ANY], final=True,
    )
    return (node_grad, weight_grad)


def solution(mesh):
    in_specs = (
        P("groups", "patch", None),
        P("groups", "patch", None),
        P(),
        P(),
        P(),
        P(),
        P("patch", None),
        P("patch"),
        P("patch", None, None),
    )
    out_specs = (P("groups", "patch", None), P(("groups", "patch"), None))
    return jax.shard_map(body, mesh=mesh, in_specs=in_specs, out_specs=out_specs, check_vma=False)
```

```python
import functools
import math

import jax
import jax.numpy as jnp
from jax import lax
from jax.experimental import pallas as pl
from jax.experimental.pallas import tpu as pltpu
from jax.sharding import PartitionSpec as P

HEADS = 16
score_cap = 5.0
MIB = 1024 * 1024
f32 = jnp.float32
bf16 = jnp.bfloat16


def nn(a, b):
    return lax.dot_general(a, b, (((1,), (0,)), ((), ())), preferred_element_type=f32)


def nt(a, b):
    return lax.dot_general(a, b, (((1,), (1,)), ((), ())), preferred_element_type=f32)


def shifted(shard, by):
    count = lax.axis_size("patch")
    return lax.ppermute(shard, "patch", [(i, (i + by) % count) for i in range(count)])


def neighbours_apart(count, stride):
    first, second = [], []
    for i in range(count):
        up, down = (i + stride) % count, (i - stride) % count
        even = i // stride % 2 == 0
        first.append((i, up if even else down))
        second.append((i, down if even else up))
    return first, second


def swap(pair, stride):
    return [
        lax.ppermute(shard, "patch", perm)
        for shard, perm in zip(pair, neighbours_apart(lax.axis_size("patch"), stride))
    ]


def to_swaps(both, odd, first_ref, second_ref):
    first_ref[...] = both[odd]
    second_ref[...] = both[1 - odd]


def from_swaps(both, odd, first_ref, second_ref):
    both[1 - odd] = first_ref[...]
    both[odd] = second_ref[...]


def sent_selector(send_rows, node_rows):
    adjacent, slots = send_rows.shape
    halo = adjacent * slots
    wide = jnp.concatenate([send_rows] * adjacent, axis=1)
    own = lax.broadcasted_iota(jnp.int32, (adjacent, halo), 1) // slots == lax.broadcasted_iota(
        jnp.int32, (adjacent, halo), 0
    )
    ids = jnp.sum(jnp.where(own, wide, 0), axis=0, keepdims=True)
    nodes = lax.broadcasted_iota(jnp.int32, (node_rows, halo), 0)
    return jnp.where(nodes == ids, 1.0, 0.0).astype(f32)


def gather_kernel(
    slots, send_hbm, x_hbm, plus_ref, minus_ref, right_ref, left_ref, x_ref, send_ref, sem
):
    copies = [
        pltpu.make_async_copy(send_hbm, send_ref, sem.at[0]),
        pltpu.make_async_copy(x_hbm, x_ref, sem.at[1]),
    ]
    for copy in copies:
        copy.start()
    copies[0].wait()
    members, node_rows, _ = x_ref.shape
    pick = sent_selector(send_ref[0], node_rows).T.astype(bf16)
    copies[1].wait()
    for m in range(members):
        rows = nn(pick, x_ref[m]).astype(bf16)

        def part(k):
            return rows[k * slots : (k + 1) * slots]

        for ref, order in ((plus_ref, (2, 6, 4)), (minus_ref, (3, 5, 7))):
            for i, k in enumerate(order):
                ref[m, i] = part(k)
        right_ref[m, 0] = part(0)
        left_ref[m, 0] = part(1)


def relay_kernel(
    me_ref, after_ref, own_right, own_left, plus_ref, minus_ref, first_ref, second_ref, both
):
    for side, own in enumerate((own_right, own_left)):
        both[side, :, 0:1] = own[...]
        both[side, :, 1:2] = plus_ref[:, 1 + side : 2 + side]
        both[side, :, 2:3] = minus_ref[:, 1 + side : 2 + side]
    to_swaps(both, me_ref[0] % 2, first_ref, second_ref)


def gray(z):
    return z ^ (z >> 1)


def plane_of(code):
    z = code
    for shift in range(1, 8):
        z = z ^ (code >> shift)
    return z


def along_z(count, bit):
    planes = count // 4
    return [(i, plane_of(gray(i // 4) ^ (1 << bit)) * 4 + i % 4) for i in range(planes * 4)]


Q, K, V, G, QT, KT, VT, GT = range(8)


def local_kernel(groups, after_ref, x_ref, *refs):
    sources, loc_refs, xt_ref = refs[:7], refs[7 : 7 + groups], refs[7 + groups]
    copied, sem = refs[8 + groups : 15 + groups], refs[-1]
    copies = [
        pltpu.make_async_copy(source, target, sem.at[i])
        for i, (source, target) in enumerate(zip(sources, copied))
    ]
    for copy in copies:
        copy.start()
    members, node_rows, width = x_ref.shape
    x = x_ref[...].reshape(members * node_rows, width)
    for m in range(members):
        xt_ref[m] = x_ref[m].T

    def put(rows, kind):
        for m in range(members):
            for g, ref in enumerate(loc_refs):
                block = rows[m * node_rows : (m + 1) * node_rows, g * 128 : (g + 1) * 128]
                ref[kind, m] = block
                ref[kind + 4, m] = block.T

    wq_ref, wk_ref, wv_ref, og_ref, _, _, wo_ref = copied
    for kind, ref in enumerate((wq_ref, wk_ref, wv_ref)):
        copies[kind].wait()
        put(nn(x, ref[...]).astype(bf16), kind)
    for copy in copies[3:]:
        copy.wait()
    og = og_ref[...].reshape(members * node_rows, width)
    put(nt(og, wo_ref[...]).astype(bf16), G)


def mask_kernel(after_ref, neigh_ref, count_ref, mask_ref):
    neigh = neigh_ref[...].T
    slots, node_rows = neigh.shape
    table = mask_ref.shape[0]
    order = lax.broadcasted_iota(jnp.int32, neigh.shape, 0)
    tail = jnp.where(order >= count_ref[...], neigh, -1)[slots // 2 :]
    half = table // 2
    for part in range(2):
        columns = lax.broadcasted_iota(jnp.int32, (half, node_rows), 0) + part * half
        kept = jnp.ones((half, node_rows), f32)
        for j in range(slots // 2):
            kept = jnp.where(tail[j : j + 1] == columns, 0.0, kept)
        mask_ref[part * half : (part + 1) * half] = kept


def halo_kernel(
    me_ref, plus_ref, minus_ref, first_in, second_in, xt_ref, wk_ref, wv_ref, *refs
):
    halo_refs, xtf_ref, both = refs[:-2], refs[-2], refs[-1]
    members, _, node_rows = xt_ref.shape
    from_swaps(both, me_ref[0] % 2, first_in, second_in)
    for m in range(members):
        pieces = [None] * 8
        for side, order in enumerate(((0, 6, 5), (1, 4, 7))):
            for i, k in enumerate(order):
                pieces[k] = both[side, m, i]
        pieces[2] = plus_ref[m, 0]
        pieces[3] = minus_ref[m, 0]
        halo = jnp.concatenate(pieces, axis=0)
        xtf_ref[m, :, :node_rows] = xt_ref[m]
        xtf_ref[m, :, node_rows:] = halo.T
        for kind, w_ref in enumerate((wk_ref, wv_ref)):
            rows = nn(halo, w_ref[...]).astype(bf16)
            for g, ref in enumerate(halo_refs):
                block = rows[:, g * 128 : (g + 1) * 128]
                ref[kind, m] = block
                ref[kind + 2, m] = block.T


def attention_kernel(extra, here, me_ref, *refs):
    refs = refs[extra:]
    locs, halos, refs = refs[:here], refs[here : 2 * here], refs[2 * here :]
    mask_ref, xtf, og_ref = refs[:3]
    outs, grads, scratch = refs[3:7], refs[7 : 7 + 3 * here], refs[7 + 3 * here :]
    for i in range(here):
        attend(
            me_ref, locs[i], halos[i], mask_ref, xtf, og_ref, outs, 512 * i,
            grads[3 * i : 3 * i + 3], scratch,
        )


def attend(me_ref, loc, halo, mask_ref, xtf, og_ref, out_refs, at, grad_refs, scratch):
    own_ref, other_ref, send_other, send_own = out_refs
    dq_ref, dk_ref, dv_ref = grad_refs
    score, grad, slope, dw, wos = scratch
    _, members, node_rows, _ = loc.shape
    table = mask_ref.shape[0]
    width = og_ref.shape[2]
    head = width // HEADS
    per = 128 // head
    scale = 1.0 / math.sqrt(head)

    row_head = lax.broadcasted_iota(jnp.int32, (128, node_rows), 0) // head
    lane_head = lax.broadcasted_iota(jnp.int32, (node_rows, 128), 1) // head

    def spread_t(block):
        zero = jnp.zeros_like(block)
        return jnp.concatenate([jnp.where(row_head == h, block, zero) for h in range(per)], axis=1)

    def spread_n(block):
        zero = jnp.zeros_like(block)
        return jnp.concatenate([jnp.where(lane_head == h, block, zero) for h in range(per)], axis=0)

    strip = 64
    for m in range(members):
        kg = jnp.concatenate([loc[K, m], halo[0, m]], axis=0)
        vg = jnp.concatenate([loc[V, m], halo[1, m]], axis=0)
        score[m] = nn(kg, spread_t(loc[QT, m]))
        grad[m] = nn(vg, spread_t(loc[GT, m]))

    wo_total = None
    kv_total = None
    q_total = None
    for m in range(members):
        probs = []
        for h in range(per):
            lanes = slice(h * node_rows, (h + 1) * node_rows)
            den = jnp.zeros((8, node_rows), f32)
            inner = jnp.zeros((8, node_rows), f32)
            for c in range(0, table, strip):
                box = (m, slice(c, c + strip), lanes)
                t = jnp.tanh(score[box] * (scale / score_cap))
                e = jnp.exp2(t * (score_cap / math.log(2.0))) * mask_ref[c : c + strip]
                den = den + jnp.sum(e.reshape(strip // 8, 8, node_rows), axis=0)
                inner = inner + jnp.sum((e * grad[box]).reshape(strip // 8, 8, node_rows), axis=0)
                score[box] = e
                slope[box] = e * (scale - scale * (t * t))
            r = 1.0 / jnp.sum(den, axis=0, keepdims=True)
            inner = jnp.sum(inner, axis=0, keepdims=True) * r
            column = []
            scores = []
            for c in range(0, table, strip):
                box = (m, slice(c, c + strip), lanes)
                column.append((score[box] * r).astype(bf16))
                scores.append(((slope[box] * r) * (grad[box] - inner)).astype(bf16))
            probs.append((jnp.concatenate(column, axis=0), jnp.concatenate(scores, axis=0)))
        pb = jnp.concatenate([p for p, _ in probs], axis=1)
        ds = jnp.concatenate([s for _, s in probs], axis=1)
        ktg = jnp.concatenate([loc[KT, m], halo[2, m]], axis=1)
        vtg = jnp.concatenate([loc[VT, m], halo[3, m]], axis=1)
        att, dqt = [], []
        for h in range(0, per, 2):
            lanes = slice(h * node_rows, (h + 2) * node_rows)
            rows = slice(h * head, (h + 2) * head)
            a = nn(vtg[rows], pb[:, lanes])
            b = nn(ktg[rows], ds[:, lanes])
            for j in range(2):
                inside = (slice(j * head, (j + 1) * head), slice(j * node_rows, (j + 1) * node_rows))
                att.append(a[inside].astype(bf16))
                dqt.append(b[inside].astype(bf16))
        att = jnp.concatenate(att, axis=0)
        dq = jnp.concatenate(dqt, axis=0).T
        dk = nn(ds, spread_n(loc[Q, m])).astype(bf16)
        dv = nn(pb, spread_n(loc[G, m])).astype(bf16)
        dq_ref[m], dk_ref[m], dv_ref[m] = dq, dk, dv
        wo_term = nn(att, og_ref[m])
        kv_term = nn(xtf[m], jnp.concatenate([dk, dv], axis=1))
        q_term = nn(xtf[m, :, :node_rows], dq)
        wo_total = wo_term if m == 0 else wo_total + wo_term
        kv_total = kv_term if m == 0 else kv_total + kv_term
        q_total = q_term if m == 0 else q_total + q_term

    planes, _, _, rows, _ = dw.shape
    inner_planes = wos.shape[0]
    dw[:, :, :, :, :128] = q_total.reshape(planes, 2, 2, rows, 128)
    dw[:, :, :, :, 128:] = kv_total.reshape(planes, 2, 2, rows, 256)
    wos[...] = wo_total.reshape(inner_planes, 2, 2, rows, width)
    me = me_ref[0]
    c, y, z = me % 2, (me // 2) % 2, me // 4
    qkv = slice(at, at + 384)
    for k in range(planes):
        zk = plane_of(gray(z) ^ k)
        own_ref[k, :, qkv] = dw[zk, y, c]
        other_ref[k, :, qkv] = dw[zk, 1 - y, c]
        send_other[k, :, qkv] = dw[zk, 1 - y, 1 - c].astype(bf16)
        send_own[k, :, qkv] = dw[zk, y, 1 - c].astype(bf16)
    last = slice(at + 384, at + 512)
    for i in range(inner_planes):
        for n in range(width // 128):
            k = n * inner_planes + i
            lanes = slice(n * 128, (n + 1) * 128)
            own_ref[k, :, last] = wos[i, y, c, :, lanes]
            other_ref[k, :, last] = wos[i, 1 - y, c, :, lanes]
            send_other[k, :, last] = wos[i, 1 - y, 1 - c, :, lanes].astype(bf16)
            send_own[k, :, last] = wos[i, y, 1 - c, :, lanes].astype(bf16)


def node_kernel(groups, skip, me_ref, *refs):
    refs = refs[skip:]
    dqs, dks, dvs = refs[:groups], refs[groups : 2 * groups], refs[2 * groups : 3 * groups]
    wq_ref, wk_ref, wv_ref, node_ref, first_ref, second_ref, plus_ref, minus_ref, both = refs[3 * groups :]
    members, node_rows, _ = dqs[0].shape
    slots = plus_ref.shape[2]

    def whole(parts, m):
        return jnp.concatenate([part[m] for part in parts], axis=1)

    for m in range(members):
        spread = nt(whole(dks, m), wk_ref[...]) + nt(whole(dvs, m), wv_ref[...])
        node_ref[m] = spread[:node_rows] + nt(whole(dqs, m), wq_ref[...])
        halo = spread[node_rows:].astype(bf16)
        for ref, order in (
            (both.at[0], (1, 4, 7)),
            (both.at[1], (0, 6, 5)),
            (plus_ref, (3,)),
            (minus_ref, (2,)),
        ):
            for i, k in enumerate(order):
                ref[m, i] = halo[k * slots : (k + 1) * slots]
    to_swaps(both, me_ref[0] % 2, first_ref, second_ref)


def sums(owns, core_in, y_in, k):
    total = jnp.concatenate(
        [own[k] + core[k].astype(f32) for own, core in zip(owns, core_in)], axis=1
    ) + y_in[k].astype(f32)
    return [total[:, at : at + 512] for at in range(0, total.shape[1], 512)]


def gather_projection(parts, k, planes, projection_ref, start):
    inner_planes = planes * 128 // projection_ref.shape[2]
    quarter, inner = divmod(k, inner_planes)
    for i, part in enumerate(parts):
        plane = start + i * inner_planes + inner
        projection_ref[plane, :, quarter * 128 : (quarter + 1) * 128] = part[:, 384:]


def pack_kernel(pieces, after_ref, *refs):
    for i, (ref, core) in enumerate(zip(refs[:pieces], refs[pieces:-1])):
        refs[-1][:, :, i * 512 : (i + 1) * 512] = (ref[...] + core[...].astype(f32)).astype(bf16)


def halve(rows, kept_ref, sent_ref):
    for i, row in enumerate(rows):
        if i % 2 == 0:
            kept_ref[i // 2] = row
            continue
        pieces = row.shape[1] // 256
        for n in range(pieces):
            sent_ref[i // 2 * pieces + n] = row[:, n * 256 : (n + 1) * 256].astype(bf16)


def add_received(kept_ref, received_ref):
    planes, _, wide = kept_ref.shape
    pieces = wide // 256
    return [
        kept_ref[i]
        + jnp.concatenate([received_ref[i * pieces + n] for n in range(pieces)], axis=1).astype(f32)
        for i in range(planes)
    ]


def flatten(rows, ref, at):
    members = rows.shape[0]
    height = ref.shape[1]
    for m in range(members):
        for i in range(3):
            flat = jnp.concatenate([rows[m, i, :, :256], rows[m, i, :, 256:]], axis=0)
            each = flat.shape[0] // height
            start = at + (m * 3 + i) * each
            ref[start : start + each] = flat.reshape(each, height, 256)


def unflatten(ref, at, m, i, slots):
    each = 2 * slots // ref.shape[1]
    start = at + (m * 3 + i) * each
    flat = ref[start : start + each].reshape(2 * slots, 256)
    return jnp.concatenate([flat[:slots], flat[slots:]], axis=1)


def first_kernel(
    stride, skip, me_ref, *refs
):
    refs = refs[skip:]
    own, core_in, y_in, back_plus, back_minus, first_in, second_in = refs[:7]
    kept_ref, projection_ref, sent_ref, home_second, came, both = refs[7:]
    planes = own.shape[0]
    rows = []
    for k in range(planes):
        parts = sums([own], [core_in], y_in, k)
        gather_projection(parts, k, planes, projection_ref, 0)
        rows.append(jnp.concatenate([part[:, :384] for part in parts], axis=1))
    halve(rows, kept_ref, sent_ref)
    from_swaps(came, me_ref[0] % 2, first_in, second_in)
    for side, own_rows in enumerate((back_plus, back_minus)):
        both[side, :, 0:1] = own_rows[...]
        both[side, :, 1:2] = came[1, :, 2 - side : 3 - side]
        both[side, :, 2:3] = came[0, :, 2 - side : 3 - side]
    odd = me_ref[0] // stride % 2
    flatten(both[odd], sent_ref, planes // 2 * rows[0].shape[1] // 256)
    flatten(both[1 - odd], home_second, 0)


def second_kernel(skip, pieces, me_ref, *refs):
    refs = refs[skip:]
    first_ref, y_in = refs[:2]
    owns, core_in = refs[2 : 2 + pieces], refs[2 + pieces : 2 + 2 * pieces]
    kept_ref, sent_ref, projection_ref = refs[2 + 2 * pieces :]
    done = first_ref.shape[0]
    planes = projection_ref.shape[0]
    projection_ref[:done] = first_ref[...]
    held = []
    for k in range(planes):
        parts = sums(owns, core_in, y_in, k)
        gather_projection(parts, k, planes, projection_ref, done)
        held.append(jnp.concatenate([part[:, :384] for part in parts], axis=1))
    z = me_ref[0] // 4
    halve(
        [
            jnp.concatenate([held[k], projection_ref[plane_of(gray(z) ^ k)]], axis=1)
            for k in range(planes)
        ],
        kept_ref, sent_ref,
    )


def step_kernel(extra, after_ref, kept_in, received, *refs):
    kept_ref, sent_ref = refs[-2:]
    halve(add_received(kept_in, received), kept_ref, sent_ref)
    if extra:
        sent_ref[sent_ref.shape[0] - extra :] = refs[0][...]


def finish_kernel(
    stride, at_first, at_second, me_ref, after_ref, send_ref, node_ref, first_in, second_in,
    home_first, home_second, out_ref, came, home,
):
    members, node_rows, _ = node_ref.shape
    slots = first_in.shape[2]
    pick = sent_selector(send_ref[0], node_rows).astype(bf16)
    from_swaps(came, me_ref[0] % 2, first_in, second_in)
    odd = me_ref[0] // stride % 2
    for m in range(members):
        for i in range(3):
            home[1 - odd, m, i] = unflatten(home_first, at_first, m, i, slots)
            home[odd, m, i] = unflatten(home_second, at_second, m, i, slots)
    for m in range(members):
        pieces = [None] * 8
        pieces[0], pieces[1] = came[1, m, 0], came[0, m, 0]
        for side, order in enumerate(((3, 5, 7), (2, 6, 4))):
            for i, k in enumerate(order):
                pieces[k] = home[side, m, i]
        arriving = jnp.concatenate(pieces, axis=0)
        out_ref[m] = (node_ref[m] + nn(pick, arriving)).astype(bf16)


def weight_kernel(after_ref, kept_a, in_a, kept_b, in_b, out_ref):
    (a,) = add_received(kept_a, in_a)
    (b,) = add_received(kept_b, in_b)
    half = a.shape[1] // 384
    width = 256 * half
    for i, part in enumerate((a, b)):
        for j in range(half):
            for n in range(3):
                at = n * width + (i * half + j) * 128
                out_ref[:, at : at + 128] = part[:, j * 384 + n * 128 : j * 384 + (n + 1) * 128]
    out_ref[:, 3 * width :] = b[:, 384 * half :]


def call(kernel, outs, operands, specs=None, scratch=(), limit=12, final=False):
    specs = list(specs or ())
    specs += [pltpu.VMEM] * (len(operands) - len(specs))
    operands = [
        pltpu.with_memory_space_constraint(o, s) if s in (pltpu.HBM, pltpu.VMEM) else o
        for o, s in zip(operands, specs)
    ]
    return pl.pallas_call(
        kernel,
        out_shape=[jax.ShapeDtypeStruct(*o) if final else pltpu.VMEM(*o) for o in outs],
        in_specs=[pl.BlockSpec(memory_space=s) for s in specs],
        scratch_shapes=list(scratch),
        compiler_params=pltpu.CompilerParams(vmem_limit_bytes=limit * MIB),
        cost_estimate=pl.CostEstimate(flops=10**6, bytes_accessed=10**4, transcendentals=0),
    )(*operands)


def body(
    node_features, out_grad, w_query, w_key, w_value, w_out, neighbours, neighbour_count, send_rows
):
    members, node_rows, width = node_features.shape
    count = lax.axis_size("patch")
    row_width = min(8, count // 4)
    _, adjacent, slots = send_rows.shape
    table = node_rows + adjacent * slots
    groups = width // 128
    me = lax.axis_index("patch")
    three = ((members, 3, slots, width), bf16)
    one = ((members, 1, slots, width), bf16)

    place = me.reshape(1)
    trio = pltpu.VMEM((2, *three[0]), bf16)
    to_plus, to_minus, own_right, own_left, x = call(
        functools.partial(gather_kernel, slots),
        [three, three, one, one, (node_features.shape, bf16)],
        (send_rows, node_features),
        specs=[pltpu.HBM] * 2,
        scratch=[pltpu.VMEM(send_rows.shape, jnp.int32), pltpu.SemaphoreType.DMA((2,))],
    )
    plus = shifted(to_plus, row_width)
    minus = shifted(to_minus, -row_width)
    square = ((width, width), bf16)
    counts = neighbour_count.reshape(1, node_rows)
    *loc, xt, wq, wk, wv, og, neigh, counts = call(
        functools.partial(local_kernel, groups),
        [((8, members, node_rows, 128), bf16)] * groups
        + [((members, width, node_rows), bf16), square, square, square, (out_grad.shape, bf16)]
        + [(neighbours.shape, jnp.int32), (counts.shape, jnp.int32)],
        (own_right, x, w_query, w_key, w_value, out_grad, neighbours, counts, w_out),
        specs=[pl.ANY, pltpu.VMEM] + [pltpu.HBM] * 7,
        scratch=[pltpu.VMEM((width, width), bf16), pltpu.SemaphoreType.DMA((7,))],
        limit=16,
    )
    outgoing = call(
        relay_kernel, [three, three], (place, loc[0], own_right, own_left, plus, minus),
        specs=[pltpu.SMEM, pl.ANY], scratch=[trio],
    )
    arrived = swap(outgoing, 1)
    (mask,) = call(
        mask_kernel, [((table, node_rows), f32)], (outgoing[0], neigh, counts), specs=[pl.ANY]
    )
    *halo, xtf = call(
        halo_kernel,
        [((4, members, node_rows, 128), bf16)] * groups + [((members, width, table), bf16)],
        (place, plus, minus, *arrived, xt, wk, wv), specs=[pltpu.SMEM], scratch=[trio],
    )

    planes, rows = count // 4, width // count
    inner_planes = planes * 128 // width
    flip = [(i, i ^ 1) for i in range(count)]
    flop = [(i, i ^ 2) for i in range(count)]
    grads = []

    def attention(extra, which):
        wide = 512 * len(which)
        outs = call(
            functools.partial(attention_kernel, len(extra), len(which)),
            [((planes, rows, wide), kind) for kind in (f32, f32, bf16, bf16)]
            + [
                ((members, node_rows, 128), bf16),
                ((members, table, 128), bf16),
                ((members, table, 128), bf16),
            ]
            * len(which),
            (
                place, *extra, *[loc[g] for g in which], *[halo[g] for g in which], mask, xtf, og,
            ),
            specs=[pltpu.SMEM] + [pl.ANY] * len(extra),
            scratch=[pltpu.VMEM((members, table, 512), f32)] * 3
            + [
                pltpu.VMEM((planes, 2, 2, rows, 384), f32),
                pltpu.VMEM((inner_planes, 2, 2, rows, width), f32),
            ],
            limit=24,
        )
        grads.extend(outs[4:])
        own, other, send_other, send_own = outs[:4]
        return own, other, lax.ppermute(send_other, "patch", flip), lax.ppermute(send_own, "patch", flip)

    half = groups // 2
    wide = 384 * half
    own_a, other, core_other, core_own = attention((), range(half))
    y_sent = (other + core_other.astype(f32)).astype(bf16)
    y_a = lax.ppermute(y_sent, "patch", flop)
    later = []
    for g in range(half, groups):
        later.append(attention((y_sent,) if g == groups - 1 else (), range(g, g + 1)))
    own_b, other_b, core_other_b, core_own_b = zip(*later)
    (y_sent,) = call(
        functools.partial(pack_kernel, len(later)), [(y_sent.shape, bf16)],
        (y_a, *other_b, *core_other_b), specs=[pl.ANY],
    )
    y_b = lax.ppermute(y_sent, "patch", flop)
    node, *outgoing, back_plus, back_minus = call(
        functools.partial(node_kernel, groups, 1),
        [((members, node_rows, width), f32), three, three, one, one],
        (place, y_sent, *grads[0::3], *grads[1::3], *grads[2::3], wq, wk, wv),
        specs=[pltpu.SMEM, pl.ANY], scratch=[trio],
    )
    back = swap(outgoing, 1)

    steps = planes.bit_length() - 1
    homeward = neighbours_apart(count, row_width)
    more = members * 6 * slots // rows
    rides = [along_z(count, i) == homeward[i] if i < steps else False for i in range(2)]

    def exchange(sent, bit):
        return lax.ppermute(sent, "patch", along_z(count, bit))

    def halves(wide, bit, riders=0):
        left = planes >> (bit + 1)
        return [((left, rows, wide), f32), ((left * wide // 256 + riders, rows, 256), bf16)]

    kept_a, projected = halves(wide, 0, more)
    kept_a, out_a, sent, home_second = call(
        functools.partial(first_kernel, row_width, 1),
        [kept_a, ((half * inner_planes, rows, width), f32), projected, ((more, rows, 256), bf16)],
        (place, y_sent, own_a, core_own, y_a, back_plus, back_minus, *back),
        specs=[pltpu.SMEM, pl.ANY], scratch=[trio, trio],
    )
    in_a = exchange(sent, 0)
    home_first = in_a if rides[0] else lax.ppermute(sent, "patch", homeward[0])
    at_first, at_second = planes // 2 * wide // 256, 0
    kept_b, sent_b = call(
        functools.partial(second_kernel, 1, len(later)), halves(wide + width, 0),
        (place, sent, out_a, y_b, *own_b, *core_own_b),
        specs=[pltpu.SMEM, pl.ANY],
        scratch=[pltpu.VMEM((planes, rows, width), f32)],
    )
    in_b = exchange(sent_b, 0)
    after = sent_b
    for bit in range(1, steps):
        riding = bit == 1 and rides[1]
        kept_a, after = call(
            functools.partial(step_kernel, more if riding else 0),
            halves(wide, bit, more if riding else 0),
            (after, kept_a, in_a) + ((home_second,) if riding else ()),
            specs=[pl.ANY],
        )
        in_a = exchange(after, bit)
        if riding:
            home_second = in_a
            at_second = (planes >> (bit + 1)) * wide // 256
        kept_b, after = call(
            functools.partial(step_kernel, 0), halves(wide + width, bit),
            (after, kept_b, in_b), specs=[pl.ANY],
        )
        in_b = exchange(after, bit)
    if not rides[1]:
        home_second = lax.ppermute(home_second, "patch", homeward[1])
    (node_grad,) = call(
        functools.partial(finish_kernel, row_width, at_first, at_second),
        [((members, node_rows, width), bf16)],
        (place, after, send_rows, node, *back, home_first, home_second),
        specs=[pltpu.SMEM, pl.ANY], scratch=[trio, trio], final=True,
    )
    (weight_grad,) = call(
        weight_kernel, [((rows, 4 * width), f32)], (node_grad, kept_a, in_a, kept_b, in_b),
        specs=[pl.ANY], final=True,
    )
    return (node_grad, weight_grad)


def solution(mesh):
    in_specs = (
        P("groups", "patch", None),
        P("groups", "patch", None),
        P(),
        P(),
        P(),
        P(),
        P("patch", None),
        P("patch"),
        P("patch", None, None),
    )
    out_specs = (P("groups", "patch", None), P(("groups", "patch"), None))
    return jax.shard_map(body, mesh=mesh, in_specs=in_specs, out_specs=out_specs, check_vma=False)
```

```python
import functools
import math

import jax
import jax.numpy as jnp
from jax import lax
from jax.experimental import pallas as pl
from jax.experimental.pallas import tpu as pltpu
from jax.sharding import PartitionSpec as P

HEADS = 16
score_cap = 5.0
MIB = 1024 * 1024
f32 = jnp.float32
bf16 = jnp.bfloat16


def nn(a, b):
    return lax.dot_general(a, b, (((1,), (0,)), ((), ())), preferred_element_type=f32)


def nt(a, b):
    return lax.dot_general(a, b, (((1,), (1,)), ((), ())), preferred_element_type=f32)


def shifted(shard, by):
    count = lax.axis_size("patch")
    return lax.ppermute(shard, "patch", [(i, (i + by) % count) for i in range(count)])


def neighbours_apart(count, stride):
    first, second = [], []
    for i in range(count):
        up, down = (i + stride) % count, (i - stride) % count
        even = i // stride % 2 == 0
        first.append((i, up if even else down))
        second.append((i, down if even else up))
    return first, second


def swap(pair, stride):
    return [
        lax.ppermute(shard, "patch", perm)
        for shard, perm in zip(pair, neighbours_apart(lax.axis_size("patch"), stride))
    ]


def to_swaps(both, odd, first_ref, second_ref):
    first_ref[...] = both[odd]
    second_ref[...] = both[1 - odd]


def from_swaps(both, odd, first_ref, second_ref):
    both[1 - odd] = first_ref[...]
    both[odd] = second_ref[...]


def sent_selector(send_rows, node_rows):
    adjacent, slots = send_rows.shape
    halo = adjacent * slots
    wide = jnp.concatenate([send_rows] * adjacent, axis=1)
    own = lax.broadcasted_iota(jnp.int32, (adjacent, halo), 1) // slots == lax.broadcasted_iota(
        jnp.int32, (adjacent, halo), 0
    )
    ids = jnp.sum(jnp.where(own, wide, 0), axis=0, keepdims=True)
    nodes = lax.broadcasted_iota(jnp.int32, (node_rows, halo), 0)
    return jnp.where(nodes == ids, 1.0, 0.0).astype(f32)


def gather_kernel(
    slots, send_hbm, x_hbm, plus_ref, minus_ref, right_ref, left_ref, x_ref, send_ref, sem
):
    copies = [
        pltpu.make_async_copy(send_hbm, send_ref, sem.at[0]),
        pltpu.make_async_copy(x_hbm, x_ref, sem.at[1]),
    ]
    for copy in copies:
        copy.start()
    copies[0].wait()
    members, node_rows, _ = x_ref.shape
    pick = sent_selector(send_ref[0], node_rows).T.astype(bf16)
    copies[1].wait()
    for m in range(members):
        rows = nn(pick, x_ref[m]).astype(bf16)

        def part(k):
            return rows[k * slots : (k + 1) * slots]

        for ref, order in ((plus_ref, (2, 6, 4)), (minus_ref, (3, 5, 7))):
            for i, k in enumerate(order):
                ref[m, i] = part(k)
        right_ref[m, 0] = part(0)
        left_ref[m, 0] = part(1)


def relay_kernel(
    me_ref, after_ref, own_right, own_left, plus_ref, minus_ref, first_ref, second_ref, both
):
    for side, own in enumerate((own_right, own_left)):
        both[side, :, 0:1] = own[...]
        both[side, :, 1:2] = plus_ref[:, 1 + side : 2 + side]
        both[side, :, 2:3] = minus_ref[:, 1 + side : 2 + side]
    to_swaps(both, me_ref[0] % 2, first_ref, second_ref)


def gray(z):
    return z ^ (z >> 1)


def plane_of(code):
    z = code
    for shift in range(1, 8):
        z = z ^ (code >> shift)
    return z


def along_z(count, bit):
    planes = count // 4
    return [(i, plane_of(gray(i // 4) ^ (1 << bit)) * 4 + i % 4) for i in range(planes * 4)]


Q, K, V, G, QT, KT, VT, GT = range(8)


def local_kernel(groups, after_ref, x_ref, *refs):
    sources, loc_refs, xt_ref = refs[:7], refs[7 : 7 + groups], refs[7 + groups]
    copied, sem = refs[8 + groups : 15 + groups], refs[-1]
    copies = [
        pltpu.make_async_copy(source, target, sem.at[i])
        for i, (source, target) in enumerate(zip(sources, copied))
    ]
    for copy in copies:
        copy.start()
    members, node_rows, width = x_ref.shape
    x = x_ref[...].reshape(members * node_rows, width)
    for m in range(members):
        xt_ref[m] = x_ref[m].T

    def put(rows, kind):
        for m in range(members):
            for g, ref in enumerate(loc_refs):
                block = rows[m * node_rows : (m + 1) * node_rows, g * 128 : (g + 1) * 128]
                ref[kind, m] = block
                ref[kind + 4, m] = block.T

    wq_ref, wk_ref, wv_ref, og_ref, _, _, wo_ref = copied
    for kind, ref in enumerate((wq_ref, wk_ref, wv_ref)):
        copies[kind].wait()
        put(nn(x, ref[...]).astype(bf16), kind)
    for copy in copies[3:]:
        copy.wait()
    og = og_ref[...].reshape(members * node_rows, width)
    put(nt(og, wo_ref[...]).astype(bf16), G)


def mask_kernel(after_ref, neigh_ref, count_ref, mask_ref):
    neigh = neigh_ref[...].T
    slots, node_rows = neigh.shape
    table = mask_ref.shape[0]
    order = lax.broadcasted_iota(jnp.int32, neigh.shape, 0)
    tail = jnp.where(order >= count_ref[...], neigh, -1)[slots // 2 :]
    half = table // 2
    for part in range(2):
        columns = lax.broadcasted_iota(jnp.int32, (half, node_rows), 0) + part * half
        kept = jnp.ones((half, node_rows), f32)
        for j in range(slots // 2):
            kept = jnp.where(tail[j : j + 1] == columns, 0.0, kept)
        mask_ref[part * half : (part + 1) * half] = kept


def halo_kernel(
    me_ref, plus_ref, minus_ref, first_in, second_in, xt_ref, wk_ref, wv_ref, *refs
):
    halo_refs, xtf_ref, both = refs[:-2], refs[-2], refs[-1]
    members, _, node_rows = xt_ref.shape
    from_swaps(both, me_ref[0] % 2, first_in, second_in)
    for m in range(members):
        pieces = [None] * 8
        for side, order in enumerate(((0, 6, 5), (1, 4, 7))):
            for i, k in enumerate(order):
                pieces[k] = both[side, m, i]
        pieces[2] = plus_ref[m, 0]
        pieces[3] = minus_ref[m, 0]
        halo = jnp.concatenate(pieces, axis=0)
        xtf_ref[m, :, :node_rows] = xt_ref[m]
        xtf_ref[m, :, node_rows:] = halo.T
        for kind, w_ref in enumerate((wk_ref, wv_ref)):
            rows = nn(halo, w_ref[...]).astype(bf16)
            for g, ref in enumerate(halo_refs):
                block = rows[:, g * 128 : (g + 1) * 128]
                ref[kind, m] = block
                ref[kind + 2, m] = block.T


def attention_kernel(extra, here, me_ref, *refs):
    refs = refs[extra:]
    locs, halos, refs = refs[:here], refs[here : 2 * here], refs[2 * here :]
    mask_ref, xtf, og_ref = refs[:3]
    split = 7 if len(refs) == 15 + 3 * (here - 1) else 6
    outs, grads, scratch = refs[3:split], refs[split : split + 3 * here], refs[split + 3 * here :]
    if split == 6:
        outs = (*outs[:2], outs[2].at[0], outs[2].at[1])
    for i in range(here):
        attend(
            me_ref, locs[i], halos[i], mask_ref, xtf, og_ref, outs, 512 * i,
            grads[3 * i : 3 * i + 3], scratch,
        )


def attend(me_ref, loc, halo, mask_ref, xtf, og_ref, out_refs, at, grad_refs, scratch):
    own_ref, other_ref, send_other, send_own = out_refs
    dq_ref, dk_ref, dv_ref = grad_refs
    score, grad, slope, dw, wos = scratch
    _, members, node_rows, _ = loc.shape
    table = mask_ref.shape[0]
    width = og_ref.shape[2]
    head = width // HEADS
    per = 128 // head
    scale = 1.0 / math.sqrt(head)

    row_head = lax.broadcasted_iota(jnp.int32, (128, node_rows), 0) // head
    lane_head = lax.broadcasted_iota(jnp.int32, (node_rows, 128), 1) // head

    def spread_t(block):
        zero = jnp.zeros_like(block)
        return jnp.concatenate([jnp.where(row_head == h, block, zero) for h in range(per)], axis=1)

    def spread_n(block):
        zero = jnp.zeros_like(block)
        return jnp.concatenate([jnp.where(lane_head == h, block, zero) for h in range(per)], axis=0)

    strip = 64
    for m in range(members):
        kg = jnp.concatenate([loc[K, m], halo[0, m]], axis=0)
        vg = jnp.concatenate([loc[V, m], halo[1, m]], axis=0)
        score[m] = nn(kg, spread_t(loc[QT, m]))
        grad[m] = nn(vg, spread_t(loc[GT, m]))

    wo_total = None
    kv_total = None
    q_total = None
    for m in range(members):
        probs = []
        for h in range(per):
            lanes = slice(h * node_rows, (h + 1) * node_rows)
            den = jnp.zeros((8, node_rows), f32)
            inner = jnp.zeros((8, node_rows), f32)
            for c in range(0, table, strip):
                box = (m, slice(c, c + strip), lanes)
                t = jnp.tanh(score[box] * (scale / score_cap))
                e = jnp.exp2(t * (score_cap / math.log(2.0))) * mask_ref[c : c + strip]
                den = den + jnp.sum(e.reshape(strip // 8, 8, node_rows), axis=0)
                inner = inner + jnp.sum((e * grad[box]).reshape(strip // 8, 8, node_rows), axis=0)
                score[box] = e
                slope[box] = e * (scale - scale * (t * t))
            r = 1.0 / jnp.sum(den, axis=0, keepdims=True)
            inner = jnp.sum(inner, axis=0, keepdims=True) * r
            column = []
            scores = []
            for c in range(0, table, strip):
                box = (m, slice(c, c + strip), lanes)
                column.append((score[box] * r).astype(bf16))
                scores.append(((slope[box] * r) * (grad[box] - inner)).astype(bf16))
            probs.append((jnp.concatenate(column, axis=0), jnp.concatenate(scores, axis=0)))
        pb = jnp.concatenate([p for p, _ in probs], axis=1)
        ds = jnp.concatenate([s for _, s in probs], axis=1)
        ktg = jnp.concatenate([loc[KT, m], halo[2, m]], axis=1)
        vtg = jnp.concatenate([loc[VT, m], halo[3, m]], axis=1)
        att, dqt = [], []
        for h in range(0, per, 2):
            lanes = slice(h * node_rows, (h + 2) * node_rows)
            rows = slice(h * head, (h + 2) * head)
            a = nn(vtg[rows], pb[:, lanes])
            b = nn(ktg[rows], ds[:, lanes])
            for j in range(2):
                inside = (slice(j * head, (j + 1) * head), slice(j * node_rows, (j + 1) * node_rows))
                att.append(a[inside].astype(bf16))
                dqt.append(b[inside].astype(bf16))
        att = jnp.concatenate(att, axis=0)
        dq = jnp.concatenate(dqt, axis=0).T
        dk = nn(ds, spread_n(loc[Q, m])).astype(bf16)
        dv = nn(pb, spread_n(loc[G, m])).astype(bf16)
        dq_ref[m], dk_ref[m], dv_ref[m] = dq, dk, dv
        wo_term = nn(att, og_ref[m])
        kv_term = nn(xtf[m], jnp.concatenate([dk, dv], axis=1))
        q_term = nn(xtf[m, :, :node_rows], dq)
        wo_total = wo_term if m == 0 else wo_total + wo_term
        kv_total = kv_term if m == 0 else kv_total + kv_term
        q_total = q_term if m == 0 else q_total + q_term

    planes, _, _, rows, _ = dw.shape
    inner_planes = wos.shape[0]
    dw[:, :, :, :, :128] = q_total.reshape(planes, 2, 2, rows, 128)
    dw[:, :, :, :, 128:] = kv_total.reshape(planes, 2, 2, rows, 256)
    wos[...] = wo_total.reshape(inner_planes, 2, 2, rows, width)
    me = me_ref[0]
    c, y, z = me % 2, (me // 2) % 2, me // 4
    qkv = slice(at, at + 384)
    for k in range(planes):
        zk = plane_of(gray(z) ^ k)
        own_ref[k, :, qkv] = dw[zk, y, c]
        other_ref[k, :, qkv] = dw[zk, 1 - y, c]
        send_other[k, :, qkv] = dw[zk, 1 - y, 1 - c].astype(bf16)
        send_own[k, :, qkv] = dw[zk, y, 1 - c].astype(bf16)
    last = slice(at + 384, at + 512)
    for i in range(inner_planes):
        for n in range(width // 128):
            k = n * inner_planes + i
            lanes = slice(n * 128, (n + 1) * 128)
            own_ref[k, :, last] = wos[i, y, c, :, lanes]
            other_ref[k, :, last] = wos[i, 1 - y, c, :, lanes]
            send_other[k, :, last] = wos[i, 1 - y, 1 - c, :, lanes].astype(bf16)
            send_own[k, :, last] = wos[i, y, 1 - c, :, lanes].astype(bf16)


def node_kernel(groups, skip, *refs):
    refs = refs[skip:]
    dqs, dks, dvs = refs[:groups], refs[groups : 2 * groups], refs[2 * groups : 3 * groups]
    wq_ref, wk_ref, wv_ref, node_ref, plus_ref, minus_ref, right_ref, left_ref = refs[3 * groups :]
    members, node_rows, _ = dqs[0].shape
    slots = plus_ref.shape[2]

    def whole(parts, m):
        return jnp.concatenate([part[m] for part in parts], axis=1)

    for m in range(members):
        spread = nt(whole(dks, m), wk_ref[...]) + nt(whole(dvs, m), wv_ref[...])
        node_ref[m] = spread[:node_rows] + nt(whole(dqs, m), wq_ref[...])
        halo = spread[node_rows:].astype(bf16)
        for ref, order in (
            (plus_ref, (3, 7, 5)),
            (minus_ref, (2, 4, 6)),
            (right_ref, (1,)),
            (left_ref, (0,)),
        ):
            for i, k in enumerate(order):
                ref[m, i] = halo[k * slots : (k + 1) * slots]


def sums(owns, core_in, y_in, k):
    total = jnp.concatenate(
        [
            own[k] + (core[1, k] if len(core.shape) == 4 else core[k]).astype(f32)
            for own, core in zip(owns, core_in)
        ],
        axis=1,
    ) + y_in[k].astype(f32)
    return [total[:, at : at + 512] for at in range(0, total.shape[1], 512)]


def gather_projection(parts, k, planes, projection_ref, start):
    inner_planes = planes * 128 // projection_ref.shape[2]
    quarter, inner = divmod(k, inner_planes)
    for i, part in enumerate(parts):
        plane = start + i * inner_planes + inner
        projection_ref[plane, :, quarter * 128 : (quarter + 1) * 128] = part[:, 384:]


def pack_kernel(pieces, *refs):
    for i, (ref, core) in enumerate(zip(refs[:pieces], refs[pieces:-1])):
        arrived = core[0] if len(core.shape) == 4 else core[...]
        refs[-1][:, :, i * 512 : (i + 1) * 512] = (ref[...] + arrived.astype(f32)).astype(bf16)


def halve(rows, kept_ref, sent_ref):
    for i, row in enumerate(rows):
        if i % 2 == 0:
            kept_ref[i // 2] = row
            continue
        pieces = row.shape[1] // 256
        for n in range(pieces):
            sent_ref[i // 2 * pieces + n] = row[:, n * 256 : (n + 1) * 256].astype(bf16)


def add_received(kept_ref, received_ref):
    planes, _, wide = kept_ref.shape
    pieces = wide // 256
    return [
        kept_ref[i]
        + jnp.concatenate([received_ref[i * pieces + n] for n in range(pieces)], axis=1).astype(f32)
        for i in range(planes)
    ]


def first_kernel(after_ref, own, core_in, y_in, kept_ref, projection_ref, sent_ref):
    planes = own.shape[0]
    rows = []
    for k in range(planes):
        parts = sums([own], [core_in], y_in, k)
        gather_projection(parts, k, planes, projection_ref, 0)
        rows.append(jnp.concatenate([part[:, :384] for part in parts], axis=1))
    halve(rows, kept_ref, sent_ref)


def second_kernel(skip, pieces, me_ref, *refs):
    refs = refs[skip:]
    first_ref, y_in = refs[:2]
    owns, core_in = refs[2 : 2 + pieces], refs[2 + pieces : 2 + 2 * pieces]
    kept_ref, sent_ref, projection_ref = refs[2 + 2 * pieces :]
    done = first_ref.shape[0]
    planes = projection_ref.shape[0]
    projection_ref[:done] = first_ref[...]
    held = []
    for k in range(planes):
        parts = sums(owns, core_in, y_in, k)
        gather_projection(parts, k, planes, projection_ref, done)
        held.append(jnp.concatenate([part[:, :384] for part in parts], axis=1))
    z = me_ref[0] // 4
    halve(
        [
            jnp.concatenate([held[k], projection_ref[plane_of(gray(z) ^ k)]], axis=1)
            for k in range(planes)
        ],
        kept_ref, sent_ref,
    )


def step_kernel(after_ref, kept_in, received, kept_ref, sent_ref):
    halve(add_received(kept_in, received), kept_ref, sent_ref)


def finish_kernel(
    me_ref, after_ref, send_ref, node_ref, plus_ref, minus_ref, first_in, second_in, out_ref, came
):
    members, node_rows, _ = node_ref.shape
    pick = sent_selector(send_ref[0], node_rows).astype(bf16)
    from_swaps(came, me_ref[0] % 2, first_in, second_in)
    for m in range(members):
        pieces = [None] * 8
        for side, order in enumerate(((1, 4, 7), (0, 6, 5))):
            for i, k in enumerate(order):
                pieces[k] = came[side, m, i]
        pieces[2], pieces[3] = plus_ref[m, 0], minus_ref[m, 0]
        arriving = jnp.concatenate(pieces, axis=0)
        out_ref[m] = (node_ref[m] + nn(pick, arriving)).astype(bf16)


def weight_kernel(after_ref, kept_a, in_a, kept_b, in_b, out_ref):
    (a,) = add_received(kept_a, in_a)
    (b,) = add_received(kept_b, in_b)
    half = a.shape[1] // 384
    width = 256 * half
    for i, part in enumerate((a, b)):
        for j in range(half):
            for n in range(3):
                at = n * width + (i * half + j) * 128
                out_ref[:, at : at + 128] = part[:, j * 384 + n * 128 : j * 384 + (n + 1) * 128]
    out_ref[:, 3 * width :] = b[:, 384 * half :]


def call(kernel, outs, operands, specs=None, scratch=(), limit=12, final=False, flops=10**6):
    specs = list(specs or ())
    specs += [pltpu.VMEM] * (len(operands) - len(specs))
    operands = [
        pltpu.with_memory_space_constraint(o, s) if s in (pltpu.HBM, pltpu.VMEM) else o
        for o, s in zip(operands, specs)
    ]
    return pl.pallas_call(
        kernel,
        out_shape=[jax.ShapeDtypeStruct(*o) if final else pltpu.VMEM(*o) for o in outs],
        in_specs=[pl.BlockSpec(memory_space=s) for s in specs],
        scratch_shapes=list(scratch),
        compiler_params=pltpu.CompilerParams(vmem_limit_bytes=limit * MIB),
        cost_estimate=pl.CostEstimate(flops=flops, bytes_accessed=10**4, transcendentals=0),
    )(*operands)


def body(
    node_features, out_grad, w_query, w_key, w_value, w_out, neighbours, neighbour_count, send_rows
):
    members, node_rows, width = node_features.shape
    count = lax.axis_size("patch")
    row_width = min(8, count // 4)
    _, adjacent, slots = send_rows.shape
    table = node_rows + adjacent * slots
    groups = width // 128
    me = lax.axis_index("patch")
    three = ((members, 3, slots, width), bf16)
    one = ((members, 1, slots, width), bf16)

    place = me.reshape(1)
    trio = pltpu.VMEM((2, *three[0]), bf16)
    to_plus, to_minus, own_right, own_left, x = call(
        functools.partial(gather_kernel, slots),
        [three, three, one, one, (node_features.shape, bf16)],
        (send_rows, node_features),
        specs=[pltpu.HBM] * 2,
        scratch=[pltpu.VMEM(send_rows.shape, jnp.int32), pltpu.SemaphoreType.DMA((2,))],
    )
    plus = shifted(to_plus, row_width)
    minus = shifted(to_minus, -row_width)
    square = ((width, width), bf16)
    counts = neighbour_count.reshape(1, node_rows)
    *loc, xt, wq, wk, wv, og, neigh, counts = call(
        functools.partial(local_kernel, groups),
        [((8, members, node_rows, 128), bf16)] * groups
        + [((members, width, node_rows), bf16), square, square, square, (out_grad.shape, bf16)]
        + [(neighbours.shape, jnp.int32), (counts.shape, jnp.int32)],
        (own_right, x, w_query, w_key, w_value, out_grad, neighbours, counts, w_out),
        specs=[pl.ANY, pltpu.VMEM] + [pltpu.HBM] * 7,
        scratch=[pltpu.VMEM((width, width), bf16), pltpu.SemaphoreType.DMA((7,))],
        limit=16,
    )
    outgoing = call(
        relay_kernel, [three, three], (place, loc[0], own_right, own_left, plus, minus),
        specs=[pltpu.SMEM, pl.ANY], scratch=[trio],
    )
    arrived = swap(outgoing, 1)
    (mask,) = call(
        mask_kernel, [((table, node_rows), f32)], (outgoing[0], neigh, counts), specs=[pl.ANY]
    )
    *halo, xtf = call(
        halo_kernel,
        [((4, members, node_rows, 128), bf16)] * groups + [((members, width, table), bf16)],
        (place, plus, minus, *arrived, xt, wk, wv), specs=[pltpu.SMEM], scratch=[trio],
    )

    planes, rows = count // 4, width // count
    inner_planes = planes * 128 // width
    flip = [(i, i ^ 1) for i in range(count)]
    flop = [(i, i ^ 2) for i in range(count)]
    grads = []

    def attention(extra, which, together):
        wide = 512 * len(which)
        sends = [((2, planes, rows, wide), bf16)] if together else [((planes, rows, wide), bf16)] * 2
        outs = call(
            functools.partial(attention_kernel, len(extra), len(which)),
            [((planes, rows, wide), f32)] * 2
            + sends
            + [
                ((members, node_rows, 128), bf16),
                ((members, table, 128), bf16),
                ((members, table, 128), bf16),
            ]
            * len(which),
            (
                place, *extra, *[loc[g] for g in which], *[halo[g] for g in which], mask, xtf, og,
            ),
            specs=[pltpu.SMEM] + [pl.ANY] * len(extra),
            scratch=[pltpu.VMEM((members, table, 512), f32)] * 3
            + [
                pltpu.VMEM((planes, 2, 2, rows, 384), f32),
                pltpu.VMEM((inner_planes, 2, 2, rows, width), f32),
            ],
            limit=24,
        )
        sent = outs[2 : 2 + len(sends)]
        grads.extend(outs[2 + len(sends) :])
        arrived = [lax.ppermute(shard, "patch", flip) for shard in sent]
        return outs[0], outs[1], arrived[0], arrived[-1]

    half = groups // 2
    wide = 384 * half
    own_a, other, core_other, core_own = attention((), range(half), False)
    y_sent = (other + core_other.astype(f32)).astype(bf16)
    y_a = lax.ppermute(y_sent, "patch", flop)
    later = []
    for g in range(half, groups):
        last = g == groups - 1
        later.append(attention((y_sent,) if last else (), range(g, g + 1), not last))
    own_b, other_b, core_other_b, core_own_b = zip(*later)
    (y_sent,) = call(
        functools.partial(pack_kernel, len(later)), [(y_sent.shape, bf16)],
        (*other_b, *core_other_b),
    )
    y_b = lax.ppermute(y_sent, "patch", flop)
    def exchange(sent, bit):
        return lax.ppermute(sent, "patch", along_z(count, bit))

    def halves(wide, bit):
        left = planes >> (bit + 1)
        return [((left, rows, wide), f32), ((left * wide // 256, rows, 256), bf16)]

    kept_a, sent_a = halves(wide, 0)
    kept_a, out_a, sent_a = call(
        first_kernel, [kept_a, ((half * inner_planes, rows, width), f32), sent_a],
        (y_sent, own_a, core_own, y_a), specs=[pl.ANY],
    )
    in_a = exchange(sent_a, 0)
    node, to_plus, to_minus, own_right, own_left = call(
        functools.partial(node_kernel, groups, 1),
        [((members, node_rows, width), f32), three, three, one, one],
        (sent_a, *grads[0::3], *grads[1::3], *grads[2::3], wq, wk, wv),
        specs=[pl.ANY], flops=2 * 10**10,
    )
    from_plus = shifted(to_minus, -row_width)
    from_minus = shifted(to_plus, row_width)
    outgoing = call(
        relay_kernel, [three, three],
        (place, in_a, own_right, own_left, from_plus, from_minus),
        specs=[pltpu.SMEM, pl.ANY], scratch=[trio],
    )
    back = swap(outgoing, 1)
    after = outgoing[0]
    for bit in range(1, planes.bit_length()):
        if bit < planes.bit_length() - 1:
            kept_a, after = call(
                step_kernel, halves(wide, bit), (after, kept_a, in_a), specs=[pl.ANY]
            )
            in_a = exchange(after, bit)
        if bit == 1:
            kept_b, after = call(
                functools.partial(second_kernel, 1, len(later)), halves(wide + width, 0),
                (place, after, out_a, y_b, *own_b, *core_own_b),
                specs=[pltpu.SMEM, pl.ANY],
                scratch=[pltpu.VMEM((planes, rows, width), f32)],
            )
        else:
            kept_b, after = call(
                step_kernel, halves(wide + width, bit - 1), (after, kept_b, in_b), specs=[pl.ANY]
            )
        in_b = exchange(after, bit - 1)
    (node_grad,) = call(
        finish_kernel, [((members, node_rows, width), bf16)],
        (place, after, send_rows, node, from_plus, from_minus, *back),
        specs=[pltpu.SMEM, pl.ANY], scratch=[trio], final=True,
    )
    (weight_grad,) = call(
        weight_kernel, [((rows, 4 * width), f32)], (node_grad, kept_a, in_a, kept_b, in_b),
        specs=[pltpu.HBM], final=True,
    )
    return (node_grad, weight_grad)


def solution(mesh):
    in_specs = (
        P("groups", "patch", None),
        P("groups", "patch", None),
        P(),
        P(),
        P(),
        P(),
        P("patch", None),
        P("patch"),
        P("patch", None, None),
    )
    out_specs = (P("groups", "patch", None), P(("groups", "patch"), None))
    return jax.shard_map(body, mesh=mesh, in_specs=in_specs, out_specs=out_specs, check_vma=False)
```

```python
import functools
import math

import jax
import jax.numpy as jnp
from jax import lax
from jax.experimental import pallas as pl
from jax.experimental.pallas import tpu as pltpu
from jax.sharding import PartitionSpec as P

HEADS = 16
score_cap = 5.0
MIB = 1024 * 1024
f32 = jnp.float32
bf16 = jnp.bfloat16


def nn(a, b):
    return lax.dot_general(a, b, (((1,), (0,)), ((), ())), preferred_element_type=f32)


def nt(a, b):
    return lax.dot_general(a, b, (((1,), (1,)), ((), ())), preferred_element_type=f32)


def shifted(shard, by):
    count = lax.axis_size("patch")
    return lax.ppermute(shard, "patch", [(i, (i + by) % count) for i in range(count)])


def neighbours_apart(count, stride):
    first, second = [], []
    for i in range(count):
        up, down = (i + stride) % count, (i - stride) % count
        even = i // stride % 2 == 0
        first.append((i, up if even else down))
        second.append((i, down if even else up))
    return first, second


def swap(pair, stride):
    return [
        lax.ppermute(shard, "patch", perm)
        for shard, perm in zip(pair, neighbours_apart(lax.axis_size("patch"), stride))
    ]


def to_swaps(both, odd, first_ref, second_ref):
    first_ref[...] = both[odd]
    second_ref[...] = both[1 - odd]


def from_swaps(both, odd, first_ref, second_ref):
    both[1 - odd] = first_ref[...]
    both[odd] = second_ref[...]


def sent_selector(send_rows, node_rows):
    adjacent, slots = send_rows.shape
    halo = adjacent * slots
    wide = jnp.concatenate([send_rows] * adjacent, axis=1)
    own = lax.broadcasted_iota(jnp.int32, (adjacent, halo), 1) // slots == lax.broadcasted_iota(
        jnp.int32, (adjacent, halo), 0
    )
    ids = jnp.sum(jnp.where(own, wide, 0), axis=0, keepdims=True)
    nodes = lax.broadcasted_iota(jnp.int32, (node_rows, halo), 0)
    return jnp.where(nodes == ids, 1.0, 0.0).astype(f32)


def gather_kernel(
    slots, send_hbm, x_hbm, plus_ref, minus_ref, right_ref, left_ref, x_ref, send_ref, sem
):
    copies = [
        pltpu.make_async_copy(send_hbm, send_ref, sem.at[0]),
        pltpu.make_async_copy(x_hbm, x_ref, sem.at[1]),
    ]
    for copy in copies:
        copy.start()
    copies[0].wait()
    members, node_rows, _ = x_ref.shape
    pick = sent_selector(send_ref[0], node_rows).T.astype(bf16)
    copies[1].wait()
    for m in range(members):
        rows = nn(pick, x_ref[m]).astype(bf16)

        def part(k):
            return rows[k * slots : (k + 1) * slots]

        for ref, order in ((plus_ref, (2, 6, 4)), (minus_ref, (3, 5, 7))):
            for i, k in enumerate(order):
                ref[m, i] = part(k)
        right_ref[m, 0] = part(0)
        left_ref[m, 0] = part(1)


def relay_kernel(
    me_ref, after_ref, own_right, own_left, plus_ref, minus_ref, first_ref, second_ref, both
):
    for side, own in enumerate((own_right, own_left)):
        both[side, :, 0:1] = own[...]
        both[side, :, 1:2] = plus_ref[:, 1 + side : 2 + side]
        both[side, :, 2:3] = minus_ref[:, 1 + side : 2 + side]
    to_swaps(both, me_ref[0] % 2, first_ref, second_ref)


def gray(z):
    return z ^ (z >> 1)


def plane_of(code):
    z = code
    for shift in range(1, 8):
        z = z ^ (code >> shift)
    return z


def along_z(count, bit):
    planes = count // 4
    return [(i, plane_of(gray(i // 4) ^ (1 << bit)) * 4 + i % 4) for i in range(planes * 4)]


Q, K, V, G, QT, KT, VT, GT = range(8)


def local_kernel(groups, after_ref, x_ref, *refs):
    sources, loc_refs, xt_ref = refs[:7], refs[7 : 7 + groups], refs[7 + groups]
    copied, sem = refs[8 + groups : 15 + groups], refs[-1]
    copies = [
        pltpu.make_async_copy(source, target, sem.at[i])
        for i, (source, target) in enumerate(zip(sources, copied))
    ]
    for copy in copies:
        copy.start()
    members, node_rows, width = x_ref.shape
    x = x_ref[...].reshape(members * node_rows, width)
    for m in range(members):
        xt_ref[m] = x_ref[m].T

    def put(rows, kind):
        for m in range(members):
            for g, ref in enumerate(loc_refs):
                block = rows[m * node_rows : (m + 1) * node_rows, g * 128 : (g + 1) * 128]
                ref[kind, m] = block
                ref[kind + 4, m] = block.T

    wq_ref, wk_ref, wv_ref, og_ref, _, _, wo_ref = copied
    for kind, ref in enumerate((wq_ref, wk_ref, wv_ref)):
        copies[kind].wait()
        put(nn(x, ref[...]).astype(bf16), kind)
    for copy in copies[3:]:
        copy.wait()
    og = og_ref[...].reshape(members * node_rows, width)
    put(nt(og, wo_ref[...]).astype(bf16), G)


def mask_kernel(after_ref, neigh_ref, count_ref, mask_ref):
    neigh = neigh_ref[...].T
    slots, node_rows = neigh.shape
    table = mask_ref.shape[0]
    order = lax.broadcasted_iota(jnp.int32, neigh.shape, 0)
    tail = jnp.where(order >= count_ref[...], neigh, -1)[slots // 2 :]
    half = table // 2
    for part in range(2):
        columns = lax.broadcasted_iota(jnp.int32, (half, node_rows), 0) + part * half
        kept = jnp.ones((half, node_rows), f32)
        for j in range(slots // 2):
            kept = jnp.where(tail[j : j + 1] == columns, 0.0, kept)
        mask_ref[part * half : (part + 1) * half] = kept


def halo_kernel(
    me_ref, plus_ref, minus_ref, first_in, second_in, xt_ref, wk_ref, wv_ref, *refs
):
    halo_refs, xtf_ref, both = refs[:-2], refs[-2], refs[-1]
    members, _, node_rows = xt_ref.shape
    from_swaps(both, me_ref[0] % 2, first_in, second_in)
    for m in range(members):
        pieces = [None] * 8
        for side, order in enumerate(((0, 6, 5), (1, 4, 7))):
            for i, k in enumerate(order):
                pieces[k] = both[side, m, i]
        pieces[2] = plus_ref[m, 0]
        pieces[3] = minus_ref[m, 0]
        halo = jnp.concatenate(pieces, axis=0)
        xtf_ref[m, :, :node_rows] = xt_ref[m]
        xtf_ref[m, :, node_rows:] = halo.T
        for kind, w_ref in enumerate((wk_ref, wv_ref)):
            rows = nn(halo, w_ref[...]).astype(bf16)
            for g, ref in enumerate(halo_refs):
                block = rows[:, g * 128 : (g + 1) * 128]
                ref[kind, m] = block
                ref[kind + 2, m] = block.T


def attention_kernel(extra, here, me_ref, *refs):
    refs = refs[extra:]
    locs, halos, refs = refs[:here], refs[here : 2 * here], refs[2 * here :]
    mask_ref, xtf, og_ref = refs[:3]
    split = 7 if len(refs) == 15 + 3 * (here - 1) else 6
    outs, grads, scratch = refs[3:split], refs[split : split + 3 * here], refs[split + 3 * here :]
    if split == 6:
        outs = (*outs[:2], outs[2].at[0], outs[2].at[1])
    for i in range(here):
        attend(
            me_ref, locs[i], halos[i], mask_ref, xtf, og_ref, outs, 512 * i,
            grads[3 * i : 3 * i + 3], scratch,
        )


def attend(me_ref, loc, halo, mask_ref, xtf, og_ref, out_refs, at, grad_refs, scratch):
    own_ref, other_ref, send_other, send_own = out_refs
    dq_ref, dk_ref, dv_ref = grad_refs
    score, grad, slope, dw, wos = scratch
    _, members, node_rows, _ = loc.shape
    table = mask_ref.shape[0]
    width = og_ref.shape[2]
    head = width // HEADS
    per = 128 // head
    scale = 1.0 / math.sqrt(head)

    row_head = lax.broadcasted_iota(jnp.int32, (128, node_rows), 0) // head
    lane_head = lax.broadcasted_iota(jnp.int32, (node_rows, 128), 1) // head

    def spread_t(block):
        zero = jnp.zeros_like(block)
        return jnp.concatenate([jnp.where(row_head == h, block, zero) for h in range(per)], axis=1)

    def spread_n(block):
        zero = jnp.zeros_like(block)
        return jnp.concatenate([jnp.where(lane_head == h, block, zero) for h in range(per)], axis=0)

    strip = 64
    for m in range(members):
        kg = jnp.concatenate([loc[K, m], halo[0, m]], axis=0)
        vg = jnp.concatenate([loc[V, m], halo[1, m]], axis=0)
        score[m] = nn(kg, spread_t(loc[QT, m]))
        grad[m] = nn(vg, spread_t(loc[GT, m]))

    wo_total = None
    kv_total = None
    q_total = None
    for m in range(members):
        probs = []
        for h in range(per):
            lanes = slice(h * node_rows, (h + 1) * node_rows)
            den = jnp.zeros((8, node_rows), f32)
            inner = jnp.zeros((8, node_rows), f32)
            for c in range(0, table, strip):
                box = (m, slice(c, c + strip), lanes)
                t = jnp.tanh(score[box] * (scale / score_cap))
                e = jnp.exp2(t * (score_cap / math.log(2.0))) * mask_ref[c : c + strip]
                den = den + jnp.sum(e.reshape(strip // 8, 8, node_rows), axis=0)
                inner = inner + jnp.sum((e * grad[box]).reshape(strip // 8, 8, node_rows), axis=0)
                score[box] = e
                slope[box] = e * (scale - scale * (t * t))
            r = 1.0 / jnp.sum(den, axis=0, keepdims=True)
            inner = jnp.sum(inner, axis=0, keepdims=True) * r
            column = []
            scores = []
            for c in range(0, table, strip):
                box = (m, slice(c, c + strip), lanes)
                column.append((score[box] * r).astype(bf16))
                scores.append(((slope[box] * r) * (grad[box] - inner)).astype(bf16))
            probs.append((jnp.concatenate(column, axis=0), jnp.concatenate(scores, axis=0)))
        pb = jnp.concatenate([p for p, _ in probs], axis=1)
        ds = jnp.concatenate([s for _, s in probs], axis=1)
        ktg = jnp.concatenate([loc[KT, m], halo[2, m]], axis=1)
        vtg = jnp.concatenate([loc[VT, m], halo[3, m]], axis=1)
        att, dqt = [], []
        for h in range(0, per, 2):
            lanes = slice(h * node_rows, (h + 2) * node_rows)
            rows = slice(h * head, (h + 2) * head)
            a = nn(vtg[rows], pb[:, lanes])
            b = nn(ktg[rows], ds[:, lanes])
            for j in range(2):
                inside = (slice(j * head, (j + 1) * head), slice(j * node_rows, (j + 1) * node_rows))
                att.append(a[inside].astype(bf16))
                dqt.append(b[inside].astype(bf16))
        att = jnp.concatenate(att, axis=0)
        dq = jnp.concatenate(dqt, axis=0).T
        dk = nn(ds, spread_n(loc[Q, m])).astype(bf16)
        dv = nn(pb, spread_n(loc[G, m])).astype(bf16)
        dq_ref[m], dk_ref[m], dv_ref[m] = dq, dk, dv
        wo_term = nn(att, og_ref[m])
        kv_term = nn(xtf[m], jnp.concatenate([dk, dv], axis=1))
        q_term = nn(xtf[m, :, :node_rows], dq)
        wo_total = wo_term if m == 0 else wo_total + wo_term
        kv_total = kv_term if m == 0 else kv_total + kv_term
        q_total = q_term if m == 0 else q_total + q_term

    planes, _, _, rows, _ = dw.shape
    inner_planes = wos.shape[0]
    dw[:, :, :, :, :128] = q_total.reshape(planes, 2, 2, rows, 128)
    dw[:, :, :, :, 128:] = kv_total.reshape(planes, 2, 2, rows, 256)
    wos[...] = wo_total.reshape(inner_planes, 2, 2, rows, width)
    me = me_ref[0]
    c, y, z = me % 2, (me // 2) % 2, me // 4
    qkv = slice(at, at + 384)
    for k in range(planes):
        zk = plane_of(gray(z) ^ k)
        own_ref[k, :, qkv] = dw[zk, y, c]
        other_ref[k, :, qkv] = dw[zk, 1 - y, c]
        send_other[k, :, qkv] = dw[zk, 1 - y, 1 - c].astype(bf16)
        send_own[k, :, qkv] = dw[zk, y, 1 - c].astype(bf16)
    last = slice(at + 384, at + 512)
    for i in range(inner_planes):
        for n in range(width // 128):
            k = n * inner_planes + i
            lanes = slice(n * 128, (n + 1) * 128)
            own_ref[k, :, last] = wos[i, y, c, :, lanes]
            other_ref[k, :, last] = wos[i, 1 - y, c, :, lanes]
            send_other[k, :, last] = wos[i, 1 - y, 1 - c, :, lanes].astype(bf16)
            send_own[k, :, last] = wos[i, y, 1 - c, :, lanes].astype(bf16)


def node_kernel(groups, skip, *refs):
    refs = refs[skip:]
    dqs, dks, dvs = refs[:groups], refs[groups : 2 * groups], refs[2 * groups : 3 * groups]
    wq_ref, wk_ref, wv_ref, node_ref, plus_ref, minus_ref, right_ref, left_ref = refs[3 * groups :]
    members, node_rows, _ = dqs[0].shape
    slots = plus_ref.shape[2]

    def whole(parts, m):
        return jnp.concatenate([part[m] for part in parts], axis=1)

    for m in range(members):
        spread = nt(whole(dks, m), wk_ref[...]) + nt(whole(dvs, m), wv_ref[...])
        node_ref[m] = spread[:node_rows] + nt(whole(dqs, m), wq_ref[...])
        halo = spread[node_rows:].astype(bf16)
        for ref, order in (
            (plus_ref, (3, 7, 5)),
            (minus_ref, (2, 4, 6)),
            (right_ref, (1,)),
            (left_ref, (0,)),
        ):
            for i, k in enumerate(order):
                ref[m, i] = halo[k * slots : (k + 1) * slots]


def sums(owns, core_in, y_in, k):
    total = jnp.concatenate(
        [
            own[k] + (core[1, k] if len(core.shape) == 4 else core[k]).astype(f32)
            for own, core in zip(owns, core_in)
        ],
        axis=1,
    ) + y_in[k].astype(f32)
    return [total[:, at : at + 512] for at in range(0, total.shape[1], 512)]


def gather_projection(parts, k, planes, projection_ref, start):
    inner_planes = planes * 128 // projection_ref.shape[2]
    quarter, inner = divmod(k, inner_planes)
    for i, part in enumerate(parts):
        plane = start + i * inner_planes + inner
        projection_ref[plane, :, quarter * 128 : (quarter + 1) * 128] = part[:, 384:]


def pack_kernel(pieces, *refs):
    for i, (ref, core) in enumerate(zip(refs[:pieces], refs[pieces:-1])):
        arrived = core[0] if len(core.shape) == 4 else core[...]
        refs[-1][:, :, i * 512 : (i + 1) * 512] = (ref[...] + arrived.astype(f32)).astype(bf16)


def halve(rows, kept_ref, sent_ref):
    for i, row in enumerate(rows):
        if i % 2 == 0:
            kept_ref[i // 2] = row
            continue
        pieces = row.shape[1] // 256
        for n in range(pieces):
            sent_ref[i // 2 * pieces + n] = row[:, n * 256 : (n + 1) * 256].astype(bf16)


def add_received(kept_ref, received_ref):
    planes, _, wide = kept_ref.shape
    pieces = wide // 256
    return [
        kept_ref[i]
        + jnp.concatenate([received_ref[i * pieces + n] for n in range(pieces)], axis=1).astype(f32)
        for i in range(planes)
    ]


def first_kernel(after_ref, own, core_in, y_in, kept_ref, projection_ref, sent_ref):
    planes = own.shape[0]
    rows = []
    for k in range(planes):
        parts = sums([own], [core_in], y_in, k)
        gather_projection(parts, k, planes, projection_ref, 0)
        rows.append(jnp.concatenate([part[:, :384] for part in parts], axis=1))
    halve(rows, kept_ref, sent_ref)


def second_kernel(skip, pieces, me_ref, *refs):
    refs = refs[skip:]
    kept_a, in_a, first_ref, y_in = refs[:4]
    owns, core_in = refs[4 : 4 + pieces], refs[4 + pieces : 4 + 2 * pieces]
    kept_ref, sent_ref, next_kept, next_sent, projection_ref = refs[4 + 2 * pieces :]
    done = first_ref.shape[0]
    planes = projection_ref.shape[0]
    projection_ref[:done] = first_ref[...]
    held = []
    for k in range(planes):
        parts = sums(owns, core_in, y_in, k)
        gather_projection(parts, k, planes, projection_ref, done)
        held.append(jnp.concatenate([part[:, :384] for part in parts], axis=1))
    z = me_ref[0] // 4
    halve(
        [
            jnp.concatenate([held[k], projection_ref[plane_of(gray(z) ^ k)]], axis=1)
            for k in range(planes)
        ],
        kept_ref, sent_ref,
    )
    halve(add_received(kept_a, in_a), next_kept, next_sent)


def step_kernel(after_ref, kept_in, received, kept_ref, sent_ref):
    halve(add_received(kept_in, received), kept_ref, sent_ref)


def finish_kernel(
    me_ref, after_ref, send_ref, node_ref, plus_ref, minus_ref, first_in, second_in, out_ref, came
):
    members, node_rows, _ = node_ref.shape
    pick = sent_selector(send_ref[0], node_rows).astype(bf16)
    from_swaps(came, me_ref[0] % 2, first_in, second_in)
    for m in range(members):
        pieces = [None] * 8
        for side, order in enumerate(((1, 4, 7), (0, 6, 5))):
            for i, k in enumerate(order):
                pieces[k] = came[side, m, i]
        pieces[2], pieces[3] = plus_ref[m, 0], minus_ref[m, 0]
        arriving = jnp.concatenate(pieces, axis=0)
        out_ref[m] = (node_ref[m] + nn(pick, arriving)).astype(bf16)


def weight_kernel(after_ref, kept_a, in_a, kept_b, in_b, out_ref):
    (a,) = add_received(kept_a, in_a)
    (b,) = add_received(kept_b, in_b)
    half = a.shape[1] // 384
    width = 256 * half
    for i, part in enumerate((a, b)):
        for j in range(half):
            for n in range(3):
                at = n * width + (i * half + j) * 128
                out_ref[:, at : at + 128] = part[:, j * 384 + n * 128 : j * 384 + (n + 1) * 128]
    out_ref[:, 3 * width :] = b[:, 384 * half :]


def call(kernel, outs, operands, specs=None, scratch=(), limit=12, final=False, flops=10**6):
    specs = list(specs or ())
    specs += [pltpu.VMEM] * (len(operands) - len(specs))
    operands = [
        pltpu.with_memory_space_constraint(o, s) if s in (pltpu.HBM, pltpu.VMEM) else o
        for o, s in zip(operands, specs)
    ]
    return pl.pallas_call(
        kernel,
        out_shape=[jax.ShapeDtypeStruct(*o) if final else pltpu.VMEM(*o) for o in outs],
        in_specs=[pl.BlockSpec(memory_space=s) for s in specs],
        scratch_shapes=list(scratch),
        compiler_params=pltpu.CompilerParams(vmem_limit_bytes=limit * MIB),
        cost_estimate=pl.CostEstimate(flops=flops, bytes_accessed=10**4, transcendentals=0),
    )(*operands)


def body(
    node_features, out_grad, w_query, w_key, w_value, w_out, neighbours, neighbour_count, send_rows
):
    members, node_rows, width = node_features.shape
    count = lax.axis_size("patch")
    row_width = min(8, count // 4)
    _, adjacent, slots = send_rows.shape
    table = node_rows + adjacent * slots
    groups = width // 128
    me = lax.axis_index("patch")
    three = ((members, 3, slots, width), bf16)
    one = ((members, 1, slots, width), bf16)

    place = me.reshape(1)
    trio = pltpu.VMEM((2, *three[0]), bf16)
    to_plus, to_minus, own_right, own_left, x = call(
        functools.partial(gather_kernel, slots),
        [three, three, one, one, (node_features.shape, bf16)],
        (send_rows, node_features),
        specs=[pltpu.HBM] * 2,
        scratch=[pltpu.VMEM(send_rows.shape, jnp.int32), pltpu.SemaphoreType.DMA((2,))],
    )
    plus = shifted(to_plus, row_width)
    minus = shifted(to_minus, -row_width)
    square = ((width, width), bf16)
    counts = neighbour_count.reshape(1, node_rows)
    *loc, xt, wq, wk, wv, og, neigh, counts = call(
        functools.partial(local_kernel, groups),
        [((8, members, node_rows, 128), bf16)] * groups
        + [((members, width, node_rows), bf16), square, square, square, (out_grad.shape, bf16)]
        + [(neighbours.shape, jnp.int32), (counts.shape, jnp.int32)],
        (own_right, x, w_query, w_key, w_value, out_grad, neighbours, counts, w_out),
        specs=[pl.ANY, pltpu.VMEM] + [pltpu.HBM] * 7,
        scratch=[pltpu.VMEM((width, width), bf16), pltpu.SemaphoreType.DMA((7,))],
        limit=16,
    )
    outgoing = call(
        relay_kernel, [three, three], (place, loc[0], own_right, own_left, plus, minus),
        specs=[pltpu.SMEM, pl.ANY], scratch=[trio],
    )
    arrived = swap(outgoing, 1)
    (mask,) = call(
        mask_kernel, [((table, node_rows), f32)], (outgoing[0], neigh, counts), specs=[pl.ANY]
    )
    *halo, xtf = call(
        halo_kernel,
        [((4, members, node_rows, 128), bf16)] * groups + [((members, width, table), bf16)],
        (place, plus, minus, *arrived, xt, wk, wv), specs=[pltpu.SMEM], scratch=[trio],
    )

    planes, rows = count // 4, width // count
    inner_planes = planes * 128 // width
    flip = [(i, i ^ 1) for i in range(count)]
    flop = [(i, i ^ 2) for i in range(count)]
    grads = []

    def attention(extra, which, together):
        wide = 512 * len(which)
        sends = [((2, planes, rows, wide), bf16)] if together else [((planes, rows, wide), bf16)] * 2
        outs = call(
            functools.partial(attention_kernel, len(extra), len(which)),
            [((planes, rows, wide), f32)] * 2
            + sends
            + [
                ((members, node_rows, 128), bf16),
                ((members, table, 128), bf16),
                ((members, table, 128), bf16),
            ]
            * len(which),
            (
                place, *extra, *[loc[g] for g in which], *[halo[g] for g in which], mask, xtf, og,
            ),
            specs=[pltpu.SMEM] + [pl.ANY] * len(extra),
            scratch=[pltpu.VMEM((members, table, 512), f32)] * 3
            + [
                pltpu.VMEM((planes, 2, 2, rows, 384), f32),
                pltpu.VMEM((inner_planes, 2, 2, rows, width), f32),
            ],
            limit=24,
        )
        sent = outs[2 : 2 + len(sends)]
        grads.extend(outs[2 + len(sends) :])
        arrived = [lax.ppermute(shard, "patch", flip) for shard in sent]
        return outs[0], outs[1], arrived[0], arrived[-1]

    half = groups // 2
    wide = 384 * half
    own_a, other, core_other, core_own = attention((), range(half), False)
    y_sent = (other + core_other.astype(f32)).astype(bf16)
    y_a = lax.ppermute(y_sent, "patch", flop)
    later = []
    for g in range(half, groups):
        last = g == groups - 1
        later.append(attention((y_sent,) if last else (), range(g, g + 1), not last))
    own_b, other_b, core_other_b, core_own_b = zip(*later)
    (y_sent,) = call(
        functools.partial(pack_kernel, len(later)), [(y_sent.shape, bf16)],
        (*other_b, *core_other_b),
    )
    y_b = lax.ppermute(y_sent, "patch", flop)
    node, to_plus, to_minus, own_right, own_left = call(
        functools.partial(node_kernel, groups, 1),
        [((members, node_rows, width), f32), three, three, one, one],
        (y_sent, *grads[0::3], *grads[1::3], *grads[2::3], wq, wk, wv),
        specs=[pl.ANY],
    )
    from_plus = shifted(to_minus, -row_width)
    from_minus = shifted(to_plus, row_width)
    def exchange(sent, bit):
        return lax.ppermute(sent, "patch", along_z(count, bit))

    def halves(wide, bit):
        left = planes >> (bit + 1)
        return [((left, rows, wide), f32), ((left * wide // 256, rows, 256), bf16)]

    kept_a, sent_a = halves(wide, 0)
    kept_a, out_a, sent_a = call(
        first_kernel, [kept_a, ((half * inner_planes, rows, width), f32), sent_a],
        (y_sent, own_a, core_own, y_a), specs=[pl.ANY], flops=2 * 10**10,
    )
    in_a = exchange(sent_a, 0)
    outgoing = call(
        relay_kernel, [three, three],
        (place, sent_a, own_right, own_left, from_plus, from_minus),
        specs=[pltpu.SMEM, pl.ANY], scratch=[trio],
    )
    back = swap(outgoing, 1)
    kept_b, after, kept_a, sent_a = call(
        functools.partial(second_kernel, 1, len(later)),
        halves(wide + width, 0) + halves(wide, 1),
        (place, outgoing[0], kept_a, in_a, out_a, y_b, *own_b, *core_own_b),
        specs=[pltpu.SMEM, pl.ANY],
        scratch=[pltpu.VMEM((planes, rows, width), f32)],
    )
    in_b = exchange(after, 0)
    in_a = exchange(sent_a, 1)
    for bit in range(1, planes.bit_length() - 1):
        kept_b, after = call(
            step_kernel, halves(wide + width, bit), (in_a, kept_b, in_b), specs=[pl.ANY]
        )
        in_b = exchange(after, bit)
        if bit < planes.bit_length() - 2:
            kept_a, after = call(
                step_kernel, halves(wide, bit + 1), (after, kept_a, in_a), specs=[pl.ANY]
            )
            in_a = exchange(after, bit + 1)
    (node_grad,) = call(
        finish_kernel, [((members, node_rows, width), bf16)],
        (place, after, send_rows, node, from_plus, from_minus, *back),
        specs=[pltpu.SMEM, pl.ANY], scratch=[trio], final=True,
    )
    (weight_grad,) = call(
        weight_kernel, [((rows, 4 * width), f32)], (node_grad, kept_a, in_a, kept_b, in_b),
        specs=[pltpu.HBM], final=True,
    )
    return (node_grad, weight_grad)


def solution(mesh):
    in_specs = (
        P("groups", "patch", None),
        P("groups", "patch", None),
        P(),
        P(),
        P(),
        P(),
        P("patch", None),
        P("patch"),
        P("patch", None, None),
    )
    out_specs = (P("groups", "patch", None), P(("groups", "patch"), None))
    return jax.shard_map(body, mesh=mesh, in_specs=in_specs, out_specs=out_specs, check_vma=False)
```

```python
import functools
import math

import jax
import jax.numpy as jnp
from jax import lax
from jax.experimental import pallas as pl
from jax.experimental.pallas import tpu as pltpu
from jax.sharding import PartitionSpec as P

HEADS = 16
score_cap = 5.0
MIB = 1024 * 1024
f32 = jnp.float32
bf16 = jnp.bfloat16


def nn(a, b):
    return lax.dot_general(a, b, (((1,), (0,)), ((), ())), preferred_element_type=f32)


def nt(a, b):
    return lax.dot_general(a, b, (((1,), (1,)), ((), ())), preferred_element_type=f32)


def shifted(shard, by):
    count = lax.axis_size("patch")
    return lax.ppermute(shard, "patch", [(i, (i + by) % count) for i in range(count)])


def neighbours_apart(count, stride):
    first, second = [], []
    for i in range(count):
        up, down = (i + stride) % count, (i - stride) % count
        even = i // stride % 2 == 0
        first.append((i, up if even else down))
        second.append((i, down if even else up))
    return first, second


def swap(pair, stride):
    return [
        lax.ppermute(shard, "patch", perm)
        for shard, perm in zip(pair, neighbours_apart(lax.axis_size("patch"), stride))
    ]


def to_swaps(both, odd, first_ref, second_ref):
    first_ref[...] = both[odd]
    second_ref[...] = both[1 - odd]


def from_swaps(both, odd, first_ref, second_ref):
    both[1 - odd] = first_ref[...]
    both[odd] = second_ref[...]


def sent_selector(send_rows, node_rows):
    adjacent, slots = send_rows.shape
    halo = adjacent * slots
    wide = jnp.concatenate([send_rows] * adjacent, axis=1)
    own = lax.broadcasted_iota(jnp.int32, (adjacent, halo), 1) // slots == lax.broadcasted_iota(
        jnp.int32, (adjacent, halo), 0
    )
    ids = jnp.sum(jnp.where(own, wide, 0), axis=0, keepdims=True)
    nodes = lax.broadcasted_iota(jnp.int32, (node_rows, halo), 0)
    return jnp.where(nodes == ids, 1.0, 0.0).astype(f32)


def gather_kernel(
    slots, send_hbm, x_hbm, plus_ref, minus_ref, right_ref, left_ref, x_ref, send_ref, sem
):
    copies = [
        pltpu.make_async_copy(send_hbm, send_ref, sem.at[0]),
        pltpu.make_async_copy(x_hbm, x_ref, sem.at[1]),
    ]
    for copy in copies:
        copy.start()
    copies[0].wait()
    members, node_rows, _ = x_ref.shape
    pick = sent_selector(send_ref[0], node_rows).T.astype(bf16)
    copies[1].wait()
    for m in range(members):
        rows = nn(pick, x_ref[m]).astype(bf16)

        def part(k):
            return rows[k * slots : (k + 1) * slots]

        for ref, order in ((plus_ref, (2, 6, 4)), (minus_ref, (3, 5, 7))):
            for i, k in enumerate(order):
                ref[m, i] = part(k)
        right_ref[m, 0] = part(0)
        left_ref[m, 0] = part(1)


def relay_kernel(
    me_ref, after_ref, own_right, own_left, plus_ref, minus_ref, first_ref, second_ref, both
):
    for side, own in enumerate((own_right, own_left)):
        both[side, :, 0:1] = own[...]
        both[side, :, 1:2] = plus_ref[:, 1 + side : 2 + side]
        both[side, :, 2:3] = minus_ref[:, 1 + side : 2 + side]
    to_swaps(both, me_ref[0] % 2, first_ref, second_ref)


def gray(z):
    return z ^ (z >> 1)


def plane_of(code):
    z = code
    for shift in range(1, 8):
        z = z ^ (code >> shift)
    return z


def along_z(count, distance):
    planes = count // 4
    return [(i, plane_of(gray(i // 4) ^ distance) * 4 + i % 4) for i in range(planes * 4)]


Q, K, V, G, QT, KT, VT, GT = range(8)


def local_kernel(groups, after_ref, x_ref, *refs):
    sources, loc_refs, xt_ref = refs[:7], refs[7 : 7 + groups], refs[7 + groups]
    copied, sem = refs[8 + groups : 15 + groups], refs[-1]
    copies = [
        pltpu.make_async_copy(source, target, sem.at[i])
        for i, (source, target) in enumerate(zip(sources, copied))
    ]
    for copy in copies:
        copy.start()
    members, node_rows, width = x_ref.shape
    x = x_ref[...].reshape(members * node_rows, width)
    for m in range(members):
        xt_ref[m] = x_ref[m].T

    def put(rows, kind):
        for m in range(members):
            for g, ref in enumerate(loc_refs):
                block = rows[m * node_rows : (m + 1) * node_rows, g * 128 : (g + 1) * 128]
                ref[kind, m] = block
                ref[kind + 4, m] = block.T

    wq_ref, wk_ref, wv_ref, og_ref, _, _, wo_ref = copied
    for kind, ref in enumerate((wq_ref, wk_ref, wv_ref)):
        copies[kind].wait()
        put(nn(x, ref[...]).astype(bf16), kind)
    for copy in copies[3:]:
        copy.wait()
    og = og_ref[...].reshape(members * node_rows, width)
    put(nt(og, wo_ref[...]).astype(bf16), G)


def mask_kernel(after_ref, neigh_ref, count_ref, mask_ref):
    neigh = neigh_ref[...].T
    slots, node_rows = neigh.shape
    table = mask_ref.shape[0]
    order = lax.broadcasted_iota(jnp.int32, neigh.shape, 0)
    tail = jnp.where(order >= count_ref[...], neigh, -1)[slots // 2 :]
    half = table // 2
    for part in range(2):
        columns = lax.broadcasted_iota(jnp.int32, (half, node_rows), 0) + part * half
        kept = jnp.ones((half, node_rows), f32)
        for j in range(slots // 2):
            kept = jnp.where(tail[j : j + 1] == columns, 0.0, kept)
        mask_ref[part * half : (part + 1) * half] = kept


def halo_kernel(
    me_ref, plus_ref, minus_ref, first_in, second_in, xt_ref, wk_ref, wv_ref, *refs
):
    halo_refs, xtf_ref, both = refs[:-2], refs[-2], refs[-1]
    members, _, node_rows = xt_ref.shape
    from_swaps(both, me_ref[0] % 2, first_in, second_in)
    for m in range(members):
        pieces = [None] * 8
        for side, order in enumerate(((0, 6, 5), (1, 4, 7))):
            for i, k in enumerate(order):
                pieces[k] = both[side, m, i]
        pieces[2] = plus_ref[m, 0]
        pieces[3] = minus_ref[m, 0]
        halo = jnp.concatenate(pieces, axis=0)
        xtf_ref[m, :, :node_rows] = xt_ref[m]
        xtf_ref[m, :, node_rows:] = halo.T
        for kind, w_ref in enumerate((wk_ref, wv_ref)):
            rows = nn(halo, w_ref[...]).astype(bf16)
            for g, ref in enumerate(halo_refs):
                block = rows[:, g * 128 : (g + 1) * 128]
                ref[kind, m] = block
                ref[kind + 2, m] = block.T


def attention_kernel(extra, here, me_ref, *refs):
    refs = refs[extra:]
    locs, halos, refs = refs[:here], refs[here : 2 * here], refs[2 * here :]
    mask_ref, xtf, og_ref = refs[:3]
    split = 7 if len(refs) == 15 + 3 * (here - 1) else 6
    outs, grads, scratch = refs[3:split], refs[split : split + 3 * here], refs[split + 3 * here :]
    if split == 6:
        outs = (*outs[:2], outs[2].at[0], outs[2].at[1])
    for i in range(here):
        attend(
            me_ref, locs[i], halos[i], mask_ref, xtf, og_ref, outs, 512 * i,
            grads[3 * i : 3 * i + 3], scratch,
        )


def attend(me_ref, loc, halo, mask_ref, xtf, og_ref, out_refs, at, grad_refs, scratch):
    own_ref, other_ref, send_other, send_own = out_refs
    dq_ref, dk_ref, dv_ref = grad_refs
    score, grad, slope, dw, wos = scratch
    _, members, node_rows, _ = loc.shape
    table = mask_ref.shape[0]
    width = og_ref.shape[2]
    head = width // HEADS
    per = 128 // head
    scale = 1.0 / math.sqrt(head)

    row_head = lax.broadcasted_iota(jnp.int32, (128, node_rows), 0) // head
    lane_head = lax.broadcasted_iota(jnp.int32, (node_rows, 128), 1) // head

    def spread_t(block):
        zero = jnp.zeros_like(block)
        return jnp.concatenate([jnp.where(row_head == h, block, zero) for h in range(per)], axis=1)

    def spread_n(block):
        zero = jnp.zeros_like(block)
        return jnp.concatenate([jnp.where(lane_head == h, block, zero) for h in range(per)], axis=0)

    strip = 64
    for m in range(members):
        kg = jnp.concatenate([loc[K, m], halo[0, m]], axis=0)
        vg = jnp.concatenate([loc[V, m], halo[1, m]], axis=0)
        score[m] = nn(kg, spread_t(loc[QT, m]))
        grad[m] = nn(vg, spread_t(loc[GT, m]))

    wo_total = None
    kv_total = None
    q_total = None
    for m in range(members):
        probs = []
        for h in range(per):
            lanes = slice(h * node_rows, (h + 1) * node_rows)
            den = jnp.zeros((8, node_rows), f32)
            inner = jnp.zeros((8, node_rows), f32)
            for c in range(0, table, strip):
                box = (m, slice(c, c + strip), lanes)
                t = jnp.tanh(score[box] * (scale / score_cap))
                e = jnp.exp2(t * (score_cap / math.log(2.0))) * mask_ref[c : c + strip]
                den = den + jnp.sum(e.reshape(strip // 8, 8, node_rows), axis=0)
                inner = inner + jnp.sum((e * grad[box]).reshape(strip // 8, 8, node_rows), axis=0)
                score[box] = e
                slope[box] = e * (scale - scale * (t * t))
            r = 1.0 / jnp.sum(den, axis=0, keepdims=True)
            inner = jnp.sum(inner, axis=0, keepdims=True) * r
            column = []
            scores = []
            for c in range(0, table, strip):
                box = (m, slice(c, c + strip), lanes)
                column.append((score[box] * r).astype(bf16))
                scores.append(((slope[box] * r) * (grad[box] - inner)).astype(bf16))
            probs.append((jnp.concatenate(column, axis=0), jnp.concatenate(scores, axis=0)))
        pb = jnp.concatenate([p for p, _ in probs], axis=1)
        ds = jnp.concatenate([s for _, s in probs], axis=1)
        ktg = jnp.concatenate([loc[KT, m], halo[2, m]], axis=1)
        vtg = jnp.concatenate([loc[VT, m], halo[3, m]], axis=1)
        att, dqt = [], []
        for h in range(0, per, 2):
            lanes = slice(h * node_rows, (h + 2) * node_rows)
            rows = slice(h * head, (h + 2) * head)
            a = nn(vtg[rows], pb[:, lanes])
            b = nn(ktg[rows], ds[:, lanes])
            for j in range(2):
                inside = (slice(j * head, (j + 1) * head), slice(j * node_rows, (j + 1) * node_rows))
                att.append(a[inside].astype(bf16))
                dqt.append(b[inside].astype(bf16))
        att = jnp.concatenate(att, axis=0)
        dq = jnp.concatenate(dqt, axis=0).T
        dk = nn(ds, spread_n(loc[Q, m])).astype(bf16)
        dv = nn(pb, spread_n(loc[G, m])).astype(bf16)
        dq_ref[m], dk_ref[m], dv_ref[m] = dq, dk, dv
        wo_term = nn(att, og_ref[m])
        kv_term = nn(xtf[m], jnp.concatenate([dk, dv], axis=1))
        q_term = nn(xtf[m, :, :node_rows], dq)
        wo_total = wo_term if m == 0 else wo_total + wo_term
        kv_total = kv_term if m == 0 else kv_total + kv_term
        q_total = q_term if m == 0 else q_total + q_term

    planes, _, _, rows, _ = dw.shape
    inner_planes = wos.shape[0]
    dw[:, :, :, :, :128] = q_total.reshape(planes, 2, 2, rows, 128)
    dw[:, :, :, :, 128:] = kv_total.reshape(planes, 2, 2, rows, 256)
    wos[...] = wo_total.reshape(inner_planes, 2, 2, rows, width)
    me = me_ref[0]
    c, y, z = me % 2, (me // 2) % 2, me // 4
    qkv = slice(at, at + 384)
    for k in range(planes):
        zk = plane_of(gray(z) ^ k)
        own_ref[k, :, qkv] = dw[zk, y, c]
        other_ref[k, :, qkv] = dw[zk, 1 - y, c]
        send_other[k, :, qkv] = dw[zk, 1 - y, 1 - c].astype(bf16)
        send_own[k, :, qkv] = dw[zk, y, 1 - c].astype(bf16)
    last = slice(at + 384, at + 512)
    for i in range(inner_planes):
        for n in range(width // 128):
            k = n * inner_planes + i
            lanes = slice(n * 128, (n + 1) * 128)
            own_ref[k, :, last] = wos[i, y, c, :, lanes]
            other_ref[k, :, last] = wos[i, 1 - y, c, :, lanes]
            send_other[k, :, last] = wos[i, 1 - y, 1 - c, :, lanes].astype(bf16)
            send_own[k, :, last] = wos[i, y, 1 - c, :, lanes].astype(bf16)


def node_kernel(groups, skip, *refs):
    refs = refs[skip:]
    dqs, dks, dvs = refs[:groups], refs[groups : 2 * groups], refs[2 * groups : 3 * groups]
    wq_ref, wk_ref, wv_ref, node_ref, plus_ref, minus_ref, right_ref, left_ref = refs[3 * groups :]
    members, node_rows, _ = dqs[0].shape
    slots = plus_ref.shape[2]

    def whole(parts, m):
        return jnp.concatenate([part[m] for part in parts], axis=1)

    for m in range(members):
        spread = nt(whole(dks, m), wk_ref[...]) + nt(whole(dvs, m), wv_ref[...])
        node_ref[m] = spread[:node_rows] + nt(whole(dqs, m), wq_ref[...])
        halo = spread[node_rows:].astype(bf16)
        for ref, order in (
            (plus_ref, (3, 7, 5)),
            (minus_ref, (2, 4, 6)),
            (right_ref, (1,)),
            (left_ref, (0,)),
        ):
            for i, k in enumerate(order):
                ref[m, i] = halo[k * slots : (k + 1) * slots]


def sums(owns, core_in, y_in, k):
    total = jnp.concatenate(
        [
            own[k] + (core[1, k] if len(core.shape) == 4 else core[k]).astype(f32)
            for own, core in zip(owns, core_in)
        ],
        axis=1,
    ) + y_in[k].astype(f32)
    return [total[:, at : at + 512] for at in range(0, total.shape[1], 512)]


def gather_projection(parts, k, planes, projection_ref, start):
    inner_planes = planes * 128 // projection_ref.shape[2]
    quarter, inner = divmod(k, inner_planes)
    for i, part in enumerate(parts):
        plane = start + i * inner_planes + inner
        projection_ref[plane, :, quarter * 128 : (quarter + 1) * 128] = part[:, 384:]


def pack_kernel(pieces, *refs):
    for i, (ref, core) in enumerate(zip(refs[:pieces], refs[pieces:-1])):
        arrived = core[0] if len(core.shape) == 4 else core[...]
        refs[-1][:, :, i * 512 : (i + 1) * 512] = (ref[...] + arrived.astype(f32)).astype(bf16)


def halve(rows, kept_ref, sent_ref):
    for i, row in enumerate(rows):
        if i % 2 == 0:
            kept_ref[i // 2] = row
            continue
        pieces = row.shape[1] // 256
        for n in range(pieces):
            sent_ref[i // 2 * pieces + n] = row[:, n * 256 : (n + 1) * 256].astype(bf16)


def add_received(kept_ref, received_ref):
    planes, _, wide = kept_ref.shape
    pieces = wide // 256
    return [
        kept_ref[i]
        + jnp.concatenate([received_ref[i * pieces + n] for n in range(pieces)], axis=1).astype(f32)
        for i in range(planes)
    ]


def first_kernel(after_ref, own, core_in, y_in, kept_ref, projection_ref, sent_ref):
    planes = own.shape[0]
    rows = []
    for k in range(planes):
        parts = sums([own], [core_in], y_in, k)
        gather_projection(parts, k, planes, projection_ref, 0)
        rows.append(jnp.concatenate([part[:, :384] for part in parts], axis=1))
    halve(rows, kept_ref, sent_ref)


def put(row, ref, at):
    for n in range(row.shape[1] // 256):
        ref[at + n] = row[:, n * 256 : (n + 1) * 256].astype(bf16)


def second_kernel(skip, pieces, me_ref, *refs):
    refs = refs[skip:]
    kept_a, in_a, first_ref, y_in = refs[:4]
    owns, core_in = refs[4 : 4 + pieces], refs[4 + pieces : 4 + 2 * pieces]
    own_a, own_b, *sent = refs[4 + 2 * pieces : -1]
    projection_ref = refs[-1]
    done = first_ref.shape[0]
    planes = projection_ref.shape[0]
    projection_ref[:done] = first_ref[...]
    held = []
    for k in range(planes):
        parts = sums(owns, core_in, y_in, k)
        gather_projection(parts, k, planes, projection_ref, done)
        held.append(jnp.concatenate([part[:, :384] for part in parts], axis=1))
    first = add_received(kept_a, in_a)
    own_a[...] = first[0]
    z = me_ref[0] // 4
    for k in range(planes):
        row = jnp.concatenate([held[k], projection_ref[plane_of(gray(z) ^ k)]], axis=1)
        if k == 0:
            own_b[...] = row
            continue
        put(row, sent[k - 1], 0)
        if k % 2 == 0:
            put(first[k // 2], sent[k - 1], row.shape[1] // 256)


def finish_kernel(
    me_ref, after_ref, send_ref, node_ref, plus_ref, minus_ref, first_in, second_in, out_ref, came
):
    members, node_rows, _ = node_ref.shape
    pick = sent_selector(send_ref[0], node_rows).astype(bf16)
    from_swaps(came, me_ref[0] % 2, first_in, second_in)
    for m in range(members):
        pieces = [None] * 8
        for side, order in enumerate(((1, 4, 7), (0, 6, 5))):
            for i, k in enumerate(order):
                pieces[k] = came[side, m, i]
        pieces[2], pieces[3] = plus_ref[m, 0], minus_ref[m, 0]
        arriving = jnp.concatenate(pieces, axis=0)
        out_ref[m] = (node_ref[m] + nn(pick, arriving)).astype(bf16)


def weight_kernel(after_ref, own_a, own_b, *refs):
    received, out_ref = refs[:-1], refs[-1]
    a, b = own_a[...], own_b[...]
    blocks, more = b.shape[1] // 256, a.shape[1] // 256
    for k, ref in enumerate(received, 1):
        b = b + jnp.concatenate([ref[n] for n in range(blocks)], axis=1).astype(f32)
        if k % 2 == 0:
            a = a + jnp.concatenate([ref[blocks + n] for n in range(more)], axis=1).astype(f32)
    half = a.shape[1] // 384
    width = 256 * half
    for i, part in enumerate((a, b)):
        for j in range(half):
            for n in range(3):
                at = n * width + (i * half + j) * 128
                out_ref[:, at : at + 128] = part[:, j * 384 + n * 128 : j * 384 + (n + 1) * 128]
    out_ref[:, 3 * width :] = b[:, 384 * half :]


def call(kernel, outs, operands, specs=None, scratch=(), limit=12, final=False, flops=10**6):
    specs = list(specs or ())
    specs += [pltpu.VMEM] * (len(operands) - len(specs))
    operands = [
        pltpu.with_memory_space_constraint(o, s) if s in (pltpu.HBM, pltpu.VMEM) else o
        for o, s in zip(operands, specs)
    ]
    return pl.pallas_call(
        kernel,
        out_shape=[jax.ShapeDtypeStruct(*o) if final else pltpu.VMEM(*o) for o in outs],
        in_specs=[pl.BlockSpec(memory_space=s) for s in specs],
        scratch_shapes=list(scratch),
        compiler_params=pltpu.CompilerParams(vmem_limit_bytes=limit * MIB),
        cost_estimate=pl.CostEstimate(flops=flops, bytes_accessed=10**4, transcendentals=0),
    )(*operands)


def body(
    node_features, out_grad, w_query, w_key, w_value, w_out, neighbours, neighbour_count, send_rows
):
    members, node_rows, width = node_features.shape
    count = lax.axis_size("patch")
    row_width = min(8, count // 4)
    _, adjacent, slots = send_rows.shape
    table = node_rows + adjacent * slots
    groups = width // 128
    me = lax.axis_index("patch")
    three = ((members, 3, slots, width), bf16)
    one = ((members, 1, slots, width), bf16)

    place = me.reshape(1)
    trio = pltpu.VMEM((2, *three[0]), bf16)
    to_plus, to_minus, own_right, own_left, x = call(
        functools.partial(gather_kernel, slots),
        [three, three, one, one, (node_features.shape, bf16)],
        (send_rows, node_features),
        specs=[pltpu.HBM] * 2,
        scratch=[pltpu.VMEM(send_rows.shape, jnp.int32), pltpu.SemaphoreType.DMA((2,))],
    )
    plus = shifted(to_plus, row_width)
    minus = shifted(to_minus, -row_width)
    square = ((width, width), bf16)
    counts = neighbour_count.reshape(1, node_rows)
    *loc, xt, wq, wk, wv, og, neigh, counts = call(
        functools.partial(local_kernel, groups),
        [((8, members, node_rows, 128), bf16)] * groups
        + [((members, width, node_rows), bf16), square, square, square, (out_grad.shape, bf16)]
        + [(neighbours.shape, jnp.int32), (counts.shape, jnp.int32)],
        (own_right, x, w_query, w_key, w_value, out_grad, neighbours, counts, w_out),
        specs=[pl.ANY, pltpu.VMEM] + [pltpu.HBM] * 7,
        scratch=[pltpu.VMEM((width, width), bf16), pltpu.SemaphoreType.DMA((7,))],
        limit=16,
    )
    outgoing = call(
        relay_kernel, [three, three], (place, loc[0], own_right, own_left, plus, minus),
        specs=[pltpu.SMEM, pl.ANY], scratch=[trio],
    )
    arrived = swap(outgoing, 1)
    (mask,) = call(
        mask_kernel, [((table, node_rows), f32)], (outgoing[0], neigh, counts), specs=[pl.ANY]
    )
    *halo, xtf = call(
        halo_kernel,
        [((4, members, node_rows, 128), bf16)] * groups + [((members, width, table), bf16)],
        (place, plus, minus, *arrived, xt, wk, wv), specs=[pltpu.SMEM], scratch=[trio],
    )

    planes, rows = count // 4, width // count
    inner_planes = planes * 128 // width
    flip = [(i, i ^ 1) for i in range(count)]
    flop = [(i, i ^ 2) for i in range(count)]
    grads = []

    def attention(extra, which, together):
        wide = 512 * len(which)
        sends = [((2, planes, rows, wide), bf16)] if together else [((planes, rows, wide), bf16)] * 2
        outs = call(
            functools.partial(attention_kernel, len(extra), len(which)),
            [((planes, rows, wide), f32)] * 2
            + sends
            + [
                ((members, node_rows, 128), bf16),
                ((members, table, 128), bf16),
                ((members, table, 128), bf16),
            ]
            * len(which),
            (
                place, *extra, *[loc[g] for g in which], *[halo[g] for g in which], mask, xtf, og,
            ),
            specs=[pltpu.SMEM] + [pl.ANY] * len(extra),
            scratch=[pltpu.VMEM((members, table, 512), f32)] * 3
            + [
                pltpu.VMEM((planes, 2, 2, rows, 384), f32),
                pltpu.VMEM((inner_planes, 2, 2, rows, width), f32),
            ],
            limit=24,
        )
        sent = outs[2 : 2 + len(sends)]
        grads.extend(outs[2 + len(sends) :])
        arrived = [lax.ppermute(shard, "patch", flip) for shard in sent]
        return outs[0], outs[1], arrived[0], arrived[-1]

    half = groups // 2
    wide = 384 * half
    own_a, other, core_other, core_own = attention((), range(half), False)
    y_sent = (other + core_other.astype(f32)).astype(bf16)
    y_a = lax.ppermute(y_sent, "patch", flop)
    later = []
    for g in range(half, groups):
        last = g == groups - 1
        later.append(attention((y_sent,) if last else (), range(g, g + 1), not last))
    own_b, other_b, core_other_b, core_own_b = zip(*later)
    (y_sent,) = call(
        functools.partial(pack_kernel, len(later)), [(y_sent.shape, bf16)],
        (*other_b, *core_other_b),
    )
    y_b = lax.ppermute(y_sent, "patch", flop)
    node, to_plus, to_minus, own_right, own_left = call(
        functools.partial(node_kernel, groups, 1),
        [((members, node_rows, width), f32), three, three, one, one],
        (y_sent, *grads[0::3], *grads[1::3], *grads[2::3], wq, wk, wv),
        specs=[pl.ANY],
    )
    from_plus = shifted(to_minus, -row_width)
    from_minus = shifted(to_plus, row_width)
    def exchange(sent, distance):
        return lax.ppermute(sent, "patch", along_z(count, distance))

    kept_a, out_a, sent_a = call(
        first_kernel,
        [
            ((planes // 2, rows, wide), f32),
            ((half * inner_planes, rows, width), f32),
            ((planes // 2 * wide // 256, rows, 256), bf16),
        ],
        (y_sent, own_a, core_own, y_a), specs=[pl.ANY], flops=2 * 10**10,
    )
    in_a = exchange(sent_a, 1)
    outgoing = call(
        relay_kernel, [three, three],
        (place, sent_a, own_right, own_left, from_plus, from_minus),
        specs=[pltpu.SMEM, pl.ANY], scratch=[trio],
    )
    back = swap(outgoing, 1)
    more, blocks = wide // 256, (wide + width) // 256
    own_a, own_b, *sent = call(
        functools.partial(second_kernel, 1, len(later)),
        [((rows, wide), f32), ((rows, wide + width), f32)]
        + [((blocks + (0 if k % 2 else more), rows, 256), bf16) for k in range(1, planes)],
        (place, outgoing[0], kept_a, in_a, out_a, y_b, *own_b, *core_own_b),
        specs=[pltpu.SMEM, pl.ANY],
        scratch=[pltpu.VMEM((planes, rows, width), f32)],
    )
    received = [exchange(shard, k) for k, shard in enumerate(sent, 1)]
    (node_grad,) = call(
        finish_kernel, [((members, node_rows, width), bf16)],
        (place, sent[0], send_rows, node, from_plus, from_minus, *back),
        specs=[pltpu.SMEM, pl.ANY], scratch=[trio], final=True,
    )
    (weight_grad,) = call(
        weight_kernel, [((rows, 4 * width), f32)], (node_grad, own_a, own_b, *received),
        specs=[pltpu.HBM], final=True,
    )
    return (node_grad, weight_grad)


def solution(mesh):
    in_specs = (
        P("groups", "patch", None),
        P("groups", "patch", None),
        P(),
        P(),
        P(),
        P(),
        P("patch", None),
        P("patch"),
        P("patch", None, None),
    )
    out_specs = (P("groups", "patch", None), P(("groups", "patch"), None))
    return jax.shard_map(body, mesh=mesh, in_specs=in_specs, out_specs=out_specs, check_vma=False)
```

```python
import functools
import math

import jax
import jax.numpy as jnp
from jax import lax
from jax.experimental import pallas as pl
from jax.experimental.pallas import tpu as pltpu
from jax.sharding import PartitionSpec as P

HEADS = 16
score_cap = 5.0
MIB = 1024 * 1024
f32 = jnp.float32
bf16 = jnp.bfloat16


def nn(a, b):
    return lax.dot_general(a, b, (((1,), (0,)), ((), ())), preferred_element_type=f32)


def nt(a, b):
    return lax.dot_general(a, b, (((1,), (1,)), ((), ())), preferred_element_type=f32)


def shifted(shard, by):
    count = lax.axis_size("patch")
    return lax.ppermute(shard, "patch", [(i, (i + by) % count) for i in range(count)])


def neighbours_apart(count, stride):
    first, second = [], []
    for i in range(count):
        up, down = (i + stride) % count, (i - stride) % count
        even = i // stride % 2 == 0
        first.append((i, up if even else down))
        second.append((i, down if even else up))
    return first, second


def swap(pair, stride):
    return [
        lax.ppermute(shard, "patch", perm)
        for shard, perm in zip(pair, neighbours_apart(lax.axis_size("patch"), stride))
    ]


def to_swaps(both, odd, first_ref, second_ref):
    first_ref[...] = both[odd]
    second_ref[...] = both[1 - odd]


def from_swaps(both, odd, first_ref, second_ref):
    both[1 - odd] = first_ref[...]
    both[odd] = second_ref[...]


def sent_selector(send_rows, node_rows):
    adjacent, slots = send_rows.shape
    halo = adjacent * slots
    wide = jnp.concatenate([send_rows] * adjacent, axis=1)
    own = lax.broadcasted_iota(jnp.int32, (adjacent, halo), 1) // slots == lax.broadcasted_iota(
        jnp.int32, (adjacent, halo), 0
    )
    ids = jnp.sum(jnp.where(own, wide, 0), axis=0, keepdims=True)
    nodes = lax.broadcasted_iota(jnp.int32, (node_rows, halo), 0)
    return jnp.where(nodes == ids, 1.0, 0.0).astype(f32)


def gather_kernel(
    slots, send_hbm, x_hbm, plus_ref, minus_ref, right_ref, left_ref, x_ref, send_ref, sem
):
    copies = [
        pltpu.make_async_copy(send_hbm, send_ref, sem.at[0]),
        pltpu.make_async_copy(x_hbm, x_ref, sem.at[1]),
    ]
    for copy in copies:
        copy.start()
    copies[0].wait()
    members, node_rows, _ = x_ref.shape
    pick = sent_selector(send_ref[0], node_rows).T.astype(bf16)
    copies[1].wait()
    for m in range(members):
        rows = nn(pick, x_ref[m]).astype(bf16)

        def part(k):
            return rows[k * slots : (k + 1) * slots]

        for ref, order in ((plus_ref, (2, 6, 4)), (minus_ref, (3, 5, 7))):
            for i, k in enumerate(order):
                ref[m, i] = part(k)
        right_ref[m, 0] = part(0)
        left_ref[m, 0] = part(1)


def relay_kernel(
    me_ref, after_ref, own_right, own_left, plus_ref, minus_ref, first_ref, second_ref, both
):
    for side, own in enumerate((own_right, own_left)):
        both[side, :, 0:1] = own[...]
        both[side, :, 1:2] = plus_ref[:, 1 + side : 2 + side]
        both[side, :, 2:3] = minus_ref[:, 1 + side : 2 + side]
    to_swaps(both, me_ref[0] % 2, first_ref, second_ref)


def gray(z):
    return z ^ (z >> 1)


def plane_of(code):
    z = code
    for shift in range(1, 8):
        z = z ^ (code >> shift)
    return z


def along_z(count, distance):
    planes = count // 4
    return [(i, plane_of(gray(i // 4) ^ distance) * 4 + i % 4) for i in range(planes * 4)]


Q, K, V, G, QT, KT, VT, GT = range(8)


def local_kernel(groups, after_ref, x_ref, *refs):
    sources, loc_refs, xt_ref = refs[:7], refs[7 : 7 + groups], refs[7 + groups]
    copied, sem = refs[8 + groups : 15 + groups], refs[-1]
    copies = [
        pltpu.make_async_copy(source, target, sem.at[i])
        for i, (source, target) in enumerate(zip(sources, copied))
    ]
    for copy in copies:
        copy.start()
    members, node_rows, width = x_ref.shape
    x = x_ref[...].reshape(members * node_rows, width)
    for m in range(members):
        xt_ref[m] = x_ref[m].T

    def put(rows, kind):
        for m in range(members):
            for g, ref in enumerate(loc_refs):
                block = rows[m * node_rows : (m + 1) * node_rows, g * 128 : (g + 1) * 128]
                ref[kind, m] = block
                ref[kind + 4, m] = block.T

    wq_ref, wk_ref, wv_ref, og_ref, _, _, wo_ref = copied
    for kind, ref in enumerate((wq_ref, wk_ref, wv_ref)):
        copies[kind].wait()
        put(nn(x, ref[...]).astype(bf16), kind)
    for copy in copies[3:]:
        copy.wait()
    og = og_ref[...].reshape(members * node_rows, width)
    put(nt(og, wo_ref[...]).astype(bf16), G)


def mask_kernel(after_ref, neigh_ref, count_ref, mask_ref):
    neigh = neigh_ref[...].T
    slots, node_rows = neigh.shape
    table = mask_ref.shape[0]
    order = lax.broadcasted_iota(jnp.int32, neigh.shape, 0)
    tail = jnp.where(order >= count_ref[...], neigh, -1)[slots // 2 :]
    half = table // 2
    for part in range(2):
        columns = lax.broadcasted_iota(jnp.int32, (half, node_rows), 0) + part * half
        kept = jnp.ones((half, node_rows), f32)
        for j in range(slots // 2):
            kept = jnp.where(tail[j : j + 1] == columns, 0.0, kept)
        mask_ref[part * half : (part + 1) * half] = kept


def halo_kernel(
    me_ref, plus_ref, minus_ref, first_in, second_in, xt_ref, wk_ref, wv_ref, *refs
):
    halo_refs, xtf_ref, both = refs[:-2], refs[-2], refs[-1]
    members, _, node_rows = xt_ref.shape
    from_swaps(both, me_ref[0] % 2, first_in, second_in)
    for m in range(members):
        pieces = [None] * 8
        for side, order in enumerate(((0, 6, 5), (1, 4, 7))):
            for i, k in enumerate(order):
                pieces[k] = both[side, m, i]
        pieces[2] = plus_ref[m, 0]
        pieces[3] = minus_ref[m, 0]
        halo = jnp.concatenate(pieces, axis=0)
        xtf_ref[m, :, :node_rows] = xt_ref[m]
        xtf_ref[m, :, node_rows:] = halo.T
        for kind, w_ref in enumerate((wk_ref, wv_ref)):
            rows = nn(halo, w_ref[...]).astype(bf16)
            for g, ref in enumerate(halo_refs):
                block = rows[:, g * 128 : (g + 1) * 128]
                ref[kind, m] = block
                ref[kind + 2, m] = block.T


def attention_kernel(extra, here, me_ref, *refs):
    refs = refs[extra:]
    locs, halos, refs = refs[:here], refs[here : 2 * here], refs[2 * here :]
    mask_ref, xtf, og_ref = refs[:3]
    split = 7 if len(refs) == 15 + 3 * (here - 1) else 6
    outs, grads, scratch = refs[3:split], refs[split : split + 3 * here], refs[split + 3 * here :]
    if split == 6:
        outs = (*outs[:2], outs[2].at[0], outs[2].at[1])
    for i in range(here):
        attend(
            me_ref, locs[i], halos[i], mask_ref, xtf, og_ref, outs, 512 * i,
            grads[3 * i : 3 * i + 3], scratch,
        )


def attend(me_ref, loc, halo, mask_ref, xtf, og_ref, out_refs, at, grad_refs, scratch):
    own_ref, other_ref, send_other, send_own = out_refs
    dq_ref, dk_ref, dv_ref = grad_refs
    score, grad, slope, dw, wos = scratch
    _, members, node_rows, _ = loc.shape
    table = mask_ref.shape[0]
    width = og_ref.shape[2]
    head = width // HEADS
    per = 128 // head
    scale = 1.0 / math.sqrt(head)

    row_head = lax.broadcasted_iota(jnp.int32, (128, node_rows), 0) // head
    lane_head = lax.broadcasted_iota(jnp.int32, (node_rows, 128), 1) // head

    def spread_t(block):
        zero = jnp.zeros_like(block)
        return jnp.concatenate([jnp.where(row_head == h, block, zero) for h in range(per)], axis=1)

    def spread_n(block):
        zero = jnp.zeros_like(block)
        return jnp.concatenate([jnp.where(lane_head == h, block, zero) for h in range(per)], axis=0)

    strip = 64
    for m in range(members):
        kg = jnp.concatenate([loc[K, m], halo[0, m]], axis=0)
        vg = jnp.concatenate([loc[V, m], halo[1, m]], axis=0)
        score[m] = nn(kg, spread_t(loc[QT, m]))
        grad[m] = nn(vg, spread_t(loc[GT, m]))

    wo_total = None
    kv_total = None
    q_total = None
    for m in range(members):
        probs = []
        for h in range(per):
            lanes = slice(h * node_rows, (h + 1) * node_rows)
            den = jnp.zeros((8, node_rows), f32)
            inner = jnp.zeros((8, node_rows), f32)
            for c in range(0, table, strip):
                box = (m, slice(c, c + strip), lanes)
                t = jnp.tanh(score[box] * (scale / score_cap))
                e = jnp.exp2(t * (score_cap / math.log(2.0))) * mask_ref[c : c + strip]
                den = den + jnp.sum(e.reshape(strip // 8, 8, node_rows), axis=0)
                inner = inner + jnp.sum((e * grad[box]).reshape(strip // 8, 8, node_rows), axis=0)
                score[box] = e
                slope[box] = e * (scale - scale * (t * t))
            r = 1.0 / jnp.sum(den, axis=0, keepdims=True)
            inner = jnp.sum(inner, axis=0, keepdims=True) * r
            column = []
            scores = []
            for c in range(0, table, strip):
                box = (m, slice(c, c + strip), lanes)
                column.append((score[box] * r).astype(bf16))
                scores.append(((slope[box] * r) * (grad[box] - inner)).astype(bf16))
            probs.append((jnp.concatenate(column, axis=0), jnp.concatenate(scores, axis=0)))
        pb = jnp.concatenate([p for p, _ in probs], axis=1)
        ds = jnp.concatenate([s for _, s in probs], axis=1)
        ktg = jnp.concatenate([loc[KT, m], halo[2, m]], axis=1)
        vtg = jnp.concatenate([loc[VT, m], halo[3, m]], axis=1)
        att, dqt = [], []
        for h in range(0, per, 2):
            lanes = slice(h * node_rows, (h + 2) * node_rows)
            rows = slice(h * head, (h + 2) * head)
            a = nn(vtg[rows], pb[:, lanes])
            b = nn(ktg[rows], ds[:, lanes])
            for j in range(2):
                inside = (slice(j * head, (j + 1) * head), slice(j * node_rows, (j + 1) * node_rows))
                att.append(a[inside].astype(bf16))
                dqt.append(b[inside].astype(bf16))
        att = jnp.concatenate(att, axis=0)
        dq = jnp.concatenate(dqt, axis=0).T
        dk = nn(ds, spread_n(loc[Q, m])).astype(bf16)
        dv = nn(pb, spread_n(loc[G, m])).astype(bf16)
        dq_ref[m], dk_ref[m], dv_ref[m] = dq, dk, dv
        wo_term = nn(att, og_ref[m])
        kv_term = nn(xtf[m], jnp.concatenate([dk, dv], axis=1))
        q_term = nn(xtf[m, :, :node_rows], dq)
        wo_total = wo_term if m == 0 else wo_total + wo_term
        kv_total = kv_term if m == 0 else kv_total + kv_term
        q_total = q_term if m == 0 else q_total + q_term

    planes, _, _, rows, _ = dw.shape
    inner_planes = wos.shape[0]
    dw[:, :, :, :, :128] = q_total.reshape(planes, 2, 2, rows, 128)
    dw[:, :, :, :, 128:] = kv_total.reshape(planes, 2, 2, rows, 256)
    wos[...] = wo_total.reshape(inner_planes, 2, 2, rows, width)
    me = me_ref[0]
    c, y, z = me % 2, (me // 2) % 2, me // 4
    qkv = slice(at, at + 384)
    for k in range(planes):
        zk = plane_of(gray(z) ^ k)
        own_ref[k, :, qkv] = dw[zk, y, c]
        other_ref[k, :, qkv] = dw[zk, 1 - y, c]
        send_other[k, :, qkv] = dw[zk, 1 - y, 1 - c].astype(bf16)
        send_own[k, :, qkv] = dw[zk, y, 1 - c].astype(bf16)
    last = slice(at + 384, at + 512)
    for i in range(inner_planes):
        for n in range(width // 128):
            k = n * inner_planes + i
            lanes = slice(n * 128, (n + 1) * 128)
            own_ref[k, :, last] = wos[i, y, c, :, lanes]
            other_ref[k, :, last] = wos[i, 1 - y, c, :, lanes]
            send_other[k, :, last] = wos[i, 1 - y, 1 - c, :, lanes].astype(bf16)
            send_own[k, :, last] = wos[i, y, 1 - c, :, lanes].astype(bf16)


def node_kernel(groups, skip, *refs):
    refs = refs[skip:]
    dqs, dks, dvs = refs[:groups], refs[groups : 2 * groups], refs[2 * groups : 3 * groups]
    wq_ref, wk_ref, wv_ref, node_ref, plus_ref, minus_ref, right_ref, left_ref = refs[3 * groups :]
    members, node_rows, _ = dqs[0].shape
    slots = plus_ref.shape[2]

    def whole(parts, m):
        return jnp.concatenate([part[m] for part in parts], axis=1)

    for m in range(members):
        spread = nt(whole(dks, m), wk_ref[...]) + nt(whole(dvs, m), wv_ref[...])
        node_ref[m] = spread[:node_rows] + nt(whole(dqs, m), wq_ref[...])
        halo = spread[node_rows:].astype(bf16)
        for ref, order in (
            (plus_ref, (3, 7, 5)),
            (minus_ref, (2, 4, 6)),
            (right_ref, (1,)),
            (left_ref, (0,)),
        ):
            for i, k in enumerate(order):
                ref[m, i] = halo[k * slots : (k + 1) * slots]


def sums(owns, core_in, y_in, k):
    total = jnp.concatenate(
        [
            own[k] + (core[1, k] if len(core.shape) == 4 else core[k]).astype(f32)
            for own, core in zip(owns, core_in)
        ],
        axis=1,
    ) + y_in[k].astype(f32)
    return [total[:, at : at + 512] for at in range(0, total.shape[1], 512)]


def gather_projection(parts, k, planes, projection_ref, start):
    inner_planes = planes * 128 // projection_ref.shape[2]
    quarter, inner = divmod(k, inner_planes)
    for i, part in enumerate(parts):
        plane = start + i * inner_planes + inner
        projection_ref[plane, :, quarter * 128 : (quarter + 1) * 128] = part[:, 384:]


def pack_kernel(pieces, *refs):
    for i, (ref, core) in enumerate(zip(refs[:pieces], refs[pieces:-1])):
        arrived = core[0] if len(core.shape) == 4 else core[...]
        refs[-1][:, :, i * 512 : (i + 1) * 512] = (ref[...] + arrived.astype(f32)).astype(bf16)


def halve(rows, kept_ref, sent_ref):
    for i, row in enumerate(rows):
        if i % 2 == 0:
            kept_ref[i // 2] = row
            continue
        pieces = row.shape[1] // 256
        for n in range(pieces):
            sent_ref[i // 2 * pieces + n] = row[:, n * 256 : (n + 1) * 256].astype(bf16)


def add_received(kept_ref, received_ref):
    planes, _, wide = kept_ref.shape
    pieces = wide // 256
    return [
        kept_ref[i]
        + jnp.concatenate([received_ref[i * pieces + n] for n in range(pieces)], axis=1).astype(f32)
        for i in range(planes)
    ]


def first_kernel(after_ref, own, core_in, y_in, kept_ref, projection_ref, sent_ref):
    planes = own.shape[0]
    rows = []
    for k in range(planes):
        parts = sums([own], [core_in], y_in, k)
        gather_projection(parts, k, planes, projection_ref, 0)
        rows.append(jnp.concatenate([part[:, :384] for part in parts], axis=1))
    halve(rows, kept_ref, sent_ref)


def put(row, ref, at):
    for n in range(row.shape[1] // 256):
        ref[at + n] = row[:, n * 256 : (n + 1) * 256].astype(bf16)


def second_kernel(skip, pieces, me_ref, *refs):
    refs = refs[skip:]
    kept_a, in_a, first_ref, y_in = refs[:4]
    owns, core_in = refs[4 : 4 + pieces], refs[4 + pieces : 4 + 2 * pieces]
    own_a, own_b, *sent = refs[4 + 2 * pieces : -1]
    projection_ref = refs[-1]
    done = first_ref.shape[0]
    planes = projection_ref.shape[0]
    projection_ref[:done] = first_ref[...]
    held = []
    for k in range(planes):
        parts = sums(owns, core_in, y_in, k)
        gather_projection(parts, k, planes, projection_ref, done)
        held.append(jnp.concatenate([part[:, :384] for part in parts], axis=1))
    first = add_received(kept_a, in_a)
    own_a[...] = first[0]
    z = me_ref[0] // 4
    for k in range(planes):
        row = jnp.concatenate([held[k], projection_ref[plane_of(gray(z) ^ k)]], axis=1)
        if k == 0:
            own_b[...] = row
            continue
        put(row, sent[k - 1], 0)
        if k % 2 == 0:
            put(first[k // 2], sent[k - 1], row.shape[1] // 256)


def finish_kernel(
    me_ref, after_ref, send_ref, node_ref, plus_ref, minus_ref, first_in, second_in, out_ref, came
):
    members, node_rows, _ = node_ref.shape
    pick = sent_selector(send_ref[0], node_rows).astype(bf16)
    from_swaps(came, me_ref[0] % 2, first_in, second_in)
    for m in range(members):
        pieces = [None] * 8
        for side, order in enumerate(((1, 4, 7), (0, 6, 5))):
            for i, k in enumerate(order):
                pieces[k] = came[side, m, i]
        pieces[2], pieces[3] = plus_ref[m, 0], minus_ref[m, 0]
        arriving = jnp.concatenate(pieces, axis=0)
        out_ref[m] = (node_ref[m] + nn(pick, arriving)).astype(bf16)


def weight_kernel(after_ref, own_a, own_b, *refs):
    received, out_ref = refs[:-1], refs[-1]
    a, b = own_a[...], own_b[...]
    blocks, more = b.shape[1] // 256, a.shape[1] // 256
    for k, ref in enumerate(received, 1):
        b = b + jnp.concatenate([ref[n] for n in range(blocks)], axis=1).astype(f32)
        if k % 2 == 0:
            a = a + jnp.concatenate([ref[blocks + n] for n in range(more)], axis=1).astype(f32)
    half = a.shape[1] // 384
    width = 256 * half
    for i, part in enumerate((a, b)):
        for j in range(half):
            for n in range(3):
                at = n * width + (i * half + j) * 128
                out_ref[:, at : at + 128] = part[:, j * 384 + n * 128 : j * 384 + (n + 1) * 128]
    out_ref[:, 3 * width :] = b[:, 384 * half :]


def call(kernel, outs, operands, specs=None, scratch=(), limit=12, final=False, flops=10**6):
    specs = list(specs or ())
    specs += [pltpu.VMEM] * (len(operands) - len(specs))
    operands = [
        pltpu.with_memory_space_constraint(o, s) if s in (pltpu.HBM, pltpu.VMEM) else o
        for o, s in zip(operands, specs)
    ]
    return pl.pallas_call(
        kernel,
        out_shape=[jax.ShapeDtypeStruct(*o) if final else pltpu.VMEM(*o) for o in outs],
        in_specs=[pl.BlockSpec(memory_space=s) for s in specs],
        scratch_shapes=list(scratch),
        compiler_params=pltpu.CompilerParams(vmem_limit_bytes=limit * MIB),
        cost_estimate=pl.CostEstimate(flops=flops, bytes_accessed=10**4, transcendentals=0),
    )(*operands)


def body(
    node_features, out_grad, w_query, w_key, w_value, w_out, neighbours, neighbour_count, send_rows
):
    members, node_rows, width = node_features.shape
    count = lax.axis_size("patch")
    row_width = min(8, count // 4)
    _, adjacent, slots = send_rows.shape
    table = node_rows + adjacent * slots
    groups = width // 128
    me = lax.axis_index("patch")
    three = ((members, 3, slots, width), bf16)
    one = ((members, 1, slots, width), bf16)

    place = me.reshape(1)
    trio = pltpu.VMEM((2, *three[0]), bf16)
    to_plus, to_minus, own_right, own_left, x = call(
        functools.partial(gather_kernel, slots),
        [three, three, one, one, (node_features.shape, bf16)],
        (send_rows, node_features),
        specs=[pltpu.HBM] * 2,
        scratch=[pltpu.VMEM(send_rows.shape, jnp.int32), pltpu.SemaphoreType.DMA((2,))],
    )
    plus = shifted(to_plus, row_width)
    minus = shifted(to_minus, -row_width)
    square = ((width, width), bf16)
    counts = neighbour_count.reshape(1, node_rows)
    *loc, xt, wq, wk, wv, og, neigh, counts = call(
        functools.partial(local_kernel, groups),
        [((8, members, node_rows, 128), bf16)] * groups
        + [((members, width, node_rows), bf16), square, square, square, (out_grad.shape, bf16)]
        + [(neighbours.shape, jnp.int32), (counts.shape, jnp.int32)],
        (own_right, x, w_query, w_key, w_value, out_grad, neighbours, counts, w_out),
        specs=[pl.ANY, pltpu.VMEM] + [pltpu.HBM] * 7,
        scratch=[pltpu.VMEM((width, width), bf16), pltpu.SemaphoreType.DMA((7,))],
        limit=16,
    )
    outgoing = call(
        relay_kernel, [three, three], (place, loc[0], own_right, own_left, plus, minus),
        specs=[pltpu.SMEM, pl.ANY], scratch=[trio],
    )
    arrived = swap(outgoing, 1)
    (mask,) = call(
        mask_kernel, [((table, node_rows), f32)], (outgoing[0], neigh, counts), specs=[pl.ANY]
    )
    *halo, xtf = call(
        halo_kernel,
        [((4, members, node_rows, 128), bf16)] * groups + [((members, width, table), bf16)],
        (place, plus, minus, *arrived, xt, wk, wv), specs=[pltpu.SMEM], scratch=[trio],
    )

    planes, rows = count // 4, width // count
    inner_planes = planes * 128 // width
    flip = [(i, i ^ 1) for i in range(count)]
    flop = [(i, i ^ 2) for i in range(count)]
    grads = []

    def attention(extra, which, together):
        wide = 512 * len(which)
        sends = [((2, planes, rows, wide), bf16)] if together else [((planes, rows, wide), bf16)] * 2
        outs = call(
            functools.partial(attention_kernel, len(extra), len(which)),
            [((planes, rows, wide), f32)] * 2
            + sends
            + [
                ((members, node_rows, 128), bf16),
                ((members, table, 128), bf16),
                ((members, table, 128), bf16),
            ]
            * len(which),
            (
                place, *extra, *[loc[g] for g in which], *[halo[g] for g in which], mask, xtf, og,
            ),
            specs=[pltpu.SMEM] + [pl.ANY] * len(extra),
            scratch=[pltpu.VMEM((members, table, 512), f32)] * 3
            + [
                pltpu.VMEM((planes, 2, 2, rows, 384), f32),
                pltpu.VMEM((inner_planes, 2, 2, rows, width), f32),
            ],
            limit=24,
        )
        sent = outs[2 : 2 + len(sends)]
        grads.extend(outs[2 + len(sends) :])
        arrived = [lax.ppermute(shard, "patch", flip) for shard in sent]
        return outs[0], outs[1], arrived[0], arrived[-1]

    half = groups // 2
    wide = 384 * half
    own_a, other, core_other, core_own = attention((), range(half), False)
    y_sent = (other + core_other.astype(f32)).astype(bf16)
    y_a = lax.ppermute(y_sent, "patch", flop)
    later = []
    for g in range(half, groups):
        last = g == groups - 1
        later.append(attention((y_sent,) if last else (), range(g, g + 1), not last))
    own_b, other_b, core_other_b, core_own_b = zip(*later)
    (y_sent,) = call(
        functools.partial(pack_kernel, len(later)), [(y_sent.shape, bf16)],
        (*other_b, *core_other_b),
    )
    y_b = lax.ppermute(y_sent, "patch", flop)
    def exchange(sent, distance):
        return lax.ppermute(sent, "patch", along_z(count, distance))

    kept_a, out_a, sent_a = call(
        first_kernel,
        [
            ((planes // 2, rows, wide), f32),
            ((half * inner_planes, rows, width), f32),
            ((planes // 2 * wide // 256, rows, 256), bf16),
        ],
        (y_sent, own_a, core_own, y_a), specs=[pl.ANY], flops=2 * 10**10,
    )
    in_a = exchange(sent_a, 1)
    node, to_plus, to_minus, own_right, own_left = call(
        functools.partial(node_kernel, groups, 1),
        [((members, node_rows, width), f32), three, three, one, one],
        (sent_a, *grads[0::3], *grads[1::3], *grads[2::3], wq, wk, wv),
        specs=[pl.ANY],
    )
    from_plus = shifted(to_minus, -row_width)
    from_minus = shifted(to_plus, row_width)
    more, blocks = wide // 256, (wide + width) // 256
    own_a, own_b, *sent = call(
        functools.partial(second_kernel, 1, len(later)),
        [((rows, wide), f32), ((rows, wide + width), f32)]
        + [((blocks + (0 if k % 2 else more), rows, 256), bf16) for k in range(1, planes)],
        (place, node, kept_a, in_a, out_a, y_b, *own_b, *core_own_b),
        specs=[pltpu.SMEM, pl.ANY],
        scratch=[pltpu.VMEM((planes, rows, width), f32)],
    )
    received = [exchange(shard, k) for k, shard in enumerate(sent, 1)]
    outgoing = call(
        relay_kernel, [three, three],
        (place, sent[0], own_right, own_left, from_plus, from_minus),
        specs=[pltpu.SMEM, pl.ANY], scratch=[trio],
    )
    back = swap(outgoing, 1)
    (node_grad,) = call(
        finish_kernel, [((members, node_rows, width), bf16)],
        (place, sent[0], send_rows, node, from_plus, from_minus, *back),
        specs=[pltpu.SMEM, pl.ANY], scratch=[trio], final=True,
    )
    (weight_grad,) = call(
        weight_kernel, [((rows, 4 * width), f32)], (node_grad, own_a, own_b, *received),
        specs=[pltpu.HBM], final=True,
    )
    return (node_grad, weight_grad)


def solution(mesh):
    in_specs = (
        P("groups", "patch", None),
        P("groups", "patch", None),
        P(),
        P(),
        P(),
        P(),
        P("patch", None),
        P("patch"),
        P("patch", None, None),
    )
    out_specs = (P("groups", "patch", None), P(("groups", "patch"), None))
    return jax.shard_map(body, mesh=mesh, in_specs=in_specs, out_specs=out_specs, check_vma=False)
```

```python
import functools
import math

import jax
import jax.numpy as jnp
from jax import lax
from jax.experimental import pallas as pl
from jax.experimental.pallas import tpu as pltpu
from jax.sharding import PartitionSpec as P

HEADS = 16
score_cap = 5.0
MIB = 1024 * 1024
f32 = jnp.float32
bf16 = jnp.bfloat16


def nn(a, b):
    return lax.dot_general(a, b, (((1,), (0,)), ((), ())), preferred_element_type=f32)


def nt(a, b):
    return lax.dot_general(a, b, (((1,), (1,)), ((), ())), preferred_element_type=f32)


def shifted(shard, by):
    count = lax.axis_size("patch")
    return lax.ppermute(shard, "patch", [(i, (i + by) % count) for i in range(count)])


def neighbours_apart(count, stride):
    first, second = [], []
    for i in range(count):
        up, down = (i + stride) % count, (i - stride) % count
        even = i // stride % 2 == 0
        first.append((i, up if even else down))
        second.append((i, down if even else up))
    return first, second


def swap(pair, stride):
    first, second = neighbours_apart(lax.axis_size("patch"), stride)
    later = lax.ppermute(pair[1], "patch", second)
    return [lax.ppermute(pair[0], "patch", first), later]


def to_swaps(both, odd, first_ref, second_ref):
    first_ref[...] = both[odd]
    second_ref[...] = both[1 - odd]


def from_swaps(both, odd, first_ref, second_ref):
    both[1 - odd] = first_ref[...]
    both[odd] = second_ref[...]


def sent_selector(send_rows, node_rows):
    adjacent, slots = send_rows.shape
    halo = adjacent * slots
    wide = jnp.concatenate([send_rows] * adjacent, axis=1)
    own = lax.broadcasted_iota(jnp.int32, (adjacent, halo), 1) // slots == lax.broadcasted_iota(
        jnp.int32, (adjacent, halo), 0
    )
    ids = jnp.sum(jnp.where(own, wide, 0), axis=0, keepdims=True)
    nodes = lax.broadcasted_iota(jnp.int32, (node_rows, halo), 0)
    return jnp.where(nodes == ids, 1.0, 0.0).astype(f32)


def gather_kernel(
    slots, send_hbm, x_hbm, plus_ref, minus_ref, right_ref, left_ref, x_ref, send_ref, sem
):
    copies = [
        pltpu.make_async_copy(send_hbm, send_ref, sem.at[0]),
        pltpu.make_async_copy(x_hbm, x_ref, sem.at[1]),
    ]
    for copy in copies:
        copy.start()
    copies[0].wait()
    members, node_rows, _ = x_ref.shape
    pick = sent_selector(send_ref[0], node_rows).T.astype(bf16)
    copies[1].wait()
    for m in range(members):
        rows = nn(pick, x_ref[m]).astype(bf16)

        def part(k):
            return rows[k * slots : (k + 1) * slots]

        for ref, order in ((plus_ref, (2, 6, 4)), (minus_ref, (3, 5, 7))):
            for i, k in enumerate(order):
                ref[m, i] = part(k)
        right_ref[m, 0] = part(0)
        left_ref[m, 0] = part(1)


def relay_kernel(
    me_ref, after_ref, own_right, own_left, plus_ref, minus_ref, first_ref, second_ref, both
):
    for side, own in enumerate((own_right, own_left)):
        both[side, :, 0:1] = own[...]
        both[side, :, 1:2] = plus_ref[:, 1 + side : 2 + side]
        both[side, :, 2:3] = minus_ref[:, 1 + side : 2 + side]
    to_swaps(both, me_ref[0] % 2, first_ref, second_ref)


def gray(z):
    return z ^ (z >> 1)


def plane_of(code):
    z = code
    for shift in range(1, 8):
        z = z ^ (code >> shift)
    return z


def along_z(count, distance):
    planes = count // 4
    return [(i, plane_of(gray(i // 4) ^ distance) * 4 + i % 4) for i in range(planes * 4)]


Q, K, V, G, QT, KT, VT, GT = range(8)


def local_kernel(groups, after_ref, x_ref, *refs):
    sources, loc_refs, xt_ref = refs[:7], refs[7 : 7 + groups], refs[7 + groups]
    copied, sem = refs[8 + groups : 15 + groups], refs[-1]
    copies = [
        pltpu.make_async_copy(source, target, sem.at[i])
        for i, (source, target) in enumerate(zip(sources, copied))
    ]
    for copy in copies:
        copy.start()
    members, node_rows, width = x_ref.shape
    x = x_ref[...].reshape(members * node_rows, width)
    for m in range(members):
        xt_ref[m] = x_ref[m].T

    def put(rows, kind):
        for m in range(members):
            for g, ref in enumerate(loc_refs):
                block = rows[m * node_rows : (m + 1) * node_rows, g * 128 : (g + 1) * 128]
                ref[kind, m] = block
                ref[kind + 4, m] = block.T

    wq_ref, wk_ref, wv_ref, og_ref, _, _, wo_ref = copied
    for kind, ref in enumerate((wq_ref, wk_ref, wv_ref)):
        copies[kind].wait()
        put(nn(x, ref[...]).astype(bf16), kind)
    for copy in copies[3:]:
        copy.wait()
    og = og_ref[...].reshape(members * node_rows, width)
    put(nt(og, wo_ref[...]).astype(bf16), G)


def mask_kernel(after_ref, neigh_ref, count_ref, mask_ref):
    neigh = neigh_ref[...].T
    slots, node_rows = neigh.shape
    table = mask_ref.shape[0]
    order = lax.broadcasted_iota(jnp.int32, neigh.shape, 0)
    tail = jnp.where(order >= count_ref[...], neigh, -1)[slots // 2 :]
    half = table // 2
    for part in range(2):
        columns = lax.broadcasted_iota(jnp.int32, (half, node_rows), 0) + part * half
        kept = jnp.ones((half, node_rows), f32)
        for j in range(slots // 2):
            kept = jnp.where(tail[j : j + 1] == columns, 0.0, kept)
        mask_ref[part * half : (part + 1) * half] = kept


def halo_kernel(
    me_ref, second_in, first_in, plus_ref, minus_ref, xt_ref, wk_ref, wv_ref, *refs
):
    halo_refs, xtf_ref, both = refs[:-2], refs[-2], refs[-1]
    members, _, node_rows = xt_ref.shape
    from_swaps(both, me_ref[0] % 2, first_in, second_in)
    for m in range(members):
        pieces = [None] * 8
        for side, order in enumerate(((0, 6, 5), (1, 4, 7))):
            for i, k in enumerate(order):
                pieces[k] = both[side, m, i]
        pieces[2] = plus_ref[m, 0]
        pieces[3] = minus_ref[m, 0]
        halo = jnp.concatenate(pieces, axis=0)
        xtf_ref[m, :, :node_rows] = xt_ref[m]
        xtf_ref[m, :, node_rows:] = halo.T
        for kind, w_ref in enumerate((wk_ref, wv_ref)):
            rows = nn(halo, w_ref[...]).astype(bf16)
            for g, ref in enumerate(halo_refs):
                block = rows[:, g * 128 : (g + 1) * 128]
                ref[kind, m] = block
                ref[kind + 2, m] = block.T


def attention_kernel(extra, here, me_ref, *refs):
    refs = refs[extra:]
    locs, halos, refs = refs[:here], refs[here : 2 * here], refs[2 * here :]
    mask_ref, xtf, og_ref = refs[:3]
    split = 7 if len(refs) == 15 + 3 * (here - 1) else 6
    outs, grads, scratch = refs[3:split], refs[split : split + 3 * here], refs[split + 3 * here :]
    if split == 6:
        outs = (*outs[:2], outs[2].at[0], outs[2].at[1])
    for i in range(here):
        attend(
            me_ref, locs[i], halos[i], mask_ref, xtf, og_ref, outs, 512 * i,
            grads[3 * i : 3 * i + 3], scratch,
        )


def attend(me_ref, loc, halo, mask_ref, xtf, og_ref, out_refs, at, grad_refs, scratch):
    own_ref, other_ref, send_other, send_own = out_refs
    dq_ref, dk_ref, dv_ref = grad_refs
    score, grad, slope, dw, wos = scratch
    _, members, node_rows, _ = loc.shape
    table = mask_ref.shape[0]
    width = og_ref.shape[2]
    head = width // HEADS
    per = 128 // head
    scale = 1.0 / math.sqrt(head)

    row_head = lax.broadcasted_iota(jnp.int32, (128, node_rows), 0) // head
    lane_head = lax.broadcasted_iota(jnp.int32, (node_rows, 128), 1) // head

    def spread_t(block):
        zero = jnp.zeros_like(block)
        return jnp.concatenate([jnp.where(row_head == h, block, zero) for h in range(per)], axis=1)

    def spread_n(block):
        zero = jnp.zeros_like(block)
        return jnp.concatenate([jnp.where(lane_head == h, block, zero) for h in range(per)], axis=0)

    strip = 64
    for m in range(members):
        kg = jnp.concatenate([loc[K, m], halo[0, m]], axis=0)
        vg = jnp.concatenate([loc[V, m], halo[1, m]], axis=0)
        score[m] = nn(kg, spread_t(loc[QT, m]))
        grad[m] = nn(vg, spread_t(loc[GT, m]))

    wo_total = None
    kv_total = None
    q_total = None
    for m in range(members):
        probs = []
        for h in range(per):
            lanes = slice(h * node_rows, (h + 1) * node_rows)
            den = jnp.zeros((8, node_rows), f32)
            inner = jnp.zeros((8, node_rows), f32)
            for c in range(0, table, strip):
                box = (m, slice(c, c + strip), lanes)
                t = jnp.tanh(score[box] * (scale / score_cap))
                e = jnp.exp2(t * (score_cap / math.log(2.0))) * mask_ref[c : c + strip]
                den = den + jnp.sum(e.reshape(strip // 8, 8, node_rows), axis=0)
                inner = inner + jnp.sum((e * grad[box]).reshape(strip // 8, 8, node_rows), axis=0)
                score[box] = e
                slope[box] = e * (scale - scale * (t * t))
            r = 1.0 / jnp.sum(den, axis=0, keepdims=True)
            inner = jnp.sum(inner, axis=0, keepdims=True) * r
            column = []
            scores = []
            for c in range(0, table, strip):
                box = (m, slice(c, c + strip), lanes)
                column.append((score[box] * r).astype(bf16))
                scores.append(((slope[box] * r) * (grad[box] - inner)).astype(bf16))
            probs.append((jnp.concatenate(column, axis=0), jnp.concatenate(scores, axis=0)))
        pb = jnp.concatenate([p for p, _ in probs], axis=1)
        ds = jnp.concatenate([s for _, s in probs], axis=1)
        ktg = jnp.concatenate([loc[KT, m], halo[2, m]], axis=1)
        vtg = jnp.concatenate([loc[VT, m], halo[3, m]], axis=1)
        att, dqt = [], []
        for h in range(0, per, 2):
            lanes = slice(h * node_rows, (h + 2) * node_rows)
            rows = slice(h * head, (h + 2) * head)
            a = nn(vtg[rows], pb[:, lanes])
            b = nn(ktg[rows], ds[:, lanes])
            for j in range(2):
                inside = (slice(j * head, (j + 1) * head), slice(j * node_rows, (j + 1) * node_rows))
                att.append(a[inside].astype(bf16))
                dqt.append(b[inside].astype(bf16))
        att = jnp.concatenate(att, axis=0)
        dq = jnp.concatenate(dqt, axis=0).T
        dk = nn(ds, spread_n(loc[Q, m])).astype(bf16)
        dv = nn(pb, spread_n(loc[G, m])).astype(bf16)
        dq_ref[m], dk_ref[m], dv_ref[m] = dq, dk, dv
        wo_term = nn(att, og_ref[m])
        kv_term = nn(xtf[m], jnp.concatenate([dk, dv], axis=1))
        q_term = nn(xtf[m, :, :node_rows], dq)
        wo_total = wo_term if m == 0 else wo_total + wo_term
        kv_total = kv_term if m == 0 else kv_total + kv_term
        q_total = q_term if m == 0 else q_total + q_term

    planes, _, _, rows, _ = dw.shape
    inner_planes = wos.shape[0]
    dw[:, :, :, :, :128] = q_total.reshape(planes, 2, 2, rows, 128)
    dw[:, :, :, :, 128:] = kv_total.reshape(planes, 2, 2, rows, 256)
    wos[...] = wo_total.reshape(inner_planes, 2, 2, rows, width)
    me = me_ref[0]
    c, y, z = me % 2, (me // 2) % 2, me // 4
    qkv = slice(at, at + 384)
    for k in range(planes):
        zk = plane_of(gray(z) ^ k)
        own_ref[k, :, qkv] = dw[zk, y, c]
        other_ref[k, :, qkv] = dw[zk, 1 - y, c]
        send_other[k, :, qkv] = dw[zk, 1 - y, 1 - c].astype(bf16)
        send_own[k, :, qkv] = dw[zk, y, 1 - c].astype(bf16)
    last = slice(at + 384, at + 512)
    for i in range(inner_planes):
        for n in range(width // 128):
            k = n * inner_planes + i
            lanes = slice(n * 128, (n + 1) * 128)
            own_ref[k, :, last] = wos[i, y, c, :, lanes]
            other_ref[k, :, last] = wos[i, 1 - y, c, :, lanes]
            send_other[k, :, last] = wos[i, 1 - y, 1 - c, :, lanes].astype(bf16)
            send_own[k, :, last] = wos[i, y, 1 - c, :, lanes].astype(bf16)


def node_kernel(groups, skip, *refs):
    refs = refs[skip:]
    dqs, dks, dvs = refs[:groups], refs[groups : 2 * groups], refs[2 * groups : 3 * groups]
    wq_ref, wk_ref, wv_ref, node_ref, plus_ref, minus_ref, right_ref, left_ref = refs[3 * groups :]
    members, node_rows, _ = dqs[0].shape
    slots = plus_ref.shape[2]

    def whole(parts, m):
        return jnp.concatenate([part[m] for part in parts], axis=1)

    for m in range(members):
        spread = nt(whole(dks, m), wk_ref[...]) + nt(whole(dvs, m), wv_ref[...])
        node_ref[m] = spread[:node_rows] + nt(whole(dqs, m), wq_ref[...])
        halo = spread[node_rows:].astype(bf16)
        for ref, order in (
            (plus_ref, (3, 7, 5)),
            (minus_ref, (2, 4, 6)),
            (right_ref, (1,)),
            (left_ref, (0,)),
        ):
            for i, k in enumerate(order):
                ref[m, i] = halo[k * slots : (k + 1) * slots]


def sums(owns, core_in, y_in, k):
    total = jnp.concatenate(
        [
            own[k] + (core[1, k] if len(core.shape) == 4 else core[k]).astype(f32)
            for own, core in zip(owns, core_in)
        ],
        axis=1,
    ) + y_in[k].astype(f32)
    return [total[:, at : at + 512] for at in range(0, total.shape[1], 512)]


def gather_projection(parts, k, planes, projection_ref, start):
    inner_planes = planes * 128 // projection_ref.shape[2]
    quarter, inner = divmod(k, inner_planes)
    for i, part in enumerate(parts):
        plane = start + i * inner_planes + inner
        projection_ref[plane, :, quarter * 128 : (quarter + 1) * 128] = part[:, 384:]


def pack_kernel(pieces, *refs):
    for i, (ref, core) in enumerate(zip(refs[:pieces], refs[pieces:-1])):
        arrived = core[0] if len(core.shape) == 4 else core[...]
        refs[-1][:, :, i * 512 : (i + 1) * 512] = (ref[...] + arrived.astype(f32)).astype(bf16)


def halve(rows, kept_ref, sent_ref):
    for i, row in enumerate(rows):
        if i % 2 == 0:
            kept_ref[i // 2] = row
            continue
        pieces = row.shape[1] // 256
        for n in range(pieces):
            sent_ref[i // 2 * pieces + n] = row[:, n * 256 : (n + 1) * 256].astype(bf16)


def add_received(kept_ref, received_ref):
    planes, _, wide = kept_ref.shape
    pieces = wide // 256
    return [
        kept_ref[i]
        + jnp.concatenate([received_ref[i * pieces + n] for n in range(pieces)], axis=1).astype(f32)
        for i in range(planes)
    ]


def first_kernel(after_ref, own, core_in, y_in, kept_ref, projection_ref, sent_ref):
    planes = own.shape[0]
    rows = []
    for k in range(planes):
        parts = sums([own], [core_in], y_in, k)
        gather_projection(parts, k, planes, projection_ref, 0)
        rows.append(jnp.concatenate([part[:, :384] for part in parts], axis=1))
    halve(rows, kept_ref, sent_ref)


def put(row, ref, at):
    for n in range(row.shape[1] // 256):
        ref[at + n] = row[:, n * 256 : (n + 1) * 256].astype(bf16)


def second_kernel(skip, pieces, me_ref, *refs):
    refs = refs[skip:]
    kept_a, in_a, first_ref, y_in = refs[:4]
    owns, core_in = refs[4 : 4 + pieces], refs[4 + pieces : 4 + 2 * pieces]
    own_a, own_b, *sent = refs[4 + 2 * pieces : -1]
    projection_ref = refs[-1]
    done = first_ref.shape[0]
    planes = projection_ref.shape[0]
    projection_ref[:done] = first_ref[...]
    held = []
    for k in range(planes):
        parts = sums(owns, core_in, y_in, k)
        gather_projection(parts, k, planes, projection_ref, done)
        held.append(jnp.concatenate([part[:, :384] for part in parts], axis=1))
    first = add_received(kept_a, in_a)
    own_a[...] = first[0]
    z = me_ref[0] // 4
    for k in range(planes):
        row = jnp.concatenate([held[k], projection_ref[plane_of(gray(z) ^ k)]], axis=1)
        if k == 0:
            own_b[...] = row
            continue
        put(row, sent[k - 1], 0)
        if k % 2 == 0:
            put(first[k // 2], sent[k - 1], row.shape[1] // 256)


def finish_kernel(
    me_ref, after_ref, second_in, first_in, send_ref, node_ref, plus_ref, minus_ref, out_ref, came
):
    members, node_rows, _ = node_ref.shape
    pick = sent_selector(send_ref[0], node_rows).astype(bf16)
    from_swaps(came, me_ref[0] % 2, first_in, second_in)
    for m in range(members):
        pieces = [None] * 8
        for side, order in enumerate(((1, 4, 7), (0, 6, 5))):
            for i, k in enumerate(order):
                pieces[k] = came[side, m, i]
        pieces[2], pieces[3] = plus_ref[m, 0], minus_ref[m, 0]
        arriving = jnp.concatenate(pieces, axis=0)
        out_ref[m] = (node_ref[m] + nn(pick, arriving)).astype(bf16)


def weight_kernel(after_ref, own_a, own_b, *refs):
    received, out_ref = refs[:-1], refs[-1]
    a, b = own_a[...], own_b[...]
    blocks, more = b.shape[1] // 256, a.shape[1] // 256
    for k, ref in enumerate(received, 1):
        b = b + jnp.concatenate([ref[n] for n in range(blocks)], axis=1).astype(f32)
        if k % 2 == 0:
            a = a + jnp.concatenate([ref[blocks + n] for n in range(more)], axis=1).astype(f32)
    half = a.shape[1] // 384
    width = 256 * half
    for i, part in enumerate((a, b)):
        for j in range(half):
            for n in range(3):
                at = n * width + (i * half + j) * 128
                out_ref[:, at : at + 128] = part[:, j * 384 + n * 128 : j * 384 + (n + 1) * 128]
    out_ref[:, 3 * width :] = b[:, 384 * half :]


def call(kernel, outs, operands, specs=None, scratch=(), limit=12, final=False, flops=10**6):
    specs = list(specs or ())
    specs += [pltpu.VMEM] * (len(operands) - len(specs))
    operands = [
        pltpu.with_memory_space_constraint(o, s) if s in (pltpu.HBM, pltpu.VMEM) else o
        for o, s in zip(operands, specs)
    ]
    return pl.pallas_call(
        kernel,
        out_shape=[jax.ShapeDtypeStruct(*o) if final else pltpu.VMEM(*o) for o in outs],
        in_specs=[pl.BlockSpec(memory_space=s) for s in specs],
        scratch_shapes=list(scratch),
        compiler_params=pltpu.CompilerParams(vmem_limit_bytes=limit * MIB),
        cost_estimate=pl.CostEstimate(flops=flops, bytes_accessed=10**4, transcendentals=0),
    )(*operands)


def body(
    node_features, out_grad, w_query, w_key, w_value, w_out, neighbours, neighbour_count, send_rows
):
    members, node_rows, width = node_features.shape
    count = lax.axis_size("patch")
    row_width = min(8, count // 4)
    _, adjacent, slots = send_rows.shape
    table = node_rows + adjacent * slots
    groups = width // 128
    me = lax.axis_index("patch")
    three = ((members, 3, slots, width), bf16)
    one = ((members, 1, slots, width), bf16)

    place = me.reshape(1)
    trio = pltpu.VMEM((2, *three[0]), bf16)
    to_plus, to_minus, own_right, own_left, x = call(
        functools.partial(gather_kernel, slots),
        [three, three, one, one, (node_features.shape, bf16)],
        (send_rows, node_features),
        specs=[pltpu.HBM] * 2,
        scratch=[pltpu.VMEM(send_rows.shape, jnp.int32), pltpu.SemaphoreType.DMA((2,))],
    )
    plus = shifted(to_plus, row_width)
    minus = shifted(to_minus, -row_width)
    square = ((width, width), bf16)
    counts = neighbour_count.reshape(1, node_rows)
    *loc, xt, wq, wk, wv, og, neigh, counts = call(
        functools.partial(local_kernel, groups),
        [((8, members, node_rows, 128), bf16)] * groups
        + [((members, width, node_rows), bf16), square, square, square, (out_grad.shape, bf16)]
        + [(neighbours.shape, jnp.int32), (counts.shape, jnp.int32)],
        (own_right, x, w_query, w_key, w_value, out_grad, neighbours, counts, w_out),
        specs=[pl.ANY, pltpu.VMEM] + [pltpu.HBM] * 7,
        scratch=[pltpu.VMEM((width, width), bf16), pltpu.SemaphoreType.DMA((7,))],
        limit=16,
    )
    outgoing = call(
        relay_kernel, [three, three], (place, loc[0], own_right, own_left, plus, minus),
        specs=[pltpu.SMEM, pl.ANY], scratch=[trio],
    )
    arrived = swap(outgoing, 1)
    (mask,) = call(
        mask_kernel, [((table, node_rows), f32)], (outgoing[1], neigh, counts), specs=[pl.ANY]
    )
    *halo, xtf = call(
        halo_kernel,
        [((4, members, node_rows, 128), bf16)] * groups + [((members, width, table), bf16)],
        (place, *arrived[::-1], plus, minus, xt, wk, wv), specs=[pltpu.SMEM], scratch=[trio],
    )

    planes, rows = count // 4, width // count
    inner_planes = planes * 128 // width
    flip = [(i, i ^ 1) for i in range(count)]
    flop = [(i, i ^ 2) for i in range(count)]
    grads = []

    def attention(extra, which, together):
        wide = 512 * len(which)
        sends = [((2, planes, rows, wide), bf16)] if together else [((planes, rows, wide), bf16)] * 2
        outs = call(
            functools.partial(attention_kernel, len(extra), len(which)),
            [((planes, rows, wide), f32)] * 2
            + sends
            + [
                ((members, node_rows, 128), bf16),
                ((members, table, 128), bf16),
                ((members, table, 128), bf16),
            ]
            * len(which),
            (
                place, *extra, *[loc[g] for g in which], *[halo[g] for g in which], mask, xtf, og,
            ),
            specs=[pltpu.SMEM] + [pl.ANY] * len(extra),
            scratch=[pltpu.VMEM((members, table, 512), f32)] * 3
            + [
                pltpu.VMEM((planes, 2, 2, rows, 384), f32),
                pltpu.VMEM((inner_planes, 2, 2, rows, width), f32),
            ],
            limit=24,
        )
        sent = outs[2 : 2 + len(sends)]
        grads.extend(outs[2 + len(sends) :])
        arrived = [lax.ppermute(shard, "patch", flip) for shard in sent]
        return outs[0], outs[1], arrived[0], arrived[-1]

    half = groups // 2
    wide = 384 * half
    own_a, other, core_other, core_own = attention((), range(half), False)
    y_sent = (other + core_other.astype(f32)).astype(bf16)
    y_a = lax.ppermute(y_sent, "patch", flop)
    later = []
    for g in range(half, groups):
        last = g == groups - 1
        later.append(attention((y_sent,) if last else (), range(g, g + 1), not last))
    own_b, other_b, core_other_b, core_own_b = zip(*later)
    (y_sent,) = call(
        functools.partial(pack_kernel, len(later)), [(y_sent.shape, bf16)],
        (*other_b, *core_other_b),
    )
    y_b = lax.ppermute(y_sent, "patch", flop)
    node, to_plus, to_minus, own_right, own_left = call(
        functools.partial(node_kernel, groups, 1),
        [((members, node_rows, width), f32), three, three, one, one],
        (y_sent, *grads[0::3], *grads[1::3], *grads[2::3], wq, wk, wv),
        specs=[pl.ANY],
    )
    from_plus = shifted(to_minus, -row_width)
    from_minus = shifted(to_plus, row_width)
    def exchange(sent, distance):
        return lax.ppermute(sent, "patch", along_z(count, distance))

    kept_a, out_a, sent_a = call(
        first_kernel,
        [
            ((planes // 2, rows, wide), f32),
            ((half * inner_planes, rows, width), f32),
            ((planes // 2 * wide // 256, rows, 256), bf16),
        ],
        (y_sent, own_a, core_own, y_a), specs=[pl.ANY], flops=2 * 10**10,
    )
    in_a = exchange(sent_a, 1)
    outgoing = call(
        relay_kernel, [three, three],
        (place, sent_a, own_right, own_left, from_plus, from_minus),
        specs=[pltpu.SMEM, pl.ANY], scratch=[trio],
    )
    back = swap(outgoing, 1)
    more, blocks = wide // 256, (wide + width) // 256
    own_a, own_b, *sent = call(
        functools.partial(second_kernel, 1, len(later)),
        [((rows, wide), f32), ((rows, wide + width), f32)]
        + [((blocks + (0 if k % 2 else more), rows, 256), bf16) for k in range(1, planes)],
        (place, outgoing[0], kept_a, in_a, out_a, y_b, *own_b, *core_own_b),
        specs=[pltpu.SMEM, pl.ANY],
        scratch=[pltpu.VMEM((planes, rows, width), f32)],
    )
    received = [exchange(shard, k) for k, shard in enumerate(sent, 1)]
    (node_grad,) = call(
        finish_kernel, [((members, node_rows, width), bf16)],
        (place, sent[0], *back[::-1], send_rows, node, from_plus, from_minus),
        specs=[pltpu.SMEM, pl.ANY], scratch=[trio], final=True,
    )
    (weight_grad,) = call(
        weight_kernel, [((rows, 4 * width), f32)], (node_grad, own_a, own_b, *received),
        specs=[pltpu.HBM], final=True,
    )
    return (node_grad, weight_grad)


def solution(mesh):
    in_specs = (
        P("groups", "patch", None),
        P("groups", "patch", None),
        P(),
        P(),
        P(),
        P(),
        P("patch", None),
        P("patch"),
        P("patch", None, None),
    )
    out_specs = (P("groups", "patch", None), P(("groups", "patch"), None))
    return jax.shard_map(body, mesh=mesh, in_specs=in_specs, out_specs=out_specs, check_vma=False)
```

```python
import functools
import math

import jax
import jax.numpy as jnp
from jax import lax
from jax.experimental import pallas as pl
from jax.experimental.pallas import tpu as pltpu
from jax.sharding import PartitionSpec as P

HEADS = 16
score_cap = 5.0
MIB = 1024 * 1024
f32 = jnp.float32
bf16 = jnp.bfloat16


def nn(a, b):
    return lax.dot_general(a, b, (((1,), (0,)), ((), ())), preferred_element_type=f32)


def nt(a, b):
    return lax.dot_general(a, b, (((1,), (1,)), ((), ())), preferred_element_type=f32)


def shifted(shard, by):
    count = lax.axis_size("patch")
    return lax.ppermute(shard, "patch", [(i, (i + by) % count) for i in range(count)])


def neighbours_apart(count, stride):
    first, second = [], []
    for i in range(count):
        up, down = (i + stride) % count, (i - stride) % count
        even = i // stride % 2 == 0
        first.append((i, up if even else down))
        second.append((i, down if even else up))
    return first, second


def swap(pair, stride):
    first, second = neighbours_apart(lax.axis_size("patch"), stride)
    later = lax.ppermute(pair[1], "patch", second)
    return [lax.ppermute(pair[0], "patch", first), later]


def to_swaps(both, odd, first_ref, second_ref):
    first_ref[...] = both[odd]
    second_ref[...] = both[1 - odd]


def from_swaps(both, odd, first_ref, second_ref):
    both[1 - odd] = first_ref[...]
    both[odd] = second_ref[...]


def sent_selector(send_rows, node_rows):
    adjacent, slots = send_rows.shape
    halo = adjacent * slots
    wide = jnp.concatenate([send_rows] * adjacent, axis=1)
    own = lax.broadcasted_iota(jnp.int32, (adjacent, halo), 1) // slots == lax.broadcasted_iota(
        jnp.int32, (adjacent, halo), 0
    )
    ids = jnp.sum(jnp.where(own, wide, 0), axis=0, keepdims=True)
    nodes = lax.broadcasted_iota(jnp.int32, (node_rows, halo), 0)
    return jnp.where(nodes == ids, 1.0, 0.0).astype(f32)


def gather_kernel(
    slots, send_hbm, x_hbm, plus_ref, minus_ref, right_ref, left_ref, x_ref, send_ref, sem
):
    copies = [
        pltpu.make_async_copy(send_hbm, send_ref, sem.at[0]),
        pltpu.make_async_copy(x_hbm, x_ref, sem.at[1]),
    ]
    for copy in copies:
        copy.start()
    copies[0].wait()
    members, node_rows, _ = x_ref.shape
    pick = sent_selector(send_ref[0], node_rows).T.astype(bf16)
    copies[1].wait()
    for m in range(members):
        rows = nn(pick, x_ref[m]).astype(bf16)

        def part(k):
            return rows[k * slots : (k + 1) * slots]

        for ref, order in ((plus_ref, (2, 6, 4)), (minus_ref, (3, 5, 7))):
            for i, k in enumerate(order):
                ref[m, i] = part(k)
        right_ref[m, 0] = part(0)
        left_ref[m, 0] = part(1)


def relay_kernel(
    me_ref, after_ref, own_right, own_left, plus_ref, minus_ref, first_ref, second_ref, both
):
    for side, own in enumerate((own_right, own_left)):
        both[side, :, 0:1] = own[...]
        both[side, :, 1:2] = plus_ref[:, 1 + side : 2 + side]
        both[side, :, 2:3] = minus_ref[:, 1 + side : 2 + side]
    to_swaps(both, me_ref[0] % 2, first_ref, second_ref)


def gray(z):
    return z ^ (z >> 1)


def plane_of(code):
    z = code
    for shift in range(1, 8):
        z = z ^ (code >> shift)
    return z


def along_z(count, distance):
    planes = count // 4
    return [(i, plane_of(gray(i // 4) ^ distance) * 4 + i % 4) for i in range(planes * 4)]


Q, K, V, G, QT, KT, VT, GT = range(8)


def local_kernel(groups, after_ref, x_ref, *refs):
    sources, loc_refs, xt_ref = refs[:7], refs[7 : 7 + groups], refs[7 + groups]
    copied, sem = refs[8 + groups : 15 + groups], refs[-1]
    copies = [
        pltpu.make_async_copy(source, target, sem.at[i])
        for i, (source, target) in enumerate(zip(sources, copied))
    ]
    for copy in copies:
        copy.start()
    members, node_rows, width = x_ref.shape
    x = x_ref[...].reshape(members * node_rows, width)
    for m in range(members):
        xt_ref[m] = x_ref[m].T

    def put(rows, kind):
        for m in range(members):
            for g, ref in enumerate(loc_refs):
                block = rows[m * node_rows : (m + 1) * node_rows, g * 128 : (g + 1) * 128]
                ref[kind, m] = block
                ref[kind + 4, m] = block.T

    wq_ref, wk_ref, wv_ref, og_ref, _, _, wo_ref = copied
    for kind, ref in enumerate((wq_ref, wk_ref, wv_ref)):
        copies[kind].wait()
        put(nn(x, ref[...]).astype(bf16), kind)
    for copy in copies[3:]:
        copy.wait()
    og = og_ref[...].reshape(members * node_rows, width)
    put(nt(og, wo_ref[...]).astype(bf16), G)


def mask_kernel(after_ref, neigh_ref, count_ref, mask_ref):
    neigh = neigh_ref[...].T
    slots, node_rows = neigh.shape
    table = mask_ref.shape[0]
    order = lax.broadcasted_iota(jnp.int32, neigh.shape, 0)
    tail = jnp.where(order >= count_ref[...], neigh, -1)[slots // 2 :]
    half = table // 2
    for part in range(2):
        columns = lax.broadcasted_iota(jnp.int32, (half, node_rows), 0) + part * half
        kept = jnp.ones((half, node_rows), f32)
        for j in range(slots // 2):
            kept = jnp.where(tail[j : j + 1] == columns, 0.0, kept)
        mask_ref[part * half : (part + 1) * half] = kept


def halo_kernel(
    me_ref, second_in, first_in, plus_ref, minus_ref, xt_ref, wk_ref, wv_ref, *refs
):
    halo_refs, xtf_ref, both = refs[:-2], refs[-2], refs[-1]
    members, _, node_rows = xt_ref.shape
    from_swaps(both, me_ref[0] % 2, first_in, second_in)
    for m in range(members):
        pieces = [None] * 8
        for side, order in enumerate(((0, 6, 5), (1, 4, 7))):
            for i, k in enumerate(order):
                pieces[k] = both[side, m, i]
        pieces[2] = plus_ref[m, 0]
        pieces[3] = minus_ref[m, 0]
        halo = jnp.concatenate(pieces, axis=0)
        xtf_ref[m, :, :node_rows] = xt_ref[m]
        xtf_ref[m, :, node_rows:] = halo.T
        for kind, w_ref in enumerate((wk_ref, wv_ref)):
            rows = nn(halo, w_ref[...]).astype(bf16)
            for g, ref in enumerate(halo_refs):
                block = rows[:, g * 128 : (g + 1) * 128]
                ref[kind, m] = block
                ref[kind + 2, m] = block.T


def attention_kernel(extra, here, me_ref, *refs):
    refs = refs[extra:]
    locs, halos, refs = refs[:here], refs[here : 2 * here], refs[2 * here :]
    mask_ref, xtf, og_ref = refs[:3]
    split = 7 if len(refs) == 15 + 3 * (here - 1) else 6
    outs, grads, scratch = refs[3:split], refs[split : split + 3 * here], refs[split + 3 * here :]
    if split == 6:
        outs = (*outs[:2], outs[2].at[0], outs[2].at[1])
    for i in range(here):
        attend(
            me_ref, locs[i], halos[i], mask_ref, xtf, og_ref, outs, 512 * i,
            grads[3 * i : 3 * i + 3], scratch,
        )


def attend(me_ref, loc, halo, mask_ref, xtf, og_ref, out_refs, at, grad_refs, scratch):
    own_ref, other_ref, send_other, send_own = out_refs
    dq_ref, dk_ref, dv_ref = grad_refs
    score, grad, slope, dw, wos = scratch
    _, members, node_rows, _ = loc.shape
    table = mask_ref.shape[0]
    width = og_ref.shape[2]
    head = width // HEADS
    per = 128 // head
    scale = 1.0 / math.sqrt(head)

    row_head = lax.broadcasted_iota(jnp.int32, (128, node_rows), 0) // head
    lane_head = lax.broadcasted_iota(jnp.int32, (node_rows, 128), 1) // head

    def spread_t(block):
        zero = jnp.zeros_like(block)
        return jnp.concatenate([jnp.where(row_head == h, block, zero) for h in range(per)], axis=1)

    def spread_n(block):
        zero = jnp.zeros_like(block)
        return jnp.concatenate([jnp.where(lane_head == h, block, zero) for h in range(per)], axis=0)

    strip = 64
    for m in range(members):
        kg = jnp.concatenate([loc[K, m], halo[0, m]], axis=0)
        vg = jnp.concatenate([loc[V, m], halo[1, m]], axis=0)
        score[m] = nn(kg, spread_t(loc[QT, m]))
        grad[m] = nn(vg, spread_t(loc[GT, m]))

    wo_total = None
    kv_total = None
    q_total = None
    for m in range(members):
        probs = []
        for h in range(per):
            lanes = slice(h * node_rows, (h + 1) * node_rows)
            den = jnp.zeros((8, node_rows), f32)
            inner = jnp.zeros((8, node_rows), f32)
            for c in range(0, table, strip):
                box = (m, slice(c, c + strip), lanes)
                t = jnp.tanh(score[box] * (scale / score_cap))
                e = jnp.exp2(t * (score_cap / math.log(2.0))) * mask_ref[c : c + strip]
                den = den + jnp.sum(e.reshape(strip // 8, 8, node_rows), axis=0)
                inner = inner + jnp.sum((e * grad[box]).reshape(strip // 8, 8, node_rows), axis=0)
                score[box] = e
                slope[box] = e * (scale - scale * (t * t))
            r = 1.0 / jnp.sum(den, axis=0, keepdims=True)
            inner = jnp.sum(inner, axis=0, keepdims=True) * r
            column = []
            scores = []
            for c in range(0, table, strip):
                box = (m, slice(c, c + strip), lanes)
                column.append((score[box] * r).astype(bf16))
                scores.append(((slope[box] * r) * (grad[box] - inner)).astype(bf16))
            probs.append((jnp.concatenate(column, axis=0), jnp.concatenate(scores, axis=0)))
        pb = jnp.concatenate([p for p, _ in probs], axis=1)
        ds = jnp.concatenate([s for _, s in probs], axis=1)
        ktg = jnp.concatenate([loc[KT, m], halo[2, m]], axis=1)
        vtg = jnp.concatenate([loc[VT, m], halo[3, m]], axis=1)
        att, dqt = [], []
        for h in range(0, per, 2):
            lanes = slice(h * node_rows, (h + 2) * node_rows)
            rows = slice(h * head, (h + 2) * head)
            a = nn(vtg[rows], pb[:, lanes])
            b = nn(ktg[rows], ds[:, lanes])
            for j in range(2):
                inside = (slice(j * head, (j + 1) * head), slice(j * node_rows, (j + 1) * node_rows))
                att.append(a[inside].astype(bf16))
                dqt.append(b[inside].astype(bf16))
        att = jnp.concatenate(att, axis=0)
        dq = jnp.concatenate(dqt, axis=0).T
        dk = nn(ds, spread_n(loc[Q, m])).astype(bf16)
        dv = nn(pb, spread_n(loc[G, m])).astype(bf16)
        dq_ref[m], dk_ref[m], dv_ref[m] = dq, dk, dv
        wo_term = nn(att, og_ref[m])
        kv_term = nn(xtf[m], jnp.concatenate([dk, dv], axis=1))
        q_term = nn(xtf[m, :, :node_rows], dq)
        wo_total = wo_term if m == 0 else wo_total + wo_term
        kv_total = kv_term if m == 0 else kv_total + kv_term
        q_total = q_term if m == 0 else q_total + q_term

    planes, _, _, rows, _ = dw.shape
    inner_planes = wos.shape[0]
    dw[:, :, :, :, :128] = q_total.reshape(planes, 2, 2, rows, 128)
    dw[:, :, :, :, 128:] = kv_total.reshape(planes, 2, 2, rows, 256)
    wos[...] = wo_total.reshape(inner_planes, 2, 2, rows, width)
    me = me_ref[0]
    c, y, z = me % 2, (me // 2) % 2, me // 4
    qkv = slice(at, at + 384)
    for k in range(planes):
        zk = plane_of(gray(z) ^ k)
        own_ref[k, :, qkv] = dw[zk, y, c]
        other_ref[k, :, qkv] = dw[zk, 1 - y, c]
        send_other[k, :, qkv] = dw[zk, 1 - y, 1 - c].astype(bf16)
        send_own[k, :, qkv] = dw[zk, y, 1 - c].astype(bf16)
    last = slice(at + 384, at + 512)
    for i in range(inner_planes):
        for n in range(width // 128):
            k = n * inner_planes + i
            lanes = slice(n * 128, (n + 1) * 128)
            own_ref[k, :, last] = wos[i, y, c, :, lanes]
            other_ref[k, :, last] = wos[i, 1 - y, c, :, lanes]
            send_other[k, :, last] = wos[i, 1 - y, 1 - c, :, lanes].astype(bf16)
            send_own[k, :, last] = wos[i, y, 1 - c, :, lanes].astype(bf16)


def node_kernel(groups, skip, *refs):
    refs = refs[skip:]
    dqs, dks, dvs = refs[:groups], refs[groups : 2 * groups], refs[2 * groups : 3 * groups]
    wq_ref, wk_ref, wv_ref, node_ref, plus_ref, minus_ref, right_ref, left_ref = refs[3 * groups :]
    members, node_rows, _ = dqs[0].shape
    slots = plus_ref.shape[2]

    def whole(parts, m):
        return jnp.concatenate([part[m] for part in parts], axis=1)

    for m in range(members):
        spread = nt(whole(dks, m), wk_ref[...]) + nt(whole(dvs, m), wv_ref[...])
        node_ref[m] = spread[:node_rows] + nt(whole(dqs, m), wq_ref[...])
        halo = spread[node_rows:].astype(bf16)
        for ref, order in (
            (plus_ref, (3, 7, 5)),
            (minus_ref, (2, 4, 6)),
            (right_ref, (1,)),
            (left_ref, (0,)),
        ):
            for i, k in enumerate(order):
                ref[m, i] = halo[k * slots : (k + 1) * slots]


def sums(owns, core_in, y_in, k):
    total = jnp.concatenate(
        [
            own[k] + (core[1, k] if len(core.shape) == 4 else core[k]).astype(f32)
            for own, core in zip(owns, core_in)
        ],
        axis=1,
    ) + y_in[k].astype(f32)
    return [total[:, at : at + 512] for at in range(0, total.shape[1], 512)]


def gather_projection(parts, k, planes, projection_ref, start):
    inner_planes = planes * 128 // projection_ref.shape[2]
    quarter, inner = divmod(k, inner_planes)
    for i, part in enumerate(parts):
        plane = start + i * inner_planes + inner
        projection_ref[plane, :, quarter * 128 : (quarter + 1) * 128] = part[:, 384:]


def pack_kernel(pieces, *refs):
    for i, (ref, core) in enumerate(zip(refs[:pieces], refs[pieces:-1])):
        arrived = core[0] if len(core.shape) == 4 else core[...]
        refs[-1][:, :, i * 512 : (i + 1) * 512] = (ref[...] + arrived.astype(f32)).astype(bf16)


def halve(rows, kept_ref, sent_ref):
    for i, row in enumerate(rows):
        if i % 2 == 0:
            kept_ref[i // 2] = row
            continue
        pieces = row.shape[1] // 128
        for n in range(pieces):
            sent_ref[i // 2 * pieces + n] = row[:, n * 128 : (n + 1) * 128].astype(bf16)


def add_received(kept_ref, received_ref):
    planes, _, wide = kept_ref.shape
    pieces = wide // 128
    return [
        kept_ref[i]
        + jnp.concatenate([received_ref[i * pieces + n] for n in range(pieces)], axis=1).astype(f32)
        for i in range(planes)
    ]


def first_kernel(after_ref, own, core_in, y_in, kept_ref, projection_ref, sent_ref):
    planes = own.shape[0]
    rows = []
    for k in range(planes):
        parts = sums([own], [core_in], y_in, k)
        gather_projection(parts, k, planes, projection_ref, 0)
        rows.append(jnp.concatenate([part[:, :384] for part in parts], axis=1))
    halve(rows, kept_ref, sent_ref)


def put(row, ref, at):
    for n in range(row.shape[1] // 128):
        ref[at + n] = row[:, n * 128 : (n + 1) * 128].astype(bf16)


def second_kernel(skip, pieces, me_ref, *refs):
    refs = refs[skip:]
    first_ref, y_in = refs[:2]
    owns, core_in = refs[2 : 2 + pieces], refs[2 + pieces : 2 + 2 * pieces]
    own_b, *sent = refs[2 + 2 * pieces : -1]
    projection_ref = refs[-1]
    done = first_ref.shape[0]
    planes = projection_ref.shape[0]
    projection_ref[:done] = first_ref[...]
    held = []
    for k in range(planes):
        parts = sums(owns, core_in, y_in, k)
        gather_projection(parts, k, planes, projection_ref, done)
        held.append(jnp.concatenate([part[:, :384] for part in parts], axis=1))
    z = me_ref[0] // 4
    for k in range(planes):
        row = jnp.concatenate([held[k], projection_ref[plane_of(gray(z) ^ k)]], axis=1)
        if k:
            put(row, sent[k - 1], 0)
        else:
            own_b[...] = row


def join_kernel(kept_a, in_a, *refs):
    count = (len(refs) - 1) // 2
    blocks, own_a, sent = refs[:count], refs[count], refs[count + 1 :]
    first = add_received(kept_a, in_a)
    own_a[...] = first[0]
    for i, ref in enumerate(sent):
        ref[: blocks[i].shape[0]] = blocks[i][...]
        put(first[i + 1], ref, blocks[i].shape[0])


def finish_kernel(
    me_ref, after_ref, second_in, first_in, send_ref, node_ref, plus_ref, minus_ref, out_ref, came
):
    members, node_rows, _ = node_ref.shape
    pick = sent_selector(send_ref[0], node_rows).astype(bf16)
    from_swaps(came, me_ref[0] % 2, first_in, second_in)
    for m in range(members):
        pieces = [None] * 8
        for side, order in enumerate(((1, 4, 7), (0, 6, 5))):
            for i, k in enumerate(order):
                pieces[k] = came[side, m, i]
        pieces[2], pieces[3] = plus_ref[m, 0], minus_ref[m, 0]
        arriving = jnp.concatenate(pieces, axis=0)
        out_ref[m] = (node_ref[m] + nn(pick, arriving)).astype(bf16)


def weight_kernel(after_ref, own_a, own_b, *refs):
    received, out_ref = refs[:-1], refs[-1]
    a, b = own_a[...], own_b[...]
    blocks, more = b.shape[1] // 128, a.shape[1] // 128
    for k, ref in enumerate(received, 1):
        b = b + jnp.concatenate([ref[n] for n in range(blocks)], axis=1).astype(f32)
        if k % 2 == 0:
            a = a + jnp.concatenate([ref[blocks + n] for n in range(more)], axis=1).astype(f32)
    width = out_ref.shape[1] // 4
    group = 0
    for part, wide in ((a, a.shape[1]), (b, b.shape[1] - width)):
        for j in range(0, wide, 384):
            for n in range(3):
                at = n * width + group * 128
                out_ref[:, at : at + 128] = part[:, j + n * 128 : j + (n + 1) * 128]
            group += 1
    out_ref[:, 3 * width :] = b[:, b.shape[1] - width :]


def call(kernel, outs, operands, specs=None, scratch=(), limit=12, final=False, flops=10**6):
    specs = list(specs or ())
    specs += [pltpu.VMEM] * (len(operands) - len(specs))
    operands = [
        pltpu.with_memory_space_constraint(o, s) if s in (pltpu.HBM, pltpu.VMEM) else o
        for o, s in zip(operands, specs)
    ]
    return pl.pallas_call(
        kernel,
        out_shape=[jax.ShapeDtypeStruct(*o) if final else pltpu.VMEM(*o) for o in outs],
        in_specs=[pl.BlockSpec(memory_space=s) for s in specs],
        scratch_shapes=list(scratch),
        compiler_params=pltpu.CompilerParams(vmem_limit_bytes=limit * MIB),
        cost_estimate=pl.CostEstimate(flops=flops, bytes_accessed=10**4, transcendentals=0),
    )(*operands)


def body(
    node_features, out_grad, w_query, w_key, w_value, w_out, neighbours, neighbour_count, send_rows
):
    members, node_rows, width = node_features.shape
    count = lax.axis_size("patch")
    row_width = min(8, count // 4)
    _, adjacent, slots = send_rows.shape
    table = node_rows + adjacent * slots
    groups = width // 128
    me = lax.axis_index("patch")
    three = ((members, 3, slots, width), bf16)
    one = ((members, 1, slots, width), bf16)

    place = me.reshape(1)
    trio = pltpu.VMEM((2, *three[0]), bf16)
    to_plus, to_minus, own_right, own_left, x = call(
        functools.partial(gather_kernel, slots),
        [three, three, one, one, (node_features.shape, bf16)],
        (send_rows, node_features),
        specs=[pltpu.HBM] * 2,
        scratch=[pltpu.VMEM(send_rows.shape, jnp.int32), pltpu.SemaphoreType.DMA((2,))],
    )
    plus = shifted(to_plus, row_width)
    minus = shifted(to_minus, -row_width)
    square = ((width, width), bf16)
    counts = neighbour_count.reshape(1, node_rows)
    *loc, xt, wq, wk, wv, og, neigh, counts = call(
        functools.partial(local_kernel, groups),
        [((8, members, node_rows, 128), bf16)] * groups
        + [((members, width, node_rows), bf16), square, square, square, (out_grad.shape, bf16)]
        + [(neighbours.shape, jnp.int32), (counts.shape, jnp.int32)],
        (own_right, x, w_query, w_key, w_value, out_grad, neighbours, counts, w_out),
        specs=[pl.ANY, pltpu.VMEM] + [pltpu.HBM] * 7,
        scratch=[pltpu.VMEM((width, width), bf16), pltpu.SemaphoreType.DMA((7,))],
        limit=16,
    )
    outgoing = call(
        relay_kernel, [three, three], (place, loc[0], own_right, own_left, plus, minus),
        specs=[pltpu.SMEM, pl.ANY], scratch=[trio],
    )
    arrived = swap(outgoing, 1)
    (mask,) = call(
        mask_kernel, [((table, node_rows), f32)], (outgoing[1], neigh, counts), specs=[pl.ANY]
    )
    *halo, xtf = call(
        halo_kernel,
        [((4, members, node_rows, 128), bf16)] * groups + [((members, width, table), bf16)],
        (place, *arrived[::-1], plus, minus, xt, wk, wv), specs=[pltpu.SMEM], scratch=[trio],
    )

    planes, rows = count // 4, width // count
    inner_planes = planes * 128 // width
    flip = [(i, i ^ 1) for i in range(count)]
    flop = [(i, i ^ 2) for i in range(count)]
    grads = []

    def attention(extra, which, together):
        wide = 512 * len(which)
        sends = [((2, planes, rows, wide), bf16)] if together else [((planes, rows, wide), bf16)] * 2
        outs = call(
            functools.partial(attention_kernel, len(extra), len(which)),
            [((planes, rows, wide), f32)] * 2
            + sends
            + [
                ((members, node_rows, 128), bf16),
                ((members, table, 128), bf16),
                ((members, table, 128), bf16),
            ]
            * len(which),
            (
                place, *extra, *[loc[g] for g in which], *[halo[g] for g in which], mask, xtf, og,
            ),
            specs=[pltpu.SMEM] + [pl.ANY] * len(extra),
            scratch=[pltpu.VMEM((members, table, 512), f32)] * 3
            + [
                pltpu.VMEM((planes, 2, 2, rows, 384), f32),
                pltpu.VMEM((inner_planes, 2, 2, rows, width), f32),
            ],
            limit=32,
        )
        sent = outs[2 : 2 + len(sends)]
        grads.extend(outs[2 + len(sends) :])
        arrived = [lax.ppermute(shard, "patch", flip) for shard in sent]
        return outs[0], outs[1], arrived[0], arrived[-1]

    half = groups - 1
    wide = 384 * half
    own_a, other, core_other, core_own = attention((), range(half), False)
    y_sent = (other + core_other.astype(f32)).astype(bf16)
    y_a = lax.ppermute(y_sent, "patch", flop)
    later = [attention((), range(half, groups), False)]
    own_b, other_b, core_other_b, core_own_b = zip(*later)
    (y_sent,) = call(
        functools.partial(pack_kernel, len(later)), [(other_b[0].shape, bf16)],
        (*other_b, *core_other_b),
    )
    y_b = lax.ppermute(y_sent, "patch", flop)
    node, to_plus, to_minus, own_right, own_left = call(
        functools.partial(node_kernel, groups, 1),
        [((members, node_rows, width), f32), three, three, one, one],
        (y_sent, *grads[0::3], *grads[1::3], *grads[2::3], wq, wk, wv),
        specs=[pl.ANY],
    )
    from_plus = shifted(to_minus, -row_width)
    from_minus = shifted(to_plus, row_width)
    def exchange(sent, distance):
        return lax.ppermute(sent, "patch", along_z(count, distance))

    kept_a, out_a, sent_a = call(
        first_kernel,
        [
            ((planes // 2, rows, wide), f32),
            ((half * inner_planes, rows, width), f32),
            ((planes // 2 * wide // 128, rows, 128), bf16),
        ],
        (node, own_a, core_own, y_a), specs=[pl.ANY], flops=2 * 10**10,
    )
    in_a = exchange(sent_a, 1)
    outgoing = call(
        relay_kernel, [three, three],
        (place, sent_a, own_right, own_left, from_plus, from_minus),
        specs=[pltpu.SMEM, pl.ANY], scratch=[trio],
    )
    back = swap(outgoing, 1)
    last = 384 * (groups - half) + width
    more, blocks = wide // 128, last // 128
    own_b, *sent = call(
        functools.partial(second_kernel, 1, len(later)),
        [((rows, last), f32)] + [((blocks, rows, 128), bf16)] * (planes - 1),
        (place, outgoing[0], out_a, y_b, *own_b, *core_own_b),
        specs=[pltpu.SMEM, pl.ANY],
        scratch=[pltpu.VMEM((planes, rows, width), f32)], flops=4 * 10**9,
    )
    own_a, *sent[1::2] = call(
        join_kernel,
        [((rows, wide), f32)] + [((blocks + more, rows, 128), bf16)] * (planes // 2 - 1),
        (kept_a, in_a, *sent[1::2]),
    )
    received = [exchange(shard, k) for k, shard in enumerate(sent, 1)]
    (node_grad,) = call(
        finish_kernel, [((members, node_rows, width), bf16)],
        (place, sent[0], *back[::-1], send_rows, node, from_plus, from_minus),
        specs=[pltpu.SMEM, pl.ANY], scratch=[trio], final=True,
    )
    (weight_grad,) = call(
        weight_kernel, [((rows, 4 * width), f32)], (node_grad, own_a, own_b, *received),
        specs=[pltpu.HBM], final=True,
    )
    return (node_grad, weight_grad)


def solution(mesh):
    in_specs = (
        P("groups", "patch", None),
        P("groups", "patch", None),
        P(),
        P(),
        P(),
        P(),
        P("patch", None),
        P("patch"),
        P("patch", None, None),
    )
    out_specs = (P("groups", "patch", None), P(("groups", "patch"), None))
    return jax.shard_map(body, mesh=mesh, in_specs=in_specs, out_specs=out_specs, check_vma=False)
```

```python
import functools
import math

import jax
import jax.numpy as jnp
from jax import lax
from jax.experimental import pallas as pl
from jax.experimental.pallas import tpu as pltpu
from jax.sharding import PartitionSpec as P

HEADS = 16
score_cap = 5.0
MIB = 1024 * 1024
f32 = jnp.float32
bf16 = jnp.bfloat16


def nn(a, b):
    return lax.dot_general(a, b, (((1,), (0,)), ((), ())), preferred_element_type=f32)


def nt(a, b):
    return lax.dot_general(a, b, (((1,), (1,)), ((), ())), preferred_element_type=f32)


def shifted(shard, by):
    count = lax.axis_size("patch")
    return lax.ppermute(shard, "patch", [(i, (i + by) % count) for i in range(count)])


def neighbours_apart(count, stride):
    first, second = [], []
    for i in range(count):
        up, down = (i + stride) % count, (i - stride) % count
        even = i // stride % 2 == 0
        first.append((i, up if even else down))
        second.append((i, down if even else up))
    return first, second


def swap(pair, stride):
    first, second = neighbours_apart(lax.axis_size("patch"), stride)
    later = lax.ppermute(pair[1], "patch", second)
    return [lax.ppermute(pair[0], "patch", first), later]


def to_swaps(both, odd, first_ref, second_ref):
    first_ref[...] = both[odd]
    second_ref[...] = both[1 - odd]


def from_swaps(both, odd, first_ref, second_ref):
    both[1 - odd] = first_ref[...]
    both[odd] = second_ref[...]


def sent_selector(send_rows, node_rows):
    adjacent, slots = send_rows.shape
    halo = adjacent * slots
    wide = jnp.concatenate([send_rows] * adjacent, axis=1)
    own = lax.broadcasted_iota(jnp.int32, (adjacent, halo), 1) // slots == lax.broadcasted_iota(
        jnp.int32, (adjacent, halo), 0
    )
    ids = jnp.sum(jnp.where(own, wide, 0), axis=0, keepdims=True)
    nodes = lax.broadcasted_iota(jnp.int32, (node_rows, halo), 0)
    return jnp.where(nodes == ids, 1.0, 0.0).astype(f32)


def gather_kernel(
    slots, send_hbm, x_hbm, plus_ref, minus_ref, right_ref, left_ref, x_ref, send_ref, sem
):
    copies = [
        pltpu.make_async_copy(send_hbm, send_ref, sem.at[0]),
        pltpu.make_async_copy(x_hbm, x_ref, sem.at[1]),
    ]
    for copy in copies:
        copy.start()
    copies[0].wait()
    members, node_rows, _ = x_ref.shape
    pick = sent_selector(send_ref[0], node_rows).T.astype(bf16)
    copies[1].wait()
    for m in range(members):
        rows = nn(pick, x_ref[m]).astype(bf16)

        def part(k):
            return rows[k * slots : (k + 1) * slots]

        for ref, order in ((plus_ref, (2, 6, 4)), (minus_ref, (3, 5, 7))):
            for i, k in enumerate(order):
                ref[m, i] = part(k)
        right_ref[m, 0] = part(0)
        left_ref[m, 0] = part(1)


def relay_kernel(
    me_ref, after_ref, own_right, own_left, plus_ref, minus_ref, first_ref, second_ref, both
):
    for side, own in enumerate((own_right, own_left)):
        both[side, :, 0:1] = own[...]
        both[side, :, 1:2] = plus_ref[:, 1 + side : 2 + side]
        both[side, :, 2:3] = minus_ref[:, 1 + side : 2 + side]
    to_swaps(both, me_ref[0] % 2, first_ref, second_ref)


def gray(z):
    return z ^ (z >> 1)


def plane_of(code):
    z = code
    for shift in range(1, 8):
        z = z ^ (code >> shift)
    return z


def along_z(count, distance):
    planes = count // 4
    return [(i, plane_of(gray(i // 4) ^ distance) * 4 + i % 4) for i in range(planes * 4)]


Q, K, V, G, QT, KT, VT, GT = range(8)


def local_kernel(groups, after_ref, x_ref, *refs):
    sources, loc_refs, xt_ref = refs[:7], refs[7 : 7 + groups], refs[7 + groups]
    copied, sem = refs[8 + groups : 15 + groups], refs[-1]
    copies = [
        pltpu.make_async_copy(source, target, sem.at[i])
        for i, (source, target) in enumerate(zip(sources, copied))
    ]
    for copy in copies:
        copy.start()
    members, node_rows, width = x_ref.shape
    x = x_ref[...].reshape(members * node_rows, width)
    for m in range(members):
        xt_ref[m] = x_ref[m].T

    def put(rows, kind):
        for m in range(members):
            for g, ref in enumerate(loc_refs):
                block = rows[m * node_rows : (m + 1) * node_rows, g * 128 : (g + 1) * 128]
                ref[kind, m] = block
                ref[kind + 4, m] = block.T

    wq_ref, wk_ref, wv_ref, og_ref, _, _, wo_ref = copied
    for kind, ref in enumerate((wq_ref, wk_ref, wv_ref)):
        copies[kind].wait()
        put(nn(x, ref[...]).astype(bf16), kind)
    for copy in copies[3:]:
        copy.wait()
    og = og_ref[...].reshape(members * node_rows, width)
    put(nt(og, wo_ref[...]).astype(bf16), G)


def mask_kernel(after_ref, neigh_ref, count_ref, mask_ref):
    neigh = neigh_ref[...].T
    slots, node_rows = neigh.shape
    table = mask_ref.shape[0]
    order = lax.broadcasted_iota(jnp.int32, neigh.shape, 0)
    tail = jnp.where(order >= count_ref[...], neigh, -1)[slots // 2 :]
    half = table // 2
    for part in range(2):
        columns = lax.broadcasted_iota(jnp.int32, (half, node_rows), 0) + part * half
        kept = jnp.ones((half, node_rows), f32)
        for j in range(slots // 2):
            kept = jnp.where(tail[j : j + 1] == columns, 0.0, kept)
        mask_ref[part * half : (part + 1) * half] = kept


def halo_kernel(
    me_ref, second_in, first_in, plus_ref, minus_ref, xt_ref, wk_ref, wv_ref, *refs
):
    halo_refs, xtf_ref, both = refs[:-2], refs[-2], refs[-1]
    members, _, node_rows = xt_ref.shape
    from_swaps(both, me_ref[0] % 2, first_in, second_in)
    for m in range(members):
        pieces = [None] * 8
        for side, order in enumerate(((0, 6, 5), (1, 4, 7))):
            for i, k in enumerate(order):
                pieces[k] = both[side, m, i]
        pieces[2] = plus_ref[m, 0]
        pieces[3] = minus_ref[m, 0]
        halo = jnp.concatenate(pieces, axis=0)
        xtf_ref[m, :, :node_rows] = xt_ref[m]
        xtf_ref[m, :, node_rows:] = halo.T
        for kind, w_ref in enumerate((wk_ref, wv_ref)):
            rows = nn(halo, w_ref[...]).astype(bf16)
            for g, ref in enumerate(halo_refs):
                block = rows[:, g * 128 : (g + 1) * 128]
                ref[kind, m] = block
                ref[kind + 2, m] = block.T


STRIP = 64


def by_head_t(block, head):
    row_head = lax.broadcasted_iota(jnp.int32, block.shape, 0) // head
    zero = jnp.zeros_like(block)
    return jnp.concatenate(
        [jnp.where(row_head == h, block, zero) for h in range(block.shape[0] // head)], axis=1
    )


def by_head_n(block, head):
    lane_head = lax.broadcasted_iota(jnp.int32, block.shape, 1) // head
    zero = jnp.zeros_like(block)
    return jnp.concatenate(
        [jnp.where(lane_head == h, block, zero) for h in range(block.shape[1] // head)], axis=0
    )


def unnormalised(scale, score, grad, slope, m, lanes, mask_ref, start):
    columns, node_rows = score.shape[1], mask_ref.shape[1]
    den = jnp.zeros((8, node_rows), f32)
    inner = jnp.zeros((8, node_rows), f32)
    for c in range(0, columns, STRIP):
        box = (m, slice(c, c + STRIP), lanes)
        t = jnp.tanh(score[box] * (scale / score_cap))
        e = jnp.exp2(t * (score_cap / math.log(2.0))) * mask_ref[start + c : start + c + STRIP]
        den = den + jnp.sum(e.reshape(STRIP // 8, 8, node_rows), axis=0)
        inner = inner + jnp.sum((e * grad[box]).reshape(STRIP // 8, 8, node_rows), axis=0)
        score[box] = e
        slope[box] = e * (scale - scale * (t * t))
    return den, inner


def own_kernel(groups, *refs):
    locs, mask_ref, outs = refs[:groups], refs[groups], refs[groups + 1 :]
    _, members, node_rows, _ = locs[0].shape
    head = 128 * groups // HEADS
    scale = 1.0 / math.sqrt(head)
    for g, loc in enumerate(locs):
        own, totals = outs[2 * g : 2 * g + 2]
        score, grad, slope = own.at[0], own.at[1], own.at[2]
        for m in range(members):
            score[m] = nn(loc[K, m], by_head_t(loc[QT, m], head))
            grad[m] = nn(loc[V, m], by_head_t(loc[GT, m], head))
        for m in range(members):
            for h in range(128 // head):
                lanes = slice(h * node_rows, (h + 1) * node_rows)
                den, inner = unnormalised(scale, score, grad, slope, m, lanes, mask_ref, 0)
                totals[0, m, :, lanes] = den
                totals[1, m, :, lanes] = inner


def attention_kernel(extra, here, me_ref, *refs):
    refs = refs[extra:]
    locs, halos, owns = refs[:here], refs[here : 2 * here], refs[2 * here : 4 * here]
    refs = refs[4 * here :]
    mask_ref, xtf, og_ref = refs[:3]
    split = 7 if len(refs) == 15 + 3 * (here - 1) else 6
    outs, grads, scratch = refs[3:split], refs[split : split + 3 * here], refs[split + 3 * here :]
    if split == 6:
        outs = (*outs[:2], outs[2].at[0], outs[2].at[1])
    for i in range(here):
        attend(
            me_ref, locs[i], halos[i], owns[2 * i : 2 * i + 2], mask_ref, xtf, og_ref, outs, 512 * i,
            grads[3 * i : 3 * i + 3], scratch,
        )


def attend(me_ref, loc, halo, own, mask_ref, xtf, og_ref, out_refs, at, grad_refs, scratch):
    own_ref, other_ref, send_other, send_own = out_refs
    dq_ref, dk_ref, dv_ref = grad_refs
    score, grad, slope, dw, wos = scratch
    _, members, node_rows, _ = loc.shape
    table = mask_ref.shape[0]
    width = og_ref.shape[2]
    head = width // HEADS
    per = 128 // head
    scale = 1.0 / math.sqrt(head)

    own, totals = own
    for m in range(members):
        score[m] = nn(halo[0, m], by_head_t(loc[QT, m], head))
        grad[m] = nn(halo[1, m], by_head_t(loc[GT, m], head))

    wo_total = None
    kv_total = None
    q_total = None
    for m in range(members):
        probs = []
        for h in range(per):
            lanes = slice(h * node_rows, (h + 1) * node_rows)
            den, inner = unnormalised(scale, score, grad, slope, m, lanes, mask_ref, node_rows)
            r = 1.0 / jnp.sum(den + totals[0, m, :, lanes], axis=0, keepdims=True)
            inner = jnp.sum(inner + totals[1, m, :, lanes], axis=0, keepdims=True) * r
            column = []
            scores = []
            for e, g, w in ((own.at[0], own.at[1], own.at[2]), (score, grad, slope)):
                for c in range(0, e.shape[1], STRIP):
                    box = (m, slice(c, c + STRIP), lanes)
                    column.append((e[box] * r).astype(bf16))
                    scores.append(((w[box] * r) * (g[box] - inner)).astype(bf16))
            probs.append((jnp.concatenate(column, axis=0), jnp.concatenate(scores, axis=0)))
        pb = jnp.concatenate([p for p, _ in probs], axis=1)
        ds = jnp.concatenate([s for _, s in probs], axis=1)
        ktg = jnp.concatenate([loc[KT, m], halo[2, m]], axis=1)
        vtg = jnp.concatenate([loc[VT, m], halo[3, m]], axis=1)
        att, dqt = [], []
        for h in range(0, per, 2):
            lanes = slice(h * node_rows, (h + 2) * node_rows)
            rows = slice(h * head, (h + 2) * head)
            a = nn(vtg[rows], pb[:, lanes])
            b = nn(ktg[rows], ds[:, lanes])
            for j in range(2):
                inside = (slice(j * head, (j + 1) * head), slice(j * node_rows, (j + 1) * node_rows))
                att.append(a[inside].astype(bf16))
                dqt.append(b[inside].astype(bf16))
        att = jnp.concatenate(att, axis=0)
        dq = jnp.concatenate(dqt, axis=0).T
        dk = nn(ds, by_head_n(loc[Q, m], head)).astype(bf16)
        dv = nn(pb, by_head_n(loc[G, m], head)).astype(bf16)
        dq_ref[m], dk_ref[m], dv_ref[m] = dq, dk, dv
        wo_term = nn(att, og_ref[m])
        kv_term = nn(xtf[m], jnp.concatenate([dk, dv], axis=1))
        q_term = nn(xtf[m, :, :node_rows], dq)
        wo_total = wo_term if m == 0 else wo_total + wo_term
        kv_total = kv_term if m == 0 else kv_total + kv_term
        q_total = q_term if m == 0 else q_total + q_term

    planes, _, _, rows, _ = dw.shape
    inner_planes = wos.shape[0]
    dw[:, :, :, :, :128] = q_total.reshape(planes, 2, 2, rows, 128)
    dw[:, :, :, :, 128:] = kv_total.reshape(planes, 2, 2, rows, 256)
    wos[...] = wo_total.reshape(inner_planes, 2, 2, rows, width)
    me = me_ref[0]
    c, y, z = me % 2, (me // 2) % 2, me // 4
    qkv = slice(at, at + 384)
    for k in range(planes):
        zk = plane_of(gray(z) ^ k)
        own_ref[k, :, qkv] = dw[zk, y, c]
        other_ref[k, :, qkv] = dw[zk, 1 - y, c]
        send_other[k, :, qkv] = dw[zk, 1 - y, 1 - c].astype(bf16)
        send_own[k, :, qkv] = dw[zk, y, 1 - c].astype(bf16)
    last = slice(at + 384, at + 512)
    for i in range(inner_planes):
        for n in range(width // 128):
            k = n * inner_planes + i
            lanes = slice(n * 128, (n + 1) * 128)
            own_ref[k, :, last] = wos[i, y, c, :, lanes]
            other_ref[k, :, last] = wos[i, 1 - y, c, :, lanes]
            send_other[k, :, last] = wos[i, 1 - y, 1 - c, :, lanes].astype(bf16)
            send_own[k, :, last] = wos[i, y, 1 - c, :, lanes].astype(bf16)


def node_kernel(groups, skip, *refs):
    refs = refs[skip:]
    dqs, dks, dvs = refs[:groups], refs[groups : 2 * groups], refs[2 * groups : 3 * groups]
    wq_ref, wk_ref, wv_ref, node_ref, plus_ref, minus_ref, right_ref, left_ref = refs[3 * groups :]
    members, node_rows, _ = dqs[0].shape
    slots = plus_ref.shape[2]

    def whole(parts, m):
        return jnp.concatenate([part[m] for part in parts], axis=1)

    for m in range(members):
        spread = nt(whole(dks, m), wk_ref[...]) + nt(whole(dvs, m), wv_ref[...])
        node_ref[m] = spread[:node_rows] + nt(whole(dqs, m), wq_ref[...])
        halo = spread[node_rows:].astype(bf16)
        for ref, order in (
            (plus_ref, (3, 7, 5)),
            (minus_ref, (2, 4, 6)),
            (right_ref, (1,)),
            (left_ref, (0,)),
        ):
            for i, k in enumerate(order):
                ref[m, i] = halo[k * slots : (k + 1) * slots]


def sums(owns, core_in, y_in, k):
    total = jnp.concatenate(
        [
            own[k] + (core[1, k] if len(core.shape) == 4 else core[k]).astype(f32)
            for own, core in zip(owns, core_in)
        ],
        axis=1,
    ) + y_in[k].astype(f32)
    return [total[:, at : at + 512] for at in range(0, total.shape[1], 512)]


def gather_projection(parts, k, planes, projection_ref, start):
    inner_planes = planes * 128 // projection_ref.shape[2]
    quarter, inner = divmod(k, inner_planes)
    for i, part in enumerate(parts):
        plane = start + i * inner_planes + inner
        projection_ref[plane, :, quarter * 128 : (quarter + 1) * 128] = part[:, 384:]


def pack_kernel(pieces, *refs):
    for i, (ref, core) in enumerate(zip(refs[:pieces], refs[pieces:-1])):
        arrived = core[0] if len(core.shape) == 4 else core[...]
        refs[-1][:, :, i * 512 : (i + 1) * 512] = (ref[...] + arrived.astype(f32)).astype(bf16)


def halve(rows, kept_ref, sent_ref):
    for i, row in enumerate(rows):
        if i % 2 == 0:
            kept_ref[i // 2] = row
            continue
        pieces = row.shape[1] // 128
        for n in range(pieces):
            sent_ref[i // 2 * pieces + n] = row[:, n * 128 : (n + 1) * 128].astype(bf16)


def add_received(kept_ref, received_ref):
    planes, _, wide = kept_ref.shape
    pieces = wide // 128
    return [
        kept_ref[i]
        + jnp.concatenate([received_ref[i * pieces + n] for n in range(pieces)], axis=1).astype(f32)
        for i in range(planes)
    ]


def first_kernel(after_ref, own, core_in, y_in, kept_ref, projection_ref, sent_ref):
    planes = own.shape[0]
    rows = []
    for k in range(planes):
        parts = sums([own], [core_in], y_in, k)
        gather_projection(parts, k, planes, projection_ref, 0)
        rows.append(jnp.concatenate([part[:, :384] for part in parts], axis=1))
    halve(rows, kept_ref, sent_ref)


def put(row, ref, at):
    for n in range(row.shape[1] // 128):
        ref[at + n] = row[:, n * 128 : (n + 1) * 128].astype(bf16)


def second_kernel(skip, pieces, me_ref, *refs):
    refs = refs[skip:]
    first_ref, y_in = refs[:2]
    owns, core_in = refs[2 : 2 + pieces], refs[2 + pieces : 2 + 2 * pieces]
    own_b, *sent = refs[2 + 2 * pieces : -1]
    projection_ref = refs[-1]
    done = first_ref.shape[0]
    planes = projection_ref.shape[0]
    projection_ref[:done] = first_ref[...]
    held = []
    for k in range(planes):
        parts = sums(owns, core_in, y_in, k)
        gather_projection(parts, k, planes, projection_ref, done)
        held.append(jnp.concatenate([part[:, :384] for part in parts], axis=1))
    z = me_ref[0] // 4
    for k in range(planes):
        row = jnp.concatenate([held[k], projection_ref[plane_of(gray(z) ^ k)]], axis=1)
        if k:
            put(row, sent[k - 1], 0)
        else:
            own_b[...] = row


def join_kernel(kept_a, in_a, *refs):
    count = (len(refs) - 1) // 2
    blocks, own_a, sent = refs[:count], refs[count], refs[count + 1 :]
    first = add_received(kept_a, in_a)
    own_a[...] = first[0]
    for i, ref in enumerate(sent):
        ref[: blocks[i].shape[0]] = blocks[i][...]
        put(first[i + 1], ref, blocks[i].shape[0])


def finish_kernel(
    me_ref, after_ref, second_in, first_in, send_ref, node_ref, plus_ref, minus_ref, out_ref, came
):
    members, node_rows, _ = node_ref.shape
    pick = sent_selector(send_ref[0], node_rows).astype(bf16)
    from_swaps(came, me_ref[0] % 2, first_in, second_in)
    for m in range(members):
        pieces = [None] * 8
        for side, order in enumerate(((1, 4, 7), (0, 6, 5))):
            for i, k in enumerate(order):
                pieces[k] = came[side, m, i]
        pieces[2], pieces[3] = plus_ref[m, 0], minus_ref[m, 0]
        arriving = jnp.concatenate(pieces, axis=0)
        out_ref[m] = (node_ref[m] + nn(pick, arriving)).astype(bf16)


def weight_kernel(after_ref, own_a, own_b, *refs):
    received, out_ref = refs[:-1], refs[-1]
    a, b = own_a[...], own_b[...]
    blocks, more = b.shape[1] // 128, a.shape[1] // 128
    for k, ref in enumerate(received, 1):
        b = b + jnp.concatenate([ref[n] for n in range(blocks)], axis=1).astype(f32)
        if k % 2 == 0:
            a = a + jnp.concatenate([ref[blocks + n] for n in range(more)], axis=1).astype(f32)
    width = out_ref.shape[1] // 4
    group = 0
    for part, wide in ((a, a.shape[1]), (b, b.shape[1] - width)):
        for j in range(0, wide, 384):
            for n in range(3):
                at = n * width + group * 128
                out_ref[:, at : at + 128] = part[:, j + n * 128 : j + (n + 1) * 128]
            group += 1
    out_ref[:, 3 * width :] = b[:, b.shape[1] - width :]


def call(kernel, outs, operands, specs=None, scratch=(), limit=12, final=False, flops=10**6):
    specs = list(specs or ())
    specs += [pltpu.VMEM] * (len(operands) - len(specs))
    operands = [
        pltpu.with_memory_space_constraint(o, s) if s in (pltpu.HBM, pltpu.VMEM) else o
        for o, s in zip(operands, specs)
    ]
    return pl.pallas_call(
        kernel,
        out_shape=[jax.ShapeDtypeStruct(*o) if final else pltpu.VMEM(*o) for o in outs],
        in_specs=[pl.BlockSpec(memory_space=s) for s in specs],
        scratch_shapes=list(scratch),
        compiler_params=pltpu.CompilerParams(vmem_limit_bytes=limit * MIB),
        cost_estimate=pl.CostEstimate(flops=flops, bytes_accessed=10**4, transcendentals=0),
    )(*operands)


def body(
    node_features, out_grad, w_query, w_key, w_value, w_out, neighbours, neighbour_count, send_rows
):
    members, node_rows, width = node_features.shape
    count = lax.axis_size("patch")
    row_width = min(8, count // 4)
    _, adjacent, slots = send_rows.shape
    table = node_rows + adjacent * slots
    groups = width // 128
    me = lax.axis_index("patch")
    three = ((members, 3, slots, width), bf16)
    one = ((members, 1, slots, width), bf16)

    place = me.reshape(1)
    trio = pltpu.VMEM((2, *three[0]), bf16)
    to_plus, to_minus, own_right, own_left, x = call(
        functools.partial(gather_kernel, slots),
        [three, three, one, one, (node_features.shape, bf16)],
        (send_rows, node_features),
        specs=[pltpu.HBM] * 2,
        scratch=[pltpu.VMEM(send_rows.shape, jnp.int32), pltpu.SemaphoreType.DMA((2,))],
    )
    plus = shifted(to_plus, row_width)
    minus = shifted(to_minus, -row_width)
    square = ((width, width), bf16)
    counts = neighbour_count.reshape(1, node_rows)
    *loc, xt, wq, wk, wv, og, neigh, counts = call(
        functools.partial(local_kernel, groups),
        [((8, members, node_rows, 128), bf16)] * groups
        + [((members, width, node_rows), bf16), square, square, square, (out_grad.shape, bf16)]
        + [(neighbours.shape, jnp.int32), (counts.shape, jnp.int32)],
        (own_right, x, w_query, w_key, w_value, out_grad, neighbours, counts, w_out),
        specs=[pl.ANY, pltpu.VMEM] + [pltpu.HBM] * 7,
        scratch=[pltpu.VMEM((width, width), bf16), pltpu.SemaphoreType.DMA((7,))],
        limit=16,
    )
    outgoing = call(
        relay_kernel, [three, three], (place, loc[0], own_right, own_left, plus, minus),
        specs=[pltpu.SMEM, pl.ANY], scratch=[trio],
    )
    arrived = swap(outgoing, 1)
    (mask,) = call(
        mask_kernel, [((table, node_rows), f32)], (outgoing[1], neigh, counts), specs=[pl.ANY]
    )
    own_part = call(
        functools.partial(own_kernel, groups),
        [
            ((3, members, node_rows, 4 * node_rows), f32),
            ((2, members, 8, 4 * node_rows), f32),
        ]
        * groups,
        (*loc, mask),
    )
    *halo, xtf = call(
        halo_kernel,
        [((4, members, node_rows, 128), bf16)] * groups + [((members, width, table), bf16)],
        (place, *arrived[::-1], plus, minus, xt, wk, wv), specs=[pltpu.SMEM], scratch=[trio],
    )

    planes, rows = count // 4, width // count
    inner_planes = planes * 128 // width
    flip = [(i, i ^ 1) for i in range(count)]
    flop = [(i, i ^ 2) for i in range(count)]
    grads = []

    def attention(extra, which, together):
        wide = 512 * len(which)
        sends = [((2, planes, rows, wide), bf16)] if together else [((planes, rows, wide), bf16)] * 2
        outs = call(
            functools.partial(attention_kernel, len(extra), len(which)),
            [((planes, rows, wide), f32)] * 2
            + sends
            + [
                ((members, node_rows, 128), bf16),
                ((members, table, 128), bf16),
                ((members, table, 128), bf16),
            ]
            * len(which),
            (
                place, *extra, *[loc[g] for g in which], *[halo[g] for g in which],
                *[part for g in which for part in own_part[2 * g : 2 * g + 2]], mask, xtf, og,
            ),
            specs=[pltpu.SMEM] + [pl.ANY] * len(extra),
            scratch=[pltpu.VMEM((members, table - node_rows, 512), f32)] * 3
            + [
                pltpu.VMEM((planes, 2, 2, rows, 384), f32),
                pltpu.VMEM((inner_planes, 2, 2, rows, width), f32),
            ],
            limit=32,
        )
        sent = outs[2 : 2 + len(sends)]
        grads.extend(outs[2 + len(sends) :])
        arrived = [lax.ppermute(shard, "patch", flip) for shard in sent]
        return outs[0], outs[1], arrived[0], arrived[-1]

    half = groups - 1
    wide = 384 * half
    own_a, other, core_other, core_own = attention((), range(half), False)
    y_sent = (other + core_other.astype(f32)).astype(bf16)
    y_a = lax.ppermute(y_sent, "patch", flop)
    later = [attention((), range(half, groups), False)]
    own_b, other_b, core_other_b, core_own_b = zip(*later)
    (y_sent,) = call(
        functools.partial(pack_kernel, len(later)), [(other_b[0].shape, bf16)],
        (*other_b, *core_other_b),
    )
    y_b = lax.ppermute(y_sent, "patch", flop)
    node, to_plus, to_minus, own_right, own_left = call(
        functools.partial(node_kernel, groups, 1),
        [((members, node_rows, width), f32), three, three, one, one],
        (y_sent, *grads[0::3], *grads[1::3], *grads[2::3], wq, wk, wv),
        specs=[pl.ANY],
    )
    from_plus = shifted(to_minus, -row_width)
    from_minus = shifted(to_plus, row_width)
    def exchange(sent, distance):
        return lax.ppermute(sent, "patch", along_z(count, distance))

    kept_a, out_a, sent_a = call(
        first_kernel,
        [
            ((planes // 2, rows, wide), f32),
            ((half * inner_planes, rows, width), f32),
            ((planes // 2 * wide // 128, rows, 128), bf16),
        ],
        (node, own_a, core_own, y_a), specs=[pl.ANY], flops=2 * 10**10,
    )
    in_a = exchange(sent_a, 1)
    outgoing = call(
        relay_kernel, [three, three],
        (place, sent_a, own_right, own_left, from_plus, from_minus),
        specs=[pltpu.SMEM, pl.ANY], scratch=[trio],
    )
    back = swap(outgoing, 1)
    last = 384 * (groups - half) + width
    more, blocks = wide // 128, last // 128
    own_b, *sent = call(
        functools.partial(second_kernel, 1, len(later)),
        [((rows, last), f32)] + [((blocks, rows, 128), bf16)] * (planes - 1),
        (place, outgoing[0], out_a, y_b, *own_b, *core_own_b),
        specs=[pltpu.SMEM, pl.ANY],
        scratch=[pltpu.VMEM((planes, rows, width), f32)], flops=4 * 10**9,
    )
    own_a, *sent[1::2] = call(
        join_kernel,
        [((rows, wide), f32)] + [((blocks + more, rows, 128), bf16)] * (planes // 2 - 1),
        (kept_a, in_a, *sent[1::2]),
    )
    received = [exchange(shard, k) for k, shard in enumerate(sent, 1)]
    (node_grad,) = call(
        finish_kernel, [((members, node_rows, width), bf16)],
        (place, sent[0], *back[::-1], send_rows, node, from_plus, from_minus),
        specs=[pltpu.SMEM, pl.ANY], scratch=[trio], final=True,
    )
    (weight_grad,) = call(
        weight_kernel, [((rows, 4 * width), f32)], (node_grad, own_a, own_b, *received),
        specs=[pltpu.HBM], final=True,
    )
    return (node_grad, weight_grad)


def solution(mesh):
    in_specs = (
        P("groups", "patch", None),
        P("groups", "patch", None),
        P(),
        P(),
        P(),
        P(),
        P("patch", None),
        P("patch"),
        P("patch", None, None),
    )
    out_specs = (P("groups", "patch", None), P(("groups", "patch"), None))
    return jax.shard_map(body, mesh=mesh, in_specs=in_specs, out_specs=out_specs, check_vma=False)
```

```python
import functools
import math

import jax
import jax.numpy as jnp
from jax import lax
from jax.experimental import pallas as pl
from jax.experimental.pallas import tpu as pltpu
from jax.sharding import PartitionSpec as P

HEADS = 16
score_cap = 5.0
MIB = 1024 * 1024
f32 = jnp.float32
bf16 = jnp.bfloat16


def nn(a, b):
    return lax.dot_general(a, b, (((1,), (0,)), ((), ())), preferred_element_type=f32)


def nt(a, b):
    return lax.dot_general(a, b, (((1,), (1,)), ((), ())), preferred_element_type=f32)


def shifted(shard, by):
    count = lax.axis_size("patch")
    return lax.ppermute(shard, "patch", [(i, (i + by) % count) for i in range(count)])


def neighbours_apart(count, stride):
    first, second = [], []
    for i in range(count):
        up, down = (i + stride) % count, (i - stride) % count
        even = i // stride % 2 == 0
        first.append((i, up if even else down))
        second.append((i, down if even else up))
    return first, second


def swap(pair, stride):
    first, second = neighbours_apart(lax.axis_size("patch"), stride)
    later = lax.ppermute(pair[1], "patch", second)
    return [lax.ppermute(pair[0], "patch", first), later]


def to_swaps(both, odd, first_ref, second_ref):
    first_ref[...] = both[odd]
    second_ref[...] = both[1 - odd]


def from_swaps(both, odd, first_ref, second_ref):
    both[1 - odd] = first_ref[...]
    both[odd] = second_ref[...]


def sent_selector(send_rows, node_rows):
    adjacent, slots = send_rows.shape
    halo = adjacent * slots
    wide = jnp.concatenate([send_rows] * adjacent, axis=1)
    own = lax.broadcasted_iota(jnp.int32, (adjacent, halo), 1) // slots == lax.broadcasted_iota(
        jnp.int32, (adjacent, halo), 0
    )
    ids = jnp.sum(jnp.where(own, wide, 0), axis=0, keepdims=True)
    nodes = lax.broadcasted_iota(jnp.int32, (node_rows, halo), 0)
    return jnp.where(nodes == ids, 1.0, 0.0).astype(f32)


def gather_kernel(
    slots, send_hbm, x_hbm, plus_ref, minus_ref, right_ref, left_ref, x_ref, send_ref, sem
):
    copies = [
        pltpu.make_async_copy(send_hbm, send_ref, sem.at[0]),
        pltpu.make_async_copy(x_hbm, x_ref, sem.at[1]),
    ]
    for copy in copies:
        copy.start()
    copies[0].wait()
    members, node_rows, _ = x_ref.shape
    pick = sent_selector(send_ref[0], node_rows).T.astype(bf16)
    copies[1].wait()
    for m in range(members):
        rows = nn(pick, x_ref[m]).astype(bf16)

        def part(k):
            return rows[k * slots : (k + 1) * slots]

        for ref, order in ((plus_ref, (2, 6, 4)), (minus_ref, (3, 5, 7))):
            for i, k in enumerate(order):
                ref[m, i] = part(k)
        right_ref[m, 0] = part(0)
        left_ref[m, 0] = part(1)


def relay_kernel(
    me_ref, after_ref, own_right, own_left, plus_ref, minus_ref, first_ref, second_ref, both
):
    for side, own in enumerate((own_right, own_left)):
        both[side, :, 0:1] = own[...]
        both[side, :, 1:2] = plus_ref[:, 1 + side : 2 + side]
        both[side, :, 2:3] = minus_ref[:, 1 + side : 2 + side]
    to_swaps(both, me_ref[0] % 2, first_ref, second_ref)


def gray(z):
    return z ^ (z >> 1)


def plane_of(code):
    z = code
    for shift in range(1, 8):
        z = z ^ (code >> shift)
    return z


def along_z(count, distance):
    planes = count // 4
    return [(i, plane_of(gray(i // 4) ^ distance) * 4 + i % 4) for i in range(planes * 4)]


Q, K, V, G, QT, KT, VT, GT = range(8)


def local_kernel(groups, after_ref, x_ref, *refs):
    sources, loc_refs, xt_ref = refs[:7], refs[7 : 7 + groups], refs[7 + groups]
    copied, sem = refs[8 + groups : 15 + groups], refs[-1]
    copies = [
        pltpu.make_async_copy(source, target, sem.at[i])
        for i, (source, target) in enumerate(zip(sources, copied))
    ]
    for copy in copies:
        copy.start()
    members, node_rows, width = x_ref.shape
    x = x_ref[...].reshape(members * node_rows, width)
    for m in range(members):
        xt_ref[m] = x_ref[m].T

    def put(rows, kind):
        for m in range(members):
            for g, ref in enumerate(loc_refs):
                block = rows[m * node_rows : (m + 1) * node_rows, g * 128 : (g + 1) * 128]
                ref[kind, m] = block
                ref[kind + 4, m] = block.T

    wq_ref, wk_ref, wv_ref, og_ref, _, _, wo_ref = copied
    for kind, ref in enumerate((wq_ref, wk_ref, wv_ref)):
        copies[kind].wait()
        put(nn(x, ref[...]).astype(bf16), kind)
    for copy in copies[3:]:
        copy.wait()
    og = og_ref[...].reshape(members * node_rows, width)
    put(nt(og, wo_ref[...]).astype(bf16), G)


def mask_kernel(after_ref, neigh_ref, count_ref, mask_ref):
    neigh = neigh_ref[...].T
    slots, node_rows = neigh.shape
    table = mask_ref.shape[0]
    order = lax.broadcasted_iota(jnp.int32, neigh.shape, 0)
    tail = jnp.where(order >= count_ref[...], neigh, -1)[slots // 2 :]
    half = table // 2
    for part in range(2):
        columns = lax.broadcasted_iota(jnp.int32, (half, node_rows), 0) + part * half
        kept = jnp.ones((half, node_rows), f32)
        for j in range(slots // 2):
            kept = jnp.where(tail[j : j + 1] == columns, 0.0, kept)
        mask_ref[part * half : (part + 1) * half] = kept


def halo_kernel(
    me_ref, second_in, first_in, plus_ref, minus_ref, xt_ref, wk_ref, wv_ref, *refs
):
    halo_refs, xtf_ref, both = refs[:-2], refs[-2], refs[-1]
    members, _, node_rows = xt_ref.shape
    from_swaps(both, me_ref[0] % 2, first_in, second_in)
    for m in range(members):
        pieces = [None] * 8
        for side, order in enumerate(((0, 6, 5), (1, 4, 7))):
            for i, k in enumerate(order):
                pieces[k] = both[side, m, i]
        pieces[2] = plus_ref[m, 0]
        pieces[3] = minus_ref[m, 0]
        halo = jnp.concatenate(pieces, axis=0)
        xtf_ref[m, :, :node_rows] = xt_ref[m]
        xtf_ref[m, :, node_rows:] = halo.T
        for kind, w_ref in enumerate((wk_ref, wv_ref)):
            rows = nn(halo, w_ref[...]).astype(bf16)
            for g, ref in enumerate(halo_refs):
                block = rows[:, g * 128 : (g + 1) * 128]
                ref[kind, m] = block
                ref[kind + 2, m] = block.T


STRIP = 64


def by_head_t(block, head):
    row_head = lax.broadcasted_iota(jnp.int32, block.shape, 0) // head
    zero = jnp.zeros_like(block)
    return jnp.concatenate(
        [jnp.where(row_head == h, block, zero) for h in range(block.shape[0] // head)], axis=1
    )


def by_head_n(block, head):
    lane_head = lax.broadcasted_iota(jnp.int32, block.shape, 1) // head
    zero = jnp.zeros_like(block)
    return jnp.concatenate(
        [jnp.where(lane_head == h, block, zero) for h in range(block.shape[1] // head)], axis=0
    )


def unnormalised(scale, score, grad, slope, m, lanes, mask_ref, start):
    columns, node_rows = score.shape[1], mask_ref.shape[1]
    den = jnp.zeros((8, node_rows), f32)
    inner = jnp.zeros((8, node_rows), f32)
    for c in range(0, columns, STRIP):
        box = (m, slice(c, c + STRIP), lanes)
        t = jnp.tanh(score[box] * (scale / score_cap))
        e = jnp.exp2(t * (score_cap / math.log(2.0))) * mask_ref[start + c : start + c + STRIP]
        den = den + jnp.sum(e.reshape(STRIP // 8, 8, node_rows), axis=0)
        inner = inner + jnp.sum((e * grad[box]).reshape(STRIP // 8, 8, node_rows), axis=0)
        score[box] = e
        slope[box] = e * (scale - scale * (t * t))
    return den, inner


def own_kernel(groups, *refs):
    locs, mask_ref, outs = refs[:groups], refs[groups], refs[groups + 1 :]
    _, members, node_rows, _ = locs[0].shape
    head = 128 * groups // HEADS
    scale = 1.0 / math.sqrt(head)
    for g, loc in enumerate(locs):
        own, totals = outs[2 * g : 2 * g + 2]
        score, grad, slope = own.at[0], own.at[1], own.at[2]
        for m in range(members):
            score[m] = nn(loc[K, m], by_head_t(loc[QT, m], head))
            grad[m] = nn(loc[V, m], by_head_t(loc[GT, m], head))
        for m in range(members):
            for h in range(128 // head):
                lanes = slice(h * node_rows, (h + 1) * node_rows)
                den, inner = unnormalised(scale, score, grad, slope, m, lanes, mask_ref, 0)
                totals[0, m, :, lanes] = den
                totals[1, m, :, lanes] = inner


def attention_kernel(extra, here, me_ref, *refs):
    refs = refs[extra:]
    locs, halos, owns = refs[:here], refs[here : 2 * here], refs[2 * here : 4 * here]
    refs = refs[4 * here :]
    mask_ref, xtf, og_ref = refs[:3]
    split = 7 if len(refs) == 15 + 3 * (here - 1) else 6
    outs, grads, scratch = refs[3:split], refs[split : split + 3 * here], refs[split + 3 * here :]
    if split == 6:
        outs = (*outs[:2], outs[2].at[0], outs[2].at[1])
    for i in range(here):
        attend(
            me_ref, locs[i], halos[i], owns[2 * i : 2 * i + 2], mask_ref, xtf, og_ref, outs, 512 * i,
            grads[3 * i : 3 * i + 3], scratch,
        )


def attend(me_ref, loc, halo, own, mask_ref, xtf, og_ref, out_refs, at, grad_refs, scratch):
    own_ref, other_ref, send_other, send_own = out_refs
    dq_ref, dk_ref, dv_ref = grad_refs
    score, grad, slope, dw, wos = scratch
    _, members, node_rows, _ = loc.shape
    table = mask_ref.shape[0]
    width = og_ref.shape[2]
    head = width // HEADS
    per = 128 // head
    scale = 1.0 / math.sqrt(head)

    own, totals = own
    for m in range(members):
        score[m] = nn(halo[0, m], by_head_t(loc[QT, m], head))
        grad[m] = nn(halo[1, m], by_head_t(loc[GT, m], head))

    wo_total = None
    kv_total = None
    q_total = None
    for m in range(members):
        probs = []
        for h in range(per):
            lanes = slice(h * node_rows, (h + 1) * node_rows)
            den, inner = unnormalised(scale, score, grad, slope, m, lanes, mask_ref, node_rows)
            r = 1.0 / jnp.sum(den + totals[0, m, :, lanes], axis=0, keepdims=True)
            inner = jnp.sum(inner + totals[1, m, :, lanes], axis=0, keepdims=True) * r
            column = []
            scores = []
            for e, g, w in ((own.at[0], own.at[1], own.at[2]), (score, grad, slope)):
                for c in range(0, e.shape[1], STRIP):
                    box = (m, slice(c, c + STRIP), lanes)
                    column.append((e[box] * r).astype(bf16))
                    scores.append(((w[box] * r) * (g[box] - inner)).astype(bf16))
            probs.append((jnp.concatenate(column, axis=0), jnp.concatenate(scores, axis=0)))
        pb = jnp.concatenate([p for p, _ in probs], axis=1)
        ds = jnp.concatenate([s for _, s in probs], axis=1)
        ktg = jnp.concatenate([loc[KT, m], halo[2, m]], axis=1)
        vtg = jnp.concatenate([loc[VT, m], halo[3, m]], axis=1)
        att, dqt = [], []
        for h in range(0, per, 2):
            lanes = slice(h * node_rows, (h + 2) * node_rows)
            rows = slice(h * head, (h + 2) * head)
            a = nn(vtg[rows], pb[:, lanes])
            b = nn(ktg[rows], ds[:, lanes])
            for j in range(2):
                inside = (slice(j * head, (j + 1) * head), slice(j * node_rows, (j + 1) * node_rows))
                att.append(a[inside].astype(bf16))
                dqt.append(b[inside].astype(bf16))
        att = jnp.concatenate(att, axis=0)
        dq = jnp.concatenate(dqt, axis=0).T
        dk = nn(ds, by_head_n(loc[Q, m], head)).astype(bf16)
        dv = nn(pb, by_head_n(loc[G, m], head)).astype(bf16)
        dq_ref[m], dk_ref[m], dv_ref[m] = dq, dk, dv
        wo_term = nn(att, og_ref[m])
        kv_term = nn(xtf[m], jnp.concatenate([dk, dv], axis=1))
        q_term = nn(xtf[m, :, :node_rows], dq)
        wo_total = wo_term if m == 0 else wo_total + wo_term
        kv_total = kv_term if m == 0 else kv_total + kv_term
        q_total = q_term if m == 0 else q_total + q_term

    planes, _, _, rows, _ = dw.shape
    inner_planes = wos.shape[0]
    dw[:, :, :, :, :128] = q_total.reshape(planes, 2, 2, rows, 128)
    dw[:, :, :, :, 128:] = kv_total.reshape(planes, 2, 2, rows, 256)
    wos[...] = wo_total.reshape(inner_planes, 2, 2, rows, width)
    me = me_ref[0]
    c, y, z = me % 2, (me // 2) % 2, me // 4
    qkv = slice(at, at + 384)
    for k in range(planes):
        zk = plane_of(gray(z) ^ k)
        own_ref[k, :, qkv] = dw[zk, y, c]
        other_ref[k, :, qkv] = dw[zk, 1 - y, c]
        send_other[k, :, qkv] = dw[zk, 1 - y, 1 - c].astype(bf16)
        send_own[k, :, qkv] = dw[zk, y, 1 - c].astype(bf16)
    last = slice(at + 384, at + 512)
    for i in range(inner_planes):
        for n in range(width // 128):
            k = n * inner_planes + i
            lanes = slice(n * 128, (n + 1) * 128)
            own_ref[k, :, last] = wos[i, y, c, :, lanes]
            other_ref[k, :, last] = wos[i, 1 - y, c, :, lanes]
            send_other[k, :, last] = wos[i, 1 - y, 1 - c, :, lanes].astype(bf16)
            send_own[k, :, last] = wos[i, y, 1 - c, :, lanes].astype(bf16)


def node_kernel(groups, skip, *refs):
    refs = refs[skip:]
    dqs, dks, dvs = refs[:groups], refs[groups : 2 * groups], refs[2 * groups : 3 * groups]
    wq_ref, wk_ref, wv_ref, node_ref, plus_ref, minus_ref, right_ref, left_ref = refs[3 * groups :]
    members, node_rows, _ = dqs[0].shape
    slots = plus_ref.shape[2]

    def whole(parts, m):
        return jnp.concatenate([part[m] for part in parts], axis=1)

    for m in range(members):
        spread = nt(whole(dks, m), wk_ref[...]) + nt(whole(dvs, m), wv_ref[...])
        node_ref[m] = spread[:node_rows] + nt(whole(dqs, m), wq_ref[...])
        halo = spread[node_rows:].astype(bf16)
        for ref, order in (
            (plus_ref, (3, 7, 5)),
            (minus_ref, (2, 4, 6)),
            (right_ref, (1,)),
            (left_ref, (0,)),
        ):
            for i, k in enumerate(order):
                ref[m, i] = halo[k * slots : (k + 1) * slots]


def sums(owns, core_in, y_in, k):
    total = jnp.concatenate(
        [
            own[k] + (core[1, k] if len(core.shape) == 4 else core[k]).astype(f32)
            for own, core in zip(owns, core_in)
        ],
        axis=1,
    ) + y_in[k].astype(f32)
    return [total[:, at : at + 512] for at in range(0, total.shape[1], 512)]


def gather_projection(parts, k, planes, projection_ref, start):
    inner_planes = planes * 128 // projection_ref.shape[2]
    quarter, inner = divmod(k, inner_planes)
    for i, part in enumerate(parts):
        plane = start + i * inner_planes + inner
        projection_ref[plane, :, quarter * 128 : (quarter + 1) * 128] = part[:, 384:]


def pack_kernel(pieces, *refs):
    for i, (ref, core) in enumerate(zip(refs[:pieces], refs[pieces:-1])):
        arrived = core[0] if len(core.shape) == 4 else core[...]
        refs[-1][:, :, i * 512 : (i + 1) * 512] = (ref[...] + arrived.astype(f32)).astype(bf16)


def halve(rows, kept_ref, sent_ref):
    for i, row in enumerate(rows):
        if i % 2 == 0:
            kept_ref[i // 2] = row
            continue
        pieces = row.shape[1] // 128
        for n in range(pieces):
            sent_ref[i // 2 * pieces + n] = row[:, n * 128 : (n + 1) * 128].astype(bf16)


def add_received(kept_ref, received_ref):
    planes, _, wide = kept_ref.shape
    pieces = wide // 128
    return [
        kept_ref[i]
        + jnp.concatenate([received_ref[i * pieces + n] for n in range(pieces)], axis=1).astype(f32)
        for i in range(planes)
    ]


def first_kernel(after_ref, own, core_in, y_in, kept_ref, projection_ref, sent_ref):
    planes = own.shape[0]
    rows = []
    for k in range(planes):
        parts = sums([own], [core_in], y_in, k)
        gather_projection(parts, k, planes, projection_ref, 0)
        rows.append(jnp.concatenate([part[:, :384] for part in parts], axis=1))
    halve(rows, kept_ref, sent_ref)


def put(row, ref, at):
    for n in range(row.shape[1] // 128):
        ref[at + n] = row[:, n * 128 : (n + 1) * 128].astype(bf16)


def second_kernel(skip, pieces, me_ref, *refs):
    refs = refs[skip:]
    first_ref, y_in = refs[:2]
    owns, core_in = refs[2 : 2 + pieces], refs[2 + pieces : 2 + 2 * pieces]
    own_b, *sent = refs[2 + 2 * pieces : -1]
    projection_ref = refs[-1]
    done = first_ref.shape[0]
    planes = projection_ref.shape[0]
    projection_ref[:done] = first_ref[...]
    held = []
    for k in range(planes):
        parts = sums(owns, core_in, y_in, k)
        gather_projection(parts, k, planes, projection_ref, done)
        held.append(jnp.concatenate([part[:, :384] for part in parts], axis=1))
    z = me_ref[0] // 4
    for k in range(planes):
        row = jnp.concatenate([held[k], projection_ref[plane_of(gray(z) ^ k)]], axis=1)
        if k:
            put(row, sent[k - 1], 0)
        else:
            own_b[...] = row


def join_kernel(kept_a, in_a, *refs):
    count = (len(refs) - 1) // 2
    blocks, own_a, sent = refs[:count], refs[count], refs[count + 1 :]
    first = add_received(kept_a, in_a)
    own_a[...] = first[0]
    for i, ref in enumerate(sent):
        ref[: blocks[i].shape[0]] = blocks[i][...]
        put(first[i + 1], ref, blocks[i].shape[0])


def finish_kernel(
    me_ref, after_ref, second_in, first_in, send_ref, node_ref, plus_ref, minus_ref, out_ref, came
):
    members, node_rows, _ = node_ref.shape
    pick = sent_selector(send_ref[0], node_rows).astype(bf16)
    from_swaps(came, me_ref[0] % 2, first_in, second_in)
    for m in range(members):
        pieces = [None] * 8
        for side, order in enumerate(((1, 4, 7), (0, 6, 5))):
            for i, k in enumerate(order):
                pieces[k] = came[side, m, i]
        pieces[2], pieces[3] = plus_ref[m, 0], minus_ref[m, 0]
        arriving = jnp.concatenate(pieces, axis=0)
        out_ref[m] = (node_ref[m] + nn(pick, arriving)).astype(bf16)


def weight_kernel(after_ref, own_a, own_b, *refs):
    received, out_ref = refs[:-1], refs[-1]
    a, b = own_a[...], own_b[...]
    blocks, more = b.shape[1] // 128, a.shape[1] // 128
    for k, ref in enumerate(received, 1):
        b = b + jnp.concatenate([ref[n] for n in range(blocks)], axis=1).astype(f32)
        if k % 2 == 0:
            a = a + jnp.concatenate([ref[blocks + n] for n in range(more)], axis=1).astype(f32)
    width = out_ref.shape[1] // 4
    group = 0
    for part, wide in ((a, a.shape[1]), (b, b.shape[1] - width)):
        for j in range(0, wide, 384):
            for n in range(3):
                at = n * width + group * 128
                out_ref[:, at : at + 128] = part[:, j + n * 128 : j + (n + 1) * 128]
            group += 1
    out_ref[:, 3 * width :] = b[:, b.shape[1] - width :]


def call(kernel, outs, operands, specs=None, scratch=(), limit=12, final=False, flops=10**6):
    specs = list(specs or ())
    specs += [pltpu.VMEM] * (len(operands) - len(specs))
    operands = [
        pltpu.with_memory_space_constraint(o, s) if s in (pltpu.HBM, pltpu.VMEM) else o
        for o, s in zip(operands, specs)
    ]
    return pl.pallas_call(
        kernel,
        out_shape=[jax.ShapeDtypeStruct(*o) if final else pltpu.VMEM(*o) for o in outs],
        in_specs=[pl.BlockSpec(memory_space=s) for s in specs],
        scratch_shapes=list(scratch),
        compiler_params=pltpu.CompilerParams(vmem_limit_bytes=limit * MIB),
        cost_estimate=pl.CostEstimate(flops=flops, bytes_accessed=10**4, transcendentals=0),
    )(*operands)


def body(
    node_features, out_grad, w_query, w_key, w_value, w_out, neighbours, neighbour_count, send_rows
):
    members, node_rows, width = node_features.shape
    count = lax.axis_size("patch")
    row_width = min(8, count // 4)
    _, adjacent, slots = send_rows.shape
    table = node_rows + adjacent * slots
    groups = width // 128
    me = lax.axis_index("patch")
    three = ((members, 3, slots, width), bf16)
    one = ((members, 1, slots, width), bf16)

    place = me.reshape(1)
    trio = pltpu.VMEM((2, *three[0]), bf16)
    to_plus, to_minus, own_right, own_left, x = call(
        functools.partial(gather_kernel, slots),
        [three, three, one, one, (node_features.shape, bf16)],
        (send_rows, node_features),
        specs=[pltpu.HBM] * 2,
        scratch=[pltpu.VMEM(send_rows.shape, jnp.int32), pltpu.SemaphoreType.DMA((2,))],
    )
    plus = shifted(to_plus, row_width)
    minus = shifted(to_minus, -row_width)
    square = ((width, width), bf16)
    counts = neighbour_count.reshape(1, node_rows)
    *loc, xt, wq, wk, wv, og, neigh, counts = call(
        functools.partial(local_kernel, groups),
        [((8, members, node_rows, 128), bf16)] * groups
        + [((members, width, node_rows), bf16), square, square, square, (out_grad.shape, bf16)]
        + [(neighbours.shape, jnp.int32), (counts.shape, jnp.int32)],
        (own_right, x, w_query, w_key, w_value, out_grad, neighbours, counts, w_out),
        specs=[pl.ANY, pltpu.VMEM] + [pltpu.HBM] * 7,
        scratch=[pltpu.VMEM((width, width), bf16), pltpu.SemaphoreType.DMA((7,))],
        limit=16,
    )
    outgoing = call(
        relay_kernel, [three, three], (place, loc[0], own_right, own_left, plus, minus),
        specs=[pltpu.SMEM, pl.ANY], scratch=[trio],
    )
    arrived = swap(outgoing, 1)
    (mask,) = call(
        mask_kernel, [((table, node_rows), f32)], (outgoing[1], neigh, counts), specs=[pl.ANY]
    )
    own_part = call(
        functools.partial(own_kernel, groups),
        [
            ((3, members, node_rows, 4 * node_rows), f32),
            ((2, members, 8, 4 * node_rows), f32),
        ]
        * groups,
        (*loc, mask),
    )
    *halo, xtf = call(
        halo_kernel,
        [((4, members, node_rows, 128), bf16)] * groups + [((members, width, table), bf16)],
        (place, *arrived[::-1], plus, minus, xt, wk, wv), specs=[pltpu.SMEM], scratch=[trio],
    )

    planes, rows = count // 4, width // count
    inner_planes = planes * 128 // width
    flip = [(i, i ^ 1) for i in range(count)]
    flop = [(i, i ^ 2) for i in range(count)]
    grads = []

    def attention(extra, which, together):
        wide = 512 * len(which)
        sends = [((2, planes, rows, wide), bf16)] if together else [((planes, rows, wide), bf16)] * 2
        outs = call(
            functools.partial(attention_kernel, len(extra), len(which)),
            [((planes, rows, wide), f32)] * 2
            + sends
            + [
                ((members, node_rows, 128), bf16),
                ((members, table, 128), bf16),
                ((members, table, 128), bf16),
            ]
            * len(which),
            (
                place, *extra, *[loc[g] for g in which], *[halo[g] for g in which],
                *[part for g in which for part in own_part[2 * g : 2 * g + 2]], mask, xtf, og,
            ),
            specs=[pltpu.SMEM] + [pl.ANY] * len(extra),
            scratch=[pltpu.VMEM((members, table - node_rows, 512), f32)] * 3
            + [
                pltpu.VMEM((planes, 2, 2, rows, 384), f32),
                pltpu.VMEM((inner_planes, 2, 2, rows, width), f32),
            ],
            limit=32,
        )
        sent = outs[2 : 2 + len(sends)]
        grads.extend(outs[2 + len(sends) :])
        arrived = [lax.ppermute(shard, "patch", flip) for shard in sent]
        return outs[0], outs[1], arrived[0], arrived[-1]

    half = groups // 2
    wide = 384 * half
    own_a, other, core_other, core_own = attention((), range(half), False)
    y_sent = (other + core_other.astype(f32)).astype(bf16)
    y_a = lax.ppermute(y_sent, "patch", flop)
    later = []
    for g in range(half, groups):
        last = g == groups - 1
        later.append(attention((y_sent,) if last else (), range(g, g + 1), not last))
    own_b, other_b, core_other_b, core_own_b = zip(*later)
    (y_sent,) = call(
        functools.partial(pack_kernel, len(later)),
        [((planes, rows, 512 * (groups - half)), bf16)],
        (*other_b, *core_other_b),
    )
    y_b = lax.ppermute(y_sent, "patch", flop)
    node, to_plus, to_minus, own_right, own_left = call(
        functools.partial(node_kernel, groups, 1),
        [((members, node_rows, width), f32), three, three, one, one],
        (y_sent, *grads[0::3], *grads[1::3], *grads[2::3], wq, wk, wv),
        specs=[pl.ANY],
    )
    from_plus = shifted(to_minus, -row_width)
    from_minus = shifted(to_plus, row_width)
    def exchange(sent, distance):
        return lax.ppermute(sent, "patch", along_z(count, distance))

    kept_a, out_a, sent_a = call(
        first_kernel,
        [
            ((planes // 2, rows, wide), f32),
            ((half * inner_planes, rows, width), f32),
            ((planes // 2 * wide // 128, rows, 128), bf16),
        ],
        (node, own_a, core_own, y_a), specs=[pl.ANY], flops=2 * 10**10,
    )
    in_a = exchange(sent_a, 1)
    outgoing = call(
        relay_kernel, [three, three],
        (place, sent_a, own_right, own_left, from_plus, from_minus),
        specs=[pltpu.SMEM, pl.ANY], scratch=[trio],
    )
    back = swap(outgoing, 1)
    last = 384 * (groups - half) + width
    more, blocks = wide // 128, last // 128
    own_b, *sent = call(
        functools.partial(second_kernel, 1, len(later)),
        [((rows, last), f32)] + [((blocks, rows, 128), bf16)] * (planes - 1),
        (place, outgoing[0], out_a, y_b, *own_b, *core_own_b),
        specs=[pltpu.SMEM, pl.ANY],
        scratch=[pltpu.VMEM((planes, rows, width), f32)], flops=4 * 10**9,
    )
    own_a, *sent[1::2] = call(
        join_kernel,
        [((rows, wide), f32)] + [((blocks + more, rows, 128), bf16)] * (planes // 2 - 1),
        (kept_a, in_a, *sent[1::2]),
    )
    received = [exchange(shard, k) for k, shard in enumerate(sent, 1)]
    (node_grad,) = call(
        finish_kernel, [((members, node_rows, width), bf16)],
        (place, sent[0], *back[::-1], send_rows, node, from_plus, from_minus),
        specs=[pltpu.SMEM, pl.ANY], scratch=[trio], final=True,
    )
    (weight_grad,) = call(
        weight_kernel, [((rows, 4 * width), f32)], (node_grad, own_a, own_b, *received),
        specs=[pltpu.HBM], final=True,
    )
    return (node_grad, weight_grad)


def solution(mesh):
    in_specs = (
        P("groups", "patch", None),
        P("groups", "patch", None),
        P(),
        P(),
        P(),
        P(),
        P("patch", None),
        P("patch"),
        P("patch", None, None),
    )
    out_specs = (P("groups", "patch", None), P(("groups", "patch"), None))
    return jax.shard_map(body, mesh=mesh, in_specs=in_specs, out_specs=out_specs, check_vma=False)
```

```python
import functools
import math

import jax
import jax.numpy as jnp
from jax import lax
from jax.experimental import pallas as pl
from jax.experimental.pallas import tpu as pltpu
from jax.sharding import PartitionSpec as P

HEADS = 16
score_cap = 5.0
MIB = 1024 * 1024
f32 = jnp.float32
bf16 = jnp.bfloat16


def nn(a, b):
    return lax.dot_general(a, b, (((1,), (0,)), ((), ())), preferred_element_type=f32)


def nt(a, b):
    return lax.dot_general(a, b, (((1,), (1,)), ((), ())), preferred_element_type=f32)


def shifted(shard, by):
    count = lax.axis_size("patch")
    return lax.ppermute(shard, "patch", [(i, (i + by) % count) for i in range(count)])


def neighbours_apart(count, stride):
    first, second = [], []
    for i in range(count):
        up, down = (i + stride) % count, (i - stride) % count
        even = i // stride % 2 == 0
        first.append((i, up if even else down))
        second.append((i, down if even else up))
    return first, second


def swap(pair, stride):
    first, second = neighbours_apart(lax.axis_size("patch"), stride)
    later = lax.ppermute(pair[1], "patch", second)
    return [lax.ppermute(pair[0], "patch", first), later]


def to_swaps(both, odd, first_ref, second_ref):
    first_ref[...] = both[odd]
    second_ref[...] = both[1 - odd]


def from_swaps(both, odd, first_ref, second_ref):
    both[1 - odd] = first_ref[...]
    both[odd] = second_ref[...]


def sent_selector(send_rows, node_rows):
    adjacent, slots = send_rows.shape
    halo = adjacent * slots
    wide = jnp.concatenate([send_rows] * adjacent, axis=1)
    own = lax.broadcasted_iota(jnp.int32, (adjacent, halo), 1) // slots == lax.broadcasted_iota(
        jnp.int32, (adjacent, halo), 0
    )
    ids = jnp.sum(jnp.where(own, wide, 0), axis=0, keepdims=True)
    nodes = lax.broadcasted_iota(jnp.int32, (node_rows, halo), 0)
    return jnp.where(nodes == ids, 1.0, 0.0).astype(f32)


def gather_kernel(
    slots, send_hbm, x_hbm, plus_ref, minus_ref, right_ref, left_ref, x_ref, send_ref, sem
):
    copies = [
        pltpu.make_async_copy(send_hbm, send_ref, sem.at[0]),
        pltpu.make_async_copy(x_hbm, x_ref, sem.at[1]),
    ]
    for copy in copies:
        copy.start()
    copies[0].wait()
    members, node_rows, _ = x_ref.shape
    pick = sent_selector(send_ref[0], node_rows).T.astype(bf16)
    copies[1].wait()
    for m in range(members):
        rows = nn(pick, x_ref[m]).astype(bf16)

        def part(k):
            return rows[k * slots : (k + 1) * slots]

        for ref, order in ((plus_ref, (2, 6, 4)), (minus_ref, (3, 5, 7))):
            for i, k in enumerate(order):
                ref[m, i] = part(k)
        right_ref[m, 0] = part(0)
        left_ref[m, 0] = part(1)


def relay_kernel(
    me_ref, after_ref, own_right, own_left, plus_ref, minus_ref, first_ref, second_ref, both
):
    for side, own in enumerate((own_right, own_left)):
        both[side, :, 0:1] = own[...]
        both[side, :, 1:2] = plus_ref[:, 1 + side : 2 + side]
        both[side, :, 2:3] = minus_ref[:, 1 + side : 2 + side]
    to_swaps(both, me_ref[0] % 2, first_ref, second_ref)


def gray(z):
    return z ^ (z >> 1)


def plane_of(code):
    z = code
    for shift in range(1, 8):
        z = z ^ (code >> shift)
    return z


def along_z(count, distance):
    planes = count // 4
    return [(i, plane_of(gray(i // 4) ^ distance) * 4 + i % 4) for i in range(planes * 4)]


Q, K, V, G, QT, KT, VT, GT = range(8)


def local_kernel(groups, after_ref, x_ref, *refs):
    sources, loc_refs, xt_ref = refs[:7], refs[7 : 7 + groups], refs[7 + groups]
    copied, sem = refs[8 + groups : 15 + groups], refs[-1]
    copies = [
        pltpu.make_async_copy(source, target, sem.at[i])
        for i, (source, target) in enumerate(zip(sources, copied))
    ]
    for copy in copies:
        copy.start()
    members, node_rows, width = x_ref.shape
    x = x_ref[...].reshape(members * node_rows, width)
    for m in range(members):
        xt_ref[m] = x_ref[m].T

    def put(rows, kind):
        for m in range(members):
            for g, ref in enumerate(loc_refs):
                block = rows[m * node_rows : (m + 1) * node_rows, g * 128 : (g + 1) * 128]
                ref[kind, m] = block
                ref[kind + 4, m] = block.T

    wq_ref, wk_ref, wv_ref, og_ref, _, _, wo_ref = copied
    for kind, ref in enumerate((wq_ref, wk_ref, wv_ref)):
        copies[kind].wait()
        put(nn(x, ref[...]).astype(bf16), kind)
    for copy in copies[3:]:
        copy.wait()
    og = og_ref[...].reshape(members * node_rows, width)
    put(nt(og, wo_ref[...]).astype(bf16), G)


def mask_kernel(after_ref, neigh_ref, count_ref, mask_ref):
    neigh = neigh_ref[...].T
    slots, node_rows = neigh.shape
    table = mask_ref.shape[0]
    order = lax.broadcasted_iota(jnp.int32, neigh.shape, 0)
    tail = jnp.where(order >= count_ref[...], neigh, -1)[slots // 2 :]
    half = table // 2
    for part in range(2):
        columns = lax.broadcasted_iota(jnp.int32, (half, node_rows), 0) + part * half
        kept = jnp.ones((half, node_rows), f32)
        for j in range(slots // 2):
            kept = jnp.where(tail[j : j + 1] == columns, 0.0, kept)
        mask_ref[part * half : (part + 1) * half] = kept


def halo_kernel(
    me_ref, second_in, first_in, plus_ref, minus_ref, xt_ref, wk_ref, wv_ref, *refs
):
    halo_refs, xtf_ref, both = refs[:-2], refs[-2], refs[-1]
    members, _, node_rows = xt_ref.shape
    from_swaps(both, me_ref[0] % 2, first_in, second_in)
    for m in range(members):
        pieces = [None] * 8
        for side, order in enumerate(((0, 6, 5), (1, 4, 7))):
            for i, k in enumerate(order):
                pieces[k] = both[side, m, i]
        pieces[2] = plus_ref[m, 0]
        pieces[3] = minus_ref[m, 0]
        halo = jnp.concatenate(pieces, axis=0)
        xtf_ref[m, :, :node_rows] = xt_ref[m]
        xtf_ref[m, :, node_rows:] = halo.T
        for kind, w_ref in enumerate((wk_ref, wv_ref)):
            rows = nn(halo, w_ref[...]).astype(bf16)
            for g, ref in enumerate(halo_refs):
                block = rows[:, g * 128 : (g + 1) * 128]
                ref[kind, m] = block
                ref[kind + 2, m] = block.T


STRIP = 64


def by_head_t(block, head):
    row_head = lax.broadcasted_iota(jnp.int32, block.shape, 0) // head
    zero = jnp.zeros_like(block)
    return jnp.concatenate(
        [jnp.where(row_head == h, block, zero) for h in range(block.shape[0] // head)], axis=1
    )


def by_head_n(block, head):
    lane_head = lax.broadcasted_iota(jnp.int32, block.shape, 1) // head
    zero = jnp.zeros_like(block)
    return jnp.concatenate(
        [jnp.where(lane_head == h, block, zero) for h in range(block.shape[1] // head)], axis=0
    )


def unnormalised(scale, score, grad, slope, m, lanes, mask_ref, start):
    columns, node_rows = score.shape[1], mask_ref.shape[1]
    den = jnp.zeros((8, node_rows), f32)
    inner = jnp.zeros((8, node_rows), f32)
    for c in range(0, columns, STRIP):
        box = (m, slice(c, c + STRIP), lanes)
        t = jnp.tanh(score[box] * (scale / score_cap))
        e = jnp.exp2(t * (score_cap / math.log(2.0))) * mask_ref[start + c : start + c + STRIP]
        den = den + jnp.sum(e.reshape(STRIP // 8, 8, node_rows), axis=0)
        inner = inner + jnp.sum((e * grad[box]).reshape(STRIP // 8, 8, node_rows), axis=0)
        score[box] = e
        slope[box] = e * (scale - scale * (t * t))
    return den, inner


def own_kernel(groups, *refs):
    locs, mask_ref, outs = refs[:groups], refs[groups], refs[groups + 1 :]
    _, members, node_rows, _ = locs[0].shape
    head = 128 * groups // HEADS
    scale = 1.0 / math.sqrt(head)
    for g, loc in enumerate(locs):
        own, totals = outs[2 * g : 2 * g + 2]
        score, grad, slope = own.at[0], own.at[1], own.at[2]
        for m in range(members):
            score[m] = nn(loc[K, m], by_head_t(loc[QT, m], head))
            grad[m] = nn(loc[V, m], by_head_t(loc[GT, m], head))
        for m in range(members):
            for h in range(128 // head):
                lanes = slice(h * node_rows, (h + 1) * node_rows)
                den, inner = unnormalised(scale, score, grad, slope, m, lanes, mask_ref, 0)
                totals[0, m, :, lanes] = den
                totals[1, m, :, lanes] = inner


def attention_kernel(extra, here, me_ref, *refs):
    refs = refs[extra:]
    locs, halos, owns = refs[:here], refs[here : 2 * here], refs[2 * here : 4 * here]
    refs = refs[4 * here :]
    mask_ref, xtf, og_ref = refs[:3]
    split = 7 if len(refs) == 15 + 3 * (here - 1) else 6
    outs, grads, scratch = refs[3:split], refs[split : split + 3 * here], refs[split + 3 * here :]
    if split == 6:
        outs = (*outs[:2], outs[2].at[0], outs[2].at[1])
    for i in range(here):
        attend(
            me_ref, locs[i], halos[i], owns[2 * i : 2 * i + 2], mask_ref, xtf, og_ref, outs, 512 * i,
            grads[3 * i : 3 * i + 3], scratch,
        )


def attend(me_ref, loc, halo, own, mask_ref, xtf, og_ref, out_refs, at, grad_refs, scratch):
    own_ref, other_ref, send_other, send_own = out_refs
    dq_ref, dk_ref, dv_ref = grad_refs
    score, grad, slope, dw, wos = scratch
    _, members, node_rows, _ = loc.shape
    table = mask_ref.shape[0]
    width = og_ref.shape[2]
    head = width // HEADS
    per = 128 // head
    scale = 1.0 / math.sqrt(head)

    own, totals = own
    for m in range(members):
        score[m] = nn(halo[0, m], by_head_t(loc[QT, m], head))
        grad[m] = nn(halo[1, m], by_head_t(loc[GT, m], head))

    wo_total = None
    kv_total = None
    q_total = None
    for m in range(members):
        probs = []
        for h in range(per):
            lanes = slice(h * node_rows, (h + 1) * node_rows)
            den, inner = unnormalised(scale, score, grad, slope, m, lanes, mask_ref, node_rows)
            r = 1.0 / jnp.sum(den + totals[0, m, :, lanes], axis=0, keepdims=True)
            inner = jnp.sum(inner + totals[1, m, :, lanes], axis=0, keepdims=True) * r
            column = []
            scores = []
            for e, g, w in ((own.at[0], own.at[1], own.at[2]), (score, grad, slope)):
                for c in range(0, e.shape[1], STRIP):
                    box = (m, slice(c, c + STRIP), lanes)
                    column.append((e[box] * r).astype(bf16))
                    scores.append(((w[box] * r) * (g[box] - inner)).astype(bf16))
            probs.append((jnp.concatenate(column, axis=0), jnp.concatenate(scores, axis=0)))
        pb = jnp.concatenate([p for p, _ in probs], axis=1)
        ds = jnp.concatenate([s for _, s in probs], axis=1)
        ktg = jnp.concatenate([loc[KT, m], halo[2, m]], axis=1)
        vtg = jnp.concatenate([loc[VT, m], halo[3, m]], axis=1)
        att, dqt = [], []
        for h in range(0, per, 2):
            lanes = slice(h * node_rows, (h + 2) * node_rows)
            rows = slice(h * head, (h + 2) * head)
            a = nn(vtg[rows], pb[:, lanes])
            b = nn(ktg[rows], ds[:, lanes])
            for j in range(2):
                inside = (slice(j * head, (j + 1) * head), slice(j * node_rows, (j + 1) * node_rows))
                att.append(a[inside].astype(bf16))
                dqt.append(b[inside].astype(bf16))
        att = jnp.concatenate(att, axis=0)
        dq = jnp.concatenate(dqt, axis=0).T
        dk = nn(ds, by_head_n(loc[Q, m], head)).astype(bf16)
        dv = nn(pb, by_head_n(loc[G, m], head)).astype(bf16)
        dq_ref[m], dk_ref[m], dv_ref[m] = dq, dk, dv
        wo_term = nn(att, og_ref[m])
        kv_term = nn(xtf[m], jnp.concatenate([dk, dv], axis=1))
        q_term = nn(xtf[m, :, :node_rows], dq)
        wo_total = wo_term if m == 0 else wo_total + wo_term
        kv_total = kv_term if m == 0 else kv_total + kv_term
        q_total = q_term if m == 0 else q_total + q_term

    planes, _, _, rows, _ = dw.shape
    inner_planes = wos.shape[0]
    dw[:, :, :, :, :128] = q_total.reshape(planes, 2, 2, rows, 128)
    dw[:, :, :, :, 128:] = kv_total.reshape(planes, 2, 2, rows, 256)
    wos[...] = wo_total.reshape(inner_planes, 2, 2, rows, width)
    me = me_ref[0]
    c, y, z = me % 2, (me // 2) % 2, me // 4
    qkv = slice(at, at + 384)
    for k in range(planes):
        zk = plane_of(gray(z) ^ k)
        own_ref[k, :, qkv] = dw[zk, y, c]
        other_ref[k, :, qkv] = dw[zk, 1 - y, c]
        send_other[k, :, qkv] = dw[zk, 1 - y, 1 - c].astype(bf16)
        send_own[k, :, qkv] = dw[zk, y, 1 - c].astype(bf16)
    last = slice(at + 384, at + 512)
    for i in range(inner_planes):
        for n in range(width // 128):
            k = n * inner_planes + i
            lanes = slice(n * 128, (n + 1) * 128)
            own_ref[k, :, last] = wos[i, y, c, :, lanes]
            other_ref[k, :, last] = wos[i, 1 - y, c, :, lanes]
            send_other[k, :, last] = wos[i, 1 - y, 1 - c, :, lanes].astype(bf16)
            send_own[k, :, last] = wos[i, y, 1 - c, :, lanes].astype(bf16)


def node_kernel(groups, skip, *refs):
    refs = refs[skip:]
    dqs, dks, dvs = refs[:groups], refs[groups : 2 * groups], refs[2 * groups : 3 * groups]
    wq_ref, wk_ref, wv_ref, node_ref, plus_ref, minus_ref, right_ref, left_ref = refs[3 * groups :]
    members, node_rows, _ = dqs[0].shape
    slots = plus_ref.shape[2]

    def whole(parts, m):
        return jnp.concatenate([part[m] for part in parts], axis=1)

    for m in range(members):
        spread = nt(whole(dks, m), wk_ref[...]) + nt(whole(dvs, m), wv_ref[...])
        node_ref[m] = spread[:node_rows] + nt(whole(dqs, m), wq_ref[...])
        halo = spread[node_rows:].astype(bf16)
        for ref, order in (
            (plus_ref, (3, 7, 5)),
            (minus_ref, (2, 4, 6)),
            (right_ref, (1,)),
            (left_ref, (0,)),
        ):
            for i, k in enumerate(order):
                ref[m, i] = halo[k * slots : (k + 1) * slots]


def sums(owns, core_in, y_in, k):
    total = jnp.concatenate(
        [
            own[k] + (core[1, k] if len(core.shape) == 4 else core[k]).astype(f32)
            for own, core in zip(owns, core_in)
        ],
        axis=1,
    ) + y_in[k].astype(f32)
    return [total[:, at : at + 512] for at in range(0, total.shape[1], 512)]


def gather_projection(parts, k, planes, projection_ref, start):
    inner_planes = planes * 128 // projection_ref.shape[2]
    quarter, inner = divmod(k, inner_planes)
    for i, part in enumerate(parts):
        plane = start + i * inner_planes + inner
        projection_ref[plane, :, quarter * 128 : (quarter + 1) * 128] = part[:, 384:]


def pack_kernel(pieces, after_ref, *refs):
    for i, (ref, core) in enumerate(zip(refs[:pieces], refs[pieces:-1])):
        arrived = core[0] if len(core.shape) == 4 else core[...]
        refs[-1][:, :, i * 512 : (i + 1) * 512] = (ref[...] + arrived.astype(f32)).astype(bf16)


def halve(rows, kept_ref, sent_ref):
    for i, row in enumerate(rows):
        if i % 2 == 0:
            kept_ref[i // 2] = row
            continue
        pieces = row.shape[1] // 128
        for n in range(pieces):
            sent_ref[i // 2 * pieces + n] = row[:, n * 128 : (n + 1) * 128].astype(bf16)


def add_received(kept_ref, received_ref):
    planes, _, wide = kept_ref.shape
    pieces = wide // 128
    return [
        kept_ref[i]
        + jnp.concatenate([received_ref[i * pieces + n] for n in range(pieces)], axis=1).astype(f32)
        for i in range(planes)
    ]


def first_kernel(after_ref, own, core_in, y_in, kept_ref, projection_ref, sent_ref):
    planes = own.shape[0]
    rows = []
    for k in range(planes):
        parts = sums([own], [core_in], y_in, k)
        gather_projection(parts, k, planes, projection_ref, 0)
        rows.append(jnp.concatenate([part[:, :384] for part in parts], axis=1))
    halve(rows, kept_ref, sent_ref)


def put(row, ref, at):
    for n in range(row.shape[1] // 128):
        ref[at + n] = row[:, n * 128 : (n + 1) * 128].astype(bf16)


def second_kernel(skip, pieces, me_ref, *refs):
    refs = refs[skip:]
    first_ref, y_in = refs[:2]
    owns, core_in = refs[2 : 2 + pieces], refs[2 + pieces : 2 + 2 * pieces]
    own_b, *sent = refs[2 + 2 * pieces : -1]
    projection_ref = refs[-1]
    done = first_ref.shape[0]
    planes = projection_ref.shape[0]
    projection_ref[:done] = first_ref[...]
    held = []
    for k in range(planes):
        parts = sums(owns, core_in, y_in, k)
        gather_projection(parts, k, planes, projection_ref, done)
        held.append(jnp.concatenate([part[:, :384] for part in parts], axis=1))
    z = me_ref[0] // 4
    for k in range(planes):
        row = jnp.concatenate([held[k], projection_ref[plane_of(gray(z) ^ k)]], axis=1)
        if k:
            put(row, sent[k - 1], 0)
        else:
            own_b[...] = row


def join_kernel(kept_a, in_a, *refs):
    count = (len(refs) - 1) // 2
    blocks, own_a, sent = refs[:count], refs[count], refs[count + 1 :]
    first = add_received(kept_a, in_a)
    own_a[...] = first[0]
    for i, ref in enumerate(sent):
        ref[: blocks[i].shape[0]] = blocks[i][...]
        put(first[i + 1], ref, blocks[i].shape[0])


def finish_kernel(
    me_ref, after_ref, second_in, first_in, send_ref, node_ref, plus_ref, minus_ref, out_ref, came
):
    members, node_rows, _ = node_ref.shape
    pick = sent_selector(send_ref[0], node_rows).astype(bf16)
    from_swaps(came, me_ref[0] % 2, first_in, second_in)
    for m in range(members):
        pieces = [None] * 8
        for side, order in enumerate(((1, 4, 7), (0, 6, 5))):
            for i, k in enumerate(order):
                pieces[k] = came[side, m, i]
        pieces[2], pieces[3] = plus_ref[m, 0], minus_ref[m, 0]
        arriving = jnp.concatenate(pieces, axis=0)
        out_ref[m] = (node_ref[m] + nn(pick, arriving)).astype(bf16)


def weight_kernel(after_ref, own_a, own_b, *refs):
    received, out_ref = refs[:-1], refs[-1]
    a, b = own_a[...], own_b[...]
    blocks, more = b.shape[1] // 128, a.shape[1] // 128
    for k, ref in enumerate(received, 1):
        b = b + jnp.concatenate([ref[n] for n in range(blocks)], axis=1).astype(f32)
        if k % 2 == 0:
            a = a + jnp.concatenate([ref[blocks + n] for n in range(more)], axis=1).astype(f32)
    width = out_ref.shape[1] // 4
    group = 0
    for part, wide in ((a, a.shape[1]), (b, b.shape[1] - width)):
        for j in range(0, wide, 384):
            for n in range(3):
                at = n * width + group * 128
                out_ref[:, at : at + 128] = part[:, j + n * 128 : j + (n + 1) * 128]
            group += 1
    out_ref[:, 3 * width :] = b[:, b.shape[1] - width :]


def call(kernel, outs, operands, specs=None, scratch=(), limit=12, final=False, flops=10**6):
    specs = list(specs or ())
    specs += [pltpu.VMEM] * (len(operands) - len(specs))
    operands = [
        pltpu.with_memory_space_constraint(o, s) if s in (pltpu.HBM, pltpu.VMEM) else o
        for o, s in zip(operands, specs)
    ]
    return pl.pallas_call(
        kernel,
        out_shape=[jax.ShapeDtypeStruct(*o) if final else pltpu.VMEM(*o) for o in outs],
        in_specs=[pl.BlockSpec(memory_space=s) for s in specs],
        scratch_shapes=list(scratch),
        compiler_params=pltpu.CompilerParams(vmem_limit_bytes=limit * MIB),
        cost_estimate=pl.CostEstimate(flops=flops, bytes_accessed=10**4, transcendentals=0),
    )(*operands)


def body(
    node_features, out_grad, w_query, w_key, w_value, w_out, neighbours, neighbour_count, send_rows
):
    members, node_rows, width = node_features.shape
    count = lax.axis_size("patch")
    row_width = min(8, count // 4)
    _, adjacent, slots = send_rows.shape
    table = node_rows + adjacent * slots
    groups = width // 128
    me = lax.axis_index("patch")
    three = ((members, 3, slots, width), bf16)
    one = ((members, 1, slots, width), bf16)

    place = me.reshape(1)
    trio = pltpu.VMEM((2, *three[0]), bf16)
    to_plus, to_minus, own_right, own_left, x = call(
        functools.partial(gather_kernel, slots),
        [three, three, one, one, (node_features.shape, bf16)],
        (send_rows, node_features),
        specs=[pltpu.HBM] * 2,
        scratch=[pltpu.VMEM(send_rows.shape, jnp.int32), pltpu.SemaphoreType.DMA((2,))],
    )
    plus = shifted(to_plus, row_width)
    minus = shifted(to_minus, -row_width)
    square = ((width, width), bf16)
    counts = neighbour_count.reshape(1, node_rows)
    *loc, xt, wq, wk, wv, og, neigh, counts = call(
        functools.partial(local_kernel, groups),
        [((8, members, node_rows, 128), bf16)] * groups
        + [((members, width, node_rows), bf16), square, square, square, (out_grad.shape, bf16)]
        + [(neighbours.shape, jnp.int32), (counts.shape, jnp.int32)],
        (own_right, x, w_query, w_key, w_value, out_grad, neighbours, counts, w_out),
        specs=[pl.ANY, pltpu.VMEM] + [pltpu.HBM] * 7,
        scratch=[pltpu.VMEM((width, width), bf16), pltpu.SemaphoreType.DMA((7,))],
        limit=16,
    )
    outgoing = call(
        relay_kernel, [three, three], (place, loc[0], own_right, own_left, plus, minus),
        specs=[pltpu.SMEM, pl.ANY], scratch=[trio],
    )
    arrived = swap(outgoing, 1)
    (mask,) = call(
        mask_kernel, [((table, node_rows), f32)], (outgoing[1], neigh, counts), specs=[pl.ANY]
    )
    own_part = call(
        functools.partial(own_kernel, groups),
        [
            ((3, members, node_rows, 4 * node_rows), f32),
            ((2, members, 8, 4 * node_rows), f32),
        ]
        * groups,
        (*loc, mask),
    )
    *halo, xtf = call(
        halo_kernel,
        [((4, members, node_rows, 128), bf16)] * groups + [((members, width, table), bf16)],
        (place, *arrived[::-1], plus, minus, xt, wk, wv), specs=[pltpu.SMEM], scratch=[trio],
    )

    planes, rows = count // 4, width // count
    inner_planes = planes * 128 // width
    flip = [(i, i ^ 1) for i in range(count)]
    flop = [(i, i ^ 2) for i in range(count)]
    grads = []

    def attention(extra, which, together):
        wide = 512 * len(which)
        sends = [((2, planes, rows, wide), bf16)] if together else [((planes, rows, wide), bf16)] * 2
        outs = call(
            functools.partial(attention_kernel, len(extra), len(which)),
            [((planes, rows, wide), f32)] * 2
            + sends
            + [
                ((members, node_rows, 128), bf16),
                ((members, table, 128), bf16),
                ((members, table, 128), bf16),
            ]
            * len(which),
            (
                place, *extra, *[loc[g] for g in which], *[halo[g] for g in which],
                *[part for g in which for part in own_part[2 * g : 2 * g + 2]], mask, xtf, og,
            ),
            specs=[pltpu.SMEM] + [pl.ANY] * len(extra),
            scratch=[pltpu.VMEM((members, table - node_rows, 512), f32)] * 3
            + [
                pltpu.VMEM((planes, 2, 2, rows, 384), f32),
                pltpu.VMEM((inner_planes, 2, 2, rows, width), f32),
            ],
            limit=32,
        )
        sent = outs[2 : 2 + len(sends)]
        grads.extend(outs[2 + len(sends) :])
        arrived = [lax.ppermute(shard, "patch", flip) for shard in sent]
        return outs[0], outs[1], arrived[0], arrived[-1]

    half = groups - 1
    wide = 384 * half
    own_a, other, core_other, core_own = attention((), range(half), False)
    y_sent = (other + core_other.astype(f32)).astype(bf16)
    y_a = lax.ppermute(y_sent, "patch", flop)
    later = [attention((), range(half, groups), False)]
    own_b, other_b, core_other_b, core_own_b = zip(*later)
    node, to_plus, to_minus, own_right, own_left = call(
        functools.partial(node_kernel, groups, 0),
        [((members, node_rows, width), f32), three, three, one, one],
        (*grads[0::3], *grads[1::3], *grads[2::3], wq, wk, wv),
    )
    (y_sent,) = call(
        functools.partial(pack_kernel, len(later)), [(other_b[0].shape, bf16)],
        (node, *other_b, *core_other_b), specs=[pl.ANY],
    )
    y_b = lax.ppermute(y_sent, "patch", flop)
    from_plus = shifted(to_minus, -row_width)
    from_minus = shifted(to_plus, row_width)
    def exchange(sent, distance):
        return lax.ppermute(sent, "patch", along_z(count, distance))

    kept_a, out_a, sent_a = call(
        first_kernel,
        [
            ((planes // 2, rows, wide), f32),
            ((half * inner_planes, rows, width), f32),
            ((planes // 2 * wide // 128, rows, 128), bf16),
        ],
        (y_sent, own_a, core_own, y_a), specs=[pl.ANY], flops=2 * 10**10,
    )
    in_a = exchange(sent_a, 1)
    outgoing = call(
        relay_kernel, [three, three],
        (place, sent_a, own_right, own_left, from_plus, from_minus),
        specs=[pltpu.SMEM, pl.ANY], scratch=[trio],
    )
    back = swap(outgoing, 1)
    last = 384 * (groups - half) + width
    more, blocks = wide // 128, last // 128
    own_b, *sent = call(
        functools.partial(second_kernel, 1, len(later)),
        [((rows, last), f32)] + [((blocks, rows, 128), bf16)] * (planes - 1),
        (place, outgoing[0], out_a, y_b, *own_b, *core_own_b),
        specs=[pltpu.SMEM, pl.ANY],
        scratch=[pltpu.VMEM((planes, rows, width), f32)], flops=4 * 10**9,
    )
    own_a, *sent[1::2] = call(
        join_kernel,
        [((rows, wide), f32)] + [((blocks + more, rows, 128), bf16)] * (planes // 2 - 1),
        (kept_a, in_a, *sent[1::2]),
    )
    received = [exchange(shard, k) for k, shard in enumerate(sent, 1)]
    (node_grad,) = call(
        finish_kernel, [((members, node_rows, width), bf16)],
        (place, sent[0], *back[::-1], send_rows, node, from_plus, from_minus),
        specs=[pltpu.SMEM, pl.ANY], scratch=[trio], final=True,
    )
    (weight_grad,) = call(
        weight_kernel, [((rows, 4 * width), f32)], (node_grad, own_a, own_b, *received),
        specs=[pltpu.HBM], final=True,
    )
    return (node_grad, weight_grad)


def solution(mesh):
    in_specs = (
        P("groups", "patch", None),
        P("groups", "patch", None),
        P(),
        P(),
        P(),
        P(),
        P("patch", None),
        P("patch"),
        P("patch", None, None),
    )
    out_specs = (P("groups", "patch", None), P(("groups", "patch"), None))
    return jax.shard_map(body, mesh=mesh, in_specs=in_specs, out_specs=out_specs, check_vma=False)
```

```python
import functools
import math

import jax
import jax.numpy as jnp
from jax import lax
from jax.experimental import pallas as pl
from jax.experimental.pallas import tpu as pltpu
from jax.sharding import PartitionSpec as P

HEADS = 16
score_cap = 5.0
MIB = 1024 * 1024
f32 = jnp.float32
bf16 = jnp.bfloat16


def nn(a, b):
    return lax.dot_general(a, b, (((1,), (0,)), ((), ())), preferred_element_type=f32)


def nt(a, b):
    return lax.dot_general(a, b, (((1,), (1,)), ((), ())), preferred_element_type=f32)


def shifted(shard, by):
    count = lax.axis_size("patch")
    return lax.ppermute(shard, "patch", [(i, (i + by) % count) for i in range(count)])


def neighbours_apart(count, stride):
    first, second = [], []
    for i in range(count):
        up, down = (i + stride) % count, (i - stride) % count
        even = i // stride % 2 == 0
        first.append((i, up if even else down))
        second.append((i, down if even else up))
    return first, second


def swap(pair, stride):
    first, second = neighbours_apart(lax.axis_size("patch"), stride)
    later = lax.ppermute(pair[1], "patch", second)
    return [lax.ppermute(pair[0], "patch", first), later]


def to_swaps(both, odd, first_ref, second_ref):
    first_ref[...] = both[odd]
    second_ref[...] = both[1 - odd]


def from_swaps(both, odd, first_ref, second_ref):
    both[1 - odd] = first_ref[...]
    both[odd] = second_ref[...]


def sent_selector(send_rows, node_rows):
    adjacent, slots = send_rows.shape
    halo = adjacent * slots
    wide = jnp.concatenate([send_rows] * adjacent, axis=1)
    own = lax.broadcasted_iota(jnp.int32, (adjacent, halo), 1) // slots == lax.broadcasted_iota(
        jnp.int32, (adjacent, halo), 0
    )
    ids = jnp.sum(jnp.where(own, wide, 0), axis=0, keepdims=True)
    nodes = lax.broadcasted_iota(jnp.int32, (node_rows, halo), 0)
    return jnp.where(nodes == ids, 1.0, 0.0).astype(f32)


def gather_kernel(
    slots, send_hbm, x_hbm, plus_ref, minus_ref, right_ref, left_ref, x_ref, send_ref, sem
):
    copies = [
        pltpu.make_async_copy(send_hbm, send_ref, sem.at[0]),
        pltpu.make_async_copy(x_hbm, x_ref, sem.at[1]),
    ]
    for copy in copies:
        copy.start()
    copies[0].wait()
    members, node_rows, _ = x_ref.shape
    pick = sent_selector(send_ref[0], node_rows).T.astype(bf16)
    copies[1].wait()
    for m in range(members):
        rows = nn(pick, x_ref[m]).astype(bf16)

        def part(k):
            return rows[k * slots : (k + 1) * slots]

        for ref, order in ((plus_ref, (2, 6, 4)), (minus_ref, (3, 5, 7))):
            for i, k in enumerate(order):
                ref[m, i] = part(k)
        right_ref[m, 0] = part(0)
        left_ref[m, 0] = part(1)


def relay_kernel(
    me_ref, after_ref, own_right, own_left, plus_ref, minus_ref, first_ref, second_ref, both
):
    for side, own in enumerate((own_right, own_left)):
        both[side, :, 0:1] = own[...]
        both[side, :, 1:2] = plus_ref[:, 1 + side : 2 + side]
        both[side, :, 2:3] = minus_ref[:, 1 + side : 2 + side]
    to_swaps(both, me_ref[0] % 2, first_ref, second_ref)


def gray(z):
    return z ^ (z >> 1)


def plane_of(code):
    z = code
    for shift in range(1, 8):
        z = z ^ (code >> shift)
    return z


def along_z(count, distance):
    planes = count // 4
    return [(i, plane_of(gray(i // 4) ^ distance) * 4 + i % 4) for i in range(planes * 4)]


Q, K, V, G, QT, KT, VT, GT = range(8)


def local_kernel(groups, after_ref, x_ref, *refs):
    sources, loc_refs, xt_ref = refs[:7], refs[7 : 7 + groups], refs[7 + groups]
    copied, sem = refs[8 + groups : 15 + groups], refs[-1]
    copies = [
        pltpu.make_async_copy(source, target, sem.at[i])
        for i, (source, target) in enumerate(zip(sources, copied))
    ]
    for copy in copies:
        copy.start()
    members, node_rows, width = x_ref.shape
    x = x_ref[...].reshape(members * node_rows, width)
    for m in range(members):
        xt_ref[m] = x_ref[m].T

    def put(rows, kind):
        for m in range(members):
            for g, ref in enumerate(loc_refs):
                block = rows[m * node_rows : (m + 1) * node_rows, g * 128 : (g + 1) * 128]
                ref[kind, m] = block
                ref[kind + 4, m] = block.T

    wq_ref, wk_ref, wv_ref, og_ref, _, _, wo_ref = copied
    for kind, ref in enumerate((wq_ref, wk_ref, wv_ref)):
        copies[kind].wait()
        put(nn(x, ref[...]).astype(bf16), kind)
    for copy in copies[3:]:
        copy.wait()
    og = og_ref[...].reshape(members * node_rows, width)
    put(nt(og, wo_ref[...]).astype(bf16), G)


def mask_kernel(after_ref, neigh_ref, count_ref, mask_ref):
    neigh = neigh_ref[...].T
    slots, node_rows = neigh.shape
    table = mask_ref.shape[0]
    order = lax.broadcasted_iota(jnp.int32, neigh.shape, 0)
    tail = jnp.where(order >= count_ref[...], neigh, -1)[slots // 2 :]
    half = table // 2
    for part in range(2):
        columns = lax.broadcasted_iota(jnp.int32, (half, node_rows), 0) + part * half
        kept = jnp.ones((half, node_rows), f32)
        for j in range(slots // 2):
            kept = jnp.where(tail[j : j + 1] == columns, 0.0, kept)
        mask_ref[part * half : (part + 1) * half] = kept


def halo_kernel(
    me_ref, second_in, first_in, plus_ref, minus_ref, xt_ref, wk_ref, wv_ref, *refs
):
    halo_refs, xtf_ref, both = refs[:-2], refs[-2], refs[-1]
    members, _, node_rows = xt_ref.shape
    from_swaps(both, me_ref[0] % 2, first_in, second_in)
    for m in range(members):
        pieces = [None] * 8
        for side, order in enumerate(((0, 6, 5), (1, 4, 7))):
            for i, k in enumerate(order):
                pieces[k] = both[side, m, i]
        pieces[2] = plus_ref[m, 0]
        pieces[3] = minus_ref[m, 0]
        halo = jnp.concatenate(pieces, axis=0)
        xtf_ref[m, :, :node_rows] = xt_ref[m]
        xtf_ref[m, :, node_rows:] = halo.T
        for kind, w_ref in enumerate((wk_ref, wv_ref)):
            rows = nn(halo, w_ref[...]).astype(bf16)
            for g, ref in enumerate(halo_refs):
                block = rows[:, g * 128 : (g + 1) * 128]
                ref[kind, m] = block
                ref[kind + 2, m] = block.T


STRIP = 64


def by_head_t(block, head):
    row_head = lax.broadcasted_iota(jnp.int32, block.shape, 0) // head
    zero = jnp.zeros_like(block)
    return jnp.concatenate(
        [jnp.where(row_head == h, block, zero) for h in range(block.shape[0] // head)], axis=1
    )


def by_head_n(block, head):
    lane_head = lax.broadcasted_iota(jnp.int32, block.shape, 1) // head
    zero = jnp.zeros_like(block)
    return jnp.concatenate(
        [jnp.where(lane_head == h, block, zero) for h in range(block.shape[1] // head)], axis=0
    )


def unnormalised(scale, score, grad, slope, m, lanes, mask_ref, start):
    columns, node_rows = score.shape[1], mask_ref.shape[1]
    den = jnp.zeros((8, node_rows), f32)
    inner = jnp.zeros((8, node_rows), f32)
    for c in range(0, columns, STRIP):
        box = (m, slice(c, c + STRIP), lanes)
        t = jnp.tanh(score[box] * (scale / score_cap))
        e = jnp.exp2(t * (score_cap / math.log(2.0))) * mask_ref[start + c : start + c + STRIP]
        den = den + jnp.sum(e.reshape(STRIP // 8, 8, node_rows), axis=0)
        inner = inner + jnp.sum((e * grad[box]).reshape(STRIP // 8, 8, node_rows), axis=0)
        score[box] = e
        slope[box] = e * (scale - scale * (t * t))
    return den, inner


def own_kernel(groups, *refs):
    locs, mask_ref, outs = refs[:groups], refs[groups], refs[groups + 1 :]
    _, members, node_rows, _ = locs[0].shape
    head = 128 * groups // HEADS
    scale = 1.0 / math.sqrt(head)
    for g, loc in enumerate(locs):
        own, totals = outs[2 * g : 2 * g + 2]
        score, grad, slope = own.at[0], own.at[1], own.at[2]
        for m in range(members):
            score[m] = nn(loc[K, m], by_head_t(loc[QT, m], head))
            grad[m] = nn(loc[V, m], by_head_t(loc[GT, m], head))
        for m in range(members):
            for h in range(128 // head):
                lanes = slice(h * node_rows, (h + 1) * node_rows)
                den, inner = unnormalised(scale, score, grad, slope, m, lanes, mask_ref, 0)
                totals[0, m, :, lanes] = den
                totals[1, m, :, lanes] = inner


def attention_kernel(extra, here, me_ref, *refs):
    refs = refs[extra:]
    locs, halos, owns = refs[:here], refs[here : 2 * here], refs[2 * here : 4 * here]
    refs = refs[4 * here :]
    mask_ref, xtf, og_ref = refs[:3]
    split = 7 if len(refs) == 15 + 3 * (here - 1) else 6
    outs, grads, scratch = refs[3:split], refs[split : split + 3 * here], refs[split + 3 * here :]
    if split == 6:
        outs = (*outs[:2], outs[2].at[0], outs[2].at[1])
    for i in range(here):
        attend(
            me_ref, locs[i], halos[i], owns[2 * i : 2 * i + 2], mask_ref, xtf, og_ref, outs, 512 * i,
            grads[3 * i : 3 * i + 3], scratch,
        )


def attend(me_ref, loc, halo, own, mask_ref, xtf, og_ref, out_refs, at, grad_refs, scratch):
    own_ref, other_ref, send_other, send_own = out_refs
    dq_ref, dk_ref, dv_ref = grad_refs
    score, grad, slope, dw, wos = scratch
    _, members, node_rows, _ = loc.shape
    table = mask_ref.shape[0]
    width = og_ref.shape[2]
    head = width // HEADS
    per = 128 // head
    scale = 1.0 / math.sqrt(head)

    own, totals = own
    for m in range(members):
        score[m] = nn(halo[0, m], by_head_t(loc[QT, m], head))
        grad[m] = nn(halo[1, m], by_head_t(loc[GT, m], head))

    wo_total = None
    kv_total = None
    q_total = None
    for m in range(members):
        probs = []
        for h in range(per):
            lanes = slice(h * node_rows, (h + 1) * node_rows)
            den, inner = unnormalised(scale, score, grad, slope, m, lanes, mask_ref, node_rows)
            r = 1.0 / jnp.sum(den + totals[0, m, :, lanes], axis=0, keepdims=True)
            inner = jnp.sum(inner + totals[1, m, :, lanes], axis=0, keepdims=True) * r
            column = []
            scores = []
            for e, g, w in ((own.at[0], own.at[1], own.at[2]), (score, grad, slope)):
                for c in range(0, e.shape[1], STRIP):
                    box = (m, slice(c, c + STRIP), lanes)
                    column.append((e[box] * r).astype(bf16))
                    scores.append(((w[box] * r) * (g[box] - inner)).astype(bf16))
            probs.append((jnp.concatenate(column, axis=0), jnp.concatenate(scores, axis=0)))
        pb = jnp.concatenate([p for p, _ in probs], axis=1)
        ds = jnp.concatenate([s for _, s in probs], axis=1)
        ktg = jnp.concatenate([loc[KT, m], halo[2, m]], axis=1)
        vtg = jnp.concatenate([loc[VT, m], halo[3, m]], axis=1)
        att, dqt = [], []
        for h in range(0, per, 2):
            lanes = slice(h * node_rows, (h + 2) * node_rows)
            rows = slice(h * head, (h + 2) * head)
            a = nn(vtg[rows], pb[:, lanes])
            b = nn(ktg[rows], ds[:, lanes])
            for j in range(2):
                inside = (slice(j * head, (j + 1) * head), slice(j * node_rows, (j + 1) * node_rows))
                att.append(a[inside].astype(bf16))
                dqt.append(b[inside].astype(bf16))
        att = jnp.concatenate(att, axis=0)
        dq = jnp.concatenate(dqt, axis=0).T
        dk = nn(ds, by_head_n(loc[Q, m], head)).astype(bf16)
        dv = nn(pb, by_head_n(loc[G, m], head)).astype(bf16)
        dq_ref[m], dk_ref[m], dv_ref[m] = dq, dk, dv
        wo_term = nn(att, og_ref[m])
        kv_term = nn(xtf[m], jnp.concatenate([dk, dv], axis=1))
        q_term = nn(xtf[m, :, :node_rows], dq)
        wo_total = wo_term if m == 0 else wo_total + wo_term
        kv_total = kv_term if m == 0 else kv_total + kv_term
        q_total = q_term if m == 0 else q_total + q_term

    planes, _, _, rows, _ = dw.shape
    inner_planes = wos.shape[0]
    dw[:, :, :, :, :128] = q_total.reshape(planes, 2, 2, rows, 128)
    dw[:, :, :, :, 128:] = kv_total.reshape(planes, 2, 2, rows, 256)
    wos[...] = wo_total.reshape(inner_planes, 2, 2, rows, width)
    me = me_ref[0]
    c, y, z = me % 2, (me // 2) % 2, me // 4
    qkv = slice(at, at + 384)
    for k in range(planes):
        zk = plane_of(gray(z) ^ k)
        own_ref[k, :, qkv] = dw[zk, y, c]
        other_ref[k, :, qkv] = dw[zk, 1 - y, c]
        send_other[k, :, qkv] = dw[zk, 1 - y, 1 - c].astype(bf16)
        send_own[k, :, qkv] = dw[zk, y, 1 - c].astype(bf16)
    last = slice(at + 384, at + 512)
    for i in range(inner_planes):
        for n in range(width // 128):
            k = n * inner_planes + i
            lanes = slice(n * 128, (n + 1) * 128)
            own_ref[k, :, last] = wos[i, y, c, :, lanes]
            other_ref[k, :, last] = wos[i, 1 - y, c, :, lanes]
            send_other[k, :, last] = wos[i, 1 - y, 1 - c, :, lanes].astype(bf16)
            send_own[k, :, last] = wos[i, y, 1 - c, :, lanes].astype(bf16)


def node_kernel(groups, skip, *refs):
    refs = refs[skip:]
    dqs, dks, dvs = refs[:groups], refs[groups : 2 * groups], refs[2 * groups : 3 * groups]
    wq_ref, wk_ref, wv_ref, node_ref, plus_ref, minus_ref, right_ref, left_ref = refs[3 * groups :]
    members, node_rows, _ = dqs[0].shape
    slots = plus_ref.shape[2]

    def whole(parts, m):
        return jnp.concatenate([part[m] for part in parts], axis=1)

    for m in range(members):
        spread = nt(whole(dks, m), wk_ref[...]) + nt(whole(dvs, m), wv_ref[...])
        node_ref[m] = spread[:node_rows] + nt(whole(dqs, m), wq_ref[...])
        halo = spread[node_rows:].astype(bf16)
        for ref, order in (
            (plus_ref, (3, 7, 5)),
            (minus_ref, (2, 4, 6)),
            (right_ref, (1,)),
            (left_ref, (0,)),
        ):
            for i, k in enumerate(order):
                ref[m, i] = halo[k * slots : (k + 1) * slots]


def sums(owns, core_in, y_in, k):
    total = jnp.concatenate(
        [
            own[k] + (core[1, k] if len(core.shape) == 4 else core[k]).astype(f32)
            for own, core in zip(owns, core_in)
        ],
        axis=1,
    ) + y_in[k].astype(f32)
    return [total[:, at : at + 512] for at in range(0, total.shape[1], 512)]


def gather_projection(parts, k, planes, projection_ref, start):
    inner_planes = planes * 128 // projection_ref.shape[2]
    quarter, inner = divmod(k, inner_planes)
    for i, part in enumerate(parts):
        plane = start + i * inner_planes + inner
        projection_ref[plane, :, quarter * 128 : (quarter + 1) * 128] = part[:, 384:]


def pack_kernel(pieces, *refs):
    for i, (ref, core) in enumerate(zip(refs[:pieces], refs[pieces:-1])):
        arrived = core[0] if len(core.shape) == 4 else core[...]
        refs[-1][:, :, i * 512 : (i + 1) * 512] = (ref[...] + arrived.astype(f32)).astype(bf16)


def halve(rows, kept_ref, sent_ref):
    for i, row in enumerate(rows):
        if i % 2 == 0:
            kept_ref[i // 2] = row
            continue
        pieces = row.shape[1] // 128
        for n in range(pieces):
            sent_ref[i // 2 * pieces + n] = row[:, n * 128 : (n + 1) * 128].astype(bf16)


def add_received(kept_ref, received_ref):
    planes, _, wide = kept_ref.shape
    pieces = wide // 128
    return [
        kept_ref[i]
        + jnp.concatenate([received_ref[i * pieces + n] for n in range(pieces)], axis=1).astype(f32)
        for i in range(planes)
    ]


def first_kernel(after_ref, own, core_in, y_in, kept_ref, projection_ref, sent_ref):
    planes = own.shape[0]
    rows = []
    for k in range(planes):
        parts = sums([own], [core_in], y_in, k)
        gather_projection(parts, k, planes, projection_ref, 0)
        rows.append(jnp.concatenate([part[:, :384] for part in parts], axis=1))
    halve(rows, kept_ref, sent_ref)


def put(row, ref, at):
    for n in range(row.shape[1] // 128):
        ref[at + n] = row[:, n * 128 : (n + 1) * 128].astype(bf16)


def second_kernel(skip, pieces, me_ref, *refs):
    refs = refs[skip:]
    first_ref, y_in = refs[:2]
    owns, core_in = refs[2 : 2 + pieces], refs[2 + pieces : 2 + 2 * pieces]
    own_b, *sent = refs[2 + 2 * pieces : -1]
    projection_ref = refs[-1]
    done = first_ref.shape[0]
    planes = projection_ref.shape[0]
    projection_ref[:done] = first_ref[...]
    held = []
    for k in range(planes):
        parts = sums(owns, core_in, y_in, k)
        gather_projection(parts, k, planes, projection_ref, done)
        held.append(jnp.concatenate([part[:, :384] for part in parts], axis=1))
    z = me_ref[0] // 4
    for k in range(planes):
        row = jnp.concatenate([held[k], projection_ref[plane_of(gray(z) ^ k)]], axis=1)
        if k:
            put(row, sent[k - 1], 0)
        else:
            own_b[...] = row


def join_kernel(kept_a, in_a, *refs):
    count = (len(refs) - 1) // 2
    blocks, own_a, sent = refs[:count], refs[count], refs[count + 1 :]
    first = add_received(kept_a, in_a)
    own_a[...] = first[0]
    for i, ref in enumerate(sent):
        ref[: blocks[i].shape[0]] = blocks[i][...]
        put(first[i + 1], ref, blocks[i].shape[0])


def finish_kernel(
    me_ref, after_ref, second_in, first_in, send_ref, node_ref, plus_ref, minus_ref, out_ref, came
):
    members, node_rows, _ = node_ref.shape
    pick = sent_selector(send_ref[0], node_rows).astype(bf16)
    from_swaps(came, me_ref[0] % 2, first_in, second_in)
    for m in range(members):
        pieces = [None] * 8
        for side, order in enumerate(((1, 4, 7), (0, 6, 5))):
            for i, k in enumerate(order):
                pieces[k] = came[side, m, i]
        pieces[2], pieces[3] = plus_ref[m, 0], minus_ref[m, 0]
        arriving = jnp.concatenate(pieces, axis=0)
        out_ref[m] = (node_ref[m] + nn(pick, arriving)).astype(bf16)


def weight_kernel(after_ref, own_a, own_b, *refs):
    received, out_ref = refs[:-1], refs[-1]
    a, b = own_a[...], own_b[...]
    blocks, more = b.shape[1] // 128, a.shape[1] // 128
    for k, ref in enumerate(received, 1):
        b = b + jnp.concatenate([ref[n] for n in range(blocks)], axis=1).astype(f32)
        if k % 2 == 0:
            a = a + jnp.concatenate([ref[blocks + n] for n in range(more)], axis=1).astype(f32)
    width = out_ref.shape[1] // 4
    group = 0
    for part, wide in ((a, a.shape[1]), (b, b.shape[1] - width)):
        for j in range(0, wide, 384):
            for n in range(3):
                at = n * width + group * 128
                out_ref[:, at : at + 128] = part[:, j + n * 128 : j + (n + 1) * 128]
            group += 1
    out_ref[:, 3 * width :] = b[:, b.shape[1] - width :]


def call(kernel, outs, operands, specs=None, scratch=(), limit=12, final=False, flops=10**6):
    specs = list(specs or ())
    specs += [pltpu.VMEM] * (len(operands) - len(specs))
    operands = [
        pltpu.with_memory_space_constraint(o, s) if s in (pltpu.HBM, pltpu.VMEM) else o
        for o, s in zip(operands, specs)
    ]
    return pl.pallas_call(
        kernel,
        out_shape=[jax.ShapeDtypeStruct(*o) if final else pltpu.VMEM(*o) for o in outs],
        in_specs=[pl.BlockSpec(memory_space=s) for s in specs],
        scratch_shapes=list(scratch),
        compiler_params=pltpu.CompilerParams(vmem_limit_bytes=limit * MIB),
        cost_estimate=pl.CostEstimate(flops=flops, bytes_accessed=10**4, transcendentals=0),
    )(*operands)


def body(
    node_features, out_grad, w_query, w_key, w_value, w_out, neighbours, neighbour_count, send_rows
):
    members, node_rows, width = node_features.shape
    count = lax.axis_size("patch")
    row_width = min(8, count // 4)
    _, adjacent, slots = send_rows.shape
    table = node_rows + adjacent * slots
    groups = width // 128
    me = lax.axis_index("patch")
    three = ((members, 3, slots, width), bf16)
    one = ((members, 1, slots, width), bf16)

    place = me.reshape(1)
    trio = pltpu.VMEM((2, *three[0]), bf16)
    to_plus, to_minus, own_right, own_left, x = call(
        functools.partial(gather_kernel, slots),
        [three, three, one, one, (node_features.shape, bf16)],
        (send_rows, node_features),
        specs=[pltpu.HBM] * 2,
        scratch=[pltpu.VMEM(send_rows.shape, jnp.int32), pltpu.SemaphoreType.DMA((2,))],
    )
    plus = shifted(to_plus, row_width)
    minus = shifted(to_minus, -row_width)
    square = ((width, width), bf16)
    counts = neighbour_count.reshape(1, node_rows)
    *loc, xt, wq, wk, wv, og, neigh, counts = call(
        functools.partial(local_kernel, groups),
        [((8, members, node_rows, 128), bf16)] * groups
        + [((members, width, node_rows), bf16), square, square, square, (out_grad.shape, bf16)]
        + [(neighbours.shape, jnp.int32), (counts.shape, jnp.int32)],
        (own_right, x, w_query, w_key, w_value, out_grad, neighbours, counts, w_out),
        specs=[pl.ANY, pltpu.VMEM] + [pltpu.HBM] * 7,
        scratch=[pltpu.VMEM((width, width), bf16), pltpu.SemaphoreType.DMA((7,))],
        limit=16,
    )
    outgoing = call(
        relay_kernel, [three, three], (place, loc[0], own_right, own_left, plus, minus),
        specs=[pltpu.SMEM, pl.ANY], scratch=[trio],
    )
    arrived = swap(outgoing, 1)
    (mask,) = call(
        mask_kernel, [((table, node_rows), f32)], (outgoing[1], neigh, counts), specs=[pl.ANY]
    )
    own_part = call(
        functools.partial(own_kernel, groups),
        [
            ((3, members, node_rows, 4 * node_rows), f32),
            ((2, members, 8, 4 * node_rows), f32),
        ]
        * groups,
        (*loc, mask),
    )
    *halo, xtf = call(
        halo_kernel,
        [((4, members, node_rows, 128), bf16)] * groups + [((members, width, table), bf16)],
        (place, *arrived[::-1], plus, minus, xt, wk, wv), specs=[pltpu.SMEM], scratch=[trio],
    )

    planes, rows = count // 4, width // count
    inner_planes = planes * 128 // width
    flip = [(i, i ^ 1) for i in range(count)]
    flop = [(i, i ^ 2) for i in range(count)]
    grads = []

    def attention(extra, which, together):
        wide = 512 * len(which)
        sends = [((2, planes, rows, wide), bf16)] if together else [((planes, rows, wide), bf16)] * 2
        outs = call(
            functools.partial(attention_kernel, len(extra), len(which)),
            [((planes, rows, wide), f32)] * 2
            + sends
            + [
                ((members, node_rows, 128), bf16),
                ((members, table, 128), bf16),
                ((members, table, 128), bf16),
            ]
            * len(which),
            (
                place, *extra, *[loc[g] for g in which], *[halo[g] for g in which],
                *[part for g in which for part in own_part[2 * g : 2 * g + 2]], mask, xtf, og,
            ),
            specs=[pltpu.SMEM] + [pl.ANY] * len(extra),
            scratch=[pltpu.VMEM((members, table - node_rows, 512), f32)] * 3
            + [
                pltpu.VMEM((planes, 2, 2, rows, 384), f32),
                pltpu.VMEM((inner_planes, 2, 2, rows, width), f32),
            ],
            limit=32,
        )
        sent = outs[2 : 2 + len(sends)]
        grads.extend(outs[2 + len(sends) :])
        arrived = [lax.ppermute(shard, "patch", flip) for shard in sent]
        return outs[0], outs[1], arrived[0], arrived[-1]

    half = groups - 1
    wide = 384 * half
    own_a, other, core_other, core_own = attention((), range(half), False)
    y_sent = (other + core_other.astype(f32)).astype(bf16)
    y_a = lax.ppermute(y_sent, "patch", flop)
    later = [attention((), range(half, groups), False)]
    own_b, other_b, core_other_b, core_own_b = zip(*later)
    (y_sent,) = call(
        functools.partial(pack_kernel, len(later)), [(other_b[0].shape, bf16)],
        (*other_b, *core_other_b),
    )
    y_b = lax.ppermute(y_sent, "patch", flop)
    node, to_plus, to_minus, own_right, own_left = call(
        functools.partial(node_kernel, groups, 1),
        [((members, node_rows, width), f32), three, three, one, one],
        (y_sent, *grads[0::3], *grads[1::3], *grads[2::3], wq, wk, wv),
        specs=[pl.ANY],
    )
    from_plus = shifted(to_minus, -row_width)
    from_minus = shifted(to_plus, row_width)
    def exchange(sent, distance):
        return lax.ppermute(sent, "patch", along_z(count, distance))

    kept_a, out_a, sent_a = call(
        first_kernel,
        [
            ((planes // 2, rows, wide), f32),
            ((half * inner_planes, rows, width), f32),
            ((planes // 2 * wide // 128, rows, 128), bf16),
        ],
        (node, own_a, core_own, y_a), specs=[pl.ANY], flops=2 * 10**10,
    )
    in_a = exchange(sent_a, 1)
    outgoing = call(
        relay_kernel, [three, three],
        (place, sent_a, own_right, own_left, from_plus, from_minus),
        specs=[pltpu.SMEM, pl.ANY], scratch=[trio],
    )
    back = swap(outgoing, 1)
    last = 384 * (groups - half) + width
    more, blocks = wide // 128, last // 128
    own_b, *sent = call(
        functools.partial(second_kernel, 1, len(later)),
        [((rows, last), f32)] + [((blocks, rows, 128), bf16)] * (planes - 1),
        (place, outgoing[0], out_a, y_b, *own_b, *core_own_b),
        specs=[pltpu.SMEM, pl.ANY],
        scratch=[pltpu.VMEM((planes, rows, width), f32)], flops=4 * 10**9,
    )
    own_a, *sent[1::2] = call(
        join_kernel,
        [((rows, wide), f32)] + [((blocks + more, rows, 128), bf16)] * (planes // 2 - 1),
        (kept_a, in_a, *sent[1::2]), flops=2 * 10**10,
    )
    received = [exchange(shard, k) for k, shard in enumerate(sent, 1)]
    (node_grad,) = call(
        finish_kernel, [((members, node_rows, width), bf16)],
        (place, sent[0], *back[::-1], send_rows, node, from_plus, from_minus),
        specs=[pltpu.SMEM, pl.ANY], scratch=[trio], final=True, flops=2 * 10**10,
    )
    (weight_grad,) = call(
        weight_kernel, [((rows, 4 * width), f32)], (node_grad, own_a, own_b, *received),
        specs=[pltpu.HBM], final=True,
    )
    return (node_grad, weight_grad)


def solution(mesh):
    in_specs = (
        P("groups", "patch", None),
        P("groups", "patch", None),
        P(),
        P(),
        P(),
        P(),
        P("patch", None),
        P("patch"),
        P("patch", None, None),
    )
    out_specs = (P("groups", "patch", None), P(("groups", "patch"), None))
    return jax.shard_map(body, mesh=mesh, in_specs=in_specs, out_specs=out_specs, check_vma=False)
```

```python
import functools
import math

import jax
import jax.numpy as jnp
from jax import lax
from jax.experimental import pallas as pl
from jax.experimental.pallas import tpu as pltpu
from jax.sharding import PartitionSpec as P

HEADS = 16
score_cap = 5.0
MIB = 1024 * 1024
f32 = jnp.float32
bf16 = jnp.bfloat16


def nn(a, b):
    return lax.dot_general(a, b, (((1,), (0,)), ((), ())), preferred_element_type=f32)


def nt(a, b):
    return lax.dot_general(a, b, (((1,), (1,)), ((), ())), preferred_element_type=f32)


def shifted(shard, by):
    count = lax.axis_size("patch")
    return lax.ppermute(shard, "patch", [(i, (i + by) % count) for i in range(count)])


def neighbours_apart(count, stride):
    first, second = [], []
    for i in range(count):
        up, down = (i + stride) % count, (i - stride) % count
        even = i // stride % 2 == 0
        first.append((i, up if even else down))
        second.append((i, down if even else up))
    return first, second


def swap(pair, stride):
    first, second = neighbours_apart(lax.axis_size("patch"), stride)
    later = lax.ppermute(pair[1], "patch", second)
    return [lax.ppermute(pair[0], "patch", first), later]


def to_swaps(both, odd, first_ref, second_ref):
    first_ref[...] = both[odd]
    second_ref[...] = both[1 - odd]


def from_swaps(both, odd, first_ref, second_ref):
    both[1 - odd] = first_ref[...]
    both[odd] = second_ref[...]


def sent_selector(send_rows, node_rows):
    adjacent, slots = send_rows.shape
    halo = adjacent * slots
    wide = jnp.concatenate([send_rows] * adjacent, axis=1)
    own = lax.broadcasted_iota(jnp.int32, (adjacent, halo), 1) // slots == lax.broadcasted_iota(
        jnp.int32, (adjacent, halo), 0
    )
    ids = jnp.sum(jnp.where(own, wide, 0), axis=0, keepdims=True)
    nodes = lax.broadcasted_iota(jnp.int32, (node_rows, halo), 0)
    return jnp.where(nodes == ids, 1.0, 0.0).astype(f32)


def gather_kernel(
    slots, send_hbm, x_hbm, plus_ref, minus_ref, right_ref, left_ref, x_ref, send_ref, sem
):
    copies = [
        pltpu.make_async_copy(send_hbm, send_ref, sem.at[0]),
        pltpu.make_async_copy(x_hbm, x_ref, sem.at[1]),
    ]
    for copy in copies:
        copy.start()
    copies[0].wait()
    members, node_rows, _ = x_ref.shape
    pick = sent_selector(send_ref[0], node_rows).T.astype(bf16)
    copies[1].wait()
    for m in range(members):
        rows = nn(pick, x_ref[m]).astype(bf16)

        def part(k):
            return rows[k * slots : (k + 1) * slots]

        for ref, order in ((plus_ref, (2, 6, 4)), (minus_ref, (3, 5, 7))):
            for i, k in enumerate(order):
                ref[m, i] = part(k)
        right_ref[m, 0] = part(0)
        left_ref[m, 0] = part(1)


def relay_kernel(
    me_ref, after_ref, minus_ref, plus_ref, own_right, own_left, first_ref, second_ref, both
):
    for side, own in enumerate((own_right, own_left)):
        both[side, :, 0:1] = own[...]
        both[side, :, 1:2] = plus_ref[:, 1 + side : 2 + side]
        both[side, :, 2:3] = minus_ref[:, 1 + side : 2 + side]
    to_swaps(both, me_ref[0] % 2, first_ref, second_ref)


def gray(z):
    return z ^ (z >> 1)


def plane_of(code):
    z = code
    for shift in range(1, 8):
        z = z ^ (code >> shift)
    return z


def along_z(count, distance):
    planes = count // 4
    return [(i, plane_of(gray(i // 4) ^ distance) * 4 + i % 4) for i in range(planes * 4)]


Q, K, V, G, QT, KT, VT, GT = range(8)


def local_kernel(groups, after_ref, x_ref, *refs):
    sources, loc_refs, xt_ref = refs[:7], refs[7 : 7 + groups], refs[7 + groups]
    copied, sem = refs[8 + groups : 15 + groups], refs[-1]
    copies = [
        pltpu.make_async_copy(source, target, sem.at[i])
        for i, (source, target) in enumerate(zip(sources, copied))
    ]
    for copy in copies:
        copy.start()
    members, node_rows, width = x_ref.shape
    x = x_ref[...].reshape(members * node_rows, width)
    for m in range(members):
        xt_ref[m] = x_ref[m].T

    def put(rows, kind):
        for m in range(members):
            for g, ref in enumerate(loc_refs):
                block = rows[m * node_rows : (m + 1) * node_rows, g * 128 : (g + 1) * 128]
                ref[kind, m] = block
                ref[kind + 4, m] = block.T

    wq_ref, wk_ref, wv_ref, og_ref, _, _, wo_ref = copied
    for kind, ref in enumerate((wq_ref, wk_ref, wv_ref)):
        copies[kind].wait()
        put(nn(x, ref[...]).astype(bf16), kind)
    for copy in copies[3:]:
        copy.wait()
    og = og_ref[...].reshape(members * node_rows, width)
    put(nt(og, wo_ref[...]).astype(bf16), G)


def mask_kernel(after_ref, neigh_ref, count_ref, mask_ref):
    neigh = neigh_ref[...].T
    slots, node_rows = neigh.shape
    table = mask_ref.shape[0]
    order = lax.broadcasted_iota(jnp.int32, neigh.shape, 0)
    tail = jnp.where(order >= count_ref[...], neigh, -1)[slots // 2 :]
    half = table // 2
    for part in range(2):
        columns = lax.broadcasted_iota(jnp.int32, (half, node_rows), 0) + part * half
        kept = jnp.ones((half, node_rows), f32)
        for j in range(slots // 2):
            kept = jnp.where(tail[j : j + 1] == columns, 0.0, kept)
        mask_ref[part * half : (part + 1) * half] = kept


def halo_kernel(
    me_ref, second_in, first_in, plus_ref, minus_ref, xt_ref, wk_ref, wv_ref, *refs
):
    halo_refs, xtf_ref, both = refs[:-2], refs[-2], refs[-1]
    members, _, node_rows = xt_ref.shape
    from_swaps(both, me_ref[0] % 2, first_in, second_in)
    for m in range(members):
        pieces = [None] * 8
        for side, order in enumerate(((0, 6, 5), (1, 4, 7))):
            for i, k in enumerate(order):
                pieces[k] = both[side, m, i]
        pieces[2] = plus_ref[m, 0]
        pieces[3] = minus_ref[m, 0]
        halo = jnp.concatenate(pieces, axis=0)
        xtf_ref[m, :, :node_rows] = xt_ref[m]
        xtf_ref[m, :, node_rows:] = halo.T
        for kind, w_ref in enumerate((wk_ref, wv_ref)):
            rows = nn(halo, w_ref[...]).astype(bf16)
            for g, ref in enumerate(halo_refs):
                block = rows[:, g * 128 : (g + 1) * 128]
                ref[kind, m] = block
                ref[kind + 2, m] = block.T


STRIP = 64


def by_head_t(block, head):
    row_head = lax.broadcasted_iota(jnp.int32, block.shape, 0) // head
    zero = jnp.zeros_like(block)
    return jnp.concatenate(
        [jnp.where(row_head == h, block, zero) for h in range(block.shape[0] // head)], axis=1
    )


def by_head_n(block, head):
    lane_head = lax.broadcasted_iota(jnp.int32, block.shape, 1) // head
    zero = jnp.zeros_like(block)
    return jnp.concatenate(
        [jnp.where(lane_head == h, block, zero) for h in range(block.shape[1] // head)], axis=0
    )


def unnormalised(scale, score, grad, slope, m, lanes, mask_ref, start):
    columns, node_rows = score.shape[1], mask_ref.shape[1]
    den = jnp.zeros((8, node_rows), f32)
    inner = jnp.zeros((8, node_rows), f32)
    for c in range(0, columns, STRIP):
        box = (m, slice(c, c + STRIP), lanes)
        t = jnp.tanh(score[box] * (scale / score_cap))
        e = jnp.exp2(t * (score_cap / math.log(2.0))) * mask_ref[start + c : start + c + STRIP]
        den = den + jnp.sum(e.reshape(STRIP // 8, 8, node_rows), axis=0)
        inner = inner + jnp.sum((e * grad[box]).reshape(STRIP // 8, 8, node_rows), axis=0)
        score[box] = e
        slope[box] = e * (scale - scale * (t * t))
    return den, inner


def own_kernel(groups, *refs):
    locs, mask_ref, outs = refs[:groups], refs[groups], refs[groups + 1 :]
    _, members, node_rows, _ = locs[0].shape
    head = 128 * groups // HEADS
    scale = 1.0 / math.sqrt(head)
    for g, loc in enumerate(locs):
        own, totals = outs[2 * g : 2 * g + 2]
        score, grad, slope = own.at[0], own.at[1], own.at[2]
        for m in range(members):
            score[m] = nn(loc[K, m], by_head_t(loc[QT, m], head))
            grad[m] = nn(loc[V, m], by_head_t(loc[GT, m], head))
        for m in range(members):
            for h in range(128 // head):
                lanes = slice(h * node_rows, (h + 1) * node_rows)
                den, inner = unnormalised(scale, score, grad, slope, m, lanes, mask_ref, 0)
                totals[0, m, :, lanes] = den
                totals[1, m, :, lanes] = inner


def attention_kernel(extra, here, me_ref, *refs):
    refs = refs[extra:]
    locs, halos, owns = refs[:here], refs[here : 2 * here], refs[2 * here : 4 * here]
    refs = refs[4 * here :]
    mask_ref, xtf, og_ref = refs[:3]
    split = 7 if len(refs) == 15 + 3 * (here - 1) else 6
    outs, grads, scratch = refs[3:split], refs[split : split + 3 * here], refs[split + 3 * here :]
    if split == 6:
        outs = (*outs[:2], outs[2].at[0], outs[2].at[1])
    for i in range(here):
        attend(
            me_ref, locs[i], halos[i], owns[2 * i : 2 * i + 2], mask_ref, xtf, og_ref, outs, 512 * i,
            grads[3 * i : 3 * i + 3], scratch,
        )


def attend(me_ref, loc, halo, own, mask_ref, xtf, og_ref, out_refs, at, grad_refs, scratch):
    own_ref, other_ref, send_other, send_own = out_refs
    dq_ref, dk_ref, dv_ref = grad_refs
    score, grad, slope, dw, wos = scratch
    _, members, node_rows, _ = loc.shape
    table = mask_ref.shape[0]
    width = og_ref.shape[2]
    head = width // HEADS
    per = 128 // head
    scale = 1.0 / math.sqrt(head)

    own, totals = own
    for m in range(members):
        score[m] = nn(halo[0, m], by_head_t(loc[QT, m], head))
        grad[m] = nn(halo[1, m], by_head_t(loc[GT, m], head))

    wo_total = None
    kv_total = None
    q_total = None
    for m in range(members):
        probs = []
        for h in range(per):
            lanes = slice(h * node_rows, (h + 1) * node_rows)
            den, inner = unnormalised(scale, score, grad, slope, m, lanes, mask_ref, node_rows)
            r = 1.0 / jnp.sum(den + totals[0, m, :, lanes], axis=0, keepdims=True)
            inner = jnp.sum(inner + totals[1, m, :, lanes], axis=0, keepdims=True) * r
            column = []
            scores = []
            for e, g, w in ((own.at[0], own.at[1], own.at[2]), (score, grad, slope)):
                for c in range(0, e.shape[1], STRIP):
                    box = (m, slice(c, c + STRIP), lanes)
                    column.append((e[box] * r).astype(bf16))
                    scores.append(((w[box] * r) * (g[box] - inner)).astype(bf16))
            probs.append((jnp.concatenate(column, axis=0), jnp.concatenate(scores, axis=0)))
        pb = jnp.concatenate([p for p, _ in probs], axis=1)
        ds = jnp.concatenate([s for _, s in probs], axis=1)
        ktg = jnp.concatenate([loc[KT, m], halo[2, m]], axis=1)
        vtg = jnp.concatenate([loc[VT, m], halo[3, m]], axis=1)
        att, dqt = [], []
        for h in range(0, per, 2):
            lanes = slice(h * node_rows, (h + 2) * node_rows)
            rows = slice(h * head, (h + 2) * head)
            a = nn(vtg[rows], pb[:, lanes])
            b = nn(ktg[rows], ds[:, lanes])
            for j in range(2):
                inside = (slice(j * head, (j + 1) * head), slice(j * node_rows, (j + 1) * node_rows))
                att.append(a[inside].astype(bf16))
                dqt.append(b[inside].astype(bf16))
        att = jnp.concatenate(att, axis=0)
        dq = jnp.concatenate(dqt, axis=0).T
        dk = nn(ds, by_head_n(loc[Q, m], head)).astype(bf16)
        dv = nn(pb, by_head_n(loc[G, m], head)).astype(bf16)
        dq_ref[m], dk_ref[m], dv_ref[m] = dq, dk, dv
        wo_term = nn(att, og_ref[m])
        kv_term = nn(xtf[m], jnp.concatenate([dk, dv], axis=1))
        q_term = nn(xtf[m, :, :node_rows], dq)
        wo_total = wo_term if m == 0 else wo_total + wo_term
        kv_total = kv_term if m == 0 else kv_total + kv_term
        q_total = q_term if m == 0 else q_total + q_term

    planes, _, _, rows, _ = dw.shape
    inner_planes = wos.shape[0]
    dw[:, :, :, :, :128] = q_total.reshape(planes, 2, 2, rows, 128)
    dw[:, :, :, :, 128:] = kv_total.reshape(planes, 2, 2, rows, 256)
    wos[...] = wo_total.reshape(inner_planes, 2, 2, rows, width)
    me = me_ref[0]
    c, y, z = me % 2, (me // 2) % 2, me // 4
    qkv = slice(at, at + 384)
    for k in range(planes):
        zk = plane_of(gray(z) ^ k)
        own_ref[k, :, qkv] = dw[zk, y, c]
        other_ref[k, :, qkv] = dw[zk, 1 - y, c]
        send_other[k, :, qkv] = dw[zk, 1 - y, 1 - c].astype(bf16)
        send_own[k, :, qkv] = dw[zk, y, 1 - c].astype(bf16)
    last = slice(at + 384, at + 512)
    for i in range(inner_planes):
        for n in range(width // 128):
            k = n * inner_planes + i
            lanes = slice(n * 128, (n + 1) * 128)
            own_ref[k, :, last] = wos[i, y, c, :, lanes]
            other_ref[k, :, last] = wos[i, 1 - y, c, :, lanes]
            send_other[k, :, last] = wos[i, 1 - y, 1 - c, :, lanes].astype(bf16)
            send_own[k, :, last] = wos[i, y, 1 - c, :, lanes].astype(bf16)


def node_kernel(groups, skip, *refs):
    refs = refs[skip:]
    dqs, dks, dvs = refs[:groups], refs[groups : 2 * groups], refs[2 * groups : 3 * groups]
    wq_ref, wk_ref, wv_ref, node_ref, plus_ref, minus_ref, right_ref, left_ref = refs[3 * groups :]
    members, node_rows, _ = dqs[0].shape
    slots = plus_ref.shape[2]

    def whole(parts, m):
        return jnp.concatenate([part[m] for part in parts], axis=1)

    for m in range(members):
        spread = nt(whole(dks, m), wk_ref[...]) + nt(whole(dvs, m), wv_ref[...])
        node_ref[m] = spread[:node_rows] + nt(whole(dqs, m), wq_ref[...])
        halo = spread[node_rows:].astype(bf16)
        for ref, order in (
            (plus_ref, (3, 7, 5)),
            (minus_ref, (2, 4, 6)),
            (right_ref, (1,)),
            (left_ref, (0,)),
        ):
            for i, k in enumerate(order):
                ref[m, i] = halo[k * slots : (k + 1) * slots]


def sums(owns, core_in, y_in, k):
    total = jnp.concatenate(
        [
            own[k] + (core[1, k] if len(core.shape) == 4 else core[k]).astype(f32)
            for own, core in zip(owns, core_in)
        ],
        axis=1,
    ) + y_in[k].astype(f32)
    return [total[:, at : at + 512] for at in range(0, total.shape[1], 512)]


def gather_projection(parts, k, planes, projection_ref, start):
    inner_planes = planes * 128 // projection_ref.shape[2]
    quarter, inner = divmod(k, inner_planes)
    for i, part in enumerate(parts):
        plane = start + i * inner_planes + inner
        projection_ref[plane, :, quarter * 128 : (quarter + 1) * 128] = part[:, 384:]


def pack_kernel(pieces, *refs):
    for i, (ref, core) in enumerate(zip(refs[:pieces], refs[pieces:-1])):
        arrived = core[0] if len(core.shape) == 4 else core[...]
        refs[-1][:, :, i * 512 : (i + 1) * 512] = (ref[...] + arrived.astype(f32)).astype(bf16)


def halve(rows, kept_ref, sent_ref):
    for i, row in enumerate(rows):
        if i % 2 == 0:
            kept_ref[i // 2] = row
            continue
        pieces = row.shape[1] // 128
        for n in range(pieces):
            sent_ref[i // 2 * pieces + n] = row[:, n * 128 : (n + 1) * 128].astype(bf16)


def add_received(kept_ref, received_ref):
    planes, _, wide = kept_ref.shape
    pieces = wide // 128
    return [
        kept_ref[i]
        + jnp.concatenate([received_ref[i * pieces + n] for n in range(pieces)], axis=1).astype(f32)
        for i in range(planes)
    ]


def first_kernel(after_ref, own, core_in, y_in, kept_ref, projection_ref, sent_ref):
    planes = own.shape[0]
    rows = []
    for k in range(planes):
        parts = sums([own], [core_in], y_in, k)
        gather_projection(parts, k, planes, projection_ref, 0)
        rows.append(jnp.concatenate([part[:, :384] for part in parts], axis=1))
    halve(rows, kept_ref, sent_ref)


def put(row, ref, at):
    for n in range(row.shape[1] // 128):
        ref[at + n] = row[:, n * 128 : (n + 1) * 128].astype(bf16)


def second_kernel(skip, pieces, me_ref, *refs):
    refs = refs[skip:]
    first_ref, y_in = refs[:2]
    owns, core_in = refs[2 : 2 + pieces], refs[2 + pieces : 2 + 2 * pieces]
    own_b, *sent = refs[2 + 2 * pieces : -1]
    projection_ref = refs[-1]
    done = first_ref.shape[0]
    planes = projection_ref.shape[0]
    projection_ref[:done] = first_ref[...]
    held = []
    for k in range(planes):
        parts = sums(owns, core_in, y_in, k)
        gather_projection(parts, k, planes, projection_ref, done)
        held.append(jnp.concatenate([part[:, :384] for part in parts], axis=1))
    z = me_ref[0] // 4
    for k in range(planes):
        row = jnp.concatenate([held[k], projection_ref[plane_of(gray(z) ^ k)]], axis=1)
        if k:
            put(row, sent[k - 1], 0)
        else:
            own_b[...] = row


def join_kernel(kept_a, in_a, *refs):
    count = (len(refs) - 1) // 2
    blocks, own_a, sent = refs[:count], refs[count], refs[count + 1 :]
    first = add_received(kept_a, in_a)
    own_a[...] = first[0]
    for i, ref in enumerate(sent):
        ref[: blocks[i].shape[0]] = blocks[i][...]
        put(first[i + 1], ref, blocks[i].shape[0])


def finish_kernel(
    me_ref, after_ref, second_in, first_in, send_ref, node_ref, plus_ref, minus_ref, out_ref, came
):
    members, node_rows, _ = node_ref.shape
    pick = sent_selector(send_ref[0], node_rows).astype(bf16)
    from_swaps(came, me_ref[0] % 2, first_in, second_in)
    for m in range(members):
        pieces = [None] * 8
        for side, order in enumerate(((1, 7, 4), (0, 5, 6))):
            for i, k in enumerate(order):
                pieces[k] = came[side, m, i]
        pieces[2], pieces[3] = plus_ref[m, 0], minus_ref[m, 0]
        arriving = jnp.concatenate(pieces, axis=0)
        out_ref[m] = (node_ref[m] + nn(pick, arriving)).astype(bf16)


def weight_kernel(after_ref, own_a, own_b, *refs):
    received, out_ref = refs[:-1], refs[-1]
    a, b = own_a[...], own_b[...]
    blocks, more = b.shape[1] // 128, a.shape[1] // 128
    for k, ref in enumerate(received, 1):
        b = b + jnp.concatenate([ref[n] for n in range(blocks)], axis=1).astype(f32)
        if k % 2 == 0:
            a = a + jnp.concatenate([ref[blocks + n] for n in range(more)], axis=1).astype(f32)
    width = out_ref.shape[1] // 4
    group = 0
    for part, wide in ((a, a.shape[1]), (b, b.shape[1] - width)):
        for j in range(0, wide, 384):
            for n in range(3):
                at = n * width + group * 128
                out_ref[:, at : at + 128] = part[:, j + n * 128 : j + (n + 1) * 128]
            group += 1
    out_ref[:, 3 * width :] = b[:, b.shape[1] - width :]


def call(kernel, outs, operands, specs=None, scratch=(), limit=12, final=False, flops=10**6):
    specs = list(specs or ())
    specs += [pltpu.VMEM] * (len(operands) - len(specs))
    operands = [
        pltpu.with_memory_space_constraint(o, s) if s in (pltpu.HBM, pltpu.VMEM) else o
        for o, s in zip(operands, specs)
    ]
    return pl.pallas_call(
        kernel,
        out_shape=[jax.ShapeDtypeStruct(*o) if final else pltpu.VMEM(*o) for o in outs],
        in_specs=[pl.BlockSpec(memory_space=s) for s in specs],
        scratch_shapes=list(scratch),
        compiler_params=pltpu.CompilerParams(vmem_limit_bytes=limit * MIB),
        cost_estimate=pl.CostEstimate(flops=flops, bytes_accessed=10**4, transcendentals=0),
    )(*operands)


def body(
    node_features, out_grad, w_query, w_key, w_value, w_out, neighbours, neighbour_count, send_rows
):
    members, node_rows, width = node_features.shape
    count = lax.axis_size("patch")
    row_width = min(8, count // 4)
    _, adjacent, slots = send_rows.shape
    table = node_rows + adjacent * slots
    groups = width // 128
    me = lax.axis_index("patch")
    three = ((members, 3, slots, width), bf16)
    one = ((members, 1, slots, width), bf16)

    place = me.reshape(1)
    trio = pltpu.VMEM((2, *three[0]), bf16)
    to_plus, to_minus, own_right, own_left, x = call(
        functools.partial(gather_kernel, slots),
        [three, three, one, one, (node_features.shape, bf16)],
        (send_rows, node_features),
        specs=[pltpu.HBM] * 2,
        scratch=[pltpu.VMEM(send_rows.shape, jnp.int32), pltpu.SemaphoreType.DMA((2,))],
    )
    plus = shifted(to_plus, row_width)
    minus = shifted(to_minus, -row_width)
    square = ((width, width), bf16)
    counts = neighbour_count.reshape(1, node_rows)
    *loc, xt, wq, wk, wv, og, neigh, counts = call(
        functools.partial(local_kernel, groups),
        [((8, members, node_rows, 128), bf16)] * groups
        + [((members, width, node_rows), bf16), square, square, square, (out_grad.shape, bf16)]
        + [(neighbours.shape, jnp.int32), (counts.shape, jnp.int32)],
        (own_right, x, w_query, w_key, w_value, out_grad, neighbours, counts, w_out),
        specs=[pl.ANY, pltpu.VMEM] + [pltpu.HBM] * 7,
        scratch=[pltpu.VMEM((width, width), bf16), pltpu.SemaphoreType.DMA((7,))],
        limit=16,
    )
    outgoing = call(
        relay_kernel, [three, three], (place, loc[0], minus, plus, own_right, own_left),
        specs=[pltpu.SMEM, pl.ANY], scratch=[trio],
    )
    arrived = swap(outgoing, 1)
    (mask,) = call(
        mask_kernel, [((table, node_rows), f32)], (outgoing[1], neigh, counts), specs=[pl.ANY]
    )
    own_part = call(
        functools.partial(own_kernel, groups),
        [
            ((3, members, node_rows, 4 * node_rows), f32),
            ((2, members, 8, 4 * node_rows), f32),
        ]
        * groups,
        (*loc, mask),
    )
    *halo, xtf = call(
        halo_kernel,
        [((4, members, node_rows, 128), bf16)] * groups + [((members, width, table), bf16)],
        (place, *arrived[::-1], plus, minus, xt, wk, wv), specs=[pltpu.SMEM], scratch=[trio],
    )

    planes, rows = count // 4, width // count
    inner_planes = planes * 128 // width
    flip = [(i, i ^ 1) for i in range(count)]
    flop = [(i, i ^ 2) for i in range(count)]
    grads = []

    def attention(extra, which, together):
        wide = 512 * len(which)
        sends = [((2, planes, rows, wide), bf16)] if together else [((planes, rows, wide), bf16)] * 2
        outs = call(
            functools.partial(attention_kernel, len(extra), len(which)),
            [((planes, rows, wide), f32)] * 2
            + sends
            + [
                ((members, node_rows, 128), bf16),
                ((members, table, 128), bf16),
                ((members, table, 128), bf16),
            ]
            * len(which),
            (
                place, *extra, *[loc[g] for g in which], *[halo[g] for g in which],
                *[part for g in which for part in own_part[2 * g : 2 * g + 2]], mask, xtf, og,
            ),
            specs=[pltpu.SMEM] + [pl.ANY] * len(extra),
            scratch=[pltpu.VMEM((members, table - node_rows, 512), f32)] * 3
            + [
                pltpu.VMEM((planes, 2, 2, rows, 384), f32),
                pltpu.VMEM((inner_planes, 2, 2, rows, width), f32),
            ],
            limit=32,
        )
        sent = outs[2 : 2 + len(sends)]
        grads.extend(outs[2 + len(sends) :])
        arrived = [lax.ppermute(shard, "patch", flip) for shard in sent]
        return outs[0], outs[1], arrived[0], arrived[-1]

    half = groups - 1
    wide = 384 * half
    own_a, other, core_other, core_own = attention((), range(half), False)
    y_sent = (other + core_other.astype(f32)).astype(bf16)
    y_a = lax.ppermute(y_sent, "patch", flop)
    later = [attention((), range(half, groups), False)]
    own_b, other_b, core_other_b, core_own_b = zip(*later)
    (y_sent,) = call(
        functools.partial(pack_kernel, len(later)), [(other_b[0].shape, bf16)],
        (*other_b, *core_other_b),
    )
    y_b = lax.ppermute(y_sent, "patch", flop)
    node, to_plus, to_minus, own_right, own_left = call(
        functools.partial(node_kernel, groups, 1),
        [((members, node_rows, width), f32), three, three, one, one],
        (y_sent, *grads[0::3], *grads[1::3], *grads[2::3], wq, wk, wv),
        specs=[pl.ANY],
    )
    from_plus = shifted(to_minus, -row_width)
    from_minus = shifted(to_plus, row_width)
    def exchange(sent, distance):
        return lax.ppermute(sent, "patch", along_z(count, distance))

    kept_a, out_a, sent_a = call(
        first_kernel,
        [
            ((planes // 2, rows, wide), f32),
            ((half * inner_planes, rows, width), f32),
            ((planes // 2 * wide // 128, rows, 128), bf16),
        ],
        (node, own_a, core_own, y_a), specs=[pl.ANY], flops=2 * 10**10,
    )
    in_a = exchange(sent_a, 1)
    outgoing = call(
        relay_kernel, [three, three],
        (place, sent_a, from_plus, from_minus, own_right, own_left),
        specs=[pltpu.SMEM, pl.ANY], scratch=[trio],
    )
    back = swap(outgoing, 1)
    last = 384 * (groups - half) + width
    more, blocks = wide // 128, last // 128
    own_b, *sent = call(
        functools.partial(second_kernel, 1, len(later)),
        [((rows, last), f32)] + [((blocks, rows, 128), bf16)] * (planes - 1),
        (place, outgoing[0], out_a, y_b, *own_b, *core_own_b),
        specs=[pltpu.SMEM, pl.ANY],
        scratch=[pltpu.VMEM((planes, rows, width), f32)], flops=4 * 10**9,
    )
    own_a, *sent[1::2] = call(
        join_kernel,
        [((rows, wide), f32)] + [((blocks + more, rows, 128), bf16)] * (planes // 2 - 1),
        (kept_a, in_a, *sent[1::2]), flops=2 * 10**10,
    )
    received = [exchange(shard, k) for k, shard in enumerate(sent, 1)]
    (node_grad,) = call(
        finish_kernel, [((members, node_rows, width), bf16)],
        (place, sent[0], *back[::-1], send_rows, node, from_plus, from_minus),
        specs=[pltpu.SMEM, pl.ANY], scratch=[trio], final=True, flops=2 * 10**10,
    )
    (weight_grad,) = call(
        weight_kernel, [((rows, 4 * width), f32)], (node_grad, own_a, own_b, *received),
        specs=[pltpu.HBM], final=True,
    )
    return (node_grad, weight_grad)


def solution(mesh):
    in_specs = (
        P("groups", "patch", None),
        P("groups", "patch", None),
        P(),
        P(),
        P(),
        P(),
        P("patch", None),
        P("patch"),
        P("patch", None, None),
    )
    out_specs = (P("groups", "patch", None), P(("groups", "patch"), None))
    return jax.shard_map(body, mesh=mesh, in_specs=in_specs, out_specs=out_specs, check_vma=False)
```

```python
import functools
import math

import jax
import jax.numpy as jnp
from jax import lax
from jax.experimental import pallas as pl
from jax.experimental.pallas import tpu as pltpu
from jax.sharding import PartitionSpec as P

HEADS = 16
score_cap = 5.0
MIB = 1024 * 1024
f32 = jnp.float32
bf16 = jnp.bfloat16


def nn(a, b):
    return lax.dot_general(a, b, (((1,), (0,)), ((), ())), preferred_element_type=f32)


def nt(a, b):
    return lax.dot_general(a, b, (((1,), (1,)), ((), ())), preferred_element_type=f32)


def shifted(shard, by):
    count = lax.axis_size("patch")
    return lax.ppermute(shard, "patch", [(i, (i + by) % count) for i in range(count)])


def neighbours_apart(count, stride):
    first, second = [], []
    for i in range(count):
        up, down = (i + stride) % count, (i - stride) % count
        even = i // stride % 2 == 0
        first.append((i, up if even else down))
        second.append((i, down if even else up))
    return first, second


def swap(pair, stride):
    first, second = neighbours_apart(lax.axis_size("patch"), stride)
    later = lax.ppermute(pair[1], "patch", second)
    return [lax.ppermute(pair[0], "patch", first), later]


def to_swaps(both, odd, first_ref, second_ref):
    first_ref[...] = both[odd]
    second_ref[...] = both[1 - odd]


def from_swaps(both, odd, first_ref, second_ref):
    both[1 - odd] = first_ref[...]
    both[odd] = second_ref[...]


def sent_selector(send_rows, node_rows):
    adjacent, slots = send_rows.shape
    halo = adjacent * slots
    wide = jnp.concatenate([send_rows] * adjacent, axis=1)
    own = lax.broadcasted_iota(jnp.int32, (adjacent, halo), 1) // slots == lax.broadcasted_iota(
        jnp.int32, (adjacent, halo), 0
    )
    ids = jnp.sum(jnp.where(own, wide, 0), axis=0, keepdims=True)
    nodes = lax.broadcasted_iota(jnp.int32, (node_rows, halo), 0)
    return jnp.where(nodes == ids, 1.0, 0.0).astype(f32)


def gather_kernel(
    slots, send_hbm, x_hbm, plus_ref, minus_ref, right_ref, left_ref, x_ref, send_ref, sem
):
    copies = [
        pltpu.make_async_copy(send_hbm, send_ref, sem.at[0]),
        pltpu.make_async_copy(x_hbm, x_ref, sem.at[1]),
    ]
    for copy in copies:
        copy.start()
    copies[0].wait()
    members, node_rows, _ = x_ref.shape
    pick = sent_selector(send_ref[0], node_rows).T.astype(bf16)
    copies[1].wait()
    for m in range(members):
        rows = nn(pick, x_ref[m]).astype(bf16)

        def part(k):
            return rows[k * slots : (k + 1) * slots]

        for ref, order in ((plus_ref, (2, 6, 4)), (minus_ref, (3, 5, 7))):
            for i, k in enumerate(order):
                ref[m, i] = part(k)
        right_ref[m, 0] = part(0)
        left_ref[m, 0] = part(1)


def relay_kernel(
    me_ref, after_ref, own_right, own_left, plus_ref, minus_ref, first_ref, second_ref, both
):
    for side, own in enumerate((own_right, own_left)):
        both[side, :, 0:1] = own[...]
        both[side, :, 1:2] = plus_ref[:, 1 + side : 2 + side]
        both[side, :, 2:3] = minus_ref[:, 1 + side : 2 + side]
    to_swaps(both, me_ref[0] % 2, first_ref, second_ref)


def gray(z):
    return z ^ (z >> 1)


def plane_of(code):
    z = code
    for shift in range(1, 8):
        z = z ^ (code >> shift)
    return z


def along_z(count, distance):
    planes = count // 4
    return [(i, plane_of(gray(i // 4) ^ distance) * 4 + i % 4) for i in range(planes * 4)]


Q, K, V, G, QT, KT, VT, GT = range(8)


def local_kernel(groups, after_ref, x_ref, *refs):
    sources, loc_refs, xt_ref = refs[:7], refs[7 : 7 + groups], refs[7 + groups]
    copied, sem = refs[8 + groups : 15 + groups], refs[-1]
    copies = [
        pltpu.make_async_copy(source, target, sem.at[i])
        for i, (source, target) in enumerate(zip(sources, copied))
    ]
    for copy in copies:
        copy.start()
    members, node_rows, width = x_ref.shape
    x = x_ref[...].reshape(members * node_rows, width)
    for m in range(members):
        xt_ref[m] = x_ref[m].T

    def put(rows, kind):
        for m in range(members):
            for g, ref in enumerate(loc_refs):
                block = rows[m * node_rows : (m + 1) * node_rows, g * 128 : (g + 1) * 128]
                ref[kind, m] = block
                ref[kind + 4, m] = block.T

    wq_ref, wk_ref, wv_ref, og_ref, _, _, wo_ref = copied
    for kind, ref in enumerate((wq_ref, wk_ref, wv_ref)):
        copies[kind].wait()
        put(nn(x, ref[...]).astype(bf16), kind)
    for copy in copies[3:]:
        copy.wait()
    og = og_ref[...].reshape(members * node_rows, width)
    put(nt(og, wo_ref[...]).astype(bf16), G)


def mask_kernel(after_ref, neigh_ref, count_ref, mask_ref):
    neigh = neigh_ref[...].T
    slots, node_rows = neigh.shape
    table = mask_ref.shape[0]
    order = lax.broadcasted_iota(jnp.int32, neigh.shape, 0)
    tail = jnp.where(order >= count_ref[...], neigh, -1)[slots // 2 :]
    half = table // 2
    for part in range(2):
        columns = lax.broadcasted_iota(jnp.int32, (half, node_rows), 0) + part * half
        kept = jnp.ones((half, node_rows), f32)
        for j in range(slots // 2):
            kept = jnp.where(tail[j : j + 1] == columns, 0.0, kept)
        mask_ref[part * half : (part + 1) * half] = kept


def halo_kernel(
    me_ref, second_in, first_in, plus_ref, minus_ref, xt_ref, wk_ref, wv_ref, *refs
):
    halo_refs, xtf_ref, both = refs[:-2], refs[-2], refs[-1]
    members, _, node_rows = xt_ref.shape
    from_swaps(both, me_ref[0] % 2, first_in, second_in)
    for m in range(members):
        pieces = [None] * 8
        for side, order in enumerate(((0, 6, 5), (1, 4, 7))):
            for i, k in enumerate(order):
                pieces[k] = both[side, m, i]
        pieces[2] = plus_ref[m, 0]
        pieces[3] = minus_ref[m, 0]
        halo = jnp.concatenate(pieces, axis=0)
        xtf_ref[m, :, :node_rows] = xt_ref[m]
        xtf_ref[m, :, node_rows:] = halo.T
        for kind, w_ref in enumerate((wk_ref, wv_ref)):
            rows = nn(halo, w_ref[...]).astype(bf16)
            for g, ref in enumerate(halo_refs):
                block = rows[:, g * 128 : (g + 1) * 128]
                ref[kind, m] = block
                ref[kind + 2, m] = block.T


STRIP = 64


def by_head_t(block, head):
    row_head = lax.broadcasted_iota(jnp.int32, block.shape, 0) // head
    zero = jnp.zeros_like(block)
    return jnp.concatenate(
        [jnp.where(row_head == h, block, zero) for h in range(block.shape[0] // head)], axis=1
    )


def by_head_n(block, head):
    lane_head = lax.broadcasted_iota(jnp.int32, block.shape, 1) // head
    zero = jnp.zeros_like(block)
    return jnp.concatenate(
        [jnp.where(lane_head == h, block, zero) for h in range(block.shape[1] // head)], axis=0
    )


def unnormalised(scale, score, grad, slope, m, lanes, mask_ref, start):
    columns, node_rows = score.shape[1], mask_ref.shape[1]
    den = jnp.zeros((8, node_rows), f32)
    inner = jnp.zeros((8, node_rows), f32)
    for c in range(0, columns, STRIP):
        box = (m, slice(c, c + STRIP), lanes)
        t = jnp.tanh(score[box] * (scale / score_cap))
        e = jnp.exp2(t * (score_cap / math.log(2.0))) * mask_ref[start + c : start + c + STRIP]
        den = den + jnp.sum(e.reshape(STRIP // 8, 8, node_rows), axis=0)
        inner = inner + jnp.sum((e * grad[box]).reshape(STRIP // 8, 8, node_rows), axis=0)
        score[box] = e
        slope[box] = e * (scale - scale * (t * t))
    return den, inner


def own_kernel(groups, *refs):
    locs, mask_ref, outs = refs[:groups], refs[groups], refs[groups + 1 :]
    _, members, node_rows, _ = locs[0].shape
    head = 128 * groups // HEADS
    scale = 1.0 / math.sqrt(head)
    for g, loc in enumerate(locs):
        own, totals = outs[2 * g : 2 * g + 2]
        score, grad, slope = own.at[0], own.at[1], own.at[2]
        for m in range(members):
            score[m] = nn(loc[K, m], by_head_t(loc[QT, m], head))
            grad[m] = nn(loc[V, m], by_head_t(loc[GT, m], head))
        for m in range(members):
            for h in range(128 // head):
                lanes = slice(h * node_rows, (h + 1) * node_rows)
                den, inner = unnormalised(scale, score, grad, slope, m, lanes, mask_ref, 0)
                totals[0, m, :, lanes] = den
                totals[1, m, :, lanes] = inner


def attention_kernel(extra, here, me_ref, *refs):
    refs = refs[extra:]
    locs, halos, owns = refs[:here], refs[here : 2 * here], refs[2 * here : 4 * here]
    refs = refs[4 * here :]
    mask_ref, xtf, og_ref = refs[:3]
    split = 7 if len(refs) == 15 + 3 * (here - 1) else 6
    outs, grads, scratch = refs[3:split], refs[split : split + 3 * here], refs[split + 3 * here :]
    if split == 6:
        outs = (*outs[:2], outs[2].at[0], outs[2].at[1])
    for i in range(here):
        attend(
            me_ref, locs[i], halos[i], owns[2 * i : 2 * i + 2], mask_ref, xtf, og_ref, outs, 512 * i,
            grads[3 * i : 3 * i + 3], scratch,
        )


def attend(me_ref, loc, halo, own, mask_ref, xtf, og_ref, out_refs, at, grad_refs, scratch):
    own_ref, other_ref, send_other, send_own = out_refs
    dq_ref, dk_ref, dv_ref = grad_refs
    score, grad, slope, dw, wos = scratch
    _, members, node_rows, _ = loc.shape
    table = mask_ref.shape[0]
    width = og_ref.shape[2]
    head = width // HEADS
    per = 128 // head
    scale = 1.0 / math.sqrt(head)

    own, totals = own
    for m in range(members):
        score[m] = nn(halo[0, m], by_head_t(loc[QT, m], head))
        grad[m] = nn(halo[1, m], by_head_t(loc[GT, m], head))

    wo_total = None
    kv_total = None
    q_total = None
    for m in range(members):
        probs = []
        for h in range(per):
            lanes = slice(h * node_rows, (h + 1) * node_rows)
            den, inner = unnormalised(scale, score, grad, slope, m, lanes, mask_ref, node_rows)
            r = 1.0 / jnp.sum(den + totals[0, m, :, lanes], axis=0, keepdims=True)
            inner = jnp.sum(inner + totals[1, m, :, lanes], axis=0, keepdims=True) * r
            column = []
            scores = []
            for e, g, w in ((own.at[0], own.at[1], own.at[2]), (score, grad, slope)):
                for c in range(0, e.shape[1], STRIP):
                    box = (m, slice(c, c + STRIP), lanes)
                    column.append((e[box] * r).astype(bf16))
                    scores.append(((w[box] * r) * (g[box] - inner)).astype(bf16))
            probs.append((jnp.concatenate(column, axis=0), jnp.concatenate(scores, axis=0)))
        pb = jnp.concatenate([p for p, _ in probs], axis=1)
        ds = jnp.concatenate([s for _, s in probs], axis=1)
        ktg = jnp.concatenate([loc[KT, m], halo[2, m]], axis=1)
        vtg = jnp.concatenate([loc[VT, m], halo[3, m]], axis=1)
        att, dqt = [], []
        for h in range(0, per, 2):
            lanes = slice(h * node_rows, (h + 2) * node_rows)
            rows = slice(h * head, (h + 2) * head)
            a = nn(vtg[rows], pb[:, lanes])
            b = nn(ktg[rows], ds[:, lanes])
            for j in range(2):
                inside = (slice(j * head, (j + 1) * head), slice(j * node_rows, (j + 1) * node_rows))
                att.append(a[inside].astype(bf16))
                dqt.append(b[inside].astype(bf16))
        att = jnp.concatenate(att, axis=0)
        dq = jnp.concatenate(dqt, axis=0).T
        dk = nn(ds, by_head_n(loc[Q, m], head)).astype(bf16)
        dv = nn(pb, by_head_n(loc[G, m], head)).astype(bf16)
        dq_ref[m], dk_ref[m], dv_ref[m] = dq, dk, dv
        wo_term = nn(att, og_ref[m])
        kv_term = nn(xtf[m], jnp.concatenate([dk, dv], axis=1))
        q_term = nn(xtf[m, :, :node_rows], dq)
        wo_total = wo_term if m == 0 else wo_total + wo_term
        kv_total = kv_term if m == 0 else kv_total + kv_term
        q_total = q_term if m == 0 else q_total + q_term

    planes, _, _, rows, _ = dw.shape
    inner_planes = wos.shape[0]
    dw[:, :, :, :, :128] = q_total.reshape(planes, 2, 2, rows, 128)
    dw[:, :, :, :, 128:] = kv_total.reshape(planes, 2, 2, rows, 256)
    wos[...] = wo_total.reshape(inner_planes, 2, 2, rows, width)
    me = me_ref[0]
    c, y, z = me % 2, (me // 2) % 2, me // 4
    qkv = slice(at, at + 384)
    for k in range(planes):
        zk = plane_of(gray(z) ^ k)
        own_ref[k, :, qkv] = dw[zk, y, c]
        other_ref[k, :, qkv] = dw[zk, 1 - y, c]
        send_other[k, :, qkv] = dw[zk, 1 - y, 1 - c].astype(bf16)
        send_own[k, :, qkv] = dw[zk, y, 1 - c].astype(bf16)
    last = slice(at + 384, at + 512)
    for i in range(inner_planes):
        for n in range(width // 128):
            k = n * inner_planes + i
            lanes = slice(n * 128, (n + 1) * 128)
            own_ref[k, :, last] = wos[i, y, c, :, lanes]
            other_ref[k, :, last] = wos[i, 1 - y, c, :, lanes]
            send_other[k, :, last] = wos[i, 1 - y, 1 - c, :, lanes].astype(bf16)
            send_own[k, :, last] = wos[i, y, 1 - c, :, lanes].astype(bf16)


def node_kernel(groups, skip, *refs):
    refs = refs[skip:]
    dqs, dks, dvs = refs[:groups], refs[groups : 2 * groups], refs[2 * groups : 3 * groups]
    wq_ref, wk_ref, wv_ref, node_ref, plus_ref, minus_ref, right_ref, left_ref = refs[3 * groups :]
    members, node_rows, _ = dqs[0].shape
    slots = plus_ref.shape[2]

    def whole(parts, m):
        return jnp.concatenate([part[m] for part in parts], axis=1)

    for m in range(members):
        spread = nt(whole(dks, m), wk_ref[...]) + nt(whole(dvs, m), wv_ref[...])
        node_ref[m] = spread[:node_rows] + nt(whole(dqs, m), wq_ref[...])
        halo = spread[node_rows:].astype(bf16)
        for ref, order in (
            (plus_ref, (3, 7, 5)),
            (minus_ref, (2, 4, 6)),
            (right_ref, (1,)),
            (left_ref, (0,)),
        ):
            for i, k in enumerate(order):
                ref[m, i] = halo[k * slots : (k + 1) * slots]


def sums(owns, core_in, y_in, k):
    total = jnp.concatenate(
        [
            own[k] + (core[1, k] if len(core.shape) == 4 else core[k]).astype(f32)
            for own, core in zip(owns, core_in)
        ],
        axis=1,
    ) + y_in[k].astype(f32)
    return [total[:, at : at + 512] for at in range(0, total.shape[1], 512)]


def gather_projection(parts, k, planes, projection_ref, start):
    inner_planes = planes * 128 // projection_ref.shape[2]
    quarter, inner = divmod(k, inner_planes)
    for i, part in enumerate(parts):
        plane = start + i * inner_planes + inner
        projection_ref[plane, :, quarter * 128 : (quarter + 1) * 128] = part[:, 384:]


def pack_kernel(pieces, *refs):
    for i, (ref, core) in enumerate(zip(refs[:pieces], refs[pieces:-1])):
        arrived = core[0] if len(core.shape) == 4 else core[...]
        refs[-1][:, :, i * 512 : (i + 1) * 512] = (ref[...] + arrived.astype(f32)).astype(bf16)


def halve(rows, kept_ref, sent_ref):
    half = len(rows) // 2
    for i, row in enumerate(rows):
        if i < half:
            kept_ref[i] = row
        else:
            put(row, sent_ref, (i - half) * row.shape[1] // 128)


def add_received(kept_ref, received_ref):
    planes, _, wide = kept_ref.shape
    pieces = wide // 128
    return [
        kept_ref[i]
        + jnp.concatenate([received_ref[i * pieces + n] for n in range(pieces)], axis=1).astype(f32)
        for i in range(planes)
    ]


def first_kernel(after_ref, own, core_in, y_in, kept_ref, projection_ref, sent_ref):
    planes = own.shape[0]
    rows = []
    for k in range(planes):
        parts = sums([own], [core_in], y_in, k)
        gather_projection(parts, k, planes, projection_ref, 0)
        rows.append(jnp.concatenate([part[:, :384] for part in parts], axis=1))
    halve(rows, kept_ref, sent_ref)


def put(row, ref, at):
    for n in range(row.shape[1] // 128):
        ref[at + n] = row[:, n * 128 : (n + 1) * 128].astype(bf16)


def second_kernel(skip, pieces, me_ref, *refs):
    refs = refs[skip:]
    first_ref, y_in = refs[:2]
    owns, core_in = refs[2 : 2 + pieces], refs[2 + pieces : 2 + 2 * pieces]
    own_b, *sent = refs[2 + 2 * pieces : -1]
    projection_ref = refs[-1]
    done = first_ref.shape[0]
    planes = projection_ref.shape[0]
    projection_ref[:done] = first_ref[...]
    held = []
    for k in range(planes):
        parts = sums(owns, core_in, y_in, k)
        gather_projection(parts, k, planes, projection_ref, done)
        held.append(jnp.concatenate([part[:, :384] for part in parts], axis=1))
    z = me_ref[0] // 4
    for k in range(planes):
        row = jnp.concatenate([held[k], projection_ref[plane_of(gray(z) ^ k)]], axis=1)
        if k:
            put(row, sent[k - 1], 0)
        else:
            own_b[...] = row


def join_kernel(kept_a, in_a, *refs):
    count = (len(refs) - 1) // 2
    blocks, own_a, sent = refs[:count], refs[count], refs[count + 1 :]
    first = add_received(kept_a, in_a)
    own_a[...] = first[0]
    for i, ref in enumerate(sent):
        ref[: blocks[i].shape[0]] = blocks[i][...]
        put(first[i + 1], ref, blocks[i].shape[0])


def finish_kernel(
    me_ref, after_ref, second_in, first_in, send_ref, node_ref, plus_ref, minus_ref, out_ref, came
):
    members, node_rows, _ = node_ref.shape
    pick = sent_selector(send_ref[0], node_rows).astype(bf16)
    from_swaps(came, me_ref[0] % 2, first_in, second_in)
    for m in range(members):
        pieces = [None] * 8
        for side, order in enumerate(((1, 4, 7), (0, 6, 5))):
            for i, k in enumerate(order):
                pieces[k] = came[side, m, i]
        pieces[2], pieces[3] = plus_ref[m, 0], minus_ref[m, 0]
        arriving = jnp.concatenate(pieces, axis=0)
        out_ref[m] = (node_ref[m] + nn(pick, arriving)).astype(bf16)


def weight_kernel(after_ref, own_a, own_b, *refs):
    received, out_ref = refs[:-1], refs[-1]
    a, b = own_a[...], own_b[...]
    blocks, more = b.shape[1] // 128, a.shape[1] // 128
    for k, ref in enumerate(received, 1):
        b = b + jnp.concatenate([ref[n] for n in range(blocks)], axis=1).astype(f32)
        if k <= len(received) // 2:
            a = a + jnp.concatenate([ref[blocks + n] for n in range(more)], axis=1).astype(f32)
    width = out_ref.shape[1] // 4
    group = 0
    for part, wide in ((a, a.shape[1]), (b, b.shape[1] - width)):
        for j in range(0, wide, 384):
            for n in range(3):
                at = n * width + group * 128
                out_ref[:, at : at + 128] = part[:, j + n * 128 : j + (n + 1) * 128]
            group += 1
    out_ref[:, 3 * width :] = b[:, b.shape[1] - width :]


def call(kernel, outs, operands, specs=None, scratch=(), limit=12, final=False, flops=10**6):
    specs = list(specs or ())
    specs += [pltpu.VMEM] * (len(operands) - len(specs))
    operands = [
        pltpu.with_memory_space_constraint(o, s) if s in (pltpu.HBM, pltpu.VMEM) else o
        for o, s in zip(operands, specs)
    ]
    return pl.pallas_call(
        kernel,
        out_shape=[jax.ShapeDtypeStruct(*o) if final else pltpu.VMEM(*o) for o in outs],
        in_specs=[pl.BlockSpec(memory_space=s) for s in specs],
        scratch_shapes=list(scratch),
        compiler_params=pltpu.CompilerParams(vmem_limit_bytes=limit * MIB),
        cost_estimate=pl.CostEstimate(flops=flops, bytes_accessed=10**4, transcendentals=0),
    )(*operands)


def body(
    node_features, out_grad, w_query, w_key, w_value, w_out, neighbours, neighbour_count, send_rows
):
    members, node_rows, width = node_features.shape
    count = lax.axis_size("patch")
    row_width = min(8, count // 4)
    _, adjacent, slots = send_rows.shape
    table = node_rows + adjacent * slots
    groups = width // 128
    me = lax.axis_index("patch")
    three = ((members, 3, slots, width), bf16)
    one = ((members, 1, slots, width), bf16)

    place = me.reshape(1)
    trio = pltpu.VMEM((2, *three[0]), bf16)
    to_plus, to_minus, own_right, own_left, x = call(
        functools.partial(gather_kernel, slots),
        [three, three, one, one, (node_features.shape, bf16)],
        (send_rows, node_features),
        specs=[pltpu.HBM] * 2,
        scratch=[pltpu.VMEM(send_rows.shape, jnp.int32), pltpu.SemaphoreType.DMA((2,))],
    )
    plus = shifted(to_plus, row_width)
    minus = shifted(to_minus, -row_width)
    square = ((width, width), bf16)
    counts = neighbour_count.reshape(1, node_rows)
    *loc, xt, wq, wk, wv, og, neigh, counts = call(
        functools.partial(local_kernel, groups),
        [((8, members, node_rows, 128), bf16)] * groups
        + [((members, width, node_rows), bf16), square, square, square, (out_grad.shape, bf16)]
        + [(neighbours.shape, jnp.int32), (counts.shape, jnp.int32)],
        (own_right, x, w_query, w_key, w_value, out_grad, neighbours, counts, w_out),
        specs=[pl.ANY, pltpu.VMEM] + [pltpu.HBM] * 7,
        scratch=[pltpu.VMEM((width, width), bf16), pltpu.SemaphoreType.DMA((7,))],
        limit=16,
    )
    outgoing = call(
        relay_kernel, [three, three], (place, loc[0], own_right, own_left, plus, minus),
        specs=[pltpu.SMEM, pl.ANY], scratch=[trio],
    )
    arrived = swap(outgoing, 1)
    (mask,) = call(
        mask_kernel, [((table, node_rows), f32)], (outgoing[1], neigh, counts), specs=[pl.ANY]
    )
    own_part = call(
        functools.partial(own_kernel, groups),
        [
            ((3, members, node_rows, 4 * node_rows), f32),
            ((2, members, 8, 4 * node_rows), f32),
        ]
        * groups,
        (*loc, mask),
    )
    *halo, xtf = call(
        halo_kernel,
        [((4, members, node_rows, 128), bf16)] * groups + [((members, width, table), bf16)],
        (place, *arrived[::-1], plus, minus, xt, wk, wv), specs=[pltpu.SMEM], scratch=[trio],
    )

    planes, rows = count // 4, width // count
    inner_planes = planes * 128 // width
    flip = [(i, i ^ 1) for i in range(count)]
    flop = [(i, i ^ 2) for i in range(count)]
    grads = []

    def attention(extra, which, together):
        wide = 512 * len(which)
        sends = [((2, planes, rows, wide), bf16)] if together else [((planes, rows, wide), bf16)] * 2
        outs = call(
            functools.partial(attention_kernel, len(extra), len(which)),
            [((planes, rows, wide), f32)] * 2
            + sends
            + [
                ((members, node_rows, 128), bf16),
                ((members, table, 128), bf16),
                ((members, table, 128), bf16),
            ]
            * len(which),
            (
                place, *extra, *[loc[g] for g in which], *[halo[g] for g in which],
                *[part for g in which for part in own_part[2 * g : 2 * g + 2]], mask, xtf, og,
            ),
            specs=[pltpu.SMEM] + [pl.ANY] * len(extra),
            scratch=[pltpu.VMEM((members, table - node_rows, 512), f32)] * 3
            + [
                pltpu.VMEM((planes, 2, 2, rows, 384), f32),
                pltpu.VMEM((inner_planes, 2, 2, rows, width), f32),
            ],
            limit=32,
        )
        sent = outs[2 : 2 + len(sends)]
        grads.extend(outs[2 + len(sends) :])
        arrived = [lax.ppermute(shard, "patch", flip) for shard in sent]
        return outs[0], outs[1], arrived[0], arrived[-1]

    half = groups - 1
    wide = 384 * half
    own_a, other, core_other, core_own = attention((), range(half), False)
    y_sent = (other + core_other.astype(f32)).astype(bf16)
    y_a = lax.ppermute(y_sent, "patch", flop)
    later = [attention((), range(half, groups), False)]
    own_b, other_b, core_other_b, core_own_b = zip(*later)
    (y_sent,) = call(
        functools.partial(pack_kernel, len(later)), [(other_b[0].shape, bf16)],
        (*other_b, *core_other_b),
    )
    y_b = lax.ppermute(y_sent, "patch", flop)
    node, to_plus, to_minus, own_right, own_left = call(
        functools.partial(node_kernel, groups, 1),
        [((members, node_rows, width), f32), three, three, one, one],
        (y_sent, *grads[0::3], *grads[1::3], *grads[2::3], wq, wk, wv),
        specs=[pl.ANY],
    )
    from_plus = shifted(to_minus, -row_width)
    from_minus = shifted(to_plus, row_width)
    def exchange(sent, distance):
        return lax.ppermute(sent, "patch", along_z(count, distance))

    kept_a, out_a, sent_a = call(
        first_kernel,
        [
            ((planes // 2, rows, wide), f32),
            ((half * inner_planes, rows, width), f32),
            ((planes // 2 * wide // 128, rows, 128), bf16),
        ],
        (node, own_a, core_own, y_a), specs=[pl.ANY], flops=2 * 10**10,
    )
    in_a = exchange(sent_a, planes // 2)
    outgoing = call(
        relay_kernel, [three, three],
        (place, sent_a, own_right, own_left, from_plus, from_minus),
        specs=[pltpu.SMEM, pl.ANY], scratch=[trio],
    )
    back = swap(outgoing, 1)
    last = 384 * (groups - half) + width
    more, blocks = wide // 128, last // 128
    own_b, *sent = call(
        functools.partial(second_kernel, 1, len(later)),
        [((rows, last), f32)] + [((blocks, rows, 128), bf16)] * (planes - 1),
        (place, outgoing[0], out_a, y_b, *own_b, *core_own_b),
        specs=[pltpu.SMEM, pl.ANY],
        scratch=[pltpu.VMEM((planes, rows, width), f32)], flops=4 * 10**9,
    )
    riding = planes // 2 - 1
    own_a, *sent[:riding] = call(
        join_kernel,
        [((rows, wide), f32)] + [((blocks + more, rows, 128), bf16)] * riding,
        (kept_a, in_a, *sent[:riding]), flops=2 * 10**10,
    )
    received = [exchange(shard, k) for k, shard in enumerate(sent, 1)]
    (node_grad,) = call(
        finish_kernel, [((members, node_rows, width), bf16)],
        (place, sent[0], *back[::-1], send_rows, node, from_plus, from_minus),
        specs=[pltpu.SMEM, pl.ANY], scratch=[trio], final=True, flops=2 * 10**10,
    )
    (weight_grad,) = call(
        weight_kernel, [((rows, 4 * width), f32)], (node_grad, own_a, own_b, *received),
        specs=[pltpu.HBM], final=True,
    )
    return (node_grad, weight_grad)


def solution(mesh):
    in_specs = (
        P("groups", "patch", None),
        P("groups", "patch", None),
        P(),
        P(),
        P(),
        P(),
        P("patch", None),
        P("patch"),
        P("patch", None, None),
    )
    out_specs = (P("groups", "patch", None), P(("groups", "patch"), None))
    return jax.shard_map(body, mesh=mesh, in_specs=in_specs, out_specs=out_specs, check_vma=False)
```

```python
import functools
import math

import jax
import jax.numpy as jnp
from jax import lax
from jax.experimental import pallas as pl
from jax.experimental.pallas import tpu as pltpu
from jax.sharding import PartitionSpec as P

HEADS = 16
score_cap = 5.0
MIB = 1024 * 1024
f32 = jnp.float32
bf16 = jnp.bfloat16


def nn(a, b):
    return lax.dot_general(a, b, (((1,), (0,)), ((), ())), preferred_element_type=f32)


def nt(a, b):
    return lax.dot_general(a, b, (((1,), (1,)), ((), ())), preferred_element_type=f32)


def shifted(shard, by):
    count = lax.axis_size("patch")
    return lax.ppermute(shard, "patch", [(i, (i + by) % count) for i in range(count)])


def neighbours_apart(count, stride):
    first, second = [], []
    for i in range(count):
        up, down = (i + stride) % count, (i - stride) % count
        even = i // stride % 2 == 0
        first.append((i, up if even else down))
        second.append((i, down if even else up))
    return first, second


def swap(pair, stride):
    first, second = neighbours_apart(lax.axis_size("patch"), stride)
    later = lax.ppermute(pair[1], "patch", second)
    return [lax.ppermute(pair[0], "patch", first), later]


def to_swaps(both, odd, first_ref, second_ref):
    first_ref[...] = both[odd]
    second_ref[...] = both[1 - odd]


def from_swaps(both, odd, first_ref, second_ref):
    both[1 - odd] = first_ref[...]
    both[odd] = second_ref[...]


def sent_selector(send_rows, node_rows):
    adjacent, slots = send_rows.shape
    halo = adjacent * slots
    wide = jnp.concatenate([send_rows] * adjacent, axis=1)
    own = lax.broadcasted_iota(jnp.int32, (adjacent, halo), 1) // slots == lax.broadcasted_iota(
        jnp.int32, (adjacent, halo), 0
    )
    ids = jnp.sum(jnp.where(own, wide, 0), axis=0, keepdims=True)
    nodes = lax.broadcasted_iota(jnp.int32, (node_rows, halo), 0)
    return jnp.where(nodes == ids, 1.0, 0.0).astype(f32)


def gather_kernel(
    slots, send_hbm, x_hbm, plus_ref, minus_ref, right_ref, left_ref, x_ref, send_ref, sem
):
    copies = [
        pltpu.make_async_copy(send_hbm, send_ref, sem.at[0]),
        pltpu.make_async_copy(x_hbm, x_ref, sem.at[1]),
    ]
    for copy in copies:
        copy.start()
    copies[0].wait()
    members, node_rows, _ = x_ref.shape
    pick = sent_selector(send_ref[0], node_rows).T.astype(bf16)
    copies[1].wait()
    for m in range(members):
        rows = nn(pick, x_ref[m]).astype(bf16)

        def part(k):
            return rows[k * slots : (k + 1) * slots]

        for ref, order in ((plus_ref, (2, 6, 4)), (minus_ref, (3, 5, 7))):
            for i, k in enumerate(order):
                ref[m, i] = part(k)
        right_ref[m, 0] = part(0)
        left_ref[m, 0] = part(1)


def relay_kernel(
    me_ref, after_ref, own_right, own_left, plus_ref, minus_ref, first_ref, second_ref, both
):
    for side, own in enumerate((own_right, own_left)):
        both[side, :, 0:1] = own[...]
        both[side, :, 1:2] = plus_ref[:, 1 + side : 2 + side]
        both[side, :, 2:3] = minus_ref[:, 1 + side : 2 + side]
    to_swaps(both, me_ref[0] % 2, first_ref, second_ref)


def gray(z):
    return z ^ (z >> 1)


def plane_of(code):
    z = code
    for shift in range(1, 8):
        z = z ^ (code >> shift)
    return z


def along_z(count, distance):
    planes = count // 4
    return [(i, plane_of(gray(i // 4) ^ distance) * 4 + i % 4) for i in range(planes * 4)]


Q, K, V, G, QT, KT, VT, GT = range(8)


def local_kernel(groups, after_ref, x_ref, *refs):
    sources, loc_refs, xt_ref = refs[:7], refs[7 : 7 + groups], refs[7 + groups]
    copied, sem = refs[8 + groups : 15 + groups], refs[-1]
    copies = [
        pltpu.make_async_copy(source, target, sem.at[i])
        for i, (source, target) in enumerate(zip(sources, copied))
    ]
    for copy in copies:
        copy.start()
    members, node_rows, width = x_ref.shape
    x = x_ref[...].reshape(members * node_rows, width)
    for m in range(members):
        xt_ref[m] = x_ref[m].T

    def put(rows, kind):
        for m in range(members):
            for g, ref in enumerate(loc_refs):
                block = rows[m * node_rows : (m + 1) * node_rows, g * 128 : (g + 1) * 128]
                ref[kind, m] = block
                ref[kind + 4, m] = block.T

    wq_ref, wk_ref, wv_ref, og_ref, _, _, wo_ref = copied
    for kind, ref in enumerate((wq_ref, wk_ref, wv_ref)):
        copies[kind].wait()
        put(nn(x, ref[...]).astype(bf16), kind)
    for copy in copies[3:]:
        copy.wait()
    og = og_ref[...].reshape(members * node_rows, width)
    put(nt(og, wo_ref[...]).astype(bf16), G)


def mask_kernel(after_ref, neigh_ref, count_ref, mask_ref):
    neigh = neigh_ref[...].T
    slots, node_rows = neigh.shape
    table = mask_ref.shape[0]
    order = lax.broadcasted_iota(jnp.int32, neigh.shape, 0)
    tail = jnp.where(order >= count_ref[...], neigh, -1)[slots // 2 :]
    half = table // 2
    for part in range(2):
        columns = lax.broadcasted_iota(jnp.int32, (half, node_rows), 0) + part * half
        kept = jnp.ones((half, node_rows), f32)
        for j in range(slots // 2):
            kept = jnp.where(tail[j : j + 1] == columns, 0.0, kept)
        mask_ref[part * half : (part + 1) * half] = kept


def halo_kernel(
    me_ref, second_in, first_in, plus_ref, minus_ref, xt_ref, wk_ref, wv_ref, *refs
):
    halo_refs, xtf_ref, both = refs[:-2], refs[-2], refs[-1]
    members, _, node_rows = xt_ref.shape
    from_swaps(both, me_ref[0] % 2, first_in, second_in)
    for m in range(members):
        pieces = [None] * 8
        for side, order in enumerate(((0, 6, 5), (1, 4, 7))):
            for i, k in enumerate(order):
                pieces[k] = both[side, m, i]
        pieces[2] = plus_ref[m, 0]
        pieces[3] = minus_ref[m, 0]
        halo = jnp.concatenate(pieces, axis=0)
        xtf_ref[m, :, :node_rows] = xt_ref[m]
        xtf_ref[m, :, node_rows:] = halo.T
        for kind, w_ref in enumerate((wk_ref, wv_ref)):
            rows = nn(halo, w_ref[...]).astype(bf16)
            for g, ref in enumerate(halo_refs):
                block = rows[:, g * 128 : (g + 1) * 128]
                ref[kind, m] = block
                ref[kind + 2, m] = block.T


STRIP = 64


def by_head_t(block, head):
    row_head = lax.broadcasted_iota(jnp.int32, block.shape, 0) // head
    zero = jnp.zeros_like(block)
    return jnp.concatenate(
        [jnp.where(row_head == h, block, zero) for h in range(block.shape[0] // head)], axis=1
    )


def by_head_n(block, head):
    lane_head = lax.broadcasted_iota(jnp.int32, block.shape, 1) // head
    zero = jnp.zeros_like(block)
    return jnp.concatenate(
        [jnp.where(lane_head == h, block, zero) for h in range(block.shape[1] // head)], axis=0
    )


def unnormalised(scale, score, grad, slope, m, lanes, mask_ref, start):
    columns, node_rows = score.shape[1], mask_ref.shape[1]
    den = jnp.zeros((8, node_rows), f32)
    inner = jnp.zeros((8, node_rows), f32)
    for c in range(0, columns, STRIP):
        box = (m, slice(c, c + STRIP), lanes)
        t = jnp.tanh(score[box] * (scale / score_cap))
        e = jnp.exp2(t * (score_cap / math.log(2.0))) * mask_ref[start + c : start + c + STRIP]
        den = den + jnp.sum(e.reshape(STRIP // 8, 8, node_rows), axis=0)
        inner = inner + jnp.sum((e * grad[box]).reshape(STRIP // 8, 8, node_rows), axis=0)
        score[box] = e
        slope[box] = e * (scale - scale * (t * t))
    return den, inner


def own_kernel(groups, *refs):
    locs, mask_ref, outs = refs[:groups], refs[groups], refs[groups + 1 :]
    _, members, node_rows, _ = locs[0].shape
    head = 128 * groups // HEADS
    scale = 1.0 / math.sqrt(head)
    for g, loc in enumerate(locs):
        own, totals = outs[2 * g : 2 * g + 2]
        score, grad, slope = own.at[0], own.at[1], own.at[2]
        for m in range(members):
            score[m] = nn(loc[K, m], by_head_t(loc[QT, m], head))
            grad[m] = nn(loc[V, m], by_head_t(loc[GT, m], head))
        for m in range(members):
            for h in range(128 // head):
                lanes = slice(h * node_rows, (h + 1) * node_rows)
                den, inner = unnormalised(scale, score, grad, slope, m, lanes, mask_ref, 0)
                totals[0, m, :, lanes] = den
                totals[1, m, :, lanes] = inner


def attention_kernel(extra, here, me_ref, *refs):
    refs = refs[extra:]
    locs, halos, owns = refs[:here], refs[here : 2 * here], refs[2 * here : 4 * here]
    refs = refs[4 * here :]
    mask_ref, xtf, og_ref = refs[:3]
    split = 7 if len(refs) == 15 + 3 * (here - 1) else 6
    outs, grads, scratch = refs[3:split], refs[split : split + 3 * here], refs[split + 3 * here :]
    if split == 6:
        outs = (*outs[:2], outs[2].at[0], outs[2].at[1])
    for i in range(here):
        attend(
            me_ref, locs[i], halos[i], owns[2 * i : 2 * i + 2], mask_ref, xtf, og_ref, outs, 512 * i,
            grads[3 * i : 3 * i + 3], scratch,
        )


def attend(me_ref, loc, halo, own, mask_ref, xtf, og_ref, out_refs, at, grad_refs, scratch):
    own_ref, other_ref, send_other, send_own = out_refs
    dq_ref, dk_ref, dv_ref = grad_refs
    score, grad, slope, dw, wos = scratch
    _, members, node_rows, _ = loc.shape
    table = mask_ref.shape[0]
    width = og_ref.shape[2]
    head = width // HEADS
    per = 128 // head
    scale = 1.0 / math.sqrt(head)

    own, totals = own
    for m in range(members):
        score[m] = nn(halo[0, m], by_head_t(loc[QT, m], head))
        grad[m] = nn(halo[1, m], by_head_t(loc[GT, m], head))

    wo_total = None
    kv_total = None
    q_total = None
    for m in range(members):
        probs = []
        for h in range(per):
            lanes = slice(h * node_rows, (h + 1) * node_rows)
            den, inner = unnormalised(scale, score, grad, slope, m, lanes, mask_ref, node_rows)
            r = 1.0 / jnp.sum(den + totals[0, m, :, lanes], axis=0, keepdims=True)
            inner = jnp.sum(inner + totals[1, m, :, lanes], axis=0, keepdims=True) * r
            column = []
            scores = []
            for e, g, w in ((own.at[0], own.at[1], own.at[2]), (score, grad, slope)):
                for c in range(0, e.shape[1], STRIP):
                    box = (m, slice(c, c + STRIP), lanes)
                    column.append((e[box] * r).astype(bf16))
                    scores.append(((w[box] * r) * (g[box] - inner)).astype(bf16))
            probs.append((jnp.concatenate(column, axis=0), jnp.concatenate(scores, axis=0)))
        pb = jnp.concatenate([p for p, _ in probs], axis=1)
        ds = jnp.concatenate([s for _, s in probs], axis=1)
        ktg = jnp.concatenate([loc[KT, m], halo[2, m]], axis=1)
        vtg = jnp.concatenate([loc[VT, m], halo[3, m]], axis=1)
        att, dqt = [], []
        for h in range(0, per, 2):
            lanes = slice(h * node_rows, (h + 2) * node_rows)
            rows = slice(h * head, (h + 2) * head)
            a = nn(vtg[rows], pb[:, lanes])
            b = nn(ktg[rows], ds[:, lanes])
            for j in range(2):
                inside = (slice(j * head, (j + 1) * head), slice(j * node_rows, (j + 1) * node_rows))
                att.append(a[inside].astype(bf16))
                dqt.append(b[inside].astype(bf16))
        att = jnp.concatenate(att, axis=0)
        dq = jnp.concatenate(dqt, axis=0).T
        dk = nn(ds, by_head_n(loc[Q, m], head)).astype(bf16)
        dv = nn(pb, by_head_n(loc[G, m], head)).astype(bf16)
        dq_ref[m], dk_ref[m], dv_ref[m] = dq, dk, dv
        wo_term = nn(att, og_ref[m])
        kv_term = nn(xtf[m], jnp.concatenate([dk, dv], axis=1))
        q_term = nn(xtf[m, :, :node_rows], dq)
        wo_total = wo_term if m == 0 else wo_total + wo_term
        kv_total = kv_term if m == 0 else kv_total + kv_term
        q_total = q_term if m == 0 else q_total + q_term

    planes, _, _, rows, _ = dw.shape
    inner_planes = wos.shape[0]
    dw[:, :, :, :, :128] = q_total.reshape(planes, 2, 2, rows, 128)
    dw[:, :, :, :, 128:] = kv_total.reshape(planes, 2, 2, rows, 256)
    wos[...] = wo_total.reshape(inner_planes, 2, 2, rows, width)
    me = me_ref[0]
    c, y, z = me % 2, (me // 2) % 2, me // 4
    qkv = slice(at, at + 384)
    for k in range(planes):
        zk = plane_of(gray(z) ^ k)
        own_ref[k, :, qkv] = dw[zk, y, c]
        other_ref[k, :, qkv] = dw[zk, 1 - y, c]
        send_other[k, :, qkv] = dw[zk, 1 - y, 1 - c].astype(bf16)
        send_own[k, :, qkv] = dw[zk, y, 1 - c].astype(bf16)
    last = slice(at + 384, at + 512)
    for i in range(inner_planes):
        for n in range(width // 128):
            k = n * inner_planes + i
            lanes = slice(n * 128, (n + 1) * 128)
            own_ref[k, :, last] = wos[i, y, c, :, lanes]
            other_ref[k, :, last] = wos[i, 1 - y, c, :, lanes]
            send_other[k, :, last] = wos[i, 1 - y, 1 - c, :, lanes].astype(bf16)
            send_own[k, :, last] = wos[i, y, 1 - c, :, lanes].astype(bf16)


def node_kernel(groups, skip, *refs):
    refs = refs[skip:]
    dqs, dks, dvs = refs[:groups], refs[groups : 2 * groups], refs[2 * groups : 3 * groups]
    wq_ref, wk_ref, wv_ref, node_ref, plus_ref, minus_ref, right_ref, left_ref = refs[3 * groups :]
    members, node_rows, _ = dqs[0].shape
    slots = plus_ref.shape[2]

    def whole(parts, m):
        return jnp.concatenate([part[m] for part in parts], axis=1)

    for m in range(members):
        spread = nt(whole(dks, m), wk_ref[...]) + nt(whole(dvs, m), wv_ref[...])
        node_ref[m] = spread[:node_rows] + nt(whole(dqs, m), wq_ref[...])
        halo = spread[node_rows:].astype(bf16)
        for ref, order in (
            (plus_ref, (3, 7, 5)),
            (minus_ref, (2, 4, 6)),
            (right_ref, (1,)),
            (left_ref, (0,)),
        ):
            for i, k in enumerate(order):
                ref[m, i] = halo[k * slots : (k + 1) * slots]


def sums(owns, core_in, y_in, k):
    total = jnp.concatenate(
        [
            own[k] + (core[1, k] if len(core.shape) == 4 else core[k]).astype(f32)
            for own, core in zip(owns, core_in)
        ],
        axis=1,
    ) + y_in[k].astype(f32)
    return [total[:, at : at + 512] for at in range(0, total.shape[1], 512)]


def gather_projection(parts, k, planes, projection_ref, start):
    inner_planes = planes * 128 // projection_ref.shape[2]
    quarter, inner = divmod(k, inner_planes)
    for i, part in enumerate(parts):
        plane = start + i * inner_planes + inner
        projection_ref[plane, :, quarter * 128 : (quarter + 1) * 128] = part[:, 384:]


def pack_kernel(pieces, *refs):
    for i, (ref, core) in enumerate(zip(refs[:pieces], refs[pieces:-1])):
        arrived = core[0] if len(core.shape) == 4 else core[...]
        refs[-1][:, :, i * 512 : (i + 1) * 512] = (ref[...] + arrived.astype(f32)).astype(bf16)


def halve(rows, kept_ref, sent_ref):
    half = len(rows) // 2
    for i in range(half):
        kept_ref[i] = rows[i]
        row = rows[i ^ (len(rows) - 1)]
        put(row, sent_ref, i * row.shape[1] // 128)


def add_received(kept_ref, received_ref):
    planes, _, wide = kept_ref.shape
    pieces = wide // 128
    return [
        kept_ref[i]
        + jnp.concatenate([received_ref[i * pieces + n] for n in range(pieces)], axis=1).astype(f32)
        for i in range(planes)
    ]


def first_kernel(after_ref, own, core_in, y_in, kept_ref, projection_ref, sent_ref):
    planes = own.shape[0]
    rows = []
    for k in range(planes):
        parts = sums([own], [core_in], y_in, k)
        gather_projection(parts, k, planes, projection_ref, 0)
        rows.append(jnp.concatenate([part[:, :384] for part in parts], axis=1))
    halve(rows, kept_ref, sent_ref)


def put(row, ref, at):
    for n in range(row.shape[1] // 128):
        ref[at + n] = row[:, n * 128 : (n + 1) * 128].astype(bf16)


def second_kernel(skip, pieces, me_ref, *refs):
    refs = refs[skip:]
    first_ref, y_in = refs[:2]
    owns, core_in = refs[2 : 2 + pieces], refs[2 + pieces : 2 + 2 * pieces]
    own_b, *sent = refs[2 + 2 * pieces : -1]
    projection_ref = refs[-1]
    done = first_ref.shape[0]
    planes = projection_ref.shape[0]
    projection_ref[:done] = first_ref[...]
    held = []
    for k in range(planes):
        parts = sums(owns, core_in, y_in, k)
        gather_projection(parts, k, planes, projection_ref, done)
        held.append(jnp.concatenate([part[:, :384] for part in parts], axis=1))
    z = me_ref[0] // 4
    for k in range(planes):
        row = jnp.concatenate([held[k], projection_ref[plane_of(gray(z) ^ k)]], axis=1)
        if k:
            put(row, sent[k - 1], 0)
        else:
            own_b[...] = row


def join_kernel(kept_a, in_a, *refs):
    count = (len(refs) - 1) // 2
    blocks, own_a, sent = refs[:count], refs[count], refs[count + 1 :]
    first = add_received(kept_a, in_a)
    own_a[...] = first[0]
    for i, ref in enumerate(sent):
        ref[: blocks[i].shape[0]] = blocks[i][...]
        put(first[i + 1], ref, blocks[i].shape[0])


def finish_kernel(
    me_ref, after_ref, second_in, first_in, send_ref, node_ref, plus_ref, minus_ref, out_ref, came
):
    members, node_rows, _ = node_ref.shape
    pick = sent_selector(send_ref[0], node_rows).astype(bf16)
    from_swaps(came, me_ref[0] % 2, first_in, second_in)
    for m in range(members):
        pieces = [None] * 8
        for side, order in enumerate(((1, 4, 7), (0, 6, 5))):
            for i, k in enumerate(order):
                pieces[k] = came[side, m, i]
        pieces[2], pieces[3] = plus_ref[m, 0], minus_ref[m, 0]
        arriving = jnp.concatenate(pieces, axis=0)
        out_ref[m] = (node_ref[m] + nn(pick, arriving)).astype(bf16)


def weight_kernel(after_ref, own_a, own_b, *refs):
    received, out_ref = refs[:-1], refs[-1]
    a, b = own_a[...], own_b[...]
    blocks, more = b.shape[1] // 128, a.shape[1] // 128
    for k, ref in enumerate(received, 1):
        b = b + jnp.concatenate([ref[n] for n in range(blocks)], axis=1).astype(f32)
        if k <= len(received) // 2:
            a = a + jnp.concatenate([ref[blocks + n] for n in range(more)], axis=1).astype(f32)
    width = out_ref.shape[1] // 4
    group = 0
    for part, wide in ((a, a.shape[1]), (b, b.shape[1] - width)):
        for j in range(0, wide, 384):
            for n in range(3):
                at = n * width + group * 128
                out_ref[:, at : at + 128] = part[:, j + n * 128 : j + (n + 1) * 128]
            group += 1
    out_ref[:, 3 * width :] = b[:, b.shape[1] - width :]


def call(kernel, outs, operands, specs=None, scratch=(), limit=12, final=False, flops=10**6):
    specs = list(specs or ())
    specs += [pltpu.VMEM] * (len(operands) - len(specs))
    operands = [
        pltpu.with_memory_space_constraint(o, s) if s in (pltpu.HBM, pltpu.VMEM) else o
        for o, s in zip(operands, specs)
    ]
    return pl.pallas_call(
        kernel,
        out_shape=[jax.ShapeDtypeStruct(*o) if final else pltpu.VMEM(*o) for o in outs],
        in_specs=[pl.BlockSpec(memory_space=s) for s in specs],
        scratch_shapes=list(scratch),
        compiler_params=pltpu.CompilerParams(vmem_limit_bytes=limit * MIB),
        cost_estimate=pl.CostEstimate(flops=flops, bytes_accessed=10**4, transcendentals=0),
    )(*operands)


def body(
    node_features, out_grad, w_query, w_key, w_value, w_out, neighbours, neighbour_count, send_rows
):
    members, node_rows, width = node_features.shape
    count = lax.axis_size("patch")
    row_width = min(8, count // 4)
    _, adjacent, slots = send_rows.shape
    table = node_rows + adjacent * slots
    groups = width // 128
    me = lax.axis_index("patch")
    three = ((members, 3, slots, width), bf16)
    one = ((members, 1, slots, width), bf16)

    place = me.reshape(1)
    trio = pltpu.VMEM((2, *three[0]), bf16)
    to_plus, to_minus, own_right, own_left, x = call(
        functools.partial(gather_kernel, slots),
        [three, three, one, one, (node_features.shape, bf16)],
        (send_rows, node_features),
        specs=[pltpu.HBM] * 2,
        scratch=[pltpu.VMEM(send_rows.shape, jnp.int32), pltpu.SemaphoreType.DMA((2,))],
    )
    plus = shifted(to_plus, row_width)
    minus = shifted(to_minus, -row_width)
    square = ((width, width), bf16)
    counts = neighbour_count.reshape(1, node_rows)
    *loc, xt, wq, wk, wv, og, neigh, counts = call(
        functools.partial(local_kernel, groups),
        [((8, members, node_rows, 128), bf16)] * groups
        + [((members, width, node_rows), bf16), square, square, square, (out_grad.shape, bf16)]
        + [(neighbours.shape, jnp.int32), (counts.shape, jnp.int32)],
        (own_right, x, w_query, w_key, w_value, out_grad, neighbours, counts, w_out),
        specs=[pl.ANY, pltpu.VMEM] + [pltpu.HBM] * 7,
        scratch=[pltpu.VMEM((width, width), bf16), pltpu.SemaphoreType.DMA((7,))],
        limit=16,
    )
    outgoing = call(
        relay_kernel, [three, three], (place, loc[0], own_right, own_left, plus, minus),
        specs=[pltpu.SMEM, pl.ANY], scratch=[trio],
    )
    arrived = swap(outgoing, 1)
    (mask,) = call(
        mask_kernel, [((table, node_rows), f32)], (outgoing[1], neigh, counts), specs=[pl.ANY]
    )
    own_part = call(
        functools.partial(own_kernel, groups),
        [
            ((3, members, node_rows, 4 * node_rows), f32),
            ((2, members, 8, 4 * node_rows), f32),
        ]
        * groups,
        (*loc, mask),
    )
    *halo, xtf = call(
        halo_kernel,
        [((4, members, node_rows, 128), bf16)] * groups + [((members, width, table), bf16)],
        (place, *arrived[::-1], plus, minus, xt, wk, wv), specs=[pltpu.SMEM], scratch=[trio],
    )

    planes, rows = count // 4, width // count
    inner_planes = planes * 128 // width
    flip = [(i, i ^ 1) for i in range(count)]
    flop = [(i, i ^ 2) for i in range(count)]
    grads = []

    def attention(extra, which, together):
        wide = 512 * len(which)
        sends = [((2, planes, rows, wide), bf16)] if together else [((planes, rows, wide), bf16)] * 2
        outs = call(
            functools.partial(attention_kernel, len(extra), len(which)),
            [((planes, rows, wide), f32)] * 2
            + sends
            + [
                ((members, node_rows, 128), bf16),
                ((members, table, 128), bf16),
                ((members, table, 128), bf16),
            ]
            * len(which),
            (
                place, *extra, *[loc[g] for g in which], *[halo[g] for g in which],
                *[part for g in which for part in own_part[2 * g : 2 * g + 2]], mask, xtf, og,
            ),
            specs=[pltpu.SMEM] + [pl.ANY] * len(extra),
            scratch=[pltpu.VMEM((members, table - node_rows, 512), f32)] * 3
            + [
                pltpu.VMEM((planes, 2, 2, rows, 384), f32),
                pltpu.VMEM((inner_planes, 2, 2, rows, width), f32),
            ],
            limit=32,
        )
        sent = outs[2 : 2 + len(sends)]
        grads.extend(outs[2 + len(sends) :])
        arrived = [lax.ppermute(shard, "patch", flip) for shard in sent]
        return outs[0], outs[1], arrived[0], arrived[-1]

    half = groups - 1
    wide = 384 * half
    own_a, other, core_other, core_own = attention((), range(half), False)
    y_sent = (other + core_other.astype(f32)).astype(bf16)
    y_a = lax.ppermute(y_sent, "patch", flop)
    later = [attention((), range(half, groups), False)]
    own_b, other_b, core_other_b, core_own_b = zip(*later)
    (y_sent,) = call(
        functools.partial(pack_kernel, len(later)), [(other_b[0].shape, bf16)],
        (*other_b, *core_other_b),
    )
    y_b = lax.ppermute(y_sent, "patch", flop)
    node, to_plus, to_minus, own_right, own_left = call(
        functools.partial(node_kernel, groups, 1),
        [((members, node_rows, width), f32), three, three, one, one],
        (y_sent, *grads[0::3], *grads[1::3], *grads[2::3], wq, wk, wv),
        specs=[pl.ANY],
    )
    from_plus = shifted(to_minus, -row_width)
    from_minus = shifted(to_plus, row_width)
    def exchange(sent, distance):
        return lax.ppermute(sent, "patch", along_z(count, distance))

    kept_a, out_a, sent_a = call(
        first_kernel,
        [
            ((planes // 2, rows, wide), f32),
            ((half * inner_planes, rows, width), f32),
            ((planes // 2 * wide // 128, rows, 128), bf16),
        ],
        (node, own_a, core_own, y_a), specs=[pl.ANY], flops=2 * 10**10,
    )
    in_a = exchange(sent_a, planes - 1)
    outgoing = call(
        relay_kernel, [three, three],
        (place, sent_a, own_right, own_left, from_plus, from_minus),
        specs=[pltpu.SMEM, pl.ANY], scratch=[trio],
    )
    back = swap(outgoing, 1)
    last = 384 * (groups - half) + width
    more, blocks = wide // 128, last // 128
    own_b, *sent = call(
        functools.partial(second_kernel, 1, len(later)),
        [((rows, last), f32)] + [((blocks, rows, 128), bf16)] * (planes - 1),
        (place, outgoing[0], out_a, y_b, *own_b, *core_own_b),
        specs=[pltpu.SMEM, pl.ANY],
        scratch=[pltpu.VMEM((planes, rows, width), f32)], flops=4 * 10**9,
    )
    riding = planes // 2 - 1
    own_a, *sent[:riding] = call(
        join_kernel,
        [((rows, wide), f32)] + [((blocks + more, rows, 128), bf16)] * riding,
        (kept_a, in_a, *sent[:riding]), flops=2 * 10**10,
    )
    received = [exchange(shard, k) for k, shard in enumerate(sent, 1)]
    (node_grad,) = call(
        finish_kernel, [((members, node_rows, width), bf16)],
        (place, sent[0], *back[::-1], send_rows, node, from_plus, from_minus),
        specs=[pltpu.SMEM, pl.ANY], scratch=[trio], final=True, flops=2 * 10**10,
    )
    (weight_grad,) = call(
        weight_kernel, [((rows, 4 * width), f32)], (node_grad, own_a, own_b, *received),
        specs=[pltpu.HBM], final=True,
    )
    return (node_grad, weight_grad)


def solution(mesh):
    in_specs = (
        P("groups", "patch", None),
        P("groups", "patch", None),
        P(),
        P(),
        P(),
        P(),
        P("patch", None),
        P("patch"),
        P("patch", None, None),
    )
    out_specs = (P("groups", "patch", None), P(("groups", "patch"), None))
    return jax.shard_map(body, mesh=mesh, in_specs=in_specs, out_specs=out_specs, check_vma=False)
```

```python
import functools
import math

import jax
import jax.numpy as jnp
from jax import lax
from jax.experimental import pallas as pl
from jax.experimental.pallas import tpu as pltpu
from jax.sharding import PartitionSpec as P

HEADS = 16
score_cap = 5.0
MIB = 1024 * 1024
f32 = jnp.float32
bf16 = jnp.bfloat16


def nn(a, b):
    return lax.dot_general(a, b, (((1,), (0,)), ((), ())), preferred_element_type=f32)


def nt(a, b):
    return lax.dot_general(a, b, (((1,), (1,)), ((), ())), preferred_element_type=f32)


def shifted(shard, by):
    count = lax.axis_size("patch")
    return lax.ppermute(shard, "patch", [(i, (i + by) % count) for i in range(count)])


def neighbours_apart(count, stride):
    first, second = [], []
    for i in range(count):
        up, down = (i + stride) % count, (i - stride) % count
        even = i // stride % 2 == 0
        first.append((i, up if even else down))
        second.append((i, down if even else up))
    return first, second


def swap(pair, stride):
    first, second = neighbours_apart(lax.axis_size("patch"), stride)
    later = lax.ppermute(pair[1], "patch", second)
    return [lax.ppermute(pair[0], "patch", first), later]


def to_swaps(both, odd, first_ref, second_ref):
    first_ref[...] = both[odd]
    second_ref[...] = both[1 - odd]


def from_swaps(both, odd, first_ref, second_ref):
    both[1 - odd] = first_ref[...]
    both[odd] = second_ref[...]


def sent_selector(send_rows, node_rows):
    adjacent, slots = send_rows.shape
    halo = adjacent * slots
    wide = jnp.concatenate([send_rows] * adjacent, axis=1)
    own = lax.broadcasted_iota(jnp.int32, (adjacent, halo), 1) // slots == lax.broadcasted_iota(
        jnp.int32, (adjacent, halo), 0
    )
    ids = jnp.sum(jnp.where(own, wide, 0), axis=0, keepdims=True)
    nodes = lax.broadcasted_iota(jnp.int32, (node_rows, halo), 0)
    return jnp.where(nodes == ids, 1.0, 0.0).astype(f32)


def gather_kernel(
    slots, send_hbm, x_hbm, plus_ref, minus_ref, right_ref, left_ref, x_ref, send_ref, sem
):
    copies = [
        pltpu.make_async_copy(send_hbm, send_ref, sem.at[0]),
        pltpu.make_async_copy(x_hbm, x_ref, sem.at[1]),
    ]
    for copy in copies:
        copy.start()
    copies[0].wait()
    members, node_rows, _ = x_ref.shape
    pick = sent_selector(send_ref[0], node_rows).T.astype(bf16)
    copies[1].wait()
    for m in range(members):
        rows = nn(pick, x_ref[m]).astype(bf16)

        def part(k):
            return rows[k * slots : (k + 1) * slots]

        for ref, order in ((plus_ref, (2, 6, 4)), (minus_ref, (3, 5, 7))):
            for i, k in enumerate(order):
                ref[m, i] = part(k)
        right_ref[m, 0] = part(0)
        left_ref[m, 0] = part(1)


def relay_kernel(
    me_ref, after_ref, own_right, own_left, plus_ref, minus_ref, first_ref, second_ref, both
):
    for side, own in enumerate((own_right, own_left)):
        both[side, :, 0:1] = own[...]
        both[side, :, 1:2] = plus_ref[:, 1 + side : 2 + side]
        both[side, :, 2:3] = minus_ref[:, 1 + side : 2 + side]
    to_swaps(both, me_ref[0] % 2, first_ref, second_ref)


def gray(z):
    return z ^ (z >> 1)


def plane_of(code):
    z = code
    for shift in range(1, 8):
        z = z ^ (code >> shift)
    return z


def along_z(count, distance):
    planes = count // 4
    return [(i, plane_of(gray(i // 4) ^ distance) * 4 + i % 4) for i in range(planes * 4)]


Q, K, V, G, QT, KT, VT, GT = range(8)


def local_kernel(groups, after_ref, x_ref, *refs):
    sources, loc_refs, xt_ref = refs[:7], refs[7 : 7 + groups], refs[7 + groups]
    copied, sem = refs[8 + groups : 15 + groups], refs[-1]
    copies = [
        pltpu.make_async_copy(source, target, sem.at[i])
        for i, (source, target) in enumerate(zip(sources, copied))
    ]
    for copy in copies:
        copy.start()
    members, node_rows, width = x_ref.shape
    x = x_ref[...].reshape(members * node_rows, width)
    for m in range(members):
        xt_ref[m] = x_ref[m].T

    def put(rows, kind):
        for m in range(members):
            for g, ref in enumerate(loc_refs):
                block = rows[m * node_rows : (m + 1) * node_rows, g * 128 : (g + 1) * 128]
                ref[kind, m] = block
                ref[kind + 4, m] = block.T

    wq_ref, wk_ref, wv_ref, og_ref, _, _, wo_ref = copied
    for kind, ref in enumerate((wq_ref, wk_ref, wv_ref)):
        copies[kind].wait()
        put(nn(x, ref[...]).astype(bf16), kind)
    for copy in copies[3:]:
        copy.wait()
    og = og_ref[...].reshape(members * node_rows, width)
    put(nt(og, wo_ref[...]).astype(bf16), G)


def mask_kernel(after_ref, neigh_ref, count_ref, mask_ref):
    neigh = neigh_ref[...].T
    slots, node_rows = neigh.shape
    table = mask_ref.shape[0]
    order = lax.broadcasted_iota(jnp.int32, neigh.shape, 0)
    tail = jnp.where(order >= count_ref[...], neigh, -1)[slots // 2 :]
    half = table // 2
    for part in range(2):
        columns = lax.broadcasted_iota(jnp.int32, (half, node_rows), 0) + part * half
        kept = jnp.ones((half, node_rows), f32)
        for j in range(slots // 2):
            kept = jnp.where(tail[j : j + 1] == columns, 0.0, kept)
        mask_ref[part * half : (part + 1) * half] = kept


def halo_kernel(
    me_ref, second_in, first_in, plus_ref, minus_ref, xt_ref, wk_ref, wv_ref, *refs
):
    halo_refs, xtf_ref, both = refs[:-2], refs[-2], refs[-1]
    members, _, node_rows = xt_ref.shape
    from_swaps(both, me_ref[0] % 2, first_in, second_in)
    for m in range(members):
        pieces = [None] * 8
        for side, order in enumerate(((0, 6, 5), (1, 4, 7))):
            for i, k in enumerate(order):
                pieces[k] = both[side, m, i]
        pieces[2] = plus_ref[m, 0]
        pieces[3] = minus_ref[m, 0]
        halo = jnp.concatenate(pieces, axis=0)
        xtf_ref[m, :, :node_rows] = xt_ref[m]
        xtf_ref[m, :, node_rows:] = halo.T
        for kind, w_ref in enumerate((wk_ref, wv_ref)):
            rows = nn(halo, w_ref[...]).astype(bf16)
            for g, ref in enumerate(halo_refs):
                block = rows[:, g * 128 : (g + 1) * 128]
                ref[kind, m] = block
                ref[kind + 2, m] = block.T


STRIP = 64


def by_head_t(block, head):
    row_head = lax.broadcasted_iota(jnp.int32, block.shape, 0) // head
    zero = jnp.zeros_like(block)
    return jnp.concatenate(
        [jnp.where(row_head == h, block, zero) for h in range(block.shape[0] // head)], axis=1
    )


def by_head_n(block, head):
    lane_head = lax.broadcasted_iota(jnp.int32, block.shape, 1) // head
    zero = jnp.zeros_like(block)
    return jnp.concatenate(
        [jnp.where(lane_head == h, block, zero) for h in range(block.shape[1] // head)], axis=0
    )


def unnormalised(scale, score, grad, slope, m, lanes, mask_ref, start):
    columns, node_rows = score.shape[1], mask_ref.shape[1]
    den = jnp.zeros((8, node_rows), f32)
    inner = jnp.zeros((8, node_rows), f32)
    for c in range(0, columns, STRIP):
        box = (m, slice(c, c + STRIP), lanes)
        t = jnp.tanh(score[box] * (scale / score_cap))
        e = jnp.exp2(t * (score_cap / math.log(2.0))) * mask_ref[start + c : start + c + STRIP]
        den = den + jnp.sum(e.reshape(STRIP // 8, 8, node_rows), axis=0)
        inner = inner + jnp.sum((e * grad[box]).reshape(STRIP // 8, 8, node_rows), axis=0)
        score[box] = e
        slope[box] = e * (scale - scale * (t * t))
    return den, inner


def own_kernel(groups, *refs):
    locs, mask_ref, outs = refs[:groups], refs[groups], refs[groups + 1 :]
    _, members, node_rows, _ = locs[0].shape
    head = 128 * groups // HEADS
    scale = 1.0 / math.sqrt(head)
    for g, loc in enumerate(locs):
        own, totals = outs[2 * g : 2 * g + 2]
        score, grad, slope = own.at[0], own.at[1], own.at[2]
        for m in range(members):
            score[m] = nn(loc[K, m], by_head_t(loc[QT, m], head))
            grad[m] = nn(loc[V, m], by_head_t(loc[GT, m], head))
        for m in range(members):
            for h in range(128 // head):
                lanes = slice(h * node_rows, (h + 1) * node_rows)
                den, inner = unnormalised(scale, score, grad, slope, m, lanes, mask_ref, 0)
                totals[0, m, :, lanes] = den
                totals[1, m, :, lanes] = inner


def attention_kernel(extra, here, me_ref, *refs):
    refs = refs[extra:]
    locs, halos, owns = refs[:here], refs[here : 2 * here], refs[2 * here : 4 * here]
    refs = refs[4 * here :]
    mask_ref, xtf, og_ref = refs[:3]
    split = 7 if len(refs) == 15 + 3 * (here - 1) else 6
    outs, grads, scratch = refs[3:split], refs[split : split + 3 * here], refs[split + 3 * here :]
    if split == 6:
        outs = (*outs[:2], outs[2].at[0], outs[2].at[1])
    for i in range(here):
        attend(
            me_ref, locs[i], halos[i], owns[2 * i : 2 * i + 2], mask_ref, xtf, og_ref, outs, 512 * i,
            grads[3 * i : 3 * i + 3], scratch,
        )


def attend(me_ref, loc, halo, own, mask_ref, xtf, og_ref, out_refs, at, grad_refs, scratch):
    own_ref, other_ref, send_other, send_own = out_refs
    dq_ref, dk_ref, dv_ref = grad_refs
    score, grad, slope, dw, wos = scratch
    _, members, node_rows, _ = loc.shape
    table = mask_ref.shape[0]
    width = og_ref.shape[2]
    head = width // HEADS
    per = 128 // head
    scale = 1.0 / math.sqrt(head)

    own, totals = own
    for m in range(members):
        score[m] = nn(halo[0, m], by_head_t(loc[QT, m], head))
        grad[m] = nn(halo[1, m], by_head_t(loc[GT, m], head))

    wo_total = None
    kv_total = None
    q_total = None
    for m in range(members):
        probs = []
        for h in range(per):
            lanes = slice(h * node_rows, (h + 1) * node_rows)
            den, inner = unnormalised(scale, score, grad, slope, m, lanes, mask_ref, node_rows)
            r = 1.0 / jnp.sum(den + totals[0, m, :, lanes], axis=0, keepdims=True)
            inner = jnp.sum(inner + totals[1, m, :, lanes], axis=0, keepdims=True) * r
            column = []
            scores = []
            for e, g, w in ((own.at[0], own.at[1], own.at[2]), (score, grad, slope)):
                for c in range(0, e.shape[1], STRIP):
                    box = (m, slice(c, c + STRIP), lanes)
                    column.append((e[box] * r).astype(bf16))
                    scores.append(((w[box] * r) * (g[box] - inner)).astype(bf16))
            probs.append((jnp.concatenate(column, axis=0), jnp.concatenate(scores, axis=0)))
        pb = jnp.concatenate([p for p, _ in probs], axis=1)
        ds = jnp.concatenate([s for _, s in probs], axis=1)
        ktg = jnp.concatenate([loc[KT, m], halo[2, m]], axis=1)
        vtg = jnp.concatenate([loc[VT, m], halo[3, m]], axis=1)
        att, dqt = [], []
        for h in range(0, per, 2):
            lanes = slice(h * node_rows, (h + 2) * node_rows)
            rows = slice(h * head, (h + 2) * head)
            a = nn(vtg[rows], pb[:, lanes])
            b = nn(ktg[rows], ds[:, lanes])
            for j in range(2):
                inside = (slice(j * head, (j + 1) * head), slice(j * node_rows, (j + 1) * node_rows))
                att.append(a[inside].astype(bf16))
                dqt.append(b[inside].astype(bf16))
        att = jnp.concatenate(att, axis=0)
        dq = jnp.concatenate(dqt, axis=0).T
        dk = nn(ds, by_head_n(loc[Q, m], head)).astype(bf16)
        dv = nn(pb, by_head_n(loc[G, m], head)).astype(bf16)
        dq_ref[m], dk_ref[m], dv_ref[m] = dq, dk, dv
        wo_term = nn(att, og_ref[m])
        kv_term = nn(xtf[m], jnp.concatenate([dk, dv], axis=1))
        q_term = nn(xtf[m, :, :node_rows], dq)
        wo_total = wo_term if m == 0 else wo_total + wo_term
        kv_total = kv_term if m == 0 else kv_total + kv_term
        q_total = q_term if m == 0 else q_total + q_term

    planes, _, _, rows, _ = dw.shape
    inner_planes = wos.shape[0]
    dw[:, :, :, :, :128] = q_total.reshape(planes, 2, 2, rows, 128)
    dw[:, :, :, :, 128:] = kv_total.reshape(planes, 2, 2, rows, 256)
    wos[...] = wo_total.reshape(inner_planes, 2, 2, rows, width)
    me = me_ref[0]
    c, y, z = me % 2, (me // 2) % 2, me // 4
    qkv = slice(at, at + 384)
    for k in range(planes):
        zk = plane_of(gray(z) ^ k)
        own_ref[k, :, qkv] = dw[zk, y, c]
        other_ref[k, :, qkv] = dw[zk, 1 - y, c]
        send_other[k, :, qkv] = dw[zk, 1 - y, 1 - c].astype(bf16)
        send_own[k, :, qkv] = dw[zk, y, 1 - c].astype(bf16)
    last = slice(at + 384, at + 512)
    for i in range(inner_planes):
        for n in range(width // 128):
            k = n * inner_planes + i
            lanes = slice(n * 128, (n + 1) * 128)
            own_ref[k, :, last] = wos[i, y, c, :, lanes]
            other_ref[k, :, last] = wos[i, 1 - y, c, :, lanes]
            send_other[k, :, last] = wos[i, 1 - y, 1 - c, :, lanes].astype(bf16)
            send_own[k, :, last] = wos[i, y, 1 - c, :, lanes].astype(bf16)


def node_kernel(groups, skip, *refs):
    refs = refs[skip:]
    dqs, dks, dvs = refs[:groups], refs[groups : 2 * groups], refs[2 * groups : 3 * groups]
    wq_ref, wk_ref, wv_ref, node_ref, plus_ref, minus_ref, right_ref, left_ref = refs[3 * groups :]
    members, node_rows, _ = dqs[0].shape
    slots = plus_ref.shape[2]

    def whole(parts, m):
        return jnp.concatenate([part[m] for part in parts], axis=1)

    for m in range(members):
        spread = nt(whole(dks, m), wk_ref[...]) + nt(whole(dvs, m), wv_ref[...])
        node_ref[m] = spread[:node_rows] + nt(whole(dqs, m), wq_ref[...])
        halo = spread[node_rows:].astype(bf16)
        for ref, order in (
            (plus_ref, (3, 7, 5)),
            (minus_ref, (2, 4, 6)),
            (right_ref, (1,)),
            (left_ref, (0,)),
        ):
            for i, k in enumerate(order):
                ref[m, i] = halo[k * slots : (k + 1) * slots]


def sums(owns, core_in, y_in, k):
    total = jnp.concatenate(
        [
            own[k] + (core[1, k] if len(core.shape) == 4 else core[k]).astype(f32)
            for own, core in zip(owns, core_in)
        ],
        axis=1,
    ) + y_in[k].astype(f32)
    return [total[:, at : at + 512] for at in range(0, total.shape[1], 512)]


def gather_projection(parts, k, planes, projection_ref, start):
    inner_planes = planes * 128 // projection_ref.shape[2]
    quarter, inner = divmod(k, inner_planes)
    for i, part in enumerate(parts):
        plane = start + i * inner_planes + inner
        projection_ref[plane, :, quarter * 128 : (quarter + 1) * 128] = part[:, 384:]


def pack_kernel(pieces, *refs):
    for i, (ref, core) in enumerate(zip(refs[:pieces], refs[pieces:-1])):
        arrived = core[0] if len(core.shape) == 4 else core[...]
        refs[-1][:, :, i * 512 : (i + 1) * 512] = (ref[...] + arrived.astype(f32)).astype(bf16)


def halve(rows, kept_ref, sent_ref):
    for i, row in enumerate(rows):
        if i % 2 == 0:
            kept_ref[i // 2] = row
            continue
        pieces = row.shape[1] // 128
        for n in range(pieces):
            sent_ref[i // 2 * pieces + n] = row[:, n * 128 : (n + 1) * 128].astype(bf16)


def add_received(kept_ref, received_ref):
    planes, _, wide = kept_ref.shape
    pieces = wide // 128
    return [
        kept_ref[i]
        + jnp.concatenate([received_ref[i * pieces + n] for n in range(pieces)], axis=1).astype(f32)
        for i in range(planes)
    ]


def first_kernel(after_ref, own, core_in, y_in, kept_ref, projection_ref, sent_ref):
    planes = own.shape[0]
    rows = []
    for k in range(planes):
        parts = sums([own], [core_in], y_in, k)
        gather_projection(parts, k, planes, projection_ref, 0)
        rows.append(jnp.concatenate([part[:, :384] for part in parts], axis=1))
    halve(rows, kept_ref, sent_ref)


def put(row, ref, at):
    for n in range(row.shape[1] // 128):
        ref[at + n] = row[:, n * 128 : (n + 1) * 128].astype(bf16)


def second_kernel(skip, pieces, me_ref, *refs):
    refs = refs[skip:]
    first_ref, y_in = refs[:2]
    owns, core_in = refs[2 : 2 + pieces], refs[2 + pieces : 2 + 2 * pieces]
    own_b, *sent = refs[2 + 2 * pieces : -1]
    projection_ref = refs[-1]
    done = first_ref.shape[0]
    planes = projection_ref.shape[0]
    projection_ref[:done] = first_ref[...]
    held = []
    for k in range(planes):
        parts = sums(owns, core_in, y_in, k)
        gather_projection(parts, k, planes, projection_ref, done)
        held.append(jnp.concatenate([part[:, :384] for part in parts], axis=1))
    z = me_ref[0] // 4
    for k in range(planes):
        row = jnp.concatenate([held[k], projection_ref[plane_of(gray(z) ^ k)]], axis=1)
        if k:
            put(row, sent[k - 1], 0)
        else:
            own_b[...] = row


def join_kernel(kept_a, in_a, *refs):
    count = (len(refs) - 1) // 2
    blocks, own_a, sent = refs[:count], refs[count], refs[count + 1 :]
    first = add_received(kept_a, in_a)
    own_a[...] = first[0]
    for i, ref in enumerate(sent):
        ref[: blocks[i].shape[0]] = blocks[i][...]
        put(first[i + 1], ref, blocks[i].shape[0])


def finish_kernel(
    me_ref, after_ref, second_in, first_in, send_ref, node_ref, plus_ref, minus_ref, out_ref, came
):
    members, node_rows, _ = node_ref.shape
    pick = sent_selector(send_ref[0], node_rows).astype(bf16)
    from_swaps(came, me_ref[0] % 2, first_in, second_in)
    for m in range(members):
        pieces = [None] * 8
        for side, order in enumerate(((1, 4, 7), (0, 6, 5))):
            for i, k in enumerate(order):
                pieces[k] = came[side, m, i]
        pieces[2], pieces[3] = plus_ref[m, 0], minus_ref[m, 0]
        arriving = jnp.concatenate(pieces, axis=0)
        out_ref[m] = (node_ref[m] + nn(pick, arriving)).astype(bf16)


def weight_kernel(after_ref, own_a, own_b, *refs):
    received, out_ref = refs[-2::-1], refs[-1]
    a, b = own_a[...], own_b[...]
    blocks, more = b.shape[1] // 128, a.shape[1] // 128
    for k, ref in enumerate(received, 1):
        b = b + jnp.concatenate([ref[n] for n in range(blocks)], axis=1).astype(f32)
        if k % 2 == 0:
            a = a + jnp.concatenate([ref[blocks + n] for n in range(more)], axis=1).astype(f32)
    width = out_ref.shape[1] // 4
    group = 0
    for part, wide in ((a, a.shape[1]), (b, b.shape[1] - width)):
        for j in range(0, wide, 384):
            for n in range(3):
                at = n * width + group * 128
                out_ref[:, at : at + 128] = part[:, j + n * 128 : j + (n + 1) * 128]
            group += 1
    out_ref[:, 3 * width :] = b[:, b.shape[1] - width :]


def call(kernel, outs, operands, specs=None, scratch=(), limit=12, final=False, flops=10**6):
    specs = list(specs or ())
    specs += [pltpu.VMEM] * (len(operands) - len(specs))
    operands = [
        pltpu.with_memory_space_constraint(o, s) if s in (pltpu.HBM, pltpu.VMEM) else o
        for o, s in zip(operands, specs)
    ]
    return pl.pallas_call(
        kernel,
        out_shape=[jax.ShapeDtypeStruct(*o) if final else pltpu.VMEM(*o) for o in outs],
        in_specs=[pl.BlockSpec(memory_space=s) for s in specs],
        scratch_shapes=list(scratch),
        compiler_params=pltpu.CompilerParams(vmem_limit_bytes=limit * MIB),
        cost_estimate=pl.CostEstimate(flops=flops, bytes_accessed=10**4, transcendentals=0),
    )(*operands)


def body(
    node_features, out_grad, w_query, w_key, w_value, w_out, neighbours, neighbour_count, send_rows
):
    members, node_rows, width = node_features.shape
    count = lax.axis_size("patch")
    row_width = min(8, count // 4)
    _, adjacent, slots = send_rows.shape
    table = node_rows + adjacent * slots
    groups = width // 128
    me = lax.axis_index("patch")
    three = ((members, 3, slots, width), bf16)
    one = ((members, 1, slots, width), bf16)

    place = me.reshape(1)
    trio = pltpu.VMEM((2, *three[0]), bf16)
    to_plus, to_minus, own_right, own_left, x = call(
        functools.partial(gather_kernel, slots),
        [three, three, one, one, (node_features.shape, bf16)],
        (send_rows, node_features),
        specs=[pltpu.HBM] * 2,
        scratch=[pltpu.VMEM(send_rows.shape, jnp.int32), pltpu.SemaphoreType.DMA((2,))],
    )
    plus = shifted(to_plus, row_width)
    minus = shifted(to_minus, -row_width)
    square = ((width, width), bf16)
    counts = neighbour_count.reshape(1, node_rows)
    *loc, xt, wq, wk, wv, og, neigh, counts = call(
        functools.partial(local_kernel, groups),
        [((8, members, node_rows, 128), bf16)] * groups
        + [((members, width, node_rows), bf16), square, square, square, (out_grad.shape, bf16)]
        + [(neighbours.shape, jnp.int32), (counts.shape, jnp.int32)],
        (own_right, x, w_query, w_key, w_value, out_grad, neighbours, counts, w_out),
        specs=[pl.ANY, pltpu.VMEM] + [pltpu.HBM] * 7,
        scratch=[pltpu.VMEM((width, width), bf16), pltpu.SemaphoreType.DMA((7,))],
        limit=16,
    )
    outgoing = call(
        relay_kernel, [three, three], (place, loc[0], own_right, own_left, plus, minus),
        specs=[pltpu.SMEM, pl.ANY], scratch=[trio],
    )
    arrived = swap(outgoing, 1)
    (mask,) = call(
        mask_kernel, [((table, node_rows), f32)], (outgoing[1], neigh, counts), specs=[pl.ANY]
    )
    own_part = call(
        functools.partial(own_kernel, groups),
        [
            ((3, members, node_rows, 4 * node_rows), f32),
            ((2, members, 8, 4 * node_rows), f32),
        ]
        * groups,
        (*loc, mask),
    )
    *halo, xtf = call(
        halo_kernel,
        [((4, members, node_rows, 128), bf16)] * groups + [((members, width, table), bf16)],
        (place, *arrived[::-1], plus, minus, xt, wk, wv), specs=[pltpu.SMEM], scratch=[trio],
    )

    planes, rows = count // 4, width // count
    inner_planes = planes * 128 // width
    flip = [(i, i ^ 1) for i in range(count)]
    flop = [(i, i ^ 2) for i in range(count)]
    grads = []

    def attention(extra, which, together):
        wide = 512 * len(which)
        sends = [((2, planes, rows, wide), bf16)] if together else [((planes, rows, wide), bf16)] * 2
        outs = call(
            functools.partial(attention_kernel, len(extra), len(which)),
            [((planes, rows, wide), f32)] * 2
            + sends
            + [
                ((members, node_rows, 128), bf16),
                ((members, table, 128), bf16),
                ((members, table, 128), bf16),
            ]
            * len(which),
            (
                place, *extra, *[loc[g] for g in which], *[halo[g] for g in which],
                *[part for g in which for part in own_part[2 * g : 2 * g + 2]], mask, xtf, og,
            ),
            specs=[pltpu.SMEM] + [pl.ANY] * len(extra),
            scratch=[pltpu.VMEM((members, table - node_rows, 512), f32)] * 3
            + [
                pltpu.VMEM((planes, 2, 2, rows, 384), f32),
                pltpu.VMEM((inner_planes, 2, 2, rows, width), f32),
            ],
            limit=32,
        )
        sent = outs[2 : 2 + len(sends)]
        grads.extend(outs[2 + len(sends) :])
        arrived = [lax.ppermute(shard, "patch", flip) for shard in sent]
        return outs[0], outs[1], arrived[0], arrived[-1]

    half = groups - 1
    wide = 384 * half
    own_a, other, core_other, core_own = attention((), range(half), False)
    y_sent = (other + core_other.astype(f32)).astype(bf16)
    y_a = lax.ppermute(y_sent, "patch", flop)
    later = [attention((), range(half, groups), False)]
    own_b, other_b, core_other_b, core_own_b = zip(*later)
    (y_sent,) = call(
        functools.partial(pack_kernel, len(later)), [(other_b[0].shape, bf16)],
        (*other_b, *core_other_b),
    )
    y_b = lax.ppermute(y_sent, "patch", flop)
    node, to_plus, to_minus, own_right, own_left = call(
        functools.partial(node_kernel, groups, 1),
        [((members, node_rows, width), f32), three, three, one, one],
        (y_sent, *grads[0::3], *grads[1::3], *grads[2::3], wq, wk, wv),
        specs=[pl.ANY],
    )
    from_plus = shifted(to_minus, -row_width)
    from_minus = shifted(to_plus, row_width)
    def exchange(sent, distance):
        return lax.ppermute(sent, "patch", along_z(count, distance))

    kept_a, out_a, sent_a = call(
        first_kernel,
        [
            ((planes // 2, rows, wide), f32),
            ((half * inner_planes, rows, width), f32),
            ((planes // 2 * wide // 128, rows, 128), bf16),
        ],
        (node, own_a, core_own, y_a), specs=[pl.ANY], flops=2 * 10**10,
    )
    in_a = exchange(sent_a, 1)
    outgoing = call(
        relay_kernel, [three, three],
        (place, sent_a, own_right, own_left, from_plus, from_minus),
        specs=[pltpu.SMEM, pl.ANY], scratch=[trio],
    )
    back = swap(outgoing, 1)
    last = 384 * (groups - half) + width
    more, blocks = wide // 128, last // 128
    own_b, *sent = call(
        functools.partial(second_kernel, 1, len(later)),
        [((rows, last), f32)] + [((blocks, rows, 128), bf16)] * (planes - 1),
        (place, outgoing[0], out_a, y_b, *own_b, *core_own_b),
        specs=[pltpu.SMEM, pl.ANY],
        scratch=[pltpu.VMEM((planes, rows, width), f32)], flops=4 * 10**9,
    )
    own_a, *sent[1::2] = call(
        join_kernel,
        [((rows, wide), f32)] + [((blocks + more, rows, 128), bf16)] * (planes // 2 - 1),
        (kept_a, in_a, *sent[1::2]), flops=2 * 10**10,
    )
    received = [exchange(shard, k) for k, shard in enumerate(sent, 1)]
    (node_grad,) = call(
        finish_kernel, [((members, node_rows, width), bf16)],
        (place, sent[0], *back[::-1], send_rows, node, from_plus, from_minus),
        specs=[pltpu.SMEM, pl.ANY], scratch=[trio], final=True, flops=2 * 10**10,
    )
    (weight_grad,) = call(
        weight_kernel, [((rows, 4 * width), f32)], (node_grad, own_a, own_b, *received[::-1]),
        specs=[pltpu.HBM], final=True,
    )
    return (node_grad, weight_grad)


def solution(mesh):
    in_specs = (
        P("groups", "patch", None),
        P("groups", "patch", None),
        P(),
        P(),
        P(),
        P(),
        P("patch", None),
        P("patch"),
        P("patch", None, None),
    )
    out_specs = (P("groups", "patch", None), P(("groups", "patch"), None))
    return jax.shard_map(body, mesh=mesh, in_specs=in_specs, out_specs=out_specs, check_vma=False)
```

```python
import functools
import math

import jax
import jax.numpy as jnp
from jax import lax
from jax.experimental import pallas as pl
from jax.experimental.pallas import tpu as pltpu
from jax.sharding import PartitionSpec as P

HEADS = 16
score_cap = 5.0
MIB = 1024 * 1024
f32 = jnp.float32
bf16 = jnp.bfloat16


def nn(a, b):
    return lax.dot_general(a, b, (((1,), (0,)), ((), ())), preferred_element_type=f32)


def nt(a, b):
    return lax.dot_general(a, b, (((1,), (1,)), ((), ())), preferred_element_type=f32)


def shifted(shard, by):
    count = lax.axis_size("patch")
    return lax.ppermute(shard, "patch", [(i, (i + by) % count) for i in range(count)])


def neighbours_apart(count, stride):
    first, second = [], []
    for i in range(count):
        up, down = (i + stride) % count, (i - stride) % count
        even = i // stride % 2 == 0
        first.append((i, up if even else down))
        second.append((i, down if even else up))
    return first, second


def swap(pair, stride):
    first, second = neighbours_apart(lax.axis_size("patch"), stride)
    later = lax.ppermute(pair[1], "patch", second)
    return [lax.ppermute(pair[0], "patch", first), later]


def to_swaps(both, odd, first_ref, second_ref):
    first_ref[...] = both[odd]
    second_ref[...] = both[1 - odd]


def from_swaps(both, odd, first_ref, second_ref):
    both[1 - odd] = first_ref[...]
    both[odd] = second_ref[...]


def sent_selector(send_rows, node_rows):
    adjacent, slots = send_rows.shape
    halo = adjacent * slots
    wide = jnp.concatenate([send_rows] * adjacent, axis=1)
    own = lax.broadcasted_iota(jnp.int32, (adjacent, halo), 1) // slots == lax.broadcasted_iota(
        jnp.int32, (adjacent, halo), 0
    )
    ids = jnp.sum(jnp.where(own, wide, 0), axis=0, keepdims=True)
    nodes = lax.broadcasted_iota(jnp.int32, (node_rows, halo), 0)
    return jnp.where(nodes == ids, 1.0, 0.0).astype(f32)


def gather_kernel(
    slots, send_hbm, x_hbm, plus_ref, minus_ref, right_ref, left_ref, x_ref, send_ref, sem
):
    copies = [
        pltpu.make_async_copy(send_hbm, send_ref, sem.at[0]),
        pltpu.make_async_copy(x_hbm, x_ref, sem.at[1]),
    ]
    for copy in copies:
        copy.start()
    copies[0].wait()
    members, node_rows, _ = x_ref.shape
    pick = sent_selector(send_ref[0], node_rows).T.astype(bf16)
    copies[1].wait()
    for m in range(members):
        rows = nn(pick, x_ref[m]).astype(bf16)

        def part(k):
            return rows[k * slots : (k + 1) * slots]

        for ref, order in ((plus_ref, (2, 6, 4)), (minus_ref, (3, 5, 7))):
            for i, k in enumerate(order):
                ref[m, i] = part(k)
        right_ref[m, 0] = part(0)
        left_ref[m, 0] = part(1)


def relay_kernel(
    me_ref, after_ref, own_right, own_left, plus_ref, minus_ref, first_ref, second_ref, both
):
    for side, own in enumerate((own_right, own_left)):
        both[side, :, 0:1] = own[...]
        both[side, :, 1:2] = plus_ref[:, 1 + side : 2 + side]
        both[side, :, 2:3] = minus_ref[:, 1 + side : 2 + side]
    to_swaps(both, me_ref[0] % 2, first_ref, second_ref)


def gray(z):
    return z ^ (z >> 1)


def plane_of(code):
    z = code
    for shift in range(1, 8):
        z = z ^ (code >> shift)
    return z


def along_z(count, distance):
    planes = count // 4
    return [(i, plane_of(gray(i // 4) ^ distance) * 4 + i % 4) for i in range(planes * 4)]


Q, K, V, G, QT, KT, VT, GT = range(8)


def local_kernel(groups, after_ref, x_ref, *refs):
    sources, loc_refs, xt_ref = refs[:7], refs[7 : 7 + groups], refs[7 + groups]
    copied, sem = refs[8 + groups : 15 + groups], refs[-1]
    copies = [
        pltpu.make_async_copy(source, target, sem.at[i])
        for i, (source, target) in enumerate(zip(sources, copied))
    ]
    for copy in copies:
        copy.start()
    members, node_rows, width = x_ref.shape
    x = x_ref[...].reshape(members * node_rows, width)
    for m in range(members):
        xt_ref[m] = x_ref[m].T

    def put(rows, kind):
        for m in range(members):
            for g, ref in enumerate(loc_refs):
                block = rows[m * node_rows : (m + 1) * node_rows, g * 128 : (g + 1) * 128]
                ref[kind, m] = block
                ref[kind + 4, m] = block.T

    wq_ref, wk_ref, wv_ref, og_ref, _, _, wo_ref = copied
    for kind, ref in enumerate((wq_ref, wk_ref, wv_ref)):
        copies[kind].wait()
        put(nn(x, ref[...]).astype(bf16), kind)
    for copy in copies[3:]:
        copy.wait()
    og = og_ref[...].reshape(members * node_rows, width)
    put(nt(og, wo_ref[...]).astype(bf16), G)


def mask_kernel(after_ref, neigh_ref, count_ref, mask_ref):
    neigh = neigh_ref[...].T
    slots, node_rows = neigh.shape
    table = mask_ref.shape[0]
    order = lax.broadcasted_iota(jnp.int32, neigh.shape, 0)
    tail = jnp.where(order >= count_ref[...], neigh, -1)[slots // 2 :]
    half = table // 2
    for part in range(2):
        columns = lax.broadcasted_iota(jnp.int32, (half, node_rows), 0) + part * half
        kept = jnp.ones((half, node_rows), f32)
        for j in range(slots // 2):
            kept = jnp.where(tail[j : j + 1] == columns, 0.0, kept)
        mask_ref[part * half : (part + 1) * half] = kept


def halo_kernel(
    me_ref, second_in, first_in, plus_ref, minus_ref, xt_ref, wk_ref, wv_ref, *refs
):
    halo_refs, xtf_ref, both = refs[:-2], refs[-2], refs[-1]
    members, _, node_rows = xt_ref.shape
    from_swaps(both, me_ref[0] % 2, first_in, second_in)
    for m in range(members):
        pieces = [None] * 8
        for side, order in enumerate(((0, 6, 5), (1, 4, 7))):
            for i, k in enumerate(order):
                pieces[k] = both[side, m, i]
        pieces[2] = plus_ref[m, 0]
        pieces[3] = minus_ref[m, 0]
        halo = jnp.concatenate(pieces, axis=0)
        xtf_ref[m, :, :node_rows] = xt_ref[m]
        xtf_ref[m, :, node_rows:] = halo.T
        for kind, w_ref in enumerate((wk_ref, wv_ref)):
            rows = nn(halo, w_ref[...]).astype(bf16)
            for g, ref in enumerate(halo_refs):
                block = rows[:, g * 128 : (g + 1) * 128]
                ref[kind, m] = block
                ref[kind + 2, m] = block.T


STRIP = 64


def by_head_t(block, head):
    row_head = lax.broadcasted_iota(jnp.int32, block.shape, 0) // head
    zero = jnp.zeros_like(block)
    return jnp.concatenate(
        [jnp.where(row_head == h, block, zero) for h in range(block.shape[0] // head)], axis=1
    )


def by_head_n(block, head):
    lane_head = lax.broadcasted_iota(jnp.int32, block.shape, 1) // head
    zero = jnp.zeros_like(block)
    return jnp.concatenate(
        [jnp.where(lane_head == h, block, zero) for h in range(block.shape[1] // head)], axis=0
    )


def unnormalised(scale, score, grad, slope, m, lanes, mask_ref, start):
    columns, node_rows = score.shape[1], mask_ref.shape[1]
    den = jnp.zeros((8, node_rows), f32)
    inner = jnp.zeros((8, node_rows), f32)
    for c in range(0, columns, STRIP):
        box = (m, slice(c, c + STRIP), lanes)
        t = jnp.tanh(score[box] * (scale / score_cap))
        e = jnp.exp2(t * (score_cap / math.log(2.0))) * mask_ref[start + c : start + c + STRIP]
        den = den + jnp.sum(e.reshape(STRIP // 8, 8, node_rows), axis=0)
        inner = inner + jnp.sum((e * grad[box]).reshape(STRIP // 8, 8, node_rows), axis=0)
        score[box] = e
        slope[box] = e * (scale - scale * (t * t))
    return den, inner


def own_kernel(groups, *refs):
    locs, mask_ref, outs = refs[:groups], refs[groups], refs[groups + 1 :]
    _, members, node_rows, _ = locs[0].shape
    head = 128 * groups // HEADS
    scale = 1.0 / math.sqrt(head)
    for g, loc in enumerate(locs):
        own, totals = outs[2 * g : 2 * g + 2]
        score, grad, slope = own.at[0], own.at[1], own.at[2]
        for m in range(members):
            score[m] = nn(loc[K, m], by_head_t(loc[QT, m], head))
            grad[m] = nn(loc[V, m], by_head_t(loc[GT, m], head))
        for m in range(members):
            for h in range(128 // head):
                lanes = slice(h * node_rows, (h + 1) * node_rows)
                den, inner = unnormalised(scale, score, grad, slope, m, lanes, mask_ref, 0)
                totals[0, m, :, lanes] = den
                totals[1, m, :, lanes] = inner


def attention_kernel(extra, here, me_ref, *refs):
    refs = refs[extra:]
    locs, halos, owns = refs[:here], refs[here : 2 * here], refs[2 * here : 4 * here]
    refs = refs[4 * here :]
    mask_ref, xtf, og_ref = refs[:3]
    split = 7 if len(refs) == 15 + 3 * (here - 1) else 6
    outs, grads, scratch = refs[3:split], refs[split : split + 3 * here], refs[split + 3 * here :]
    if split == 6:
        outs = (*outs[:2], outs[2].at[0], outs[2].at[1])
    for i in range(here):
        attend(
            me_ref, locs[i], halos[i], owns[2 * i : 2 * i + 2], mask_ref, xtf, og_ref, outs, 512 * i,
            grads[3 * i : 3 * i + 3], scratch,
        )


def attend(me_ref, loc, halo, own, mask_ref, xtf, og_ref, out_refs, at, grad_refs, scratch):
    own_ref, other_ref, send_other, send_own = out_refs
    dq_ref, dk_ref, dv_ref = grad_refs
    score, grad, slope, dw, wos = scratch
    _, members, node_rows, _ = loc.shape
    table = mask_ref.shape[0]
    width = og_ref.shape[2]
    head = width // HEADS
    per = 128 // head
    scale = 1.0 / math.sqrt(head)

    own, totals = own
    for m in range(members):
        score[m] = nn(halo[0, m], by_head_t(loc[QT, m], head))
        grad[m] = nn(halo[1, m], by_head_t(loc[GT, m], head))

    wo_total = None
    kv_total = None
    q_total = None
    for m in range(members):
        probs = []
        for h in range(per):
            lanes = slice(h * node_rows, (h + 1) * node_rows)
            den, inner = unnormalised(scale, score, grad, slope, m, lanes, mask_ref, node_rows)
            r = 1.0 / jnp.sum(den + totals[0, m, :, lanes], axis=0, keepdims=True)
            inner = jnp.sum(inner + totals[1, m, :, lanes], axis=0, keepdims=True) * r
            column = []
            scores = []
            for e, g, w in ((own.at[0], own.at[1], own.at[2]), (score, grad, slope)):
                for c in range(0, e.shape[1], STRIP):
                    box = (m, slice(c, c + STRIP), lanes)
                    column.append((e[box] * r).astype(bf16))
                    scores.append(((w[box] * r) * (g[box] - inner)).astype(bf16))
            probs.append((jnp.concatenate(column, axis=0), jnp.concatenate(scores, axis=0)))
        pb = jnp.concatenate([p for p, _ in probs], axis=1)
        ds = jnp.concatenate([s for _, s in probs], axis=1)
        ktg = jnp.concatenate([loc[KT, m], halo[2, m]], axis=1)
        vtg = jnp.concatenate([loc[VT, m], halo[3, m]], axis=1)
        att, dqt = [], []
        for h in range(0, per, 2):
            lanes = slice(h * node_rows, (h + 2) * node_rows)
            rows = slice(h * head, (h + 2) * head)
            a = nn(vtg[rows], pb[:, lanes])
            b = nn(ktg[rows], ds[:, lanes])
            for j in range(2):
                inside = (slice(j * head, (j + 1) * head), slice(j * node_rows, (j + 1) * node_rows))
                att.append(a[inside].astype(bf16))
                dqt.append(b[inside].astype(bf16))
        att = jnp.concatenate(att, axis=0)
        dq = jnp.concatenate(dqt, axis=0).T
        dk = nn(ds, by_head_n(loc[Q, m], head)).astype(bf16)
        dv = nn(pb, by_head_n(loc[G, m], head)).astype(bf16)
        dq_ref[m], dk_ref[m], dv_ref[m] = dq, dk, dv
        wo_term = nn(att, og_ref[m])
        kv_term = nn(xtf[m], jnp.concatenate([dk, dv], axis=1))
        q_term = nn(xtf[m, :, :node_rows], dq)
        wo_total = wo_term if m == 0 else wo_total + wo_term
        kv_total = kv_term if m == 0 else kv_total + kv_term
        q_total = q_term if m == 0 else q_total + q_term

    planes, _, _, rows, _ = dw.shape
    inner_planes = wos.shape[0]
    dw[:, :, :, :, :128] = q_total.reshape(planes, 2, 2, rows, 128)
    dw[:, :, :, :, 128:] = kv_total.reshape(planes, 2, 2, rows, 256)
    wos[...] = wo_total.reshape(inner_planes, 2, 2, rows, width)
    me = me_ref[0]
    c, y, z = me % 2, (me // 2) % 2, me // 4
    qkv = slice(at, at + 384)
    for k in range(planes):
        zk = plane_of(gray(z) ^ k)
        own_ref[k, :, qkv] = dw[zk, y, c]
        other_ref[k, :, qkv] = dw[zk, 1 - y, c]
        send_other[k, :, qkv] = dw[zk, 1 - y, 1 - c].astype(bf16)
        send_own[k, :, qkv] = dw[zk, y, 1 - c].astype(bf16)
    last = slice(at + 384, at + 512)
    for i in range(inner_planes):
        for n in range(width // 128):
            k = n * inner_planes + i
            lanes = slice(n * 128, (n + 1) * 128)
            own_ref[k, :, last] = wos[i, y, c, :, lanes]
            other_ref[k, :, last] = wos[i, 1 - y, c, :, lanes]
            send_other[k, :, last] = wos[i, 1 - y, 1 - c, :, lanes].astype(bf16)
            send_own[k, :, last] = wos[i, y, 1 - c, :, lanes].astype(bf16)


def node_kernel(groups, skip, *refs):
    refs = refs[skip:]
    dqs, dks, dvs = refs[:groups], refs[groups : 2 * groups], refs[2 * groups : 3 * groups]
    wq_ref, wk_ref, wv_ref, node_ref, plus_ref, minus_ref, right_ref, left_ref = refs[3 * groups :]
    members, node_rows, _ = dqs[0].shape
    slots = plus_ref.shape[2]

    def whole(parts, m):
        return jnp.concatenate([part[m] for part in parts], axis=1)

    for m in range(members):
        spread = nt(whole(dks, m), wk_ref[...]) + nt(whole(dvs, m), wv_ref[...])
        node_ref[m] = spread[:node_rows] + nt(whole(dqs, m), wq_ref[...])
        halo = spread[node_rows:].astype(bf16)
        for ref, order in (
            (plus_ref, (3, 7, 5)),
            (minus_ref, (2, 4, 6)),
            (right_ref, (1,)),
            (left_ref, (0,)),
        ):
            for i, k in enumerate(order):
                ref[m, i] = halo[k * slots : (k + 1) * slots]


def sums(owns, core_in, y_in, k):
    total = jnp.concatenate(
        [
            own[k] + (core[1, k] if len(core.shape) == 4 else core[k]).astype(f32)
            for own, core in zip(owns, core_in)
        ],
        axis=1,
    ) + y_in[k].astype(f32)
    return [total[:, at : at + 512] for at in range(0, total.shape[1], 512)]


def gather_projection(parts, k, planes, projection_ref, start):
    inner_planes = planes * 128 // projection_ref.shape[2]
    quarter, inner = divmod(k, inner_planes)
    for i, part in enumerate(parts):
        plane = start + i * inner_planes + inner
        projection_ref[plane, :, quarter * 128 : (quarter + 1) * 128] = part[:, 384:]


def pack_kernel(pieces, *refs):
    for i, (ref, core) in enumerate(zip(refs[:pieces], refs[pieces:-1])):
        arrived = core[0] if len(core.shape) == 4 else core[...]
        refs[-1][:, :, i * 512 : (i + 1) * 512] = (ref[...] + arrived.astype(f32)).astype(bf16)


def halve(rows, kept_ref, sent_ref):
    for i, row in enumerate(rows):
        if i % 2 == 0:
            kept_ref[i // 2] = row
            continue
        pieces = row.shape[1] // 128
        for n in range(pieces):
            sent_ref[i // 2 * pieces + n] = row[:, n * 128 : (n + 1) * 128].astype(bf16)


def add_received(kept_ref, received_ref):
    planes, _, wide = kept_ref.shape
    pieces = wide // 128
    return [
        kept_ref[i]
        + jnp.concatenate([received_ref[i * pieces + n] for n in range(pieces)], axis=1).astype(f32)
        for i in range(planes)
    ]


def first_kernel(after_ref, own, core_in, y_in, kept_ref, projection_ref, sent_ref):
    planes = own.shape[0]
    rows = []
    for k in range(planes):
        parts = sums([own], [core_in], y_in, k)
        gather_projection(parts, k, planes, projection_ref, 0)
        rows.append(jnp.concatenate([part[:, :384] for part in parts], axis=1))
    halve(rows, kept_ref, sent_ref)


def put(row, ref, at):
    for n in range(row.shape[1] // 128):
        ref[at + n] = row[:, n * 128 : (n + 1) * 128].astype(bf16)


def second_kernel(skip, pieces, me_ref, *refs):
    refs = refs[skip:]
    first_ref, y_in = refs[:2]
    owns, core_in = refs[2 : 2 + pieces], refs[2 + pieces : 2 + 2 * pieces]
    own_b, *sent = refs[2 + 2 * pieces : -1]
    projection_ref = refs[-1]
    done = first_ref.shape[0]
    planes = projection_ref.shape[0]
    projection_ref[:done] = first_ref[...]
    held = []
    for k in range(planes):
        parts = sums(owns, core_in, y_in, k)
        gather_projection(parts, k, planes, projection_ref, done)
        held.append(jnp.concatenate([part[:, :384] for part in parts], axis=1))
    z = me_ref[0] // 4
    for k in range(planes):
        row = jnp.concatenate([held[k], projection_ref[plane_of(gray(z) ^ k)]], axis=1)
        if k:
            put(row, sent[k - 1], 0)
        else:
            own_b[...] = row


def join_kernel(kept_a, in_a, near, *refs):
    count = (len(refs) - 2) // 2
    blocks, own_a, near_out, sent = refs[:count], refs[count], refs[count + 1], refs[count + 2 :]
    near_out[...] = near[...]
    first = add_received(kept_a, in_a)
    own_a[...] = first[0]
    for i, ref in enumerate(sent):
        ref[: blocks[i].shape[0]] = blocks[i][...]
        put(first[i + 1], ref, blocks[i].shape[0])


def finish_kernel(
    me_ref, after_ref, second_in, first_in, send_ref, node_ref, plus_ref, minus_ref, out_ref, came
):
    members, node_rows, _ = node_ref.shape
    pick = sent_selector(send_ref[0], node_rows).astype(bf16)
    from_swaps(came, me_ref[0] % 2, first_in, second_in)
    for m in range(members):
        pieces = [None] * 8
        for side, order in enumerate(((1, 4, 7), (0, 6, 5))):
            for i, k in enumerate(order):
                pieces[k] = came[side, m, i]
        pieces[2], pieces[3] = plus_ref[m, 0], minus_ref[m, 0]
        arriving = jnp.concatenate(pieces, axis=0)
        out_ref[m] = (node_ref[m] + nn(pick, arriving)).astype(bf16)


def weight_kernel(after_ref, own_a, own_b, *refs):
    received, out_ref = refs[-2::-1], refs[-1]
    a, b = own_a[...], own_b[...]
    blocks, more = b.shape[1] // 128, a.shape[1] // 128
    for k, ref in enumerate(received, 1):
        b = b + jnp.concatenate([ref[n] for n in range(blocks)], axis=1).astype(f32)
        if k % 2 == 0:
            a = a + jnp.concatenate([ref[blocks + n] for n in range(more)], axis=1).astype(f32)
    width = out_ref.shape[1] // 4
    group = 0
    for part, wide in ((a, a.shape[1]), (b, b.shape[1] - width)):
        for j in range(0, wide, 384):
            for n in range(3):
                at = n * width + group * 128
                out_ref[:, at : at + 128] = part[:, j + n * 128 : j + (n + 1) * 128]
            group += 1
    out_ref[:, 3 * width :] = b[:, b.shape[1] - width :]


def call(kernel, outs, operands, specs=None, scratch=(), limit=12, final=False, flops=10**6):
    specs = list(specs or ())
    specs += [pltpu.VMEM] * (len(operands) - len(specs))
    operands = [
        pltpu.with_memory_space_constraint(o, s) if s in (pltpu.HBM, pltpu.VMEM) else o
        for o, s in zip(operands, specs)
    ]
    return pl.pallas_call(
        kernel,
        out_shape=[jax.ShapeDtypeStruct(*o) if final else pltpu.VMEM(*o) for o in outs],
        in_specs=[pl.BlockSpec(memory_space=s) for s in specs],
        scratch_shapes=list(scratch),
        compiler_params=pltpu.CompilerParams(vmem_limit_bytes=limit * MIB),
        cost_estimate=pl.CostEstimate(flops=flops, bytes_accessed=10**4, transcendentals=0),
    )(*operands)


def body(
    node_features, out_grad, w_query, w_key, w_value, w_out, neighbours, neighbour_count, send_rows
):
    members, node_rows, width = node_features.shape
    count = lax.axis_size("patch")
    row_width = min(8, count // 4)
    _, adjacent, slots = send_rows.shape
    table = node_rows + adjacent * slots
    groups = width // 128
    me = lax.axis_index("patch")
    three = ((members, 3, slots, width), bf16)
    one = ((members, 1, slots, width), bf16)

    place = me.reshape(1)
    trio = pltpu.VMEM((2, *three[0]), bf16)
    to_plus, to_minus, own_right, own_left, x = call(
        functools.partial(gather_kernel, slots),
        [three, three, one, one, (node_features.shape, bf16)],
        (send_rows, node_features),
        specs=[pltpu.HBM] * 2,
        scratch=[pltpu.VMEM(send_rows.shape, jnp.int32), pltpu.SemaphoreType.DMA((2,))],
    )
    plus = shifted(to_plus, row_width)
    minus = shifted(to_minus, -row_width)
    square = ((width, width), bf16)
    counts = neighbour_count.reshape(1, node_rows)
    *loc, xt, wq, wk, wv, og, neigh, counts = call(
        functools.partial(local_kernel, groups),
        [((8, members, node_rows, 128), bf16)] * groups
        + [((members, width, node_rows), bf16), square, square, square, (out_grad.shape, bf16)]
        + [(neighbours.shape, jnp.int32), (counts.shape, jnp.int32)],
        (own_right, x, w_query, w_key, w_value, out_grad, neighbours, counts, w_out),
        specs=[pl.ANY, pltpu.VMEM] + [pltpu.HBM] * 7,
        scratch=[pltpu.VMEM((width, width), bf16), pltpu.SemaphoreType.DMA((7,))],
        limit=16,
    )
    outgoing = call(
        relay_kernel, [three, three], (place, loc[0], own_right, own_left, plus, minus),
        specs=[pltpu.SMEM, pl.ANY], scratch=[trio],
    )
    arrived = swap(outgoing, 1)
    (mask,) = call(
        mask_kernel, [((table, node_rows), f32)], (outgoing[1], neigh, counts), specs=[pl.ANY]
    )
    own_part = call(
        functools.partial(own_kernel, groups),
        [
            ((3, members, node_rows, 4 * node_rows), f32),
            ((2, members, 8, 4 * node_rows), f32),
        ]
        * groups,
        (*loc, mask),
    )
    *halo, xtf = call(
        halo_kernel,
        [((4, members, node_rows, 128), bf16)] * groups + [((members, width, table), bf16)],
        (place, *arrived[::-1], plus, minus, xt, wk, wv), specs=[pltpu.SMEM], scratch=[trio],
    )

    planes, rows = count // 4, width // count
    inner_planes = planes * 128 // width
    flip = [(i, i ^ 1) for i in range(count)]
    flop = [(i, i ^ 2) for i in range(count)]
    grads = []

    def attention(extra, which, together):
        wide = 512 * len(which)
        sends = [((2, planes, rows, wide), bf16)] if together else [((planes, rows, wide), bf16)] * 2
        outs = call(
            functools.partial(attention_kernel, len(extra), len(which)),
            [((planes, rows, wide), f32)] * 2
            + sends
            + [
                ((members, node_rows, 128), bf16),
                ((members, table, 128), bf16),
                ((members, table, 128), bf16),
            ]
            * len(which),
            (
                place, *extra, *[loc[g] for g in which], *[halo[g] for g in which],
                *[part for g in which for part in own_part[2 * g : 2 * g + 2]], mask, xtf, og,
            ),
            specs=[pltpu.SMEM] + [pl.ANY] * len(extra),
            scratch=[pltpu.VMEM((members, table - node_rows, 512), f32)] * 3
            + [
                pltpu.VMEM((planes, 2, 2, rows, 384), f32),
                pltpu.VMEM((inner_planes, 2, 2, rows, width), f32),
            ],
            limit=32,
        )
        sent = outs[2 : 2 + len(sends)]
        grads.extend(outs[2 + len(sends) :])
        arrived = [lax.ppermute(shard, "patch", flip) for shard in sent]
        return outs[0], outs[1], arrived[0], arrived[-1]

    half = groups - 1
    wide = 384 * half
    own_a, other, core_other, core_own = attention((), range(half), False)
    y_sent = (other + core_other.astype(f32)).astype(bf16)
    y_a = lax.ppermute(y_sent, "patch", flop)
    later = [attention((), range(half, groups), False)]
    own_b, other_b, core_other_b, core_own_b = zip(*later)
    (y_sent,) = call(
        functools.partial(pack_kernel, len(later)), [(other_b[0].shape, bf16)],
        (*other_b, *core_other_b),
    )
    y_b = lax.ppermute(y_sent, "patch", flop)
    node, to_plus, to_minus, own_right, own_left = call(
        functools.partial(node_kernel, groups, 1),
        [((members, node_rows, width), f32), three, three, one, one],
        (y_sent, *grads[0::3], *grads[1::3], *grads[2::3], wq, wk, wv),
        specs=[pl.ANY],
    )
    from_plus = shifted(to_minus, -row_width)
    from_minus = shifted(to_plus, row_width)
    def exchange(sent, distance):
        return lax.ppermute(sent, "patch", along_z(count, distance))

    kept_a, out_a, sent_a = call(
        first_kernel,
        [
            ((planes // 2, rows, wide), f32),
            ((half * inner_planes, rows, width), f32),
            ((planes // 2 * wide // 128, rows, 128), bf16),
        ],
        (node, own_a, core_own, y_a), specs=[pl.ANY], flops=2 * 10**10,
    )
    in_a = exchange(sent_a, 1)
    outgoing = call(
        relay_kernel, [three, three],
        (place, sent_a, own_right, own_left, from_plus, from_minus),
        specs=[pltpu.SMEM, pl.ANY], scratch=[trio],
    )
    back = swap(outgoing, 1)
    last = 384 * (groups - half) + width
    more, blocks = wide // 128, last // 128
    own_b, *sent = call(
        functools.partial(second_kernel, 1, len(later)),
        [((rows, last), f32)] + [((blocks, rows, 128), bf16)] * (planes - 1),
        (place, outgoing[0], out_a, y_b, *own_b, *core_own_b),
        specs=[pltpu.SMEM, pl.ANY],
        scratch=[pltpu.VMEM((planes, rows, width), f32)], flops=4 * 10**9,
    )
    own_a, sent[0], *sent[1::2] = call(
        join_kernel,
        [((rows, wide), f32), ((blocks, rows, 128), bf16)]
        + [((blocks + more, rows, 128), bf16)] * (planes // 2 - 1),
        (kept_a, in_a, sent[0], *sent[1::2]), flops=2 * 10**10,
    )
    received = [exchange(shard, k) for k, shard in enumerate(sent, 1)]
    (node_grad,) = call(
        finish_kernel, [((members, node_rows, width), bf16)],
        (place, sent[0], *back[::-1], send_rows, node, from_plus, from_minus),
        specs=[pltpu.SMEM, pl.ANY], scratch=[trio], final=True, flops=2 * 10**10,
    )
    (weight_grad,) = call(
        weight_kernel, [((rows, 4 * width), f32)], (node_grad, own_a, own_b, *received[::-1]),
        specs=[pltpu.HBM], final=True,
    )
    return (node_grad, weight_grad)


def solution(mesh):
    in_specs = (
        P("groups", "patch", None),
        P("groups", "patch", None),
        P(),
        P(),
        P(),
        P(),
        P("patch", None),
        P("patch"),
        P("patch", None, None),
    )
    out_specs = (P("groups", "patch", None), P(("groups", "patch"), None))
    return jax.shard_map(body, mesh=mesh, in_specs=in_specs, out_specs=out_specs, check_vma=False)
```

```python
import functools
import math

import jax
import jax.numpy as jnp
from jax import lax
from jax.experimental import pallas as pl
from jax.experimental.pallas import tpu as pltpu
from jax.sharding import PartitionSpec as P

HEADS = 16
score_cap = 5.0
MIB = 1024 * 1024
f32 = jnp.float32
bf16 = jnp.bfloat16


def nn(a, b):
    return lax.dot_general(a, b, (((1,), (0,)), ((), ())), preferred_element_type=f32)


def nt(a, b):
    return lax.dot_general(a, b, (((1,), (1,)), ((), ())), preferred_element_type=f32)


def shifted(shard, by):
    count = lax.axis_size("patch")
    return lax.ppermute(shard, "patch", [(i, (i + by) % count) for i in range(count)])


def neighbours_apart(count, stride):
    first, second = [], []
    for i in range(count):
        up, down = (i + stride) % count, (i - stride) % count
        even = i // stride % 2 == 0
        first.append((i, up if even else down))
        second.append((i, down if even else up))
    return first, second


def swap(pair, stride):
    first, second = neighbours_apart(lax.axis_size("patch"), stride)
    later = lax.ppermute(pair[1], "patch", second)
    return [lax.ppermute(pair[0], "patch", first), later]


def to_swaps(both, odd, first_ref, second_ref):
    first_ref[...] = both[odd]
    second_ref[...] = both[1 - odd]


def from_swaps(both, odd, first_ref, second_ref):
    both[1 - odd] = first_ref[...]
    both[odd] = second_ref[...]


def sent_selector(send_rows, node_rows):
    adjacent, slots = send_rows.shape
    halo = adjacent * slots
    wide = jnp.concatenate([send_rows] * adjacent, axis=1)
    own = lax.broadcasted_iota(jnp.int32, (adjacent, halo), 1) // slots == lax.broadcasted_iota(
        jnp.int32, (adjacent, halo), 0
    )
    ids = jnp.sum(jnp.where(own, wide, 0), axis=0, keepdims=True)
    nodes = lax.broadcasted_iota(jnp.int32, (node_rows, halo), 0)
    return jnp.where(nodes == ids, 1.0, 0.0).astype(f32)


def gather_kernel(
    slots, send_hbm, x_hbm, plus_ref, minus_ref, right_ref, left_ref, x_ref, send_ref, sem
):
    copies = [
        pltpu.make_async_copy(send_hbm, send_ref, sem.at[0]),
    ]
    members, node_rows, _ = x_ref.shape
    copies += [
        pltpu.make_async_copy(x_hbm.at[m], x_ref.at[m], sem.at[1 + m]) for m in range(members)
    ]
    for copy in copies:
        copy.start()
    copies[0].wait()
    pick = sent_selector(send_ref[0], node_rows).T.astype(bf16)
    for m in range(members):
        copies[1 + m].wait()
        rows = nn(pick, x_ref[m]).astype(bf16)

        def part(k):
            return rows[k * slots : (k + 1) * slots]

        for ref, order in ((plus_ref, (2, 6, 4)), (minus_ref, (3, 5, 7))):
            for i, k in enumerate(order):
                ref[m, i] = part(k)
        right_ref[m, 0] = part(0)
        left_ref[m, 0] = part(1)


def relay_kernel(
    me_ref, after_ref, own_right, own_left, plus_ref, minus_ref, first_ref, second_ref, both
):
    for side, own in enumerate((own_right, own_left)):
        both[side, :, 0:1] = own[...]
        both[side, :, 1:2] = plus_ref[:, 1 + side : 2 + side]
        both[side, :, 2:3] = minus_ref[:, 1 + side : 2 + side]
    to_swaps(both, me_ref[0] % 2, first_ref, second_ref)


def gray(z):
    return z ^ (z >> 1)


def plane_of(code):
    z = code
    for shift in range(1, 8):
        z = z ^ (code >> shift)
    return z


def along_z(count, distance):
    planes = count // 4
    return [(i, plane_of(gray(i // 4) ^ distance) * 4 + i % 4) for i in range(planes * 4)]


Q, K, V, G, QT, KT, VT, GT = range(8)


def local_kernel(groups, after_ref, x_ref, *refs):
    sources, loc_refs, xt_ref = refs[:7], refs[7 : 7 + groups], refs[7 + groups]
    copied, sem = refs[8 + groups : 15 + groups], refs[-1]
    copies = [
        pltpu.make_async_copy(source, target, sem.at[i])
        for i, (source, target) in enumerate(zip(sources, copied))
    ]
    for copy in copies:
        copy.start()
    members, node_rows, width = x_ref.shape
    x = x_ref[...].reshape(members * node_rows, width)
    for m in range(members):
        xt_ref[m] = x_ref[m].T

    def put(rows, kind):
        for m in range(members):
            for g, ref in enumerate(loc_refs):
                block = rows[m * node_rows : (m + 1) * node_rows, g * 128 : (g + 1) * 128]
                ref[kind, m] = block
                ref[kind + 4, m] = block.T

    wq_ref, wk_ref, wv_ref, og_ref, _, _, wo_ref = copied
    for kind, ref in enumerate((wq_ref, wk_ref, wv_ref)):
        copies[kind].wait()
        put(nn(x, ref[...]).astype(bf16), kind)
    for copy in copies[3:]:
        copy.wait()
    og = og_ref[...].reshape(members * node_rows, width)
    put(nt(og, wo_ref[...]).astype(bf16), G)


def mask_kernel(after_ref, neigh_ref, count_ref, mask_ref):
    neigh = neigh_ref[...].T
    slots, node_rows = neigh.shape
    table = mask_ref.shape[0]
    order = lax.broadcasted_iota(jnp.int32, neigh.shape, 0)
    tail = jnp.where(order >= count_ref[...], neigh, -1)[slots // 2 :]
    half = table // 2
    for part in range(2):
        columns = lax.broadcasted_iota(jnp.int32, (half, node_rows), 0) + part * half
        kept = jnp.ones((half, node_rows), f32)
        for j in range(slots // 2):
            kept = jnp.where(tail[j : j + 1] == columns, 0.0, kept)
        mask_ref[part * half : (part + 1) * half] = kept


def halo_kernel(
    me_ref, second_in, first_in, plus_ref, minus_ref, wk_ref, wv_ref, *refs
):
    halo_refs, xtf_ref, both = refs[:-2], refs[-2], refs[-1]
    members = plus_ref.shape[0]
    from_swaps(both, me_ref[0] % 2, first_in, second_in)
    for m in range(members):
        pieces = [None] * 8
        for side, order in enumerate(((0, 6, 5), (1, 4, 7))):
            for i, k in enumerate(order):
                pieces[k] = both[side, m, i]
        pieces[2] = plus_ref[m, 0]
        pieces[3] = minus_ref[m, 0]
        halo = jnp.concatenate(pieces, axis=0)
        xtf_ref[m] = halo.T
        for kind, w_ref in enumerate((wk_ref, wv_ref)):
            rows = nn(halo, w_ref[...]).astype(bf16)
            for g, ref in enumerate(halo_refs):
                block = rows[:, g * 128 : (g + 1) * 128]
                ref[kind, m] = block
                ref[kind + 2, m] = block.T


STRIP = 64


def by_head_t(block, head):
    row_head = lax.broadcasted_iota(jnp.int32, block.shape, 0) // head
    zero = jnp.zeros_like(block)
    return jnp.concatenate(
        [jnp.where(row_head == h, block, zero) for h in range(block.shape[0] // head)], axis=1
    )


def by_head_n(block, head):
    lane_head = lax.broadcasted_iota(jnp.int32, block.shape, 1) // head
    zero = jnp.zeros_like(block)
    return jnp.concatenate(
        [jnp.where(lane_head == h, block, zero) for h in range(block.shape[1] // head)], axis=0
    )


def unnormalised(scale, score, grad, slope, m, lanes, mask_ref, start):
    columns, node_rows = score.shape[1], mask_ref.shape[1]
    den = jnp.zeros((8, node_rows), f32)
    inner = jnp.zeros((8, node_rows), f32)
    for c in range(0, columns, STRIP):
        box = (m, slice(c, c + STRIP), lanes)
        t = jnp.tanh(score[box] * (scale / score_cap))
        e = jnp.exp2(t * (score_cap / math.log(2.0))) * mask_ref[start + c : start + c + STRIP]
        den = den + jnp.sum(e.reshape(STRIP // 8, 8, node_rows), axis=0)
        inner = inner + jnp.sum((e * grad[box]).reshape(STRIP // 8, 8, node_rows), axis=0)
        score[box] = e
        slope[box] = e * (scale - scale * (t * t))
    return den, inner


def own_kernel(groups, *refs):
    locs, mask_ref, outs = refs[:groups], refs[groups], refs[groups + 1 :]
    _, members, node_rows, _ = locs[0].shape
    head = 128 * groups // HEADS
    scale = 1.0 / math.sqrt(head)
    for g, loc in enumerate(locs):
        own, totals = outs[2 * g : 2 * g + 2]
        score, grad, slope = own.at[0], own.at[1], own.at[2]
        for m in range(members):
            score[m] = nn(loc[K, m], by_head_t(loc[QT, m], head))
            grad[m] = nn(loc[V, m], by_head_t(loc[GT, m], head))
        for m in range(members):
            for h in range(128 // head):
                lanes = slice(h * node_rows, (h + 1) * node_rows)
                den, inner = unnormalised(scale, score, grad, slope, m, lanes, mask_ref, 0)
                totals[0, m, :, lanes] = den
                totals[1, m, :, lanes] = inner


def attention_kernel(extra, here, me_ref, *refs):
    refs = refs[extra:]
    locs, halos, owns = refs[:here], refs[here : 2 * here], refs[2 * here : 4 * here]
    refs = refs[4 * here :]
    mask_ref, xt, xth, og_ref = refs[:4]
    refs = refs[1:]
    xtf = (xt, xth)
    split = 7 if len(refs) == 15 + 3 * (here - 1) else 6
    outs, grads, scratch = refs[3:split], refs[split : split + 3 * here], refs[split + 3 * here :]
    if split == 6:
        outs = (*outs[:2], outs[2].at[0], outs[2].at[1])
    for i in range(here):
        attend(
            me_ref, locs[i], halos[i], owns[2 * i : 2 * i + 2], mask_ref, xtf, og_ref, outs, 512 * i,
            grads[3 * i : 3 * i + 3], scratch,
        )


def attend(me_ref, loc, halo, own, mask_ref, xtf, og_ref, out_refs, at, grad_refs, scratch):
    own_ref, other_ref, send_other, send_own = out_refs
    dq_ref, dk_ref, dv_ref = grad_refs
    score, grad, slope, dw, wos = scratch
    _, members, node_rows, _ = loc.shape
    table = mask_ref.shape[0]
    width = og_ref.shape[2]
    head = width // HEADS
    per = 128 // head
    scale = 1.0 / math.sqrt(head)

    own, totals = own
    for m in range(members):
        score[m] = nn(halo[0, m], by_head_t(loc[QT, m], head))
        grad[m] = nn(halo[1, m], by_head_t(loc[GT, m], head))

    wo_total = None
    kv_total = None
    q_total = None
    for m in range(members):
        probs = []
        for h in range(per):
            lanes = slice(h * node_rows, (h + 1) * node_rows)
            den, inner = unnormalised(scale, score, grad, slope, m, lanes, mask_ref, node_rows)
            r = 1.0 / jnp.sum(den + totals[0, m, :, lanes], axis=0, keepdims=True)
            inner = jnp.sum(inner + totals[1, m, :, lanes], axis=0, keepdims=True) * r
            column = []
            scores = []
            for e, g, w in ((own.at[0], own.at[1], own.at[2]), (score, grad, slope)):
                for c in range(0, e.shape[1], STRIP):
                    box = (m, slice(c, c + STRIP), lanes)
                    column.append((e[box] * r).astype(bf16))
                    scores.append(((w[box] * r) * (g[box] - inner)).astype(bf16))
            probs.append((jnp.concatenate(column, axis=0), jnp.concatenate(scores, axis=0)))
        pb = jnp.concatenate([p for p, _ in probs], axis=1)
        ds = jnp.concatenate([s for _, s in probs], axis=1)
        ktg = jnp.concatenate([loc[KT, m], halo[2, m]], axis=1)
        vtg = jnp.concatenate([loc[VT, m], halo[3, m]], axis=1)
        att, dqt = [], []
        for h in range(0, per, 2):
            lanes = slice(h * node_rows, (h + 2) * node_rows)
            rows = slice(h * head, (h + 2) * head)
            a = nn(vtg[rows], pb[:, lanes])
            b = nn(ktg[rows], ds[:, lanes])
            for j in range(2):
                inside = (slice(j * head, (j + 1) * head), slice(j * node_rows, (j + 1) * node_rows))
                att.append(a[inside].astype(bf16))
                dqt.append(b[inside].astype(bf16))
        att = jnp.concatenate(att, axis=0)
        dq = jnp.concatenate(dqt, axis=0).T
        dk = nn(ds, by_head_n(loc[Q, m], head)).astype(bf16)
        dv = nn(pb, by_head_n(loc[G, m], head)).astype(bf16)
        dq_ref[m], dk_ref[m], dv_ref[m] = dq, dk, dv
        wo_term = nn(att, og_ref[m])
        kv_term = nn(jnp.concatenate([xtf[0][m], xtf[1][m]], axis=1), jnp.concatenate([dk, dv], axis=1))
        q_term = nn(xtf[0][m], dq)
        wo_total = wo_term if m == 0 else wo_total + wo_term
        kv_total = kv_term if m == 0 else kv_total + kv_term
        q_total = q_term if m == 0 else q_total + q_term

    planes, _, _, rows, _ = dw.shape
    inner_planes = wos.shape[0]
    dw[:, :, :, :, :128] = q_total.reshape(planes, 2, 2, rows, 128)
    dw[:, :, :, :, 128:] = kv_total.reshape(planes, 2, 2, rows, 256)
    wos[...] = wo_total.reshape(inner_planes, 2, 2, rows, width)
    me = me_ref[0]
    c, y, z = me % 2, (me // 2) % 2, me // 4
    qkv = slice(at, at + 384)
    for k in range(planes):
        zk = plane_of(gray(z) ^ k)
        own_ref[k, :, qkv] = dw[zk, y, c]
        other_ref[k, :, qkv] = dw[zk, 1 - y, c]
        send_other[k, :, qkv] = dw[zk, 1 - y, 1 - c].astype(bf16)
        send_own[k, :, qkv] = dw[zk, y, 1 - c].astype(bf16)
    last = slice(at + 384, at + 512)
    for i in range(inner_planes):
        for n in range(width // 128):
            k = n * inner_planes + i
            lanes = slice(n * 128, (n + 1) * 128)
            own_ref[k, :, last] = wos[i, y, c, :, lanes]
            other_ref[k, :, last] = wos[i, 1 - y, c, :, lanes]
            send_other[k, :, last] = wos[i, 1 - y, 1 - c, :, lanes].astype(bf16)
            send_own[k, :, last] = wos[i, y, 1 - c, :, lanes].astype(bf16)


def node_kernel(groups, skip, *refs):
    refs = refs[skip:]
    dqs, dks, dvs = refs[:groups], refs[groups : 2 * groups], refs[2 * groups : 3 * groups]
    wq_ref, wk_ref, wv_ref, node_ref, plus_ref, minus_ref, right_ref, left_ref = refs[3 * groups :]
    members, node_rows, _ = dqs[0].shape
    slots = plus_ref.shape[2]

    def whole(parts, m):
        return jnp.concatenate([part[m] for part in parts], axis=1)

    for m in range(members):
        spread = nt(whole(dks, m), wk_ref[...]) + nt(whole(dvs, m), wv_ref[...])
        node_ref[m] = spread[:node_rows] + nt(whole(dqs, m), wq_ref[...])
        halo = spread[node_rows:].astype(bf16)
        for ref, order in (
            (plus_ref, (3, 7, 5)),
            (minus_ref, (2, 4, 6)),
            (right_ref, (1,)),
            (left_ref, (0,)),
        ):
            for i, k in enumerate(order):
                ref[m, i] = halo[k * slots : (k + 1) * slots]


def sums(owns, core_in, y_in, k):
    total = jnp.concatenate(
        [
            own[k] + (core[1, k] if len(core.shape) == 4 else core[k]).astype(f32)
            for own, core in zip(owns, core_in)
        ],
        axis=1,
    ) + y_in[k].astype(f32)
    return [total[:, at : at + 512] for at in range(0, total.shape[1], 512)]


def gather_projection(parts, k, planes, projection_ref, start):
    inner_planes = planes * 128 // projection_ref.shape[2]
    quarter, inner = divmod(k, inner_planes)
    for i, part in enumerate(parts):
        plane = start + i * inner_planes + inner
        projection_ref[plane, :, quarter * 128 : (quarter + 1) * 128] = part[:, 384:]


def pack_kernel(pieces, *refs):
    for i, (ref, core) in enumerate(zip(refs[:pieces], refs[pieces:-1])):
        arrived = core[0] if len(core.shape) == 4 else core[...]
        refs[-1][:, :, i * 512 : (i + 1) * 512] = (ref[...] + arrived.astype(f32)).astype(bf16)


def halve(rows, kept_ref, sent_ref):
    for i, row in enumerate(rows):
        if i % 2 == 0:
            kept_ref[i // 2] = row
            continue
        pieces = row.shape[1] // 128
        for n in range(pieces):
            sent_ref[i // 2 * pieces + n] = row[:, n * 128 : (n + 1) * 128].astype(bf16)


def add_received(kept_ref, received_ref):
    planes, _, wide = kept_ref.shape
    pieces = wide // 128
    return [
        kept_ref[i]
        + jnp.concatenate([received_ref[i * pieces + n] for n in range(pieces)], axis=1).astype(f32)
        for i in range(planes)
    ]


def first_kernel(after_ref, own, core_in, y_in, kept_ref, projection_ref, sent_ref):
    planes = own.shape[0]
    rows = []
    for k in range(planes):
        parts = sums([own], [core_in], y_in, k)
        gather_projection(parts, k, planes, projection_ref, 0)
        rows.append(jnp.concatenate([part[:, :384] for part in parts], axis=1))
    halve(rows, kept_ref, sent_ref)


def put(row, ref, at):
    for n in range(row.shape[1] // 128):
        ref[at + n] = row[:, n * 128 : (n + 1) * 128].astype(bf16)


def second_kernel(skip, pieces, me_ref, *refs):
    refs = refs[skip:]
    first_ref, y_in = refs[:2]
    owns, core_in = refs[2 : 2 + pieces], refs[2 + pieces : 2 + 2 * pieces]
    own_b, *sent = refs[2 + 2 * pieces : -1]
    projection_ref = refs[-1]
    done = first_ref.shape[0]
    planes = projection_ref.shape[0]
    projection_ref[:done] = first_ref[...]
    held = []
    for k in range(planes):
        parts = sums(owns, core_in, y_in, k)
        gather_projection(parts, k, planes, projection_ref, done)
        held.append(jnp.concatenate([part[:, :384] for part in parts], axis=1))
    z = me_ref[0] // 4
    for k in range(planes):
        row = jnp.concatenate([held[k], projection_ref[plane_of(gray(z) ^ k)]], axis=1)
        if k:
            put(row, sent[k - 1], 0)
        else:
            own_b[...] = row


def join_kernel(kept_a, in_a, *refs):
    count = (len(refs) - 1) // 2
    blocks, own_a, sent = refs[:count], refs[count], refs[count + 1 :]
    first = add_received(kept_a, in_a)
    own_a[...] = first[0]
    for i, ref in enumerate(sent):
        ref[: blocks[i].shape[0]] = blocks[i][...]
        put(first[i + 1], ref, blocks[i].shape[0])


def finish_kernel(
    me_ref, after_ref, second_in, first_in, send_ref, node_ref, plus_ref, minus_ref, out_ref, came
):
    members, node_rows, _ = node_ref.shape
    pick = sent_selector(send_ref[0], node_rows).astype(bf16)
    from_swaps(came, me_ref[0] % 2, first_in, second_in)
    for m in range(members):
        pieces = [None] * 8
        for side, order in enumerate(((1, 4, 7), (0, 6, 5))):
            for i, k in enumerate(order):
                pieces[k] = came[side, m, i]
        pieces[2], pieces[3] = plus_ref[m, 0], minus_ref[m, 0]
        arriving = jnp.concatenate(pieces, axis=0)
        out_ref[m] = (node_ref[m] + nn(pick, arriving)).astype(bf16)


def weight_kernel(after_ref, own_a, own_b, *refs):
    received, out_ref = refs[-2::-1], refs[-1]
    a, b = own_a[...], own_b[...]
    blocks, more = b.shape[1] // 128, a.shape[1] // 128
    for k, ref in enumerate(received, 1):
        b = b + jnp.concatenate([ref[n] for n in range(blocks)], axis=1).astype(f32)
        if k % 2 == 0:
            a = a + jnp.concatenate([ref[blocks + n] for n in range(more)], axis=1).astype(f32)
    width = out_ref.shape[1] // 4
    group = 0
    for part, wide in ((a, a.shape[1]), (b, b.shape[1] - width)):
        for j in range(0, wide, 384):
            for n in range(3):
                at = n * width + group * 128
                out_ref[:, at : at + 128] = part[:, j + n * 128 : j + (n + 1) * 128]
            group += 1
    out_ref[:, 3 * width :] = b[:, b.shape[1] - width :]


def call(kernel, outs, operands, specs=None, scratch=(), limit=12, final=False, flops=10**6):
    specs = list(specs or ())
    specs += [pltpu.VMEM] * (len(operands) - len(specs))
    operands = [
        pltpu.with_memory_space_constraint(o, s) if s in (pltpu.HBM, pltpu.VMEM) else o
        for o, s in zip(operands, specs)
    ]
    return pl.pallas_call(
        kernel,
        out_shape=[jax.ShapeDtypeStruct(*o) if final else pltpu.VMEM(*o) for o in outs],
        in_specs=[pl.BlockSpec(memory_space=s) for s in specs],
        scratch_shapes=list(scratch),
        compiler_params=pltpu.CompilerParams(vmem_limit_bytes=limit * MIB),
        cost_estimate=pl.CostEstimate(flops=flops, bytes_accessed=10**4, transcendentals=0),
    )(*operands)


def body(
    node_features, out_grad, w_query, w_key, w_value, w_out, neighbours, neighbour_count, send_rows
):
    members, node_rows, width = node_features.shape
    count = lax.axis_size("patch")
    row_width = min(8, count // 4)
    _, adjacent, slots = send_rows.shape
    table = node_rows + adjacent * slots
    groups = width // 128
    me = lax.axis_index("patch")
    three = ((members, 3, slots, width), bf16)
    one = ((members, 1, slots, width), bf16)

    place = me.reshape(1)
    trio = pltpu.VMEM((2, *three[0]), bf16)
    to_plus, to_minus, own_right, own_left, x = call(
        functools.partial(gather_kernel, slots),
        [three, three, one, one, (node_features.shape, bf16)],
        (send_rows, node_features),
        specs=[pltpu.HBM] * 2,
        scratch=[pltpu.VMEM(send_rows.shape, jnp.int32), pltpu.SemaphoreType.DMA((1 + members,))],
    )
    plus = shifted(to_plus, row_width)
    minus = shifted(to_minus, -row_width)
    square = ((width, width), bf16)
    counts = neighbour_count.reshape(1, node_rows)
    *loc, xt, wq, wk, wv, og, neigh, counts = call(
        functools.partial(local_kernel, groups),
        [((8, members, node_rows, 128), bf16)] * groups
        + [((members, width, node_rows), bf16), square, square, square, (out_grad.shape, bf16)]
        + [(neighbours.shape, jnp.int32), (counts.shape, jnp.int32)],
        (own_right, x, w_query, w_key, w_value, out_grad, neighbours, counts, w_out),
        specs=[pl.ANY, pltpu.VMEM] + [pltpu.HBM] * 7,
        scratch=[pltpu.VMEM((width, width), bf16), pltpu.SemaphoreType.DMA((7,))],
        limit=16,
    )
    outgoing = call(
        relay_kernel, [three, three], (place, loc[0], own_right, own_left, plus, minus),
        specs=[pltpu.SMEM, pl.ANY], scratch=[trio],
    )
    arrived = swap(outgoing, 1)
    (mask,) = call(
        mask_kernel, [((table, node_rows), f32)], (outgoing[1], neigh, counts), specs=[pl.ANY]
    )
    own_part = call(
        functools.partial(own_kernel, groups),
        [
            ((3, members, node_rows, 4 * node_rows), f32),
            ((2, members, 8, 4 * node_rows), f32),
        ]
        * groups,
        (*loc, mask),
    )
    *halo, xtf = call(
        halo_kernel,
        [((4, members, node_rows, 128), bf16)] * groups
        + [((members, width, table - node_rows), bf16)],
        (place, *arrived[::-1], plus, minus, wk, wv), specs=[pltpu.SMEM], scratch=[trio],
    )

    planes, rows = count // 4, width // count
    inner_planes = planes * 128 // width
    flip = [(i, i ^ 1) for i in range(count)]
    flop = [(i, i ^ 2) for i in range(count)]
    grads = []

    def attention(extra, which, together):
        wide = 512 * len(which)
        sends = [((2, planes, rows, wide), bf16)] if together else [((planes, rows, wide), bf16)] * 2
        outs = call(
            functools.partial(attention_kernel, len(extra), len(which)),
            [((planes, rows, wide), f32)] * 2
            + sends
            + [
                ((members, node_rows, 128), bf16),
                ((members, table, 128), bf16),
                ((members, table, 128), bf16),
            ]
            * len(which),
            (
                place, *extra, *[loc[g] for g in which], *[halo[g] for g in which],
                *[part for g in which for part in own_part[2 * g : 2 * g + 2]], mask, xt, xtf, og,
            ),
            specs=[pltpu.SMEM] + [pl.ANY] * len(extra),
            scratch=[pltpu.VMEM((members, table - node_rows, 512), f32)] * 3
            + [
                pltpu.VMEM((planes, 2, 2, rows, 384), f32),
                pltpu.VMEM((inner_planes, 2, 2, rows, width), f32),
            ],
            limit=32,
        )
        sent = outs[2 : 2 + len(sends)]
        grads.extend(outs[2 + len(sends) :])
        arrived = [lax.ppermute(shard, "patch", flip) for shard in sent]
        return outs[0], outs[1], arrived[0], arrived[-1]

    half = groups - 1
    wide = 384 * half
    own_a, other, core_other, core_own = attention((), range(half), False)
    y_sent = (other + core_other.astype(f32)).astype(bf16)
    y_a = lax.ppermute(y_sent, "patch", flop)
    later = [attention((), range(half, groups), False)]
    own_b, other_b, core_other_b, core_own_b = zip(*later)
    (y_sent,) = call(
        functools.partial(pack_kernel, len(later)), [(other_b[0].shape, bf16)],
        (*other_b, *core_other_b),
    )
    y_b = lax.ppermute(y_sent, "patch", flop)
    node, to_plus, to_minus, own_right, own_left = call(
        functools.partial(node_kernel, groups, 1),
        [((members, node_rows, width), f32), three, three, one, one],
        (y_sent, *grads[0::3], *grads[1::3], *grads[2::3], wq, wk, wv),
        specs=[pl.ANY],
    )
    from_plus = shifted(to_minus, -row_width)
    from_minus = shifted(to_plus, row_width)
    def exchange(sent, distance):
        return lax.ppermute(sent, "patch", along_z(count, distance))

    kept_a, out_a, sent_a = call(
        first_kernel,
        [
            ((planes // 2, rows, wide), f32),
            ((half * inner_planes, rows, width), f32),
            ((planes // 2 * wide // 128, rows, 128), bf16),
        ],
        (node, own_a, core_own, y_a), specs=[pl.ANY], flops=2 * 10**10,
    )
    in_a = exchange(sent_a, 1)
    outgoing = call(
        relay_kernel, [three, three],
        (place, sent_a, own_right, own_left, from_plus, from_minus),
        specs=[pltpu.SMEM, pl.ANY], scratch=[trio],
    )
    back = swap(outgoing, 1)
    last = 384 * (groups - half) + width
    more, blocks = wide // 128, last // 128
    own_b, *sent = call(
        functools.partial(second_kernel, 1, len(later)),
        [((rows, last), f32)] + [((blocks, rows, 128), bf16)] * (planes - 1),
        (place, outgoing[0], out_a, y_b, *own_b, *core_own_b),
        specs=[pltpu.SMEM, pl.ANY],
        scratch=[pltpu.VMEM((planes, rows, width), f32)], flops=4 * 10**9,
    )
    own_a, *sent[1::2] = call(
        join_kernel,
        [((rows, wide), f32)] + [((blocks + more, rows, 128), bf16)] * (planes // 2 - 1),
        (kept_a, in_a, *sent[1::2]), flops=2 * 10**10,
    )
    received = [exchange(shard, k) for k, shard in enumerate(sent, 1)]
    (node_grad,) = call(
        finish_kernel, [((members, node_rows, width), bf16)],
        (place, sent[0], *back[::-1], send_rows, node, from_plus, from_minus),
        specs=[pltpu.SMEM, pl.ANY], scratch=[trio], final=True, flops=2 * 10**10,
    )
    (weight_grad,) = call(
        weight_kernel, [((rows, 4 * width), f32)], (node_grad, own_a, own_b, *received[::-1]),
        specs=[pltpu.HBM], final=True,
    )
    return (node_grad, weight_grad)


def solution(mesh):
    in_specs = (
        P("groups", "patch", None),
        P("groups", "patch", None),
        P(),
        P(),
        P(),
        P(),
        P("patch", None),
        P("patch"),
        P("patch", None, None),
    )
    out_specs = (P("groups", "patch", None), P(("groups", "patch"), None))
    return jax.shard_map(body, mesh=mesh, in_specs=in_specs, out_specs=out_specs, check_vma=False)
```
